32 devices in a mesh: dp: 2 (over x), seq: 16 (over z, y, core).
Axes of the slice: x: 2, y: 2, z: 4, core: 2. Of those that a mesh axis runs over, the one named last changes fastest.
Arguments:
- tokens: bfloat16 [4, 2048, 768], P('dp', 'seq'), may hold values from -6 to 6
- char_ids: int32 [4, 8192], P('dp', 'seq'), may hold values from 0 to 249
- span_lengths: int32 [4, 16, 128], P('dp', 'seq'), may hold values from 1 to 12, 512 in all within a row
- script_group: int32 [4], P('dp'), may hold values from 0 to 3
- w_qkv: bfloat16 [768, 2304], P('seq'), may hold values from -0.21875 to 0.21875
- w_out: bfloat16 [768, 768], P('seq'), may hold values from -4 to 4
- w_up: bfloat16 [768, 3072], P('seq'), may hold values from -0.21875 to 0.21875
- w_down: bfloat16 [3072, 768], P('seq'), may hold values from -0.109375 to 0.109375
- char_table: bfloat16 [256, 1000], P('seq'), may hold values from -6 to 6
- w_gru: bfloat16 [256, 1536], P('seq'), may hold values from -0.375 to 0.375
- gru_bias: bfloat16 [1536], P('seq'), may hold values from -11 to 2.5
- w_stream: bfloat16 [2, 768, 768], P(None, 'seq'), may hold values from -0.21875 to 0.21875
- w_conv: bfloat16 [3, 1536, 1536], P(None, 'seq'), may hold values from -0.09375 to 0.09375
- norms: bfloat16 [4, 2, 768], P(None, None, 'seq'), may hold values from 0.25 to 1.75
- grad_token: bfloat16 [4, 2048, 768], P('dp', 'seq'), may hold values from -6 to 6
- grad_char: bfloat16 [4, 2048, 768], P('dp', 'seq'), may hold values from -6 to 6
Outputs:
- out_token: bfloat16 [4, 2048, 768], P('dp', 'seq')
- out_char: bfloat16 [4, 2048, 768], P('dp', 'seq')
- grad_tokens: float32 [4, 2048, 768], P('dp', 'seq')
- grad_w_qkv: float32 [768, 2304], P('seq')
- grad_w_out: float32 [768, 768], P('seq')
- grad_w_up: float32 [768, 3072], P('seq')
- grad_w_down: float32 [3072, 768], P('seq')
- grad_char_table: float32 [256, 1000], P('seq')
- grad_w_gru: float32 [256, 1536], P('seq')
- grad_gru_bias: float32 [1536], P('seq')
- grad_w_stream: float32 [2, 768, 768], P(None, 'seq')
- grad_w_conv: float32 [3, 1536, 1536], P(None, 'seq')
- grad_norms: float32 [4, 2, 768], P(None, None, 'seq')
The draws below stay inside these ranges and needn't reach their ends.
Inputs may be any that keep to these rules, and one draw needn't show every extreme that they name: `span_lengths`: each row sums to 512.
All inputs are finite; a program needn't handle non-finite values.
Results may differ from the reference program's by a relative error of at most 0.025.
Values may be sent and summed in bfloat16 or wider, within the bound.
A program may use at most 192 MiB of HBM per device.

```python
import math
import jax
import jax.numpy as jnp
import numpy as np
from jax import lax

D = 768
HEADS = 12
HDIM = 64
FF = 3072
CE = 256
VOCAB_CHAR = 1000
GROUPS = 4
SPAN_MOST = 12
HGRU = 384
GROUP_CHARS = 250
TSEQ = 128
LEN = 2048
CH_DEV = 512
CLEN = 8192
SEQS = 4
N_SEQ = 16


def draw_gru_bias(key, part):
    key = jax.random.fold_in(key, 11)
    pick_key, slow_key, fast_key, cand_key = jax.random.split(key, 4)
    unit_count = 2 * HGRU
    fast_share = 0.5
    cand_floor = -2.0
    cand_ceiling = 2.0
    slow_rate = jnp.exp(jax.random.uniform(slow_key, (unit_count,), jnp.float32, jnp.log(0.2 / CLEN), jnp.log(2.0 / CLEN)))
    fast_rate = jnp.exp(jax.random.uniform(fast_key, (unit_count,), jnp.float32, jnp.log(1.0 / 50.0), jnp.log(1.0 / 30.0)))
    chosen = jax.random.uniform(pick_key, (unit_count,), jnp.float32) < fast_share
    rates_all = jnp.where(chosen, fast_rate, slow_rate)
    gate_bias = jnp.maximum(jnp.log(rates_all) - jnp.log1p(-rates_all), -11.0)
    cand_bias = jax.random.uniform(cand_key, (unit_count,), jnp.float32, cand_floor, cand_ceiling)
    return jnp.concatenate([gate_bias[:HGRU], cand_bias[:HGRU], gate_bias[HGRU:], cand_bias[HGRU:]]).astype(jnp.bfloat16)


def touch_ends(entries, key, smallest, largest):
    longest = entries.shape.index(max(entries.shape))
    spots = []
    for shift in (0, 1):
        where = [jax.random.randint(jax.random.fold_in(key, axis), (), 0, length) for axis, length in enumerate(entries.shape)]
        where[longest] = (where[longest] + shift) % entries.shape[longest]
        spots.append(tuple(where))
    return entries.at[spots[0]].set(smallest).at[spots[1]].set(largest)


def level_of(key, shape, shards, smallest, top_value):
    loudness = 1.0
    for axis_at, parts in shards:
        steps = jax.random.uniform(jax.random.fold_in(jax.random.fold_in(key, 6), axis_at), (parts,), jnp.float32, smallest / len(shards), top_value / len(shards))
        loudness = loudness * jnp.repeat(jnp.exp(steps), shape[axis_at] // parts).reshape((-1,) + (1,) * (len(shape) - 1 - axis_at))
    return loudness


def profile(number_of, total, most, lean):
    loads = [(1 << 20) // math.isqrt(rank ** lean) + 1 for rank in range(2, number_of + 1)]
    rest, holding = total - most - (number_of - 1), [1] * (number_of - 1)
    while rest > 0:
        free = [i for i in range(number_of - 1) if holding[i] < most]
        pool, remaining = sum([loads[i] for i in free]), rest
        for i in free:
            addition = min(most - holding[i], max(1, remaining * loads[i] // pool), rest)
            holding[i] = holding[i] + addition
            rest = rest - addition
    return np.array([most] + holding)


def uneven(rng, count, total, limit, skew):
    if count == 2:
        one = jax.random.randint(rng, (), max(1, total - limit), min(limit, total - 1) + 1)
        return jnp.stack([one, total - one])
    lengths = jnp.asarray(profile(count, total, limit, skew), jnp.int32)
    couples = (count - 1) // 2
    source_of, sink = lengths[1:1 + 2 * couples:2], lengths[2:2 + 2 * couples:2]
    slack = jnp.minimum(source_of - 1, limit - sink)
    moved = jax.random.randint(jax.random.fold_in(rng, 1), (couples,), 0, 1 << 20) % (slack + 1)
    lengths = lengths.at[1:1 + 2 * couples:2].set(source_of - moved).at[2:2 + 2 * couples:2].set(sink + moved)
    return lengths[jax.random.permutation(jax.random.fold_in(rng, 2), count)]


def noise(own_key, dims, scale, limit, shards=(), kind=jnp.bfloat16):
    factor_of = level_of(own_key, dims, shards, -0.22, 0.18) if shards else 1.0
    array = jax.random.normal(own_key, dims, jnp.float32) * scale * factor_of
    return jnp.minimum(jnp.maximum(array, -limit), limit).astype(kind)


def setup_inputs(seed: int = 0) -> dict:
    splits = jax.random.split(jax.random.key(seed), 17)
    tokens = noise(splits[0], (SEQS, LEN, D), 1.0, 6.0, ((0, 2), (1, 16)))
    char_ids = touch_ends(jax.random.randint(splits[1], (SEQS, CLEN), 0, GROUP_CHARS), jax.random.fold_in(splits[1], 1), 0, GROUP_CHARS - 1).astype(jnp.int32)
    span_lengths = jax.vmap(lambda own: uneven(own, TSEQ, CH_DEV, SPAN_MOST, 0))(jax.random.split(splits[2], SEQS * N_SEQ)).reshape((SEQS, N_SEQ, TSEQ)).astype(jnp.int32)
    script_group = touch_ends(jax.random.randint(splits[3], (SEQS,), 0, GROUPS), jax.random.fold_in(splits[3], 1), 0, GROUPS - 1).astype(jnp.int32)
    w_qkv = noise(splits[4], (D, 3 * D), D ** -0.5, 0.21875, ((0, 16),))
    w_out = noise(splits[5], (D, D), 2 ** -0.5, 4.0, ((0, 16),))
    w_up = noise(splits[6], (D, FF), D ** -0.5, 0.21875, ((0, 16),))
    w_down = noise(splits[7], (FF, D), FF ** -0.5, 0.109375, ((0, 16),))
    char_table = noise(splits[8], (CE, VOCAB_CHAR), 1.0, 6.0, ((0, 16),))
    w_gru = noise(splits[9], (CE, 4 * HGRU), CE ** -0.5, 0.375, ((0, 16),))
    gru_bias = draw_gru_bias(jax.random.fold_in(splits[16], 71), 0)
    w_stream = noise(splits[11], (2, D, D), D ** -0.5, 0.21875, ((1, 16),))
    w_conv = noise(splits[12], (3, 2 * D, 2 * D), (6 * D) ** -0.5, 0.09375, ((1, 16),))
    norms = jnp.clip(1.0 + 0.15 * jax.random.normal(splits[13], (4, 2, D), jnp.float32), 0.25, 1.75).astype(jnp.bfloat16)
    grad_token = noise(splits[14], (SEQS, LEN, D), 1.0, 6.0, ((0, 2), (1, 16)))
    grad_char = noise(splits[15], (SEQS, LEN, D), 1.0, 6.0, ((0, 2), (1, 16)))
    return {"tokens": tokens, "char_ids": char_ids, "span_lengths": span_lengths, "script_group": script_group, "w_qkv": w_qkv, "w_out": w_out, "w_up": w_up, "w_down": w_down, "char_table": char_table, "w_gru": w_gru, "gru_bias": gru_bias, "w_stream": w_stream, "w_conv": w_conv, "norms": norms, "grad_token": grad_token, "grad_char": grad_char}


@jax.custom_vjp
def low(v):
    return lax.optimization_barrier(v.astype(jnp.bfloat16)).astype(jnp.float32)

@jax.custom_vjp
def low_back(v):
    return v

def low_keep(v):
    return (low(v), None)

def low_pass(kept, grad):
    return (grad,)

def back_keep(v):
    return (v, None)

def back_low(kept, grad):
    return (low(grad),)
low.defvjp(low_keep, low_pass)
low_back.defvjp(back_keep, back_low)
HIGHEST = lax.Precision.HIGHEST
EPSILON = 1e-05

def layer_norm(values, gain_row, shift_row):
    center = values - lax.optimization_barrier(jnp.mean(values, -1, keepdims=True))
    spread = lax.optimization_barrier(jnp.mean(center * center, -1, keepdims=True))
    return center * lax.rsqrt(spread + EPSILON) * gain_row + shift_row

def product(left_side, right_side):
    return jnp.dot(left_side, right_side, precision=HIGHEST, preferred_element_type=jnp.float32)

def attention(query_rows, key_rows, value_rows):
    length = query_rows.shape[0]
    block_rows = math.gcd(length, 512)
    scale_factor = HDIM ** (-0.5)
    query_heads = query_rows.reshape(length // block_rows, block_rows, HEADS, HDIM)
    key_heads = key_rows.reshape(length, HEADS, HDIM)
    value_heads = value_rows.reshape(length, HEADS, HDIM)

    def one_block(query_block):
        scores = jnp.einsum('qhd,khd->hqk', query_block, key_heads, precision=HIGHEST) * scale_factor
        probability = low(jax.nn.softmax(low_back(scores), axis=-1))
        return jnp.einsum('hqk,khd->qhd', probability, value_heads, precision=HIGHEST)
    context = lax.map(jax.checkpoint(one_block), query_heads)
    return context.reshape(length, HEADS * HDIM)

def recurrence(rate_rows, drives, reverse):

    def advance(state_now, inputs):
        rate_now, drive_now = inputs
        state_now = (1.0 - rate_now) * state_now + drive_now
        return (state_now, state_now)
    start_state = jnp.zeros((rate_rows.shape[1],), jnp.float32)
    _, states = lax.scan(advance, start_state, (rate_rows, drives), reverse=reverse)
    return states

def layer_forward(weights, inputs, char_rows, span_count):
    w_qkv, w_out, w_up, w_down, char_table, w_gru, gru_bias, w_stream, w_conv, norms = weights
    model_width = inputs.shape[1]
    half_width = model_width // 2
    qkv_rows = low(low_back(product(inputs, w_qkv)))
    context = attention(qkv_rows[:, :model_width], qkv_rows[:, model_width:2 * model_width], qkv_rows[:, 2 * model_width:])
    context = low(low_back(context))
    attended = low_back(product(context, w_out))
    normed = layer_norm(inputs + attended, norms[0, 0], norms[0, 1])
    raised = low_back(product(low(normed), w_up))
    hidden = low(jax.nn.gelu(raised))
    lowered = low_back(product(hidden, w_down))
    token_state = layer_norm(normed + lowered, norms[1, 0], norms[1, 1])
    embedded = low_back(jnp.transpose(char_table)[char_rows])
    preact = low_back(product(embedded, w_gru) + gru_bias)
    rate_f = jax.nn.sigmoid(preact[:, :half_width])
    cand_f = preact[:, half_width:2 * half_width]
    rate_b = jax.nn.sigmoid(preact[:, 2 * half_width:3 * half_width])
    cand_b = preact[:, 3 * half_width:]
    states_f = recurrence(rate_f, rate_f * cand_f, False)
    states_b = recurrence(rate_b, rate_b * cand_b, True)
    char_states = low(jnp.concatenate([states_f, states_b], -1))
    blocks = span_count.shape[0]
    per_block = char_states.shape[0] // blocks
    span_ends = jnp.cumsum(span_count, -1).astype(jnp.int32)
    starts = span_ends - span_count
    char_place = jnp.arange(per_block, dtype=jnp.int32)
    member = ((char_place >= starts[..., None]) & (char_place < span_ends[..., None])).astype(jnp.float32)
    summed = jnp.einsum('btc,bcd->btd', member, char_states.reshape(blocks, per_block, model_width), precision=HIGHEST)
    pooled = low_back((summed / span_count[..., None].astype(jnp.float32)).reshape(-1, model_width))
    merged = jnp.concatenate([product(low(token_state), w_stream[0]), product(low(pooled), w_stream[1])], -1)
    merged = low(low_back(merged))
    zero_row = jnp.zeros((1, merged.shape[1]), jnp.float32)
    before = jnp.concatenate([zero_row, merged[:-1]], 0)
    after = jnp.concatenate([merged[1:], zero_row], 0)
    mixed_rows = low_back(product(before, w_conv[0]) + product(merged, w_conv[1]) + product(after, w_conv[2]))
    gated_rows = jax.nn.gelu(mixed_rows)
    out_token = layer_norm(token_state + gated_rows[:, :model_width], norms[2, 0], norms[2, 1])
    out_char = layer_norm(pooled + gated_rows[:, model_width:], norms[3, 0], norms[3, 1])
    return (out_token, out_char)

def reference(tokens, char_ids, span_lengths, script_group, w_qkv, w_out, w_up, w_down, char_table, w_gru, gru_bias, w_stream, w_conv, norms, grad_token, grad_char):
    weights = tuple((item.astype(jnp.float32) for item in (w_qkv, w_out, w_up, w_down, char_table, w_gru, gru_bias, w_stream, w_conv, norms)))

    def per_sequence(totals, seq_items):
        token_seq, ids_seq, spans_seq, group_seq, cot_token, cot_char = seq_items
        char_rows = (ids_seq + group_seq * GROUP_CHARS).astype(jnp.int32)

        def run_layer(layer_weights, inputs):
            return layer_forward(layer_weights, inputs, char_rows, spans_seq)
        outputs, pullback = jax.vjp(run_layer, weights, token_seq.astype(jnp.float32))
        weight_grads, input_grad = pullback((cot_token.astype(jnp.float32), cot_char.astype(jnp.float32)))
        totals = jax.tree.map(jnp.add, totals, weight_grads)
        return (totals, (outputs[0].astype(jnp.bfloat16), outputs[1].astype(jnp.bfloat16), input_grad))
    zero_grads = tuple((jnp.zeros_like(item) for item in weights))
    totals, (out_token, out_char, grad_tokens) = lax.scan(per_sequence, zero_grads, (tokens, char_ids, span_lengths, script_group, grad_token, grad_char))
    return (out_token, out_char, grad_tokens, totals[0], totals[1], totals[2], totals[3], totals[4], totals[5], totals[6], totals[7], totals[8], totals[9])
```

```python
import functools
import jax
import jax.numpy as jnp
from jax import lax
from jax.experimental import pallas as pl
from jax.experimental.pallas import tpu as pltpu
from jax.sharding import PartitionSpec as P

HEADS = 12
HDIM = 64
VOCAB_CHAR = 1000
GROUP_CHARS = 250
HG = 384
EPSILON = 1e-05
MESH = pl.DeviceIdType.MESH
BF = jnp.bfloat16
F32 = jnp.float32
NCH = 8
HB = HG // 128

def seq_dims(n):
    return {16: (4, 2, 2), 32: (8, 4, 1)}.get(n, (n, 1, 1))


def gather_kernel(dims, planes, specs, routes, *refs):
    Z, Y, C = dims
    n = len(specs)
    src, dst = refs[:n], refs[n:2 * n]
    own_sem, recv, zs, ds, ys, ss, xs = refs[2 * n:]
    dp = lax.axis_index("dp")
    me = lax.axis_index("seq")
    c = lax.rem(me, C)
    y = lax.rem(lax.div(me, C), Y)
    z = lax.div(me, C * Y)

    def at(zz, yy, cc):
        return (zz * Y + yy) * C + cc

    def to(zz, yy, cc):
        return (dp, at(zz, yy, cc))

    def view(i, slot):
        axis, rows = specs[i]
        s = pl.ds(pl.multiple_of(slot * rows, rows), rows)
        return dst[i].at[s] if axis == 0 else dst[i].at[:, s]

    def copy(i, slot, send, where, own=False):
        return pltpu.make_async_remote_copy(
            src_ref=src[i] if own else view(i, slot), dst_ref=view(i, slot),
            send_sem=send, recv_sem=recv.at[i, slot], device_id=where, device_id_type=MESH)

    sib = to(z, y, 1 - c) if C == 2 else None
    xp = (1 - dp, me)
    use_x = planes == 2 and any(routes)

    def owner(i):
        return None if not (use_x and routes[i]) else dp == routes[i] - 1

    def when(cond, f):
        if cond is None:
            f()
        else:
            pl.when(cond)(f)

    def both(a, b):
        return b if a is None else jnp.logical_and(a, b)

    bar = pltpu.get_barrier_semaphore()
    count = 0
    peers = [(z > 0, to(z - 1, y, c)), (z < Z - 1, to(z + 1, y, c))]
    if Y > 1:
        peers += [(y > 0, to(z, y - 1, c)), (y < Y - 1, to(z, y + 1, c))]
    if C == 2:
        peers.append((None, sib))
    if use_x:
        peers.append((None, xp))
    for cond, where in peers:
        when(cond, functools.partial(pl.semaphore_signal, bar, inc=1, device_id=where, device_id_type=MESH))
        count = count + (1 if cond is None else cond.astype(jnp.int32))
    pl.semaphore_wait(bar, count)

    def y_send(i, slot, up, down, own=False):
        if Y == 1:
            return
        if up is not None:
            pl.when(jnp.logical_and(up, y < Y - 1))(lambda: copy(i, slot, ys.at[i, slot], to(z, y + 1, c), own).start())
        if down is not None:
            pl.when(jnp.logical_and(down, y > 0))(lambda: copy(i, slot, (ds if own else ys).at[(i, slot) if not own else (i, 1)], to(z, y - 1, c), own).start())

    T = jnp.bool_(True)
    for i in range(n):
        pltpu.make_async_copy(src[i], view(i, me), own_sem.at[i]).start()
        def own_sends(i=i):
            pl.when(z < Z - 1)(lambda: copy(i, me, zs.at[i, me], to(z + 1, y, c), True).start())
            pl.when(z > 0)(lambda: copy(i, me, ds.at[i, 0], to(z - 1, y, c), True).start())
            y_send(i, me, T, T, True)
        when(owner(i), own_sends)
        if C == 2:
            copy(i, me, ss.at[i, me], sib, True).start()

    def arrive_z(zz, s_up):
        slot = at(zz, y, c)
        for i in range(n):
            copy(i, slot, ss.at[i, slot], xp).wait_recv()
            def fwd(i=i):
                if s_up:
                    pl.when(z < Z - 1)(lambda: copy(i, slot, zs.at[i, slot], to(z + 1, y, c)).start())
                else:
                    pl.when(z > 0)(lambda: copy(i, slot, zs.at[i, slot], to(z - 1, y, c)).start())
                if Y > 1:
                    pl.when(y < Y - 1)(lambda: copy(i, slot, ys.at[i, slot], to(z, y + 1, c)).start())
                    if Y == 2:
                        pl.when(y > 0)(lambda: copy(i, slot, ys.at[i, slot], to(z, y - 1, c)).start())
                    else:
                        pl.when(y > 0)(lambda: copy(i, slot, xs.at[i, slot], to(z, y - 1, c)).start())
                if use_x and routes[i]:
                    copy(i, slot, xs.at[i, slot], xp).start()
            when(owner(i), fwd)
            if C == 2:
                copy(i, slot, ss.at[i, slot], sib).start()

    def arrive_y(zz, yy, up):
        slot = at(zz, yy, c)
        for i in range(n):
            copy(i, slot, ss.at[i, slot], xp).wait_recv()
            def fwd(i=i):
                if Y > 2:
                    if up:
                        pl.when(y < Y - 1)(lambda: copy(i, slot, ys.at[i, slot], to(z, y + 1, c)).start())
                    else:
                        pl.when(y > 0)(lambda: copy(i, slot, ys.at[i, slot], to(z, y - 1, c)).start())
                if use_x and routes[i]:
                    copy(i, slot, xs.at[i, slot], xp).start()
            when(owner(i), fwd)
            if C == 2:
                copy(i, slot, ss.at[i, slot], sib).start()

    def all_y(zz):
        for t in range(1, Y):
            pl.when(y - t >= 0)(lambda: arrive_y(zz, y - t, True))
            pl.when(y + t < Y)(lambda: arrive_y(zz, y + t, False))

    def step(s, _):
        pl.when(z - s >= 0)(lambda: arrive_z(z - s, True))
        pl.when(z + s < Z)(lambda: arrive_z(z + s, False))
        q = s - 1
        pl.when(z - q >= 0)(lambda: all_y(z - q))
        pl.when(jnp.logical_and(q > 0, z + q < Z))(lambda: all_y(z + q))
        return 0

    lax.fori_loop(1, Z, step, 0)
    q = Z - 1
    pl.when(z - q >= 0)(lambda: all_y(z - q))
    pl.when(z + q < Z)(lambda: all_y(z + q))

    def drain(k, _):
        zz, yy = lax.div(k, Y), lax.rem(k, Y)
        slot = at(zz, yy, c)
        is_own = slot == me
        own_y = yy == y
        for i in range(n):
            o = owner(i)
            if C == 2:
                other = at(zz, yy, 1 - c)
                copy(i, other, ss.at[i, other], sib).wait_recv()
                copy(i, slot, ss.at[i, slot], sib).wait_send()
            fz = jnp.logical_and(own_y, jnp.logical_or(jnp.logical_and(zz <= z, z < Z - 1), jnp.logical_and(zz > z, z > 0)))
            pl.when(both(o, fz))(lambda: copy(i, slot, zs.at[i, slot], xp).wait_send())
            if Y == 2:
                pl.when(both(o, jnp.logical_and(own_y, jnp.logical_or(jnp.logical_not(is_own), y < Y - 1))))(
                    lambda: copy(i, slot, ys.at[i, slot], xp).wait_send())
            elif Y > 2:
                fy = jnp.logical_or(jnp.logical_and(yy <= y, y < Y - 1), jnp.logical_and(yy > y, y > 0))
                pl.when(both(o, fy))(lambda: copy(i, slot, ys.at[i, slot], xp).wait_send())
                fy2 = jnp.logical_and(jnp.logical_and(own_y, y > 0), jnp.logical_not(is_own))
                pl.when(both(o, fy2))(lambda: copy(i, slot, xs.at[i, slot], xp).wait_send())
            if use_x and routes[i]:
                pl.when(both(o, jnp.logical_not(is_own)))(lambda: copy(i, slot, xs.at[i, slot], xp).wait_send())
        return 0

    lax.fori_loop(0, Z * Y, drain, 0)
    for i in range(n):
        pltpu.make_async_copy(src[i], view(i, me), own_sem.at[i]).wait()
        o = owner(i)
        pl.when(both(o, z > 0))(lambda: copy(i, me, ds.at[i, 0], xp, True).wait_send())
        if Y > 1:
            pl.when(both(o, y > 0))(lambda: copy(i, me, ds.at[i, 1], xp, True).wait_send())


def gather(arrays, axes, routes, cid, planes, nseq):
    dims = seq_dims(nseq)
    specs = tuple((a, x.shape[a]) for x, a in zip(arrays, axes))
    if planes != 2 or dims[1] != 2 or dims[2] != 2:
        routes = (0,) * len(arrays)
    shapes = []
    for x, a in zip(arrays, axes):
        s = list(x.shape); s[a] *= nseq
        shapes.append(jax.ShapeDtypeStruct(tuple(s), x.dtype))
    n = len(arrays)
    D = pltpu.SemaphoreType.DMA
    return pl.pallas_call(
        functools.partial(gather_kernel, dims, planes, specs, tuple(routes)),
        out_shape=shapes,
        in_specs=[pl.BlockSpec(memory_space=pl.ANY)] * n,
        out_specs=[pl.BlockSpec(memory_space=pl.ANY)] * n,
        scratch_shapes=[D((n,)), D((n, nseq)), D((n, nseq)), D((n, 2)), D((n, nseq)), D((n, nseq)), D((n, nseq))],
        compiler_params=pltpu.CompilerParams(collective_id=cid, has_side_effects=True, vmem_limit_bytes=60 << 20),
    )(*arrays)


def dot(a, b):
    return jnp.dot(a, b, preferred_element_type=F32)


def dot_t(a, b):
    return lax.dot_general(a, b, (((1,), (1,)), ((), ())), preferred_element_type=F32)


def wgrad(a, b):
    return lax.dot_general(a, b, (((0,), (0,)), ((), ())), preferred_element_type=F32)


def vmem(mib):
    return pltpu.CompilerParams(vmem_limit_bytes=mib << 20)


def layer_norm(values, gain_row, shift_row):
    center = values - jnp.mean(values, -1, keepdims=True)
    spread = jnp.mean(center * center, -1, keepdims=True)
    return center * lax.rsqrt(spread + EPSILON) * gain_row + shift_row


def fill(pre_ref, decay, drive=None):
    for k in range(2):
        for j in range(HB):
            at = 2 * k * HG + j * 128
            rate = jax.nn.sigmoid(pre_ref[:, at : at + 128])
            decay[k * HB + j] = 1.0 - rate
            if drive is not None:
                drive[k * HB + j] = rate * pre_ref[:, at + HG : at + HG + 128]


def row(x, i):
    return lax.slice_in_dim(x, i, i + 1, axis=0)


def cat(parts):
    return jnp.concatenate(parts, 1)


def blocks(x):
    return [x[:, j * 128 : (j + 1) * 128] for j in range(HB)]


def totals_kernel(pre_ref, tot_ref, chunk_ref, decay, drive):
    length = pre_ref.shape[0] // NCH
    fill(pre_ref, decay, drive)

    def step(t, carry):
        place = (pl.ds(t, NCH, stride=length), pl.ds(length - 1 - t, NCH, stride=length))
        out = []
        for i in range(2 * HB):
            c, h = carry[i]
            a = decay[i, place[i // HB], :]
            out.append((c * a, a * h + drive[i, place[i // HB], :]))
        return tuple(out)

    one, zero = jnp.ones((NCH, 128), F32), jnp.zeros((NCH, 128), F32)
    ends = lax.fori_loop(0, length, step, ((one, zero),) * (2 * HB))
    cf, hf = cat([e[0] for e in ends[:HB]]), cat([e[1] for e in ends[:HB]])
    cb, hb = cat([e[0] for e in ends[HB:]]), cat([e[1] for e in ends[HB:]])
    chunk_ref[0:NCH, :] = cf
    chunk_ref[NCH : 2 * NCH, :] = hf
    chunk_ref[2 * NCH : 3 * NCH, :] = cb
    chunk_ref[3 * NCH :, :] = hb
    one, zero = jnp.ones((1, HG), F32), jnp.zeros((1, HG), F32)
    tf, sf, tb, sb = one, zero, one, zero
    for k in range(NCH):
        sf, tf = row(cf, k) * sf + row(hf, k), tf * row(cf, k)
        j = NCH - 1 - k
        sb, tb = row(cb, j) * sb + row(hb, j), tb * row(cb, j)
    tot_ref[...] = jnp.concatenate([tf, sf, tb, sb] + [zero] * 4, 0)


def states_kernel(me_ref, pre_ref, chunk_ref, all_ref, ends_ref, pooled_ref, prev_ref, decay, drive, state, prev):
    chars = pre_ref.shape[0]
    length = chars // NCH
    me = me_ref[0]
    nseq = all_ref.shape[0]
    fill(pre_ref, decay, drive)
    ef = jnp.zeros((1, HG), F32)
    eb = ef
    for d in range(nseq):
        got = all_ref[d]
        ef = jnp.where(d < me, row(got, 0) * ef + row(got, 1), ef)
        got = all_ref[nseq - 1 - d]
        eb = jnp.where(nseq - 1 - d > me, row(got, 2) * eb + row(got, 3), eb)
    cf, hf = chunk_ref[0:NCH, :], chunk_ref[NCH : 2 * NCH, :]
    cb, hb = chunk_ref[2 * NCH : 3 * NCH, :], chunk_ref[3 * NCH :, :]
    rows_f, rows_b = [], []
    for k in range(NCH):
        rows_f.append(ef)
        ef = row(cf, k) * ef + row(hf, k)
        j = NCH - 1 - k
        rows_b.append(eb)
        eb = row(cb, j) * eb + row(hb, j)

    def step(t, carry):
        place = (pl.ds(t, NCH, stride=length), pl.ds(length - 1 - t, NCH, stride=length))
        out = []
        for i in range(2 * HB):
            at = place[i // HB]
            prev[i, at, :] = carry[i]
            h = decay[i, at, :] * carry[i] + drive[i, at, :]
            state[i, at, :] = h
            out.append(h)
        return tuple(out)

    lax.fori_loop(0, length, step, tuple(blocks(jnp.concatenate(rows_f, 0)) + blocks(jnp.concatenate(rows_b[::-1], 0))))
    first = ends_ref[:, 0:1]
    last = ends_ref[:, 1:2]
    place = lax.broadcasted_iota(jnp.int32, (ends_ref.shape[0], chars), 1)
    member = jnp.where((place >= first) & (place < last), 1.0, 0.0).astype(BF)
    prev_ref[...] = cat([prev[i] for i in range(2 * HB)])
    pooled_ref[...] = dot(member, cat([state[i].astype(BF) for i in range(2 * HB)])) / (last - first).astype(F32)


def flows_kernel(pre_ref, dpool_ref, ends_ref, chunk_ref, ds_ref, tot_ref, gch_ref, decay, ds):
    chars = pre_ref.shape[0]
    length = chars // NCH
    fill(pre_ref, decay)
    first = ends_ref[0:1, :]
    last = ends_ref[1:2, :]
    place = lax.broadcasted_iota(jnp.int32, (chars, ends_ref.shape[1]), 0)
    inside = (place >= first) & (place < last)
    span = jnp.sum(jnp.where(inside, (last - first).astype(F32), 0.0), 1, keepdims=True)
    member = jnp.where(inside, 1.0, 0.0).astype(BF)
    spread = dot(member, dpool_ref[...]) / span
    ds_ref[...] = spread
    for i in range(2 * HB):
        ds[i] = spread[:, i * 128 : (i + 1) * 128]

    def step(t, carry):
        place = (pl.ds(length - 1 - t, NCH, stride=length), pl.ds(t, NCH, stride=length))
        return tuple(
            decay[i, place[i // HB], :] * (ds[i, place[i // HB], :] + carry[i]) for i in range(2 * HB)
        )

    ends = lax.fori_loop(0, length, step, (jnp.zeros((NCH, 128), F32),) * (2 * HB))
    gf, gb = cat(ends[:HB]), cat(ends[HB:])
    gch_ref[0:NCH, :] = gf
    gch_ref[NCH:, :] = gb
    cf, cb = chunk_ref[0:NCH, :], chunk_ref[2 * NCH : 3 * NCH, :]
    zero = jnp.zeros((1, HG), F32)
    tf, tb = zero, zero
    for k in range(NCH):
        j = NCH - 1 - k
        tf = row(cf, j) * tf + row(gf, j)
        tb = row(cb, k) * tb + row(gb, k)
    tot_ref[...] = jnp.concatenate([tf, tb] + [zero] * 6, 0)


def dpre_kernel(me_ref, pre_ref, ds_ref, prev_ref, chunk_ref, gch_ref, all_ref, gall_ref, dpre_ref, bias_ref, decay, ds):
    chars = pre_ref.shape[0]
    length = chars // NCH
    me = me_ref[0]
    nseq = all_ref.shape[0]
    fill(pre_ref, decay)
    for i in range(2 * HB):
        ds[i] = ds_ref[:, i * 128 : (i + 1) * 128]
    ef = jnp.zeros((1, HG), F32)
    eb = ef
    for d in range(nseq):
        j = nseq - 1 - d
        ef = jnp.where(j > me, row(all_ref[j], 0) * ef + row(gall_ref[j], 0), ef)
        eb = jnp.where(d < me, row(all_ref[d], 2) * eb + row(gall_ref[d], 1), eb)
    cf, cb = chunk_ref[0:NCH, :], chunk_ref[2 * NCH : 3 * NCH, :]
    gf, gb = gch_ref[0:NCH, :], gch_ref[NCH:, :]
    rows_f, rows_b = [], []
    for k in range(NCH):
        j = NCH - 1 - k
        rows_f.append(ef)
        ef = row(cf, j) * ef + row(gf, j)
        rows_b.append(eb)
        eb = row(cb, k) * eb + row(gb, k)

    def step(t, carry):
        place = (pl.ds(length - 1 - t, NCH, stride=length), pl.ds(t, NCH, stride=length))
        out = []
        for i in range(2 * HB):
            at = place[i // HB]
            g = ds[i, at, :] + carry[i]
            ds[i, at, :] = g
            out.append(decay[i, at, :] * g)
        return tuple(out)

    lax.fori_loop(0, length, step, tuple(blocks(jnp.concatenate(rows_f[::-1], 0)) + blocks(jnp.concatenate(rows_b, 0))))
    for i in range(2 * HB):
        k, j = i // HB, i % HB
        at = 2 * k * HG + j * 128
        g = ds[i]
        rate = jax.nn.sigmoid(pre_ref[:, at : at + 128])
        cand = pre_ref[:, at + HG : at + HG + 128]
        prev = prev_ref[:, i * 128 : (i + 1) * 128]
        dgate = (g * (cand - prev) * rate * decay[i]).astype(BF)
        dcand = (g * rate).astype(BF)
        for to, v in ((at, dgate), (at + HG, dcand)):
            dpre_ref[:, to : to + 128] = v
            bias_ref[:, to : to + 128] = jnp.broadcast_to(jnp.sum(v.astype(F32), 0, keepdims=True), (8, 128))


def rows_spec(rows, cols):
    return pl.BlockSpec((rows, cols), lambda s: (s, 0))


def scr(*shapes):
    return [pltpu.VMEM(s, F32) for s in shapes]


def char_totals(pre, seqs, chars):
    return pl.pallas_call(
        totals_kernel,
        grid=(seqs,),
        out_shape=[jax.ShapeDtypeStruct((seqs * 8, HG), F32), jax.ShapeDtypeStruct((seqs * 4 * NCH, HG), F32)],
        in_specs=[rows_spec(chars, 4 * HG)],
        out_specs=[rows_spec(8, HG), rows_spec(4 * NCH, HG)],
        scratch_shapes=scr(*[(2 * HB, chars, 128)] * 2),
        compiler_params=vmem(40),
    )(pre)


def smem_spec():
    return pl.BlockSpec(memory_space=pltpu.SMEM)


def all_spec(nseq):
    return pl.BlockSpec((nseq, None, 8, HG), lambda s: (0, s, 0, 0))


def char_states(me, pre, chunk, gathered, ends, seqs, chars, toks):
    nseq = gathered.shape[0]
    return pl.pallas_call(
        states_kernel,
        grid=(seqs,),
        out_shape=[jax.ShapeDtypeStruct((seqs * toks, 2 * HG), F32), jax.ShapeDtypeStruct((seqs * chars, 2 * HG), F32)],
        in_specs=[smem_spec(), rows_spec(chars, 4 * HG), rows_spec(4 * NCH, HG), all_spec(nseq), rows_spec(toks, 2)],
        out_specs=[rows_spec(toks, 2 * HG), rows_spec(chars, 2 * HG)],
        scratch_shapes=scr(*[(2 * HB, chars, 128)] * 4),
        compiler_params=vmem(48),
    )(me, pre, chunk, gathered, ends)


def char_flows(pre, dpool, ends_row, chunk, seqs, chars, toks):
    return pl.pallas_call(
        flows_kernel,
        grid=(seqs,),
        out_shape=[
            jax.ShapeDtypeStruct((seqs * chars, 2 * HG), F32),
            jax.ShapeDtypeStruct((seqs * 8, HG), F32),
            jax.ShapeDtypeStruct((seqs * 2 * NCH, HG), F32),
        ],
        in_specs=[rows_spec(chars, 4 * HG), rows_spec(toks, 2 * HG), rows_spec(8, toks), rows_spec(4 * NCH, HG)],
        out_specs=[rows_spec(chars, 2 * HG), rows_spec(8, HG), rows_spec(2 * NCH, HG)],
        scratch_shapes=scr(*[(2 * HB, chars, 128)] * 2),
        compiler_params=vmem(48),
    )(pre, dpool, ends_row, chunk)


def char_dpre(me, pre, ds, prev, chunk, gch, gathered, ggathered, seqs, chars):
    nseq = gathered.shape[0]
    return pl.pallas_call(
        dpre_kernel,
        grid=(seqs,),
        out_shape=[jax.ShapeDtypeStruct((seqs * chars, 4 * HG), BF), jax.ShapeDtypeStruct((seqs * 8, 4 * HG), F32)],
        in_specs=[
            smem_spec(), rows_spec(chars, 4 * HG), rows_spec(chars, 2 * HG), rows_spec(chars, 2 * HG),
            rows_spec(4 * NCH, HG), rows_spec(2 * NCH, HG), all_spec(nseq), all_spec(nseq),
        ],
        out_specs=[rows_spec(chars, 4 * HG), rows_spec(8, 4 * HG)],
        scratch_shapes=scr(*[(2 * HB, chars, 128)] * 2),
        compiler_params=vmem(48),
    )(me, pre, ds, prev, chunk, gch, gathered, ggathered)


def pair_rows(x):
    lane = lax.broadcasted_iota(jnp.int32, x.shape, 1)
    zero = jnp.zeros_like(x)
    return jnp.concatenate([jnp.where(lane < HDIM, x, zero), jnp.where(lane >= HDIM, x, zero)], 0)


def pair_lanes(x):
    half = x.shape[0] // 2
    lane = lax.broadcasted_iota(jnp.int32, (half, x.shape[1]), 1)
    return jnp.where(lane < HDIM, x[:half], x[half:])


def attn_fwd_kernel(q_ref, k_ref, v_ref, ctx_ref, low_ref, lse_ref):
    toks = q_ref.shape[0]
    s = dot_t(pair_rows(q_ref[...] * (HDIM ** -0.5)), k_ref[...])
    top = jnp.max(s, 1, keepdims=True)
    p = jnp.exp(s - top)
    total = jnp.sum(p, 1, keepdims=True)
    o = pair_lanes(dot(p.astype(BF), v_ref[...]) / total)
    ctx_ref[...] = o
    low_ref[...] = o.astype(BF)
    lse = top + jnp.log(total)
    lse_ref[...] = jnp.concatenate([lse[:toks], lse[toks:]], 1)


def head_spec(rows, base=0):
    return pl.BlockSpec((None, rows, 2 * HDIM), lambda s, h: (s, 0, h + base))


def attention_fwd(qkv, keys, values):
    seqs, toks, _ = qkv.shape
    length = keys.shape[1]
    pairs = HEADS // 2
    return pl.pallas_call(
        attn_fwd_kernel,
        grid=(seqs, pairs),
        out_shape=[
            jax.ShapeDtypeStruct((seqs, toks, HEADS * HDIM), F32),
            jax.ShapeDtypeStruct((seqs, toks, HEADS * HDIM), BF),
            jax.ShapeDtypeStruct((seqs, pairs, toks, 2), F32),
        ],
        in_specs=[head_spec(toks), head_spec(length), head_spec(length)],
        out_specs=[head_spec(toks), head_spec(toks), pl.BlockSpec((None, None, toks, 2), lambda s, h: (s, h, 0, 0))],
        compiler_params=vmem(48),
    )(qkv, keys, values)


def attn_bwd_kernel(q_ref, ko_ref, vo_ref, dc_ref, col_ref, ka_ref, va_ref, qa_ref, dca_ref, row_ref, dq_ref, dk_ref, dv_ref):
    toks = q_ref.shape[0]
    scale = HDIM ** -0.5
    lse = jnp.concatenate([col_ref[:, 0:1], col_ref[:, 1:2]], 0)
    delta = jnp.concatenate([col_ref[:, 2:3], col_ref[:, 3:4]], 0)
    p = jnp.exp(dot_t(pair_rows(q_ref[...] * scale), ka_ref[...]) - lse)
    dp = dot_t(pair_rows(dc_ref[...]), va_ref[...])
    ds = (p * (dp - delta)).astype(BF)
    dq_ref[...] = (pair_lanes(dot(ds, ka_ref[...])) * scale).astype(BF)

    def spread(i):
        n = row_ref.shape[1]
        return jnp.concatenate(
            [jnp.broadcast_to(row_ref[i : i + 1, :], (toks, n)), jnp.broadcast_to(row_ref[i + 1 : i + 2, :], (toks, n))], 0
        )

    p = jnp.exp(dot_t(pair_rows(ko_ref[...] * scale), qa_ref[...]) - spread(0))
    dv_ref[...] = pair_lanes(dot(p.astype(BF), dca_ref[...])).astype(BF)
    dp = dot_t(pair_rows(vo_ref[...]), dca_ref[...])
    ds = (p * (dp - spread(2))).astype(BF)
    dk_ref[...] = (pair_lanes(dot(ds, qa_ref[...])) * scale).astype(BF)


def attention_bwd(qkv, dctx, col, keys, values, queries, dctx_all, rows):
    seqs, toks, _ = qkv.shape
    length = keys.shape[1]
    pairs = HEADS // 2
    width = HEADS * HDIM
    stat = lambda a, b: pl.BlockSpec((None, None, a, b), lambda s, h: (s, h, 0, 0))
    return pl.pallas_call(
        attn_bwd_kernel,
        grid=(seqs, pairs),
        out_shape=[jax.ShapeDtypeStruct((seqs, toks, width), BF)] * 3,
        in_specs=[
            head_spec(toks), head_spec(toks, pairs), head_spec(toks, 2 * pairs), head_spec(toks), stat(toks, 4),
            head_spec(length), head_spec(length), head_spec(length), head_spec(length), stat(4, length),
        ],
        out_specs=[head_spec(toks)] * 3,
        compiler_params=vmem(56),
    )(qkv, qkv, qkv, dctx, col, keys, values, queries, dctx_all, rows)


def shifted(x, seqs):
    n = lax.axis_size("seq")
    up = [(i, i + 1) for i in range(n - 1)]
    down = [(i + 1, i) for i in range(n - 1)]
    y = x.reshape(seqs, -1, x.shape[1])
    before = lax.ppermute(y[:, -1:], "seq", up)
    after = lax.ppermute(y[:, :1], "seq", down)
    prev = jnp.concatenate([before, y[:, :-1]], 1).reshape(x.shape)
    follow = jnp.concatenate([y[:, 1:], after], 1).reshape(x.shape)
    return prev, follow


def scatter(total, axis):
    part = lax.psum_scatter(total, "seq", scatter_dimension=axis, tiled=True)
    return lax.psum(part, "dp").astype(F32)


def body(tokens, char_ids, span_lengths, script_group, w_qkv, w_out, w_up, w_down, char_table, w_gru, gru_bias, w_stream, w_conv, norms, grad_token, grad_char):
    nseq, planes = lax.axis_size("seq"), lax.axis_size("dp")
    me = lax.axis_index("seq").astype(jnp.int32).reshape(1)
    seqs, toks, width = tokens.shape
    chars = char_ids.shape[1]
    rows = seqs * toks
    bias_n, norm_n = gru_bias.shape[0], norms.shape[2]
    small = jnp.concatenate([gru_bias, norms.reshape(-1)])
    small = jnp.pad(small, (0, 2048 - small.shape[0])).reshape(16, 128)
    got = gather(
        [w_qkv, w_out, w_up, w_down, char_table, w_gru, w_stream, w_conv[0], w_conv[1], w_conv[2], small],
        [0, 0, 0, 0, 0, 0, 1, 0, 0, 0, 0],
        [0, 0, 1, 2, 0, 0, 0, 1, 0, 2, 0],
        1, planes, nseq,
    )
    w_qkv, w_out, w_up, w_down, char_table, w_gru, w_stream, conv0, conv1, conv2, small = got
    small = small.reshape(nseq, 2048)
    bias = small[:, :bias_n].reshape(-1).astype(F32)
    nrm = small[:, bias_n : bias_n + 8 * norm_n].reshape(nseq, 4, 2, norm_n).transpose(1, 2, 0, 3).reshape(4, 2, width).astype(F32)

    x_low = tokens.reshape(rows, width)
    x = x_low.astype(F32)
    qkv = dot(x_low, w_qkv).astype(BF)
    qkv3 = qkv.reshape(seqs, toks, 3 * width)

    char_rows = (char_ids + script_group[:, None] * GROUP_CHARS).reshape(seqs * chars, 1)
    onehot = (char_rows == jnp.arange(VOCAB_CHAR, dtype=jnp.int32)).astype(BF)
    embedded = dot_t(onehot, char_table).astype(BF)
    pre = dot(embedded, w_gru) + bias
    tot, chunk = char_totals(pre, seqs, chars)

    queries, keys, values, tot_all = gather(
        [qkv3[..., :width], qkv3[..., width : 2 * width], qkv3[..., 2 * width :], tot], [1, 1, 1, 0], [0] * 4, 2, planes, nseq
    )
    tot_all = tot_all.reshape(nseq, seqs, 8, HG)

    span = span_lengths[:, 0]
    span_ends = jnp.cumsum(span, -1)
    starts = span_ends - span
    ends_col = jnp.stack([starts, span_ends], -1).reshape(rows, 2)
    ends_row = jnp.pad(jnp.stack([starts, span_ends], 1), ((0, 0), (0, 6), (0, 0))).reshape(seqs * 8, toks)
    pooled, prev = char_states(me, pre, chunk, tot_all, ends_col, seqs, chars, toks)
    pooled_low = pooled.astype(BF)

    ctx3, ctx_low3, lse = attention_fwd(qkv3, keys, values)
    context, context_low = ctx3.reshape(rows, width), ctx_low3.reshape(rows, width)
    normed, back_one = jax.vjp(layer_norm, x + dot(context_low, w_out), nrm[0, 0], nrm[0, 1])
    normed_low = normed.astype(BF)
    raised = dot(normed_low, w_up)
    hidden_full, gelu_up = jax.vjp(jax.nn.gelu, raised)
    hidden = hidden_full.astype(BF)
    token_state, back_two = jax.vjp(layer_norm, normed + dot(hidden, w_down), nrm[1, 0], nrm[1, 1])
    state_low = token_state.astype(BF)
    merged = jnp.concatenate([dot(state_low, w_stream[0]), dot(pooled_low, w_stream[1])], -1).astype(BF)
    mprev, mnext = shifted(merged, seqs)
    mixed = dot(mprev, conv0) + dot(merged, conv1) + dot(mnext, conv2)
    gated, gelu_mix = jax.vjp(jax.nn.gelu, mixed)
    out_token, back_three = jax.vjp(layer_norm, token_state + gated[:, :width], nrm[2, 0], nrm[2, 1])
    out_char, back_four = jax.vjp(layer_norm, pooled + gated[:, width:], nrm[3, 0], nrm[3, 1])

    dsum_token, gain_three, shift_three = back_three(grad_token.reshape(rows, width).astype(F32))
    dsum_char, gain_four, shift_four = back_four(grad_char.reshape(rows, width).astype(F32))
    (dmixed,) = gelu_mix(jnp.concatenate([dsum_token, dsum_char], -1))
    dmixed_low = dmixed.astype(BF)
    g_conv = [wgrad(mprev, dmixed_low), wgrad(merged, dmixed_low), wgrad(mnext, dmixed_low)]
    dprev, dnext = shifted(dmixed_low, seqs)
    dfused = (dot_t(dnext, conv0) + dot_t(dmixed_low, conv1) + dot_t(dprev, conv2)).astype(BF)
    g_stream = [wgrad(state_low, dfused[:, :width]), wgrad(pooled_low, dfused[:, width:])]
    dstate = dsum_token + dot_t(dfused[:, :width], w_stream[0])
    dpooled = (dsum_char + dot_t(dfused[:, width:], w_stream[1])).astype(BF)
    ds, gtot, gch = char_flows(pre, dpooled, ends_row, chunk, seqs, chars, toks)

    dstate_sum, gain_two, shift_two = back_two(dstate)
    dlowered = dstate_sum.astype(BF)
    g_down = wgrad(hidden, dlowered)
    (draised,) = gelu_up(dot_t(dlowered, w_down))
    draised_low = draised.astype(BF)
    g_up = wgrad(normed_low, draised_low)
    dinput_sum, gain_one, shift_one = back_one(dstate_sum + dot_t(draised_low, w_up))
    dattended = dinput_sum.astype(BF)
    g_out = wgrad(context_low, dattended)
    dctx = dot_t(dattended, w_out).astype(BF)
    delta = jnp.sum((dctx.astype(F32) * context).reshape(seqs, toks, HEADS // 2, 2, HDIM), -1).transpose(0, 2, 1, 3)
    col = jnp.concatenate([lse, delta], -1)
    stat_rows = seqs * (HEADS // 2) * 4
    stat = jnp.swapaxes(col, 2, 3).reshape(stat_rows, toks)
    dctx3 = dctx.reshape(seqs, toks, width)
    dctx_all, stat_all, gtot_all = gather([dctx3, stat, gtot], [1, 0, 0], [0] * 3, 3, planes, nseq)
    stat_all = stat_all.reshape(nseq, seqs, HEADS // 2, 4, toks).transpose(1, 2, 3, 0, 4).reshape(seqs, HEADS // 2, 4, nseq * toks)
    gtot_all = gtot_all.reshape(nseq, seqs, 8, HG)
    dpre, dbias = char_dpre(me, pre, ds, prev, chunk, gch, tot_all, gtot_all, seqs, chars)
    g_gru = wgrad(embedded, dpre)
    g_bias = dbias.reshape(seqs, 8, 4 * HG)[:, 0].sum(0)
    dembed = dot_t(dpre, w_gru).astype(BF)
    g_table = wgrad(dembed, onehot)

    dq, dk, dv = attention_bwd(qkv3, dctx3, col, keys, values, queries, dctx_all, stat_all)
    dqkv = jnp.concatenate([dq, dk, dv], -1).reshape(rows, 3 * width)
    g_qkv = wgrad(x_low, dqkv)
    dinputs = dinput_sum + dot_t(dqkv, w_qkv)
    g_norms = jnp.stack([
        jnp.stack([gain_one, shift_one]), jnp.stack([gain_two, shift_two]),
        jnp.stack([gain_three, shift_three]), jnp.stack([gain_four, shift_four]),
    ])
    shape = (seqs, toks, width)
    return (
        out_token.astype(BF).reshape(shape),
        out_char.astype(BF).reshape(shape),
        dinputs.reshape(shape),
        scatter(g_qkv.astype(BF), 0),
        scatter(g_out.astype(BF), 0),
        scatter(g_up.astype(BF), 0),
        scatter(g_down.astype(BF), 0),
        scatter(g_table.astype(BF), 0),
        scatter(g_gru.astype(BF), 0),
        scatter(g_bias.astype(BF), 0),
        scatter(jnp.stack(g_stream).astype(BF), 1),
        scatter(jnp.stack(g_conv).astype(BF), 1),
        scatter(g_norms.astype(BF), 2),
    )


def solution(mesh):
    placed = (
        P("dp", "seq", None),
        P("dp", "seq"),
        P("dp", "seq", None),
        P("dp"),
        P("seq", None),
        P("seq", None),
        P("seq", None),
        P("seq", None),
        P("seq", None),
        P("seq", None),
        P("seq"),
        P(None, "seq", None),
        P(None, "seq", None),
        P(None, None, "seq"),
        P("dp", "seq", None),
        P("dp", "seq", None),
    )
    return jax.shard_map(
        body,
        mesh=mesh,
        in_specs=placed,
        out_specs=(
            P("dp", "seq", None),
            P("dp", "seq", None),
            P("dp", "seq", None),
            P("seq", None),
            P("seq", None),
            P("seq", None),
            P("seq", None),
            P("seq", None),
            P("seq", None),
            P("seq"),
            P(None, "seq", None),
            P(None, "seq", None),
            P(None, None, "seq"),
        ),
        check_vma=False,
    )
```

```python
import functools
import jax
import jax.numpy as jnp
from jax import lax
from jax.experimental import pallas as pl
from jax.experimental.pallas import tpu as pltpu
from jax.sharding import PartitionSpec as P

HEADS = 12
HDIM = 64
VOCAB_CHAR = 1000
GROUP_CHARS = 250
HG = 384
EPSILON = 1e-05
MESH = pl.DeviceIdType.MESH
BF = jnp.bfloat16
F32 = jnp.float32
NCH = 8
HB = HG // 128

def seq_dims(n):
    return {16: (4, 2, 2), 32: (8, 4, 1)}.get(n, (n, 1, 1))


def gather_kernel(dims, planes, specs, routes, *refs):
    Z, Y, C = dims
    n = len(specs)
    src, dst = refs[:n], refs[n:2 * n]
    own_sem, recv, zs, ds, ys, ss, xs = refs[2 * n:]
    dp = lax.axis_index("dp")
    me = lax.axis_index("seq")
    c = lax.rem(me, C)
    y = lax.rem(lax.div(me, C), Y)
    z = lax.div(me, C * Y)

    def at(zz, yy, cc):
        return (zz * Y + yy) * C + cc

    def to(zz, yy, cc):
        return (dp, at(zz, yy, cc))

    def view(i, slot):
        axis, rows = specs[i]
        s = pl.ds(pl.multiple_of(slot * rows, rows), rows)
        return dst[i].at[s] if axis == 0 else dst[i].at[:, s]

    def copy(i, slot, send, where, own=False):
        return pltpu.make_async_remote_copy(
            src_ref=src[i] if own else view(i, slot), dst_ref=view(i, slot),
            send_sem=send, recv_sem=recv.at[i, slot], device_id=where, device_id_type=MESH)

    sib = to(z, y, 1 - c) if C == 2 else None
    xp = (1 - dp, me)
    use_x = planes == 2 and any(routes)

    def owner(i):
        return None if not (use_x and routes[i]) else dp == routes[i] - 1

    def when(cond, f):
        if cond is None:
            f()
        else:
            pl.when(cond)(f)

    def both(a, b):
        return b if a is None else jnp.logical_and(a, b)

    bar = pltpu.get_barrier_semaphore()
    count = 0
    peers = [(z > 0, to(z - 1, y, c)), (z < Z - 1, to(z + 1, y, c))]
    if Y > 1:
        peers += [(y > 0, to(z, y - 1, c)), (y < Y - 1, to(z, y + 1, c))]
    if C == 2:
        peers.append((None, sib))
    if use_x:
        peers.append((None, xp))
    for cond, where in peers:
        when(cond, functools.partial(pl.semaphore_signal, bar, inc=1, device_id=where, device_id_type=MESH))
        count = count + (1 if cond is None else cond.astype(jnp.int32))
    pl.semaphore_wait(bar, count)

    def y_send(i, slot, up, down, own=False):
        if Y == 1:
            return
        if up is not None:
            pl.when(jnp.logical_and(up, y < Y - 1))(lambda: copy(i, slot, ys.at[i, slot], to(z, y + 1, c), own).start())
        if down is not None:
            pl.when(jnp.logical_and(down, y > 0))(lambda: copy(i, slot, (ds if own else ys).at[(i, slot) if not own else (i, 1)], to(z, y - 1, c), own).start())

    T = jnp.bool_(True)
    for i in range(n):
        pltpu.make_async_copy(src[i], view(i, me), own_sem.at[i]).start()
        def own_sends(i=i):
            pl.when(z < Z - 1)(lambda: copy(i, me, zs.at[i, me], to(z + 1, y, c), True).start())
            pl.when(z > 0)(lambda: copy(i, me, ds.at[i, 0], to(z - 1, y, c), True).start())
            y_send(i, me, T, T, True)
        when(owner(i), own_sends)
        if C == 2:
            copy(i, me, ss.at[i, me], sib, True).start()

    def arrive_z(zz, s_up):
        slot = at(zz, y, c)
        def one(i):
            copy(i, slot, ss.at[i, slot], xp).wait_recv()
            if True:
                if s_up:
                    pl.when(z < Z - 1)(lambda: copy(i, slot, zs.at[i, slot], to(z + 1, y, c)).start())
                else:
                    pl.when(z > 0)(lambda: copy(i, slot, zs.at[i, slot], to(z - 1, y, c)).start())
                if Y > 1:
                    pl.when(y < Y - 1)(lambda: copy(i, slot, ys.at[i, slot], to(z, y + 1, c)).start())
                    if Y == 2:
                        pl.when(y > 0)(lambda: copy(i, slot, ys.at[i, slot], to(z, y - 1, c)).start())
                    else:
                        pl.when(y > 0)(lambda: copy(i, slot, xs.at[i, slot], to(z, y - 1, c)).start())
                if use_x and routes[i]:
                    copy(i, slot, xs.at[i, slot], xp).start()
            if C == 2:
                copy(i, slot, ss.at[i, slot], sib).start()

        for i in range(n):
            when(owner(i), functools.partial(one, i))

    def arrive_y(zz, yy, up):
        slot = at(zz, yy, c)
        def one(i):
            copy(i, slot, ss.at[i, slot], xp).wait_recv()
            if True:
                if Y > 2:
                    if up:
                        pl.when(y < Y - 1)(lambda: copy(i, slot, ys.at[i, slot], to(z, y + 1, c)).start())
                    else:
                        pl.when(y > 0)(lambda: copy(i, slot, ys.at[i, slot], to(z, y - 1, c)).start())
                if use_x and routes[i]:
                    copy(i, slot, xs.at[i, slot], xp).start()
            if C == 2:
                copy(i, slot, ss.at[i, slot], sib).start()

        for i in range(n):
            when(owner(i), functools.partial(one, i))

    def all_y(zz):
        for t in range(1, Y):
            pl.when(y - t >= 0)(lambda: arrive_y(zz, y - t, True))
            pl.when(y + t < Y)(lambda: arrive_y(zz, y + t, False))

    def step(s, _):
        pl.when(z - s >= 0)(lambda: arrive_z(z - s, True))
        pl.when(z + s < Z)(lambda: arrive_z(z + s, False))
        q = s - 1
        pl.when(z - q >= 0)(lambda: all_y(z - q))
        pl.when(jnp.logical_and(q > 0, z + q < Z))(lambda: all_y(z + q))
        return 0

    lax.fori_loop(1, Z, step, 0)
    q = Z - 1
    pl.when(z - q >= 0)(lambda: all_y(z - q))
    pl.when(z + q < Z)(lambda: all_y(z + q))

    if use_x:
        def far(k, _):
            slot = at(lax.rem(z + lax.div(k, Y), Z), lax.rem(y + lax.rem(k, Y), Y), c)
            def one(i):
                copy(i, slot, ss.at[i, slot], xp).wait_recv()
                if C == 2:
                    copy(i, slot, ss.at[i, slot], sib).start()
            for i in range(n):
                if routes[i]:
                    pl.when(dp != routes[i] - 1)(functools.partial(one, i))
            return 0
        lax.fori_loop(1, Z * Y, far, 0)

    def drain(k, _):
        zz, yy = lax.div(k, Y), lax.rem(k, Y)
        slot = at(zz, yy, c)
        is_own = slot == me
        own_y = yy == y
        for i in range(n):
            o = owner(i)
            if C == 2:
                other = at(zz, yy, 1 - c)
                copy(i, other, ss.at[i, other], sib).wait_recv()
                copy(i, slot, ss.at[i, slot], sib).wait_send()
            fz = jnp.logical_and(own_y, jnp.logical_or(jnp.logical_and(zz <= z, z < Z - 1), jnp.logical_and(zz > z, z > 0)))
            pl.when(both(o, fz))(lambda: copy(i, slot, zs.at[i, slot], xp).wait_send())
            if Y == 2:
                pl.when(both(o, jnp.logical_and(own_y, jnp.logical_or(jnp.logical_not(is_own), y < Y - 1))))(
                    lambda: copy(i, slot, ys.at[i, slot], xp).wait_send())
            elif Y > 2:
                fy = jnp.logical_or(jnp.logical_and(yy <= y, y < Y - 1), jnp.logical_and(yy > y, y > 0))
                pl.when(both(o, fy))(lambda: copy(i, slot, ys.at[i, slot], xp).wait_send())
                fy2 = jnp.logical_and(jnp.logical_and(own_y, y > 0), jnp.logical_not(is_own))
                pl.when(both(o, fy2))(lambda: copy(i, slot, xs.at[i, slot], xp).wait_send())
            if use_x and routes[i]:
                pl.when(both(o, jnp.logical_not(is_own)))(lambda: copy(i, slot, xs.at[i, slot], xp).wait_send())
        return 0

    lax.fori_loop(0, Z * Y, drain, 0)
    for i in range(n):
        pltpu.make_async_copy(src[i], view(i, me), own_sem.at[i]).wait()
        o = owner(i)
        pl.when(both(o, z > 0))(lambda: copy(i, me, ds.at[i, 0], xp, True).wait_send())
        if Y > 1:
            pl.when(both(o, y > 0))(lambda: copy(i, me, ds.at[i, 1], xp, True).wait_send())


def gather(arrays, axes, routes, cid, planes, nseq):
    dims = seq_dims(nseq)
    specs = tuple((a, x.shape[a]) for x, a in zip(arrays, axes))
    if planes != 2 or dims[1] != 2 or dims[2] != 2:
        routes = (0,) * len(arrays)
    shapes = []
    for x, a in zip(arrays, axes):
        s = list(x.shape); s[a] *= nseq
        shapes.append(jax.ShapeDtypeStruct(tuple(s), x.dtype))
    n = len(arrays)
    D = pltpu.SemaphoreType.DMA
    return pl.pallas_call(
        functools.partial(gather_kernel, dims, planes, specs, tuple(routes)),
        out_shape=shapes,
        in_specs=[pl.BlockSpec(memory_space=pl.ANY)] * n,
        out_specs=[pl.BlockSpec(memory_space=pl.ANY)] * n,
        scratch_shapes=[D((n,)), D((n, nseq)), D((n, nseq)), D((n, 2)), D((n, nseq)), D((n, nseq)), D((n, nseq))],
        compiler_params=pltpu.CompilerParams(collective_id=cid, has_side_effects=True, vmem_limit_bytes=60 << 20),
    )(*arrays)


def dot(a, b):
    return jnp.dot(a, b, preferred_element_type=F32)


def dot_t(a, b):
    return lax.dot_general(a, b, (((1,), (1,)), ((), ())), preferred_element_type=F32)


def wgrad(a, b):
    return lax.dot_general(a, b, (((0,), (0,)), ((), ())), preferred_element_type=F32)


def vmem(mib):
    return pltpu.CompilerParams(vmem_limit_bytes=mib << 20)


def layer_norm(values, gain_row, shift_row):
    center = values - jnp.mean(values, -1, keepdims=True)
    spread = jnp.mean(center * center, -1, keepdims=True)
    return center * lax.rsqrt(spread + EPSILON) * gain_row + shift_row


def fill(pre_ref, decay, drive=None):
    for k in range(2):
        for j in range(HB):
            at = 2 * k * HG + j * 128
            rate = jax.nn.sigmoid(pre_ref[:, at : at + 128])
            decay[k * HB + j] = 1.0 - rate
            if drive is not None:
                drive[k * HB + j] = rate * pre_ref[:, at + HG : at + HG + 128]


def row(x, i):
    return lax.slice_in_dim(x, i, i + 1, axis=0)


def cat(parts):
    return jnp.concatenate(parts, 1)


def blocks(x):
    return [x[:, j * 128 : (j + 1) * 128] for j in range(HB)]


def totals_kernel(pre_ref, tot_ref, chunk_ref, decay, drive):
    length = pre_ref.shape[0] // NCH
    fill(pre_ref, decay, drive)

    def step(t, carry):
        place = (pl.ds(t, NCH, stride=length), pl.ds(length - 1 - t, NCH, stride=length))
        out = []
        for i in range(2 * HB):
            c, h = carry[i]
            a = decay[i, place[i // HB], :]
            out.append((c * a, a * h + drive[i, place[i // HB], :]))
        return tuple(out)

    one, zero = jnp.ones((NCH, 128), F32), jnp.zeros((NCH, 128), F32)
    ends = lax.fori_loop(0, length, step, ((one, zero),) * (2 * HB))
    cf, hf = cat([e[0] for e in ends[:HB]]), cat([e[1] for e in ends[:HB]])
    cb, hb = cat([e[0] for e in ends[HB:]]), cat([e[1] for e in ends[HB:]])
    chunk_ref[0:NCH, :] = cf
    chunk_ref[NCH : 2 * NCH, :] = hf
    chunk_ref[2 * NCH : 3 * NCH, :] = cb
    chunk_ref[3 * NCH :, :] = hb
    one, zero = jnp.ones((1, HG), F32), jnp.zeros((1, HG), F32)
    tf, sf, tb, sb = one, zero, one, zero
    for k in range(NCH):
        sf, tf = row(cf, k) * sf + row(hf, k), tf * row(cf, k)
        j = NCH - 1 - k
        sb, tb = row(cb, j) * sb + row(hb, j), tb * row(cb, j)
    tot_ref[...] = jnp.concatenate([tf, sf, tb, sb] + [zero] * 4, 0)


def states_kernel(me_ref, pre_ref, chunk_ref, all_ref, ends_ref, pooled_ref, prev_ref, decay, drive, state, prev):
    chars = pre_ref.shape[0]
    length = chars // NCH
    me = me_ref[0]
    nseq = all_ref.shape[0]
    fill(pre_ref, decay, drive)
    ef = jnp.zeros((1, HG), F32)
    eb = ef
    for d in range(nseq):
        got = all_ref[d]
        ef = jnp.where(d < me, row(got, 0) * ef + row(got, 1), ef)
        got = all_ref[nseq - 1 - d]
        eb = jnp.where(nseq - 1 - d > me, row(got, 2) * eb + row(got, 3), eb)
    cf, hf = chunk_ref[0:NCH, :], chunk_ref[NCH : 2 * NCH, :]
    cb, hb = chunk_ref[2 * NCH : 3 * NCH, :], chunk_ref[3 * NCH :, :]
    rows_f, rows_b = [], []
    for k in range(NCH):
        rows_f.append(ef)
        ef = row(cf, k) * ef + row(hf, k)
        j = NCH - 1 - k
        rows_b.append(eb)
        eb = row(cb, j) * eb + row(hb, j)

    def step(t, carry):
        place = (pl.ds(t, NCH, stride=length), pl.ds(length - 1 - t, NCH, stride=length))
        out = []
        for i in range(2 * HB):
            at = place[i // HB]
            prev[i, at, :] = carry[i]
            h = decay[i, at, :] * carry[i] + drive[i, at, :]
            state[i, at, :] = h
            out.append(h)
        return tuple(out)

    lax.fori_loop(0, length, step, tuple(blocks(jnp.concatenate(rows_f, 0)) + blocks(jnp.concatenate(rows_b[::-1], 0))))
    first = ends_ref[:, 0:1]
    last = ends_ref[:, 1:2]
    place = lax.broadcasted_iota(jnp.int32, (ends_ref.shape[0], chars), 1)
    member = jnp.where((place >= first) & (place < last), 1.0, 0.0).astype(BF)
    prev_ref[...] = cat([prev[i] for i in range(2 * HB)])
    pooled_ref[...] = dot(member, cat([state[i].astype(BF) for i in range(2 * HB)])) / (last - first).astype(F32)


def flows_kernel(pre_ref, dpool_ref, ends_ref, chunk_ref, ds_ref, tot_ref, gch_ref, decay, ds):
    chars = pre_ref.shape[0]
    length = chars // NCH
    fill(pre_ref, decay)
    first = ends_ref[0:1, :]
    last = ends_ref[1:2, :]
    place = lax.broadcasted_iota(jnp.int32, (chars, ends_ref.shape[1]), 0)
    inside = (place >= first) & (place < last)
    span = jnp.sum(jnp.where(inside, (last - first).astype(F32), 0.0), 1, keepdims=True)
    member = jnp.where(inside, 1.0, 0.0).astype(BF)
    spread = dot(member, dpool_ref[...]) / span
    ds_ref[...] = spread
    for i in range(2 * HB):
        ds[i] = spread[:, i * 128 : (i + 1) * 128]

    def step(t, carry):
        place = (pl.ds(length - 1 - t, NCH, stride=length), pl.ds(t, NCH, stride=length))
        return tuple(
            decay[i, place[i // HB], :] * (ds[i, place[i // HB], :] + carry[i]) for i in range(2 * HB)
        )

    ends = lax.fori_loop(0, length, step, (jnp.zeros((NCH, 128), F32),) * (2 * HB))
    gf, gb = cat(ends[:HB]), cat(ends[HB:])
    gch_ref[0:NCH, :] = gf
    gch_ref[NCH:, :] = gb
    cf, cb = chunk_ref[0:NCH, :], chunk_ref[2 * NCH : 3 * NCH, :]
    zero = jnp.zeros((1, HG), F32)
    tf, tb = zero, zero
    for k in range(NCH):
        j = NCH - 1 - k
        tf = row(cf, j) * tf + row(gf, j)
        tb = row(cb, k) * tb + row(gb, k)
    tot_ref[...] = jnp.concatenate([tf, tb] + [zero] * 6, 0)


def dpre_kernel(me_ref, pre_ref, ds_ref, prev_ref, chunk_ref, gch_ref, all_ref, gall_ref, dpre_ref, bias_ref, decay, ds):
    chars = pre_ref.shape[0]
    length = chars // NCH
    me = me_ref[0]
    nseq = all_ref.shape[0]
    fill(pre_ref, decay)
    for i in range(2 * HB):
        ds[i] = ds_ref[:, i * 128 : (i + 1) * 128]
    ef = jnp.zeros((1, HG), F32)
    eb = ef
    for d in range(nseq):
        j = nseq - 1 - d
        ef = jnp.where(j > me, row(all_ref[j], 0) * ef + row(gall_ref[j], 0), ef)
        eb = jnp.where(d < me, row(all_ref[d], 2) * eb + row(gall_ref[d], 1), eb)
    cf, cb = chunk_ref[0:NCH, :], chunk_ref[2 * NCH : 3 * NCH, :]
    gf, gb = gch_ref[0:NCH, :], gch_ref[NCH:, :]
    rows_f, rows_b = [], []
    for k in range(NCH):
        j = NCH - 1 - k
        rows_f.append(ef)
        ef = row(cf, j) * ef + row(gf, j)
        rows_b.append(eb)
        eb = row(cb, k) * eb + row(gb, k)

    def step(t, carry):
        place = (pl.ds(length - 1 - t, NCH, stride=length), pl.ds(t, NCH, stride=length))
        out = []
        for i in range(2 * HB):
            at = place[i // HB]
            g = ds[i, at, :] + carry[i]
            ds[i, at, :] = g
            out.append(decay[i, at, :] * g)
        return tuple(out)

    lax.fori_loop(0, length, step, tuple(blocks(jnp.concatenate(rows_f[::-1], 0)) + blocks(jnp.concatenate(rows_b, 0))))
    for i in range(2 * HB):
        k, j = i // HB, i % HB
        at = 2 * k * HG + j * 128
        g = ds[i]
        rate = jax.nn.sigmoid(pre_ref[:, at : at + 128])
        cand = pre_ref[:, at + HG : at + HG + 128]
        prev = prev_ref[:, i * 128 : (i + 1) * 128]
        dgate = (g * (cand - prev) * rate * decay[i]).astype(BF)
        dcand = (g * rate).astype(BF)
        for to, v in ((at, dgate), (at + HG, dcand)):
            dpre_ref[:, to : to + 128] = v
            bias_ref[:, to : to + 128] = jnp.broadcast_to(jnp.sum(v.astype(F32), 0, keepdims=True), (8, 128))


def rows_spec(rows, cols):
    return pl.BlockSpec((rows, cols), lambda s: (s, 0))


def scr(*shapes):
    return [pltpu.VMEM(s, F32) for s in shapes]


def char_totals(pre, seqs, chars):
    return pl.pallas_call(
        totals_kernel,
        grid=(seqs,),
        out_shape=[jax.ShapeDtypeStruct((seqs * 8, HG), F32), jax.ShapeDtypeStruct((seqs * 4 * NCH, HG), F32)],
        in_specs=[rows_spec(chars, 4 * HG)],
        out_specs=[rows_spec(8, HG), rows_spec(4 * NCH, HG)],
        scratch_shapes=scr(*[(2 * HB, chars, 128)] * 2),
        compiler_params=vmem(40),
    )(pre)


def smem_spec():
    return pl.BlockSpec(memory_space=pltpu.SMEM)


def all_spec(nseq):
    return pl.BlockSpec((nseq, None, 8, HG), lambda s: (0, s, 0, 0))


def char_states(me, pre, chunk, gathered, ends, seqs, chars, toks):
    nseq = gathered.shape[0]
    return pl.pallas_call(
        states_kernel,
        grid=(seqs,),
        out_shape=[jax.ShapeDtypeStruct((seqs * toks, 2 * HG), F32), jax.ShapeDtypeStruct((seqs * chars, 2 * HG), F32)],
        in_specs=[smem_spec(), rows_spec(chars, 4 * HG), rows_spec(4 * NCH, HG), all_spec(nseq), rows_spec(toks, 2)],
        out_specs=[rows_spec(toks, 2 * HG), rows_spec(chars, 2 * HG)],
        scratch_shapes=scr(*[(2 * HB, chars, 128)] * 4),
        compiler_params=vmem(48),
    )(me, pre, chunk, gathered, ends)


def char_flows(pre, dpool, ends_row, chunk, seqs, chars, toks):
    return pl.pallas_call(
        flows_kernel,
        grid=(seqs,),
        out_shape=[
            jax.ShapeDtypeStruct((seqs * chars, 2 * HG), F32),
            jax.ShapeDtypeStruct((seqs * 8, HG), F32),
            jax.ShapeDtypeStruct((seqs * 2 * NCH, HG), F32),
        ],
        in_specs=[rows_spec(chars, 4 * HG), rows_spec(toks, 2 * HG), rows_spec(8, toks), rows_spec(4 * NCH, HG)],
        out_specs=[rows_spec(chars, 2 * HG), rows_spec(8, HG), rows_spec(2 * NCH, HG)],
        scratch_shapes=scr(*[(2 * HB, chars, 128)] * 2),
        compiler_params=vmem(48),
    )(pre, dpool, ends_row, chunk)


def char_dpre(me, pre, ds, prev, chunk, gch, gathered, ggathered, seqs, chars):
    nseq = gathered.shape[0]
    return pl.pallas_call(
        dpre_kernel,
        grid=(seqs,),
        out_shape=[jax.ShapeDtypeStruct((seqs * chars, 4 * HG), BF), jax.ShapeDtypeStruct((seqs * 8, 4 * HG), F32)],
        in_specs=[
            smem_spec(), rows_spec(chars, 4 * HG), rows_spec(chars, 2 * HG), rows_spec(chars, 2 * HG),
            rows_spec(4 * NCH, HG), rows_spec(2 * NCH, HG), all_spec(nseq), all_spec(nseq),
        ],
        out_specs=[rows_spec(chars, 4 * HG), rows_spec(8, 4 * HG)],
        scratch_shapes=scr(*[(2 * HB, chars, 128)] * 2),
        compiler_params=vmem(48),
    )(me, pre, ds, prev, chunk, gch, gathered, ggathered)


def pair_rows(x):
    lane = lax.broadcasted_iota(jnp.int32, x.shape, 1)
    zero = jnp.zeros_like(x)
    return jnp.concatenate([jnp.where(lane < HDIM, x, zero), jnp.where(lane >= HDIM, x, zero)], 0)


def pair_lanes(x):
    half = x.shape[0] // 2
    lane = lax.broadcasted_iota(jnp.int32, (half, x.shape[1]), 1)
    return jnp.where(lane < HDIM, x[:half], x[half:])


def attn_fwd_kernel(q_ref, k_ref, v_ref, ctx_ref, low_ref, lse_ref):
    toks = q_ref.shape[0]
    s = dot_t(pair_rows(q_ref[...] * (HDIM ** -0.5)), k_ref[...])
    top = jnp.max(s, 1, keepdims=True)
    p = jnp.exp(s - top)
    total = jnp.sum(p, 1, keepdims=True)
    o = pair_lanes(dot(p.astype(BF), v_ref[...]) / total)
    ctx_ref[...] = o
    low_ref[...] = o.astype(BF)
    lse = top + jnp.log(total)
    lse_ref[...] = jnp.concatenate([lse[:toks], lse[toks:]], 1)


def head_spec(rows, base=0):
    return pl.BlockSpec((None, rows, 2 * HDIM), lambda s, h: (s, 0, h + base))


def attention_fwd(qkv, keys, values):
    seqs, toks, _ = qkv.shape
    length = keys.shape[1]
    pairs = HEADS // 2
    return pl.pallas_call(
        attn_fwd_kernel,
        grid=(seqs, pairs),
        out_shape=[
            jax.ShapeDtypeStruct((seqs, toks, HEADS * HDIM), F32),
            jax.ShapeDtypeStruct((seqs, toks, HEADS * HDIM), BF),
            jax.ShapeDtypeStruct((seqs, pairs, toks, 2), F32),
        ],
        in_specs=[head_spec(toks), head_spec(length), head_spec(length)],
        out_specs=[head_spec(toks), head_spec(toks), pl.BlockSpec((None, None, toks, 2), lambda s, h: (s, h, 0, 0))],
        compiler_params=vmem(48),
    )(qkv, keys, values)


def attn_bwd_kernel(q_ref, ko_ref, vo_ref, dc_ref, col_ref, ka_ref, va_ref, qa_ref, dca_ref, row_ref, dq_ref, dk_ref, dv_ref):
    toks = q_ref.shape[0]
    scale = HDIM ** -0.5
    lse = jnp.concatenate([col_ref[:, 0:1], col_ref[:, 1:2]], 0)
    delta = jnp.concatenate([col_ref[:, 2:3], col_ref[:, 3:4]], 0)
    p = jnp.exp(dot_t(pair_rows(q_ref[...] * scale), ka_ref[...]) - lse)
    dp = dot_t(pair_rows(dc_ref[...]), va_ref[...])
    ds = (p * (dp - delta)).astype(BF)
    dq_ref[...] = (pair_lanes(dot(ds, ka_ref[...])) * scale).astype(BF)

    def spread(i):
        n = row_ref.shape[1]
        return jnp.concatenate(
            [jnp.broadcast_to(row_ref[i : i + 1, :], (toks, n)), jnp.broadcast_to(row_ref[i + 1 : i + 2, :], (toks, n))], 0
        )

    p = jnp.exp(dot_t(pair_rows(ko_ref[...] * scale), qa_ref[...]) - spread(0))
    dv_ref[...] = pair_lanes(dot(p.astype(BF), dca_ref[...])).astype(BF)
    dp = dot_t(pair_rows(vo_ref[...]), dca_ref[...])
    ds = (p * (dp - spread(2))).astype(BF)
    dk_ref[...] = (pair_lanes(dot(ds, qa_ref[...])) * scale).astype(BF)


def attention_bwd(qkv, dctx, col, keys, values, queries, dctx_all, rows):
    seqs, toks, _ = qkv.shape
    length = keys.shape[1]
    pairs = HEADS // 2
    width = HEADS * HDIM
    stat = lambda a, b: pl.BlockSpec((None, None, a, b), lambda s, h: (s, h, 0, 0))
    return pl.pallas_call(
        attn_bwd_kernel,
        grid=(seqs, pairs),
        out_shape=[jax.ShapeDtypeStruct((seqs, toks, width), BF)] * 3,
        in_specs=[
            head_spec(toks), head_spec(toks, pairs), head_spec(toks, 2 * pairs), head_spec(toks), stat(toks, 4),
            head_spec(length), head_spec(length), head_spec(length), head_spec(length), stat(4, length),
        ],
        out_specs=[head_spec(toks)] * 3,
        compiler_params=vmem(56),
    )(qkv, qkv, qkv, dctx, col, keys, values, queries, dctx_all, rows)


RZ, RY, RC = 4, 2, 2
PW = 384
PR = 48
LX, LY, LH, LF = 5, 8, 1, 13
HRING = LY + 1


def reduce_kernel(npieces, nmisc, tab_ref, left_ref, right_ref, misc_ref, out_ref, part, r0, held, r1, r2, up, dn, fin, fx,
                  d_send, d_recv, x_send, x_recv, y_send, y_recv, u_send, u_recv, n_send, n_recv, f_send, f_recv):
    dp = lax.axis_index("dp")
    me = lax.axis_index("seq")
    c = lax.rem(me, RC)
    y = lax.rem(lax.div(me, RC), RY)
    z = lax.div(me, RC * RY)

    def to(zz, yy, cc):
        return (dp, (zz * RY + yy) * RC + cc)

    sib, ynb, zup, zdn, xnb = to(z, y, 1 - c), to(z, 1 - y, c), to(z + 1, y, c), to(z - 1, y, c), (1 - dp, me)
    bar = pltpu.get_barrier_semaphore()
    for where in (sib, ynb, xnb):
        pl.semaphore_signal(bar, inc=1, device_id=where, device_id_type=MESH)
    pl.when(z > 0)(lambda: pl.semaphore_signal(bar, inc=1, device_id=zdn, device_id_type=MESH))
    pl.when(z < RZ - 1)(lambda: pl.semaphore_signal(bar, inc=1, device_id=zup, device_id_type=MESH))
    pl.semaphore_wait(bar, 3 + (z > 0).astype(jnp.int32) + (z < RZ - 1).astype(jnp.int32))

    def copy(src, dst, send, recv, where):
        return pltpu.make_async_remote_copy(src_ref=src, dst_ref=dst, send_sem=send, recv_sem=recv, device_id=where, device_id_type=MESH)

    def d2d(t):
        b = lax.rem(t, 2)
        return copy(part.at[b, :, :, 1 - c], r0.at[b], d_send.at[b], d_recv.at[b], sib)

    def across(t):
        return copy(held.at[lax.rem(t, HRING)], r1.at[lax.div(t, 3)], x_send.at[t], x_recv.at[t], xnb)

    def along_y(t):
        return copy(held.at[lax.rem(t, HRING), :, 1 - y], r2.at[t], y_send.at[t], y_recv.at[t], ynb)

    def final(t):
        return copy(fin.at[t], fx.at[t], f_send.at[t], f_recv.at[t], xnb)

    def go_up(t, k):
        src = r2.at[t, pl.ds(k + 1, RZ - 1 - k)] if k == 0 else up.at[t, pl.ds(k, RZ - 1 - k)]
        return copy(src, up.at[t, pl.ds(k, RZ - 1 - k)], u_send.at[t], u_recv.at[t], zup)

    def from_below(t, k):
        ref = up.at[t, pl.ds(k - 1, RZ - k)]
        return copy(ref, ref, u_send.at[t], u_recv.at[t], zdn)

    def go_down(t, k):
        src = r2.at[t, pl.ds(0, k)] if k == RZ - 1 else dn.at[t, pl.ds(0, k)]
        return copy(src, dn.at[t, pl.ds(0, k)], n_send.at[t], n_recv.at[t], zdn)

    def from_above(t, k):
        ref = dn.at[t, pl.ds(0, k + 1)]
        return copy(ref, ref, n_send.at[t], n_recv.at[t], zup)

    def add(a, b):
        return (a.astype(F32) + b.astype(F32)).astype(BF)

    def live(t):
        return jnp.logical_and(t >= 0, t < npieces)

    def mine(t):
        r = lax.rem(t, 3)
        return jnp.logical_or(r == 0, r - 1 == dp)

    def finish(t):
        r = lax.rem(t, 3)

        @pl.when(r == 0)
        def _():
            final(t).wait_recv()
            out_ref[t] = fin[t].astype(F32) + fx[t].astype(F32)

        @pl.when(jnp.logical_and(r > 0, r - 1 == dp))
        def _():
            out_ref[t] = fin[t].astype(F32)

        @pl.when(jnp.logical_and(r > 0, r - 1 != dp))
        def _():
            final(t).wait_recv()
            out_ref[t] = fx[t].astype(F32)

        pl.when(mine(t))(lambda: final(t).wait_send())

    def sum_up(t):
        for k in range(RZ):
            @pl.when(z == k)
            def _(k=k):
                if k > 0:
                    from_below(t, k).wait_recv()
                    for q in range(k + 1, RZ):
                        up[t, q - 1] = add(up[t, q - 1], r2[t, q])
                if k < RZ - 1:
                    go_up(t, k).start()

    def sum_down(t):
        for k in range(RZ):
            @pl.when(z == k)
            def _(k=k):
                if k < RZ - 1:
                    from_above(t, k).wait_recv()
                    for q in range(k):
                        dn[t, q] = add(dn[t, q], r2[t, q])
                if k > 0:
                    go_down(t, k).start()

    def close(t):
        for k in range(RZ):
            @pl.when(z == k)
            def _(k=k):
                total = r2[t, k].astype(F32)
                if k > 0:
                    total = total + up[t, k - 1].astype(F32)
                    go_down(t, k).wait_send()
                if k < RZ - 1:
                    total = total + dn[t, k].astype(F32)
                    go_up(t, k).wait_send()
                fin[t] = total.astype(BF)
        final(t).start()

    def join_y(t):
        along_y(t).wait_recv()
        along_y(t).wait_send()
        h = lax.rem(t, HRING)
        for q in range(RZ):
            r2[t, q] = add(r2[t, q], held[h, q, y])

    def join_x(t):
        h = lax.rem(t, HRING)

        @pl.when(lax.rem(t, 3) > 0)
        def _():
            across(t).wait_recv()
            for q in range(RZ):
                held[h, q] = add(held[h, q], r1[lax.div(t, 3), q])

        along_y(t).start()

    def join_core(t):
        b = lax.rem(t, 2)
        h = lax.rem(t, HRING)
        d2d(t).wait_recv()
        d2d(t).wait_send()
        for q in range(RZ):
            held[h, q] = add(part[b, q, :, c], r0[b, q])
        pl.when(jnp.logical_not(mine(t)))(lambda: across(t).start())

    def make(t):
        b = lax.rem(t, 2)

        @pl.when(t < npieces - nmisc)
        def _():
            li, ri = tab_ref[t, 0], tab_ref[t, 1]
            right = right_ref[ri]
            for q in range(RZ // 2):
                got = jnp.dot(left_ref[li, q * 384 : (q + 1) * 384], right, preferred_element_type=F32)
                part[b, 2 * q : 2 * q + 2] = got.astype(BF).reshape(2, RY, RC, PR, PW)

        @pl.when(t >= npieces - nmisc)
        def _():
            part[b] = misc_ref[t - (npieces - nmisc)]

        d2d(t).start()

    def tick(T, _):
        def do(t, f, cond=None):
            ok = live(t)
            pl.when(ok if cond is None else jnp.logical_and(ok, cond(t)))(lambda: f(t))

        do(T - LF, finish)
        do(T - LY - z * LH, sum_up, mine)
        do(T - LY - (RZ - 1 - z) * LH, sum_down, mine)
        do(T - LY - (RZ - 1) * LH, close, mine)
        do(T - LY + 1, join_y, mine)
        do(T - LX, join_x, mine)
        do(T - LX, lambda t: across(t).wait_send(), lambda t: jnp.logical_not(mine(t)))
        do(T - 1, join_core)
        do(T, make)
        return 0

    lax.fori_loop(0, npieces + LF + 1, tick, 0)


def reduce_pieces(table, left, right, misc, cid):
    npieces, nmisc = table.shape[0], misc.shape[0]
    D = pltpu.SemaphoreType.DMA
    v = lambda *s: pltpu.VMEM(s, BF)
    spec = pl.BlockSpec(memory_space=pltpu.VMEM)
    return pl.pallas_call(
        functools.partial(reduce_kernel, npieces, nmisc),
        out_shape=jax.ShapeDtypeStruct((npieces, PR, PW), F32),
        in_specs=[pl.BlockSpec(memory_space=pltpu.SMEM), spec, spec, spec],
        out_specs=spec,
        scratch_shapes=[
            v(2, RZ, RY, RC, PR, PW), v(2, RZ, RY, PR, PW), v(HRING, RZ, RY, PR, PW), v(npieces // 3 + 1, RZ, RY, PR, PW),
            v(npieces, RZ, PR, PW), v(npieces, RZ - 1, PR, PW), v(npieces, RZ - 1, PR, PW), v(npieces, PR, PW), v(npieces, PR, PW),
            D((2,)), D((2,)), D((npieces,)), D((npieces,)), D((npieces,)), D((npieces,)),
            D((npieces,)), D((npieces,)), D((npieces,)), D((npieces,)), D((npieces,)), D((npieces,)),
        ],
        compiler_params=pltpu.CompilerParams(collective_id=cid, has_side_effects=True, vmem_limit_bytes=62 << 20),
    )(table, left, right, misc)


def lefts(x, slots):
    k = x.shape[1] // (slots * PR)
    return x.T.reshape(slots, k, PR, x.shape[0]).transpose(1, 0, 2, 3).reshape(k, slots * PR, x.shape[0])


def rights(x):
    return x.reshape(x.shape[0], -1, PW).transpose(1, 0, 2)


def reduce_all(lhs, rhs, g_gru, g_table, g_bias, g_norms, nseq, cid):
    x, ctx, normed, hidden, state, pooled, before, merged, after = lhs
    dqkv, dattended, draised, dlowered, dfused, dmixed = rhs
    left = jnp.concatenate([lefts(a, nseq) for a in lhs])
    right = jnp.concatenate([rights(a) for a in rhs])
    count = lambda group: [a.shape[1] for a in group]
    lat, rat = [0], [0]
    for a in count(lhs):
        lat.append(lat[-1] + a // (nseq * PR))
    for a in count(rhs):
        rat.append(rat[-1] + a // PW)
    span = lambda at, i: range(at[i], at[i + 1])
    half = (rat[5] - rat[4]) // 2
    groups = {}
    table = []

    def put(name, ls, rs):
        groups[name] = (len(table), len(ls), len(rs))
        table.extend((l, r) for l in ls for r in rs)

    put("conv0", span(lat, 6), span(rat, 5))
    put("conv1", span(lat, 7), span(rat, 5))
    put("conv2", span(lat, 8), span(rat, 5))
    put("stream0", span(lat, 4), range(rat[4], rat[4] + half))
    put("stream1", span(lat, 5), range(rat[4] + half, rat[5]))
    put("down", span(lat, 3), span(rat, 3))
    put("up", span(lat, 2), span(rat, 2))
    put("out", span(lat, 1), span(rat, 1))
    put("qkv", span(lat, 0), span(rat, 0))
    wide = 2 * PR * nseq
    def rows(g):
        g = jnp.pad(g.astype(BF), ((0, 0), (0, wide - g.shape[1]))).reshape(nseq, -1, 2, wide // 2)
        return g.transpose(0, 2, 1, 3).reshape(nseq, -1, wide // 2)
    per = g_bias.shape[0] // nseq
    tiny = jnp.concatenate([g_bias.reshape(nseq, per), g_norms.reshape(4, 2, nseq, -1).transpose(2, 0, 1, 3).reshape(nseq, -1)], 1).astype(BF)
    tiny = jnp.pad(tiny[:, None], ((0, 0), (0, 31), (0, wide // 2 - tiny.shape[1])))
    misc = jnp.concatenate([rows(g_gru), rows(g_table), tiny], 1)
    nb = wide // 2 // PW
    misc = misc.reshape(nseq, 2, PR, nb, PW).transpose(1, 3, 0, 2, 4).reshape(2 * nb, RZ, RY, RC, PR, PW)
    table.extend([(0, 0)] * (2 * nb))
    out = reduce_pieces(jnp.asarray(table, jnp.int32), left, right, misc, cid)

    def take(name):
        at, nl, nr = groups[name]
        return out[at : at + nl * nr].reshape(nl, nr, PR, PW).transpose(0, 2, 1, 3).reshape(nl * PR, nr * PW)

    rest = out[len(table) - 2 * nb :].reshape(2, nb, PR, PW).transpose(0, 2, 1, 3).reshape(2 * PR, wide // 2)
    unrow = lambda a, n: a.reshape(2, -1, wide // 2).transpose(1, 0, 2).reshape(-1, wide)[:, :n]
    return (
        take("qkv"), take("out"), take("up"), take("down"),
        unrow(rest[32:64], g_table.shape[1]), unrow(rest[:32], g_gru.shape[1]), rest[64, :per],
        jnp.stack([take("stream0"), take("stream1")]),
        jnp.stack([take("conv0"), take("conv1"), take("conv2")]),
        rest[64, per : per + 384].reshape(4, 2, -1),
    )


def shifted(x, seqs):
    n = lax.axis_size("seq")
    up = [(i, i + 1) for i in range(n - 1)]
    down = [(i + 1, i) for i in range(n - 1)]
    y = x.reshape(seqs, -1, x.shape[1])
    before = lax.ppermute(y[:, -1:], "seq", up)
    after = lax.ppermute(y[:, :1], "seq", down)
    prev = jnp.concatenate([before, y[:, :-1]], 1).reshape(x.shape)
    follow = jnp.concatenate([y[:, 1:], after], 1).reshape(x.shape)
    return prev, follow


def scatter(total, axis):
    part = lax.psum_scatter(total, "seq", scatter_dimension=axis, tiled=True)
    return lax.psum(part, "dp").astype(F32)


def body(tokens, char_ids, span_lengths, script_group, w_qkv, w_out, w_up, w_down, char_table, w_gru, gru_bias, w_stream, w_conv, norms, grad_token, grad_char):
    nseq, planes = lax.axis_size("seq"), lax.axis_size("dp")
    me = lax.axis_index("seq").astype(jnp.int32).reshape(1)
    seqs, toks, width = tokens.shape
    chars = char_ids.shape[1]
    rows = seqs * toks
    bias_n, norm_n = gru_bias.shape[0], norms.shape[2]
    small = jnp.concatenate([gru_bias, norms.reshape(-1)])
    small = jnp.pad(small, (0, 2048 - small.shape[0])).reshape(16, 128)
    got = gather(
        [w_qkv, w_out, w_up, w_down, char_table, w_gru, w_stream, w_conv[0], w_conv[1], w_conv[2], small],
        [0, 0, 0, 0, 0, 0, 1, 0, 0, 0, 0],
        [0, 0, 1, 2, 0, 0, 0, 1, 0, 2, 0],
        1, planes, nseq,
    )
    w_qkv, w_out, w_up, w_down, char_table, w_gru, w_stream, conv0, conv1, conv2, small = got
    small = small.reshape(nseq, 2048)
    bias = small[:, :bias_n].reshape(-1).astype(F32)
    nrm = small[:, bias_n : bias_n + 8 * norm_n].reshape(nseq, 4, 2, norm_n).transpose(1, 2, 0, 3).reshape(4, 2, width).astype(F32)

    x_low = tokens.reshape(rows, width)
    x = x_low.astype(F32)
    qkv = dot(x_low, w_qkv).astype(BF)
    qkv3 = qkv.reshape(seqs, toks, 3 * width)

    char_rows = (char_ids + script_group[:, None] * GROUP_CHARS).reshape(seqs * chars, 1)
    onehot = (char_rows == jnp.arange(VOCAB_CHAR, dtype=jnp.int32)).astype(BF)
    embedded = dot_t(onehot, char_table).astype(BF)
    pre = dot(embedded, w_gru) + bias
    tot, chunk = char_totals(pre, seqs, chars)

    queries, keys, values, tot_all = gather(
        [qkv3[..., :width], qkv3[..., width : 2 * width], qkv3[..., 2 * width :], tot], [1, 1, 1, 0], [0] * 4, 2, planes, nseq
    )
    tot_all = tot_all.reshape(nseq, seqs, 8, HG)

    span = span_lengths[:, 0]
    span_ends = jnp.cumsum(span, -1)
    starts = span_ends - span
    ends_col = jnp.stack([starts, span_ends], -1).reshape(rows, 2)
    ends_row = jnp.pad(jnp.stack([starts, span_ends], 1), ((0, 0), (0, 6), (0, 0))).reshape(seqs * 8, toks)
    pooled, prev = char_states(me, pre, chunk, tot_all, ends_col, seqs, chars, toks)
    pooled_low = pooled.astype(BF)

    ctx3, ctx_low3, lse = attention_fwd(qkv3, keys, values)
    context, context_low = ctx3.reshape(rows, width), ctx_low3.reshape(rows, width)
    normed, back_one = jax.vjp(layer_norm, x + dot(context_low, w_out), nrm[0, 0], nrm[0, 1])
    normed_low = normed.astype(BF)
    raised = dot(normed_low, w_up)
    hidden_full, gelu_up = jax.vjp(jax.nn.gelu, raised)
    hidden = hidden_full.astype(BF)
    token_state, back_two = jax.vjp(layer_norm, normed + dot(hidden, w_down), nrm[1, 0], nrm[1, 1])
    state_low = token_state.astype(BF)
    merged = jnp.concatenate([dot(state_low, w_stream[0]), dot(pooled_low, w_stream[1])], -1).astype(BF)
    mprev, mnext = shifted(merged, seqs)
    mixed = dot(mprev, conv0) + dot(merged, conv1) + dot(mnext, conv2)
    gated, gelu_mix = jax.vjp(jax.nn.gelu, mixed)
    out_token, back_three = jax.vjp(layer_norm, token_state + gated[:, :width], nrm[2, 0], nrm[2, 1])
    out_char, back_four = jax.vjp(layer_norm, pooled + gated[:, width:], nrm[3, 0], nrm[3, 1])

    dsum_token, gain_three, shift_three = back_three(grad_token.reshape(rows, width).astype(F32))
    dsum_char, gain_four, shift_four = back_four(grad_char.reshape(rows, width).astype(F32))
    (dmixed,) = gelu_mix(jnp.concatenate([dsum_token, dsum_char], -1))
    dmixed_low = dmixed.astype(BF)
    dprev, dnext = shifted(dmixed_low, seqs)
    dfused = (dot_t(dnext, conv0) + dot_t(dmixed_low, conv1) + dot_t(dprev, conv2)).astype(BF)
    dstate = dsum_token + dot_t(dfused[:, :width], w_stream[0])
    dpooled = (dsum_char + dot_t(dfused[:, width:], w_stream[1])).astype(BF)
    ds, gtot, gch = char_flows(pre, dpooled, ends_row, chunk, seqs, chars, toks)

    dstate_sum, gain_two, shift_two = back_two(dstate)
    dlowered = dstate_sum.astype(BF)
    (draised,) = gelu_up(dot_t(dlowered, w_down))
    draised_low = draised.astype(BF)
    dinput_sum, gain_one, shift_one = back_one(dstate_sum + dot_t(draised_low, w_up))
    dattended = dinput_sum.astype(BF)
    dctx = dot_t(dattended, w_out).astype(BF)
    delta = jnp.sum((dctx.astype(F32) * context).reshape(seqs, toks, HEADS // 2, 2, HDIM), -1).transpose(0, 2, 1, 3)
    col = jnp.concatenate([lse, delta], -1)
    stat_rows = seqs * (HEADS // 2) * 4
    stat = jnp.swapaxes(col, 2, 3).reshape(stat_rows, toks)
    dctx3 = dctx.reshape(seqs, toks, width)
    dctx_all, stat_all, gtot_all = gather([dctx3, stat, gtot], [1, 0, 0], [0] * 3, 3, planes, nseq)
    stat_all = stat_all.reshape(nseq, seqs, HEADS // 2, 4, toks).transpose(1, 2, 3, 0, 4).reshape(seqs, HEADS // 2, 4, nseq * toks)
    gtot_all = gtot_all.reshape(nseq, seqs, 8, HG)
    dpre, dbias = char_dpre(me, pre, ds, prev, chunk, gch, tot_all, gtot_all, seqs, chars)
    g_gru = wgrad(embedded, dpre)
    g_bias = dbias.reshape(seqs, 8, 4 * HG)[:, 0].sum(0)
    dembed = dot_t(dpre, w_gru).astype(BF)
    g_table = wgrad(dembed, onehot)

    dq, dk, dv = attention_bwd(qkv3, dctx3, col, keys, values, queries, dctx_all, stat_all)
    dqkv = jnp.concatenate([dq, dk, dv], -1).reshape(rows, 3 * width)
    dinputs = dinput_sum + dot_t(dqkv, w_qkv)
    g_norms = jnp.stack([
        jnp.stack([gain_one, shift_one]), jnp.stack([gain_two, shift_two]),
        jnp.stack([gain_three, shift_three]), jnp.stack([gain_four, shift_four]),
    ])
    shape = (seqs, toks, width)
    if seq_dims(nseq) == (RZ, RY, RC) and planes == 2:
        lhs = (x_low, context_low, normed_low, hidden, state_low, pooled_low, mprev, merged, mnext)
        rhs = (dqkv, dattended, draised_low, dlowered, dfused, dmixed_low)
        owned = reduce_all(lhs, rhs, g_gru, g_table, g_bias, g_norms, nseq, 4)
    else:
        g_stream = [wgrad(state_low, dfused[:, :width]), wgrad(pooled_low, dfused[:, width:])]
        owned = (
            scatter(wgrad(x_low, dqkv).astype(BF), 0),
            scatter(wgrad(context_low, dattended).astype(BF), 0),
            scatter(wgrad(normed_low, draised_low).astype(BF), 0),
            scatter(wgrad(hidden, dlowered).astype(BF), 0),
            scatter(g_table.astype(BF), 0),
            scatter(g_gru.astype(BF), 0),
            scatter(g_bias.astype(BF), 0),
            scatter(jnp.stack(g_stream).astype(BF), 1),
            scatter(jnp.stack([wgrad(m, dmixed_low) for m in (mprev, merged, mnext)]).astype(BF), 1),
            scatter(g_norms.astype(BF), 2),
        )
    return (
        out_token.astype(BF).reshape(shape),
        out_char.astype(BF).reshape(shape),
        dinputs.reshape(shape),
    ) + owned


def solution(mesh):
    placed = (
        P("dp", "seq", None),
        P("dp", "seq"),
        P("dp", "seq", None),
        P("dp"),
        P("seq", None),
        P("seq", None),
        P("seq", None),
        P("seq", None),
        P("seq", None),
        P("seq", None),
        P("seq"),
        P(None, "seq", None),
        P(None, "seq", None),
        P(None, None, "seq"),
        P("dp", "seq", None),
        P("dp", "seq", None),
    )
    return jax.shard_map(
        body,
        mesh=mesh,
        in_specs=placed,
        out_specs=(
            P("dp", "seq", None),
            P("dp", "seq", None),
            P("dp", "seq", None),
            P("seq", None),
            P("seq", None),
            P("seq", None),
            P("seq", None),
            P("seq", None),
            P("seq", None),
            P("seq"),
            P(None, "seq", None),
            P(None, "seq", None),
            P(None, None, "seq"),
        ),
        check_vma=False,
    )
```

```python
import collections
import functools
import jax
import jax.numpy as jnp
from jax import lax
from jax.experimental import pallas as pl
from jax.experimental.pallas import tpu as pltpu
from jax.sharding import PartitionSpec as P

HEADS = 12
HDIM = 64
VOCAB_CHAR = 1000
GROUP_CHARS = 250
HG = 384
EPSILON = 1e-05
MESH = pl.DeviceIdType.MESH
BF = jnp.bfloat16
F32 = jnp.float32
NCH = 8
UNROLL = 8
CONV1, TAPS = False, (0, 1, 2)
HB = HG // 128

def seq_dims(n):
    return {16: (4, 2, 2), 32: (8, 4, 1)}.get(n, (n, 1, 1))


Move = collections.namedtuple("Move", ("array", "axis", "rows", "cols", "route", "yfirst"))


def gather_kernel(dims, planes, moves, n_arrays, task, *refs):
    Z, Y, C = dims
    n = len(moves)
    n_in, n_out = (task.n_in, task.n_out) if task else (0, 0)
    src, task_in = refs[:n_arrays], refs[n_arrays : n_arrays + n_in]
    refs = refs[n_arrays + n_in :]
    dst, task_out = refs[:n_arrays], refs[n_arrays : n_arrays + n_out]
    own_sem, recv, zs, ds, ys, ss, xs, *task_scratch = refs[n_arrays + n_out :]
    dp = lax.axis_index("dp")
    me = lax.axis_index("seq")
    c = lax.rem(me, C)
    y = lax.rem(lax.div(me, C), Y)
    z = lax.div(me, C * Y)
    up_z, down_z = z < Z - 1, z > 0

    def at(zz, yy, cc):
        return (zz * Y + yy) * C + cc

    def to(zz, yy, cc):
        return (dp, at(zz, yy, cc))

    def view(i, slot):
        m = moves[i]
        s = pl.ds(pl.multiple_of(slot * m.rows, m.rows), m.rows)
        ref = dst[m.array]
        if m.cols is None:
            return ref.at[s] if m.axis == 0 else ref.at[:, s]
        return ref.at[:, s, pl.ds(*m.cols)]

    def mine(i):
        m = moves[i]
        return src[m.array] if m.cols is None else src[m.array].at[:, :, pl.ds(*m.cols)]

    def copy(i, slot, send, where, own=False):
        return pltpu.make_async_remote_copy(
            src_ref=mine(i) if own else view(i, slot), dst_ref=view(i, slot),
            send_sem=send, recv_sem=recv.at[i, slot], device_id=where, device_id_type=MESH)

    sib = to(z, y, 1 - c) if C == 2 else None
    xp = (1 - dp, me)
    use_x = planes == 2 and any(m.route for m in moves)
    some = sib if C == 2 else to(z, y, c)

    def owner(i):
        return None if not (use_x and moves[i].route) else dp == moves[i].route - 1

    def when(cond, f):
        if cond is None:
            f()
        else:
            pl.when(cond)(f)

    def both(a, b):
        return b if a is None else jnp.logical_and(a, b)

    nseq = Z * Y * C
    if task:
        push, *task_in = task_in
        push_all, *task_out = task_out
        p_send, p_recv, i_sem, *task_scratch = task_scratch
        held, task_scratch = task_scratch[: n_in - 1], task_scratch[n_in - 1 :]
        loads = [pltpu.make_async_copy(a, b, i_sem.at[k]) for k, (a, b) in enumerate(zip(task_in, held))]
        for load in loads:
            load.start()
    bar = pltpu.get_barrier_semaphore()
    if task:
        peers = [(None, (dp, lax.rem(me + k, nseq))) for k in range(1, nseq)]
    else:
        peers = [(z > 0, to(z - 1, y, c)), (z < Z - 1, to(z + 1, y, c))]
        if Y > 1:
            peers += [(y > 0, to(z, y - 1, c)), (y < Y - 1, to(z, y + 1, c))]
        if C == 2:
            peers.append((None, sib))
    if use_x:
        peers.append((None, xp))
    count = 0
    for cond, where in peers:
        when(cond, functools.partial(pl.semaphore_signal, bar, inc=1, device_id=where, device_id_type=MESH))
        count = count + (1 if cond is None else cond.astype(jnp.int32))
    pl.semaphore_wait(bar, count)
    if task:
        push_all[me] = push[...]

        def pushed(k, slot, where):
            return pltpu.make_async_remote_copy(
                src_ref=push, dst_ref=push_all.at[slot], send_sem=p_send.at[k], recv_sem=p_recv.at[slot], device_id=where, device_id_type=MESH)

        def push_one(k, _):
            pushed(k, me, (dp, lax.rem(me + k, nseq))).start()
            return 0

        def push_wait(k, _):
            other = lax.rem(me + k, nseq)
            pushed(k, other, (dp, other)).wait_recv()
            pushed(k, me, (dp, other)).wait_send()
            return 0

        lax.fori_loop(1, nseq, push_one, 0)

    def work(q):
        if task:
            task.run(me, q, push_all, *held, *task_out, *task_scratch)

    def go_z(i, slot, up, sem, own=False):
        where = to(z + 1, y, c) if up else to(z - 1, y, c)
        pl.when(up_z if up else down_z)(lambda: copy(i, slot, sem, where, own).start())

    def go_y(i, slot, up, sem, own=False):
        where = to(z, y + 1, c) if up else to(z, y - 1, c)
        pl.when(y < Y - 1 if up else y > 0)(lambda: copy(i, slot, sem, where, own).start())

    def go_core(i, slot, own=False):
        if C == 2:
            copy(i, slot, ss.at[i, slot], sib, own).start()

    def wait_in(i, slot):
        copy(i, slot, ss.at[i, slot], some).wait_recv()

    for i in range(n):
        pltpu.make_async_copy(mine(i), view(i, me), own_sem.at[i]).start()

        def own_sends(i=i):
            go_z(i, me, True, zs.at[i, me], True)
            go_z(i, me, False, ds.at[i, 0], True)
            if Y > 1:
                go_y(i, me, True, ys.at[i, me], True)
                go_y(i, me, False, ys.at[i, me] if moves[i].yfirst else ds.at[i, 1], True)

        when(owner(i), own_sends)
        go_core(i, me, True)

    def arrive_z(zz, up):
        slot = at(zz, y, c)

        def one(i):
            wait_in(i, slot)
            go_z(i, slot, up, zs.at[i, slot])
            if moves[i].yfirst:
                other = at(zz, 1 - y, c)
                go_core(i, slot)
                wait_in(i, other)
                go_z(i, other, up, zs.at[i, other])
                go_core(i, other)
                return
            if Y > 1:
                go_y(i, slot, True, ys.at[i, slot])
                go_y(i, slot, False, ys.at[i, slot] if Y == 2 else xs.at[i, slot])
            if use_x and moves[i].route:
                copy(i, slot, xs.at[i, slot], xp).start()
            go_core(i, slot)

        for i in range(n):
            when(owner(i), functools.partial(one, i))

    def arrive_y(zz, yy, up):
        slot = at(zz, yy, c)

        def one(i):
            wait_in(i, slot)
            if Y > 2:
                go_y(i, slot, up, ys.at[i, slot])
            if use_x and moves[i].route:
                copy(i, slot, xs.at[i, slot], xp).start()
            go_core(i, slot)

        for i in range(n):
            if not moves[i].yfirst:
                when(owner(i), functools.partial(one, i))

    def all_y(zz):
        for t in range(1, Y):
            pl.when(y - t >= 0)(lambda: arrive_y(zz, y - t, True))
            pl.when(y + t < Y)(lambda: arrive_y(zz, y + t, False))

    if task:
        lax.fori_loop(1, nseq, push_wait, 0)
        for load in loads:
            load.wait()
    for i in range(n):
        if moves[i].yfirst:
            other = at(z, 1 - y, c)
            wait_in(i, other)
            go_z(i, other, True, zs.at[i, other])
            go_z(i, other, False, ds.at[i, 1])
            go_core(i, other)

    def step(s, _):
        pl.when(z - s >= 0)(lambda: arrive_z(z - s, True))
        pl.when(z + s < Z)(lambda: arrive_z(z + s, False))
        q = s - 1
        pl.when(z - q >= 0)(lambda: all_y(z - q))
        pl.when(jnp.logical_and(q > 0, z + q < Z))(lambda: all_y(z + q))
        return 0

    if task:
        for s in (1, 2):
            if s < Z:
                step(s, 0)
            work(s - 1)
        lax.fori_loop(3, Z, step, 0)
    else:
        lax.fori_loop(1, Z, step, 0)
    q = Z - 1
    pl.when(z - q >= 0)(lambda: all_y(z - q))
    pl.when(z + q < Z)(lambda: all_y(z + q))

    if use_x:

        def far(k, _):
            slot = at(lax.rem(z + lax.div(k, Y), Z), lax.rem(y + lax.rem(k, Y), Y), c)

            def one(i):
                wait_in(i, slot)
                go_core(i, slot)

            for i in range(n):
                if moves[i].route:
                    pl.when(dp != moves[i].route - 1)(functools.partial(one, i))
            return 0

        lax.fori_loop(1, Z * Y, far, 0)

    def drain(k, _):
        zz, yy = lax.div(k, Y), lax.rem(k, Y)
        slot = at(zz, yy, c)
        is_own = slot == me
        own_y = yy == y
        fz = jnp.logical_or(jnp.logical_and(zz <= z, up_z), jnp.logical_and(zz > z, down_z))
        for i in range(n):
            o = owner(i)
            if C == 2:
                wait_in(i, at(zz, yy, 1 - c))
                copy(i, slot, ss.at[i, slot], some).wait_send()
            sent = lambda sem: copy(i, slot, sem, some).wait_send()
            if moves[i].yfirst:
                pl.when(fz)(lambda: sent(zs.at[i, slot]))
                pl.when(is_own)(lambda: sent(ys.at[i, slot]))
                continue
            pl.when(both(o, jnp.logical_and(own_y, fz)))(lambda: sent(zs.at[i, slot]))
            if Y == 2:
                pl.when(both(o, jnp.logical_and(own_y, jnp.logical_or(jnp.logical_not(is_own), y < Y - 1))))(lambda: sent(ys.at[i, slot]))
            elif Y > 2:
                fy = jnp.logical_or(jnp.logical_and(yy <= y, y < Y - 1), jnp.logical_and(yy > y, y > 0))
                pl.when(both(o, fy))(lambda: sent(ys.at[i, slot]))
                fy2 = jnp.logical_and(jnp.logical_and(own_y, y > 0), jnp.logical_not(is_own))
                pl.when(both(o, fy2))(lambda: sent(xs.at[i, slot]))
            if use_x and moves[i].route:
                pl.when(both(o, jnp.logical_not(is_own)))(lambda: sent(xs.at[i, slot]))
        return 0

    lax.fori_loop(0, Z * Y, drain, 0)
    for i in range(n):
        pltpu.make_async_copy(mine(i), view(i, me), own_sem.at[i]).wait()
        o = owner(i)
        pl.when(both(o, down_z))(lambda: copy(i, me, ds.at[i, 0], some, True).wait_send())
        if moves[i].yfirst:
            pl.when(down_z)(lambda: copy(i, me, ds.at[i, 1], some, True).wait_send())
        elif Y > 1:
            pl.when(both(o, y > 0))(lambda: copy(i, me, ds.at[i, 1], some, True).wait_send())


Task = collections.namedtuple("Task", ("n_in", "n_out", "run"))


def gather(arrays, cid, planes, nseq, task=None, inputs=(), outputs=(), scratch=()):
    dims = seq_dims(nseq)
    moves, shapes = [], []
    for k, (x, axis, route, ahead) in enumerate(arrays):
        rows = x.shape[axis]
        if planes != 2 or dims[1:] != (2, 2):
            route, ahead = 0, 0
        if ahead and ahead < x.shape[-1]:
            moves.append(Move(k, axis, rows, (0, ahead), 0, True))
            moves.append(Move(k, axis, rows, (ahead, x.shape[-1] - ahead), 0, False))
        else:
            moves.append(Move(k, axis, rows, None, route, bool(ahead)))
        shape = list(x.shape)
        shape[axis] *= nseq
        shapes.append(jax.ShapeDtypeStruct(tuple(shape), x.dtype))
    moves.sort(key=lambda m: not m.route)
    n = len(moves)
    D = pltpu.SemaphoreType.DMA
    scratch = [D((n,)), D((n, nseq)), D((n, nseq)), D((n, 2)), D((n, nseq)), D((n, nseq)), D((n, nseq))] + list(scratch)
    far, here = pl.BlockSpec(memory_space=pl.ANY), pl.BlockSpec(memory_space=pltpu.VMEM)
    return pl.pallas_call(
        functools.partial(gather_kernel, dims, planes, tuple(moves), len(arrays), task),
        out_shape=shapes + list(outputs),
        in_specs=[far] * len(arrays) + [here] * min(len(inputs), 1) + [far] * max(len(inputs) - 1, 0),
        out_specs=[far] * len(arrays) + [here] * len(outputs),
        scratch_shapes=scratch,
        compiler_params=pltpu.CompilerParams(collective_id=cid, has_side_effects=True, vmem_limit_bytes=60 << 20),
    )(*[x for x, _, _, _ in arrays], *inputs)


def gather_with(run, push, arrays, cid, planes, nseq, inputs, outputs, scratch):
    D = pltpu.SemaphoreType.DMA
    outputs = [jax.ShapeDtypeStruct((nseq,) + push.shape, push.dtype)] + outputs
    return gather(
        arrays, cid, planes, nseq, Task(1 + len(inputs), len(outputs), run), (push,) + tuple(inputs), outputs, [D((nseq,)), D((nseq,)), D((len(inputs),))] + [pltpu.VMEM(a.shape, a.dtype) for a in inputs] + scratch
    )


def dot(a, b):
    return jnp.dot(a, b, preferred_element_type=F32)


def dot_t(a, b):
    return lax.dot_general(a, b, (((1,), (1,)), ((), ())), preferred_element_type=F32)


def wgrad(a, b):
    return lax.dot_general(a, b, (((0,), (0,)), ((), ())), preferred_element_type=F32)


def vmem(mib):
    return pltpu.CompilerParams(vmem_limit_bytes=mib << 20)


def layer_norm(values, gain_row, shift_row):
    center = values - jnp.mean(values, -1, keepdims=True)
    spread = jnp.mean(center * center, -1, keepdims=True)
    return center * lax.rsqrt(spread + EPSILON) * gain_row + shift_row


def fill(pre_ref, decay, drive=None):
    for k in range(2):
        for j in range(HB):
            at = 2 * k * HG + j * 128
            rate = jax.nn.sigmoid(pre_ref[:, at : at + 128])
            decay[k * HB + j] = 1.0 - rate
            if drive is not None:
                drive[k * HB + j] = rate * pre_ref[:, at + HG : at + HG + 128]


def row(x, i):
    return lax.slice_in_dim(x, i, i + 1, axis=0)


def cat(parts):
    return jnp.concatenate(parts, 1)


def blocks(x):
    return [x[:, j * 128 : (j + 1) * 128] for j in range(HB)]


def totals_kernel(pre_ref, tot_ref, chunk_ref, decay, drive):
    length = pre_ref.shape[0] // NCH
    fill(pre_ref, decay, drive)

    def step(t, carry):
        place = (pl.ds(t, NCH, stride=length), pl.ds(length - 1 - t, NCH, stride=length))
        out = []
        for i in range(2 * HB):
            c, h = carry[i]
            a = decay[i, place[i // HB], :]
            out.append((c * a, a * h + drive[i, place[i // HB], :]))
        return tuple(out)

    one, zero = jnp.ones((NCH, 128), F32), jnp.zeros((NCH, 128), F32)
    ends = lax.fori_loop(0, length, step, ((one, zero),) * (2 * HB), unroll=UNROLL)
    cf, hf = cat([e[0] for e in ends[:HB]]), cat([e[1] for e in ends[:HB]])
    cb, hb = cat([e[0] for e in ends[HB:]]), cat([e[1] for e in ends[HB:]])
    chunk_ref[0:NCH, :] = cf
    chunk_ref[NCH : 2 * NCH, :] = hf
    chunk_ref[2 * NCH : 3 * NCH, :] = cb
    chunk_ref[3 * NCH :, :] = hb
    one, zero = jnp.ones((1, HG), F32), jnp.zeros((1, HG), F32)
    tf, sf, tb, sb = one, zero, one, zero
    for k in range(NCH):
        sf, tf = row(cf, k) * sf + row(hf, k), tf * row(cf, k)
        j = NCH - 1 - k
        sb, tb = row(cb, j) * sb + row(hb, j), tb * row(cb, j)
    tot_ref[...] = jnp.concatenate([tf, sf, tb, sb], 0)


def states_work(me, q, seqs, all_ref, pre_all, chunk_all, ends_all, pooled_all, prev_all, decay, drive, state, prev):
    pre_ref, chunk_ref, ends_ref, pooled_ref, prev_ref = (
        r.at[pl.ds(q * (r.shape[0] // seqs), r.shape[0] // seqs)] for r in (pre_all, chunk_all, ends_all, pooled_all, prev_all)
    )
    chars = pre_all.shape[0] // seqs
    length = chars // NCH
    nseq = all_ref.shape[0]
    fill(pre_ref, decay, drive)
    ef = jnp.zeros((1, HG), F32)
    eb = ef
    for d in range(nseq):
        got = all_ref[d]
        ef = jnp.where(d < me, row(got, 4 * q) * ef + row(got, 4 * q + 1), ef)
        got = all_ref[nseq - 1 - d]
        eb = jnp.where(nseq - 1 - d > me, row(got, 4 * q + 2) * eb + row(got, 4 * q + 3), eb)
    cf, hf = chunk_ref[0:NCH, :], chunk_ref[NCH : 2 * NCH, :]
    cb, hb = chunk_ref[2 * NCH : 3 * NCH, :], chunk_ref[3 * NCH :, :]
    rows_f, rows_b = [], []
    for k in range(NCH):
        rows_f.append(ef)
        ef = row(cf, k) * ef + row(hf, k)
        j = NCH - 1 - k
        rows_b.append(eb)
        eb = row(cb, j) * eb + row(hb, j)

    def step(t, carry):
        place = (pl.ds(t, NCH, stride=length), pl.ds(length - 1 - t, NCH, stride=length))
        out = []
        for i in range(2 * HB):
            at = place[i // HB]
            prev[i, at, :] = carry[i]
            h = decay[i, at, :] * carry[i] + drive[i, at, :]
            state[i, at, :] = h
            out.append(h)
        return tuple(out)

    lax.fori_loop(0, length, step, tuple(blocks(jnp.concatenate(rows_f, 0)) + blocks(jnp.concatenate(rows_b[::-1], 0))), unroll=UNROLL)
    first = ends_ref[:, 0:1]
    last = ends_ref[:, 1:2]
    place = lax.broadcasted_iota(jnp.int32, (ends_all.shape[0] // seqs, chars), 1)
    member = jnp.where((place >= first) & (place < last), 1.0, 0.0).astype(BF)
    prev_ref[...] = cat([prev[i] for i in range(2 * HB)])
    pooled_ref[...] = dot(member, cat([state[i].astype(BF) for i in range(2 * HB)])) / (last - first).astype(F32)


def flows_kernel(pre_ref, dpool_ref, ends_ref, chunk_ref, ds_ref, tot_ref, gch_ref, decay, ds):
    chars = pre_ref.shape[0]
    length = chars // NCH
    fill(pre_ref, decay)
    first = ends_ref[0:1, :]
    last = ends_ref[1:2, :]
    place = lax.broadcasted_iota(jnp.int32, (chars, ends_ref.shape[1]), 0)
    inside = (place >= first) & (place < last)
    span = jnp.sum(jnp.where(inside, (last - first).astype(F32), 0.0), 1, keepdims=True)
    member = jnp.where(inside, 1.0, 0.0).astype(BF)
    spread = dot(member, dpool_ref[...]) / span
    ds_ref[...] = spread
    for i in range(2 * HB):
        ds[i] = spread[:, i * 128 : (i + 1) * 128]

    def step(t, carry):
        place = (pl.ds(length - 1 - t, NCH, stride=length), pl.ds(t, NCH, stride=length))
        return tuple(
            decay[i, place[i // HB], :] * (ds[i, place[i // HB], :] + carry[i]) for i in range(2 * HB)
        )

    ends = lax.fori_loop(0, length, step, (jnp.zeros((NCH, 128), F32),) * (2 * HB), unroll=UNROLL)
    gf, gb = cat(ends[:HB]), cat(ends[HB:])
    gch_ref[0:NCH, :] = gf
    gch_ref[NCH:, :] = gb
    cf, cb = chunk_ref[0:NCH, :], chunk_ref[2 * NCH : 3 * NCH, :]
    zero = jnp.zeros((1, HG), F32)
    tf, tb = zero, zero
    for k in range(NCH):
        j = NCH - 1 - k
        tf = row(cf, j) * tf + row(gf, j)
        tb = row(cb, k) * tb + row(gb, k)
    tot_ref[...] = jnp.concatenate([tf, tb, zero, zero], 0)


def dpre_work(me, q, seqs, gall_ref, all_ref, pre_all, ds_all, prev_all, chunk_all, gch_all, dpre_all, bias_all, decay, ds):
    pre_ref, ds_ref, prev_ref, chunk_ref, gch_ref, dpre_ref, bias_ref = (
        r.at[pl.ds(q * (r.shape[0] // seqs), r.shape[0] // seqs)] for r in (pre_all, ds_all, prev_all, chunk_all, gch_all, dpre_all, bias_all)
    )
    chars = pre_all.shape[0] // seqs
    length = chars // NCH
    nseq = all_ref.shape[0]
    fill(pre_ref, decay)
    for i in range(2 * HB):
        ds[i] = ds_ref[:, i * 128 : (i + 1) * 128]
    ef = jnp.zeros((1, HG), F32)
    eb = ef
    for d in range(nseq):
        j = nseq - 1 - d
        ef = jnp.where(j > me, row(all_ref[j], 4 * q) * ef + row(gall_ref[j], 4 * q), ef)
        eb = jnp.where(d < me, row(all_ref[d], 4 * q + 2) * eb + row(gall_ref[d], 4 * q + 1), eb)
    cf, cb = chunk_ref[0:NCH, :], chunk_ref[2 * NCH : 3 * NCH, :]
    gf, gb = gch_ref[0:NCH, :], gch_ref[NCH:, :]
    rows_f, rows_b = [], []
    for k in range(NCH):
        j = NCH - 1 - k
        rows_f.append(ef)
        ef = row(cf, j) * ef + row(gf, j)
        rows_b.append(eb)
        eb = row(cb, k) * eb + row(gb, k)

    def step(t, carry):
        place = (pl.ds(length - 1 - t, NCH, stride=length), pl.ds(t, NCH, stride=length))
        out = []
        for i in range(2 * HB):
            at = place[i // HB]
            g = ds[i, at, :] + carry[i]
            ds[i, at, :] = g
            out.append(decay[i, at, :] * g)
        return tuple(out)

    lax.fori_loop(0, length, step, tuple(blocks(jnp.concatenate(rows_f[::-1], 0)) + blocks(jnp.concatenate(rows_b, 0))), unroll=UNROLL)
    for i in range(2 * HB):
        k, j = i // HB, i % HB
        at = 2 * k * HG + j * 128
        g = ds[i]
        rate = jax.nn.sigmoid(pre_ref[:, at : at + 128])
        cand = pre_ref[:, at + HG : at + HG + 128]
        prev = prev_ref[:, i * 128 : (i + 1) * 128]
        dgate = (g * (cand - prev) * rate * decay[i]).astype(BF)
        dcand = (g * rate).astype(BF)
        for to, v in ((at, dgate), (at + HG, dcand)):
            dpre_ref[:, to : to + 128] = v
            bias_ref[:, to : to + 128] = jnp.broadcast_to(jnp.sum(v.astype(F32), 0, keepdims=True), (8, 128))


def rows_spec(rows, cols):
    return pl.BlockSpec((rows, cols), lambda s: (s, 0))


def four_spec():
    return pl.BlockSpec((None, 4, HG), lambda s: (s, 0, 0))


def scr(*shapes):
    return [pltpu.VMEM(s, F32) for s in shapes]


def char_totals(pre, seqs, chars):
    return pl.pallas_call(
        totals_kernel,
        grid=(seqs,),
        out_shape=[jax.ShapeDtypeStruct((seqs, 4, HG), F32), jax.ShapeDtypeStruct((seqs * 4 * NCH, HG), F32)],
        in_specs=[rows_spec(chars, 4 * HG)],
        out_specs=[four_spec(), rows_spec(4 * NCH, HG)],
        scratch_shapes=scr(*[(2 * HB, chars, 128)] * 2),
        compiler_params=vmem(40),
    )(pre)


def char_flows(pre, dpool, ends_row, chunk, seqs, chars, toks):
    return pl.pallas_call(
        flows_kernel,
        grid=(seqs,),
        out_shape=[
            jax.ShapeDtypeStruct((seqs * chars, 2 * HG), F32),
            jax.ShapeDtypeStruct((seqs, 4, HG), F32),
            jax.ShapeDtypeStruct((seqs * 2 * NCH, HG), F32),
        ],
        in_specs=[rows_spec(chars, 4 * HG), rows_spec(toks, 2 * HG), rows_spec(8, toks), rows_spec(4 * NCH, HG)],
        out_specs=[rows_spec(chars, 2 * HG), four_spec(), rows_spec(2 * NCH, HG)],
        scratch_shapes=scr(*[(2 * HB, chars, 128)] * 2),
        compiler_params=vmem(48),
    )(pre, dpool, ends_row, chunk)


def pair_rows(x):
    lane = lax.broadcasted_iota(jnp.int32, x.shape, 1)
    zero = jnp.zeros_like(x)
    return jnp.concatenate([jnp.where(lane < HDIM, x, zero), jnp.where(lane >= HDIM, x, zero)], 0)


def pair_lanes(x):
    half = x.shape[0] // 2
    lane = lax.broadcasted_iota(jnp.int32, (half, x.shape[1]), 1)
    return jnp.where(lane < HDIM, x[:half], x[half:])


def attn_fwd_kernel(q_ref, k_ref, v_ref, ctx_ref, low_ref, lse_ref):
    toks = q_ref.shape[0]
    s = dot_t(pair_rows(q_ref[...] * (HDIM ** -0.5)), k_ref[...])
    top = jnp.max(s, 1, keepdims=True)
    p = jnp.exp(s - top)
    total = jnp.sum(p, 1, keepdims=True)
    o = pair_lanes(dot(p.astype(BF), v_ref[...]) / total)
    ctx_ref[...] = o
    low_ref[...] = o.astype(BF)
    lse = top + jnp.log(total)
    lse_ref[...] = jnp.concatenate([lse[:toks], lse[toks:]], 1)


def head_spec(rows, base=0):
    return pl.BlockSpec((None, rows, 2 * HDIM), lambda s, h: (s, 0, h + base))


def attention_fwd(qkv, keys, values):
    seqs, toks, _ = qkv.shape
    length = keys.shape[1]
    pairs = HEADS // 2
    return pl.pallas_call(
        attn_fwd_kernel,
        grid=(seqs, pairs),
        out_shape=[
            jax.ShapeDtypeStruct((seqs, toks, HEADS * HDIM), F32),
            jax.ShapeDtypeStruct((seqs, toks, HEADS * HDIM), BF),
            jax.ShapeDtypeStruct((seqs, pairs, toks, 2), F32),
        ],
        in_specs=[head_spec(toks), head_spec(length), head_spec(length)],
        out_specs=[head_spec(toks), head_spec(toks), pl.BlockSpec((None, None, toks, 2), lambda s, h: (s, h, 0, 0))],
        compiler_params=vmem(48),
    )(qkv, keys, values)


def attn_bwd_kernel(q_ref, ko_ref, vo_ref, dc_ref, col_ref, ka_ref, va_ref, qa_ref, dca_ref, row_ref, dq_ref, dk_ref, dv_ref):
    toks = q_ref.shape[0]
    scale = HDIM ** -0.5
    lse = jnp.concatenate([col_ref[:, 0:1], col_ref[:, 1:2]], 0)
    delta = jnp.concatenate([col_ref[:, 2:3], col_ref[:, 3:4]], 0)
    p = jnp.exp(dot_t(pair_rows(q_ref[...] * scale), ka_ref[...]) - lse)
    dp = dot_t(pair_rows(dc_ref[...]), va_ref[...])
    ds = (p * (dp - delta)).astype(BF)
    dq_ref[...] = (pair_lanes(dot(ds, ka_ref[...])) * scale).astype(BF)

    def spread(i):
        n = row_ref.shape[1]
        return jnp.concatenate(
            [jnp.broadcast_to(row_ref[i : i + 1, :], (toks, n)), jnp.broadcast_to(row_ref[i + 1 : i + 2, :], (toks, n))], 0
        )

    p = jnp.exp(dot_t(pair_rows(ko_ref[...] * scale), qa_ref[...]) - spread(0))
    dv_ref[...] = pair_lanes(dot(p.astype(BF), dca_ref[...])).astype(BF)
    dp = dot_t(pair_rows(vo_ref[...]), dca_ref[...])
    ds = (p * (dp - spread(2))).astype(BF)
    dk_ref[...] = (pair_lanes(dot(ds, qa_ref[...])) * scale).astype(BF)


def attention_bwd(qkv, dctx, col, keys, values, queries, dctx_all, rows):
    seqs, toks, _ = qkv.shape
    length = keys.shape[1]
    pairs = HEADS // 2
    width = HEADS * HDIM
    stat = lambda a, b: pl.BlockSpec((None, None, a, b), lambda s, h: (s, h, 0, 0))
    return pl.pallas_call(
        attn_bwd_kernel,
        grid=(seqs, pairs),
        out_shape=[jax.ShapeDtypeStruct((seqs, toks, width), BF)] * 3,
        in_specs=[
            head_spec(toks), head_spec(toks, pairs), head_spec(toks, 2 * pairs), head_spec(toks), stat(toks, 4),
            head_spec(length), head_spec(length), head_spec(length), head_spec(length), stat(4, length),
        ],
        out_specs=[head_spec(toks)] * 3,
        compiler_params=vmem(56),
    )(qkv, qkv, qkv, dctx, col, keys, values, queries, dctx_all, rows)


GELU_A = 0.7978845608028654
GELU_B = 0.044715


def norm_both(v, gain, shift, dy):
    center = v - jnp.mean(v, -1, keepdims=True)
    inv = lax.rsqrt(jnp.mean(center * center, -1, keepdims=True) + EPSILON)
    hat = center * inv
    dhat = dy * gain
    dv = inv * (dhat - jnp.mean(dhat, -1, keepdims=True) - hat * jnp.mean(dhat * hat, -1, keepdims=True))
    return hat * gain + shift, dv, jnp.sum(dy * hat, 0, keepdims=True), jnp.sum(dy, 0, keepdims=True)


def conv_kernel(seqs, state_ref, pooled_ref, gtok_ref, gchr_ref, nrm_ref, ws_ref, c0_ref, c1_ref, c2_ref,
                otok_ref, ochr_ref, slow_ref, plow_ref, mprev_ref, merged_ref, mnext_ref, dmix_ref, dfus_ref, dstate_ref, dpool_ref, dnorm_ref,
                taps, acc, edge, before, after, dside, dchar, w_sem, e_send, b_recv, a_recv):
    me = lax.axis_index("seq")
    dp = lax.axis_index("dp")
    n = lax.axis_size("seq")
    rows, width = state_ref.shape
    toks = rows // seqs
    wide = 2 * width
    loads = [pltpu.make_async_copy(c, taps.at[k], w_sem.at[k]) for k, c in ((1, c1_ref), (0, c0_ref), (2, c2_ref))]
    for load in loads:
        load.start()
    edge[...] = jnp.zeros_like(edge)
    dnorm_ref[4:8, :] = jnp.zeros((4, width), F32)
    right, left = (dp, me + 1), (dp, me - 1)
    has_l, has_r = me > 0, me < n - 1
    bar = pltpu.get_barrier_semaphore()
    pl.when(has_l)(lambda: pl.semaphore_signal(bar, inc=1, device_id=left, device_id_type=MESH))
    pl.when(has_r)(lambda: pl.semaphore_signal(bar, inc=1, device_id=right, device_id_type=MESH))
    pl.semaphore_wait(bar, has_l.astype(jnp.int32) + has_r.astype(jnp.int32))

    def send(k):
        def to_right():
            return pltpu.make_async_remote_copy(
                src_ref=edge.at[k, 0], dst_ref=before.at[k], send_sem=e_send.at[k, 0], recv_sem=b_recv.at[k], device_id=right, device_id_type=MESH)

        def to_left():
            return pltpu.make_async_remote_copy(
                src_ref=edge.at[k, 1], dst_ref=after.at[k], send_sem=e_send.at[k, 1], recv_sem=a_recv.at[k], device_id=left, device_id_type=MESH)

        return to_right, to_left

    def start(k, ref):
        for s in range(seqs):
            edge[k, 0, s : s + 1, :] = ref[(s + 1) * toks - 16 : (s + 1) * toks, :].astype(F32)[15:16]
            edge[k, 1, s : s + 1, :] = ref[s * toks : s * toks + 16, :].astype(F32)[0:1]
        to_right, to_left = send(k)
        pl.when(has_r)(lambda: to_right().start())
        pl.when(has_l)(lambda: to_left().start())

    def finish(k):
        to_right, to_left = send(k)
        pl.when(has_r)(lambda: to_left().wait_recv())
        pl.when(has_l)(lambda: to_right().wait_recv())
        pl.when(has_r)(lambda: to_right().wait_send())
        pl.when(has_l)(lambda: to_left().wait_send())

    def shifts(k, ref, prev_ref, next_ref):
        for j in range(0, wide, 512):
            x = ref[:, j : j + 512].astype(F32)
            at = lax.broadcasted_iota(jnp.int32, x.shape, 0)
            prev, follow = pltpu.roll(x, 1, 0), pltpu.roll(x, rows - 1, 0)
            for s in range(seqs):
                b = jnp.where(has_l, before[k, s : s + 1, j : j + 512], 0.0)
                a = jnp.where(has_r, after[k, s : s + 1, j : j + 512], 0.0)
                prev = jnp.where(at == s * toks, b, prev)
                follow = jnp.where(at == (s + 1) * toks - 1, a, follow)
            prev_ref[:, j : j + 512] = prev.astype(BF)
            next_ref[:, j : j + 512] = follow.astype(BF)

    slow = state_ref[...].astype(BF)
    plow = pooled_ref[...].astype(BF)
    slow_ref[...] = slow
    plow_ref[...] = plow
    merged_ref[:, :width] = dot(slow, ws_ref[0]).astype(BF)
    merged_ref[:, width:] = dot(plow, ws_ref[1]).astype(BF)
    start(0, merged_ref)
    loads[0].wait()

    def centre(j, _):
        cols = pl.ds(pl.multiple_of(j * 512, 512), 512)
        acc[:, cols] = dot(merged_ref[...], taps[1, :, cols])
        return 0

    lax.fori_loop(0, wide // 512, centre, 0)
    finish(0)
    shifts(0, merged_ref, mprev_ref, mnext_ref)
    loads[1].wait()
    loads[2].wait()

    def sides(j, _):
        cols = pl.ds(pl.multiple_of(j * 512, 512), 512)
        acc[:, cols] += dot(mprev_ref[...], taps[0, :, cols]) + dot(mnext_ref[...], taps[2, :, cols])
        return 0

    lax.fori_loop(0, wide // 512, sides, 0)
    for part, (base_ref, grad_ref, out_ref) in enumerate(((state_ref, gtok_ref, otok_ref), (pooled_ref, gchr_ref, ochr_ref))):
        mixed = acc[:, part * width : (part + 1) * width]
        square = mixed * mixed
        curve = jnp.tanh(GELU_A * (mixed + GELU_B * mixed * square))
        gated = 0.5 * mixed * (1.0 + curve)
        slope = 0.5 * (1.0 + curve) + 0.5 * mixed * (1.0 - curve * curve) * (GELU_A * (1.0 + 3.0 * GELU_B * square))
        r = 4 + 2 * part
        out, dsum, dgain, dshift = norm_both(base_ref[...] + gated, nrm_ref[r : r + 1, :], nrm_ref[r + 1 : r + 2, :], grad_ref[...].astype(F32))
        out_ref[...] = out.astype(BF)
        dnorm_ref[2 * part : 2 * part + 1, :] = dgain
        dnorm_ref[2 * part + 1 : 2 * part + 2, :] = dshift
        dmix_ref[:, part * width : (part + 1) * width] = (dsum * slope).astype(BF)
        if part == 0:
            dstate_ref[...] = dsum
        else:
            dchar[...] = dsum
    start(1, dmix_ref)

    def centre_back(j, _):
        cols = pl.ds(pl.multiple_of(j * 512, 512), 512)
        acc[:, cols] = dot_t(dmix_ref[...], taps[1, cols, :])
        return 0

    lax.fori_loop(0, wide // 512, centre_back, 0)
    finish(1)
    shifts(1, dmix_ref, dside.at[0], dside.at[1])

    def sides_back(j, _):
        cols = pl.ds(pl.multiple_of(j * 512, 512), 512)
        dfus_ref[:, cols] = (acc[:, cols] + dot_t(dside[1], taps[0, cols, :]) + dot_t(dside[0], taps[2, cols, :])).astype(BF)
        return 0

    lax.fori_loop(0, wide // 512, sides_back, 0)
    dstate_ref[...] += dot_t(dfus_ref[:, :width], ws_ref[0])
    dpool_ref[...] = (dchar[...] + dot_t(dfus_ref[:, width:], ws_ref[1])).astype(BF)


def conv_both(seqs, token_state, pooled, grad_token, grad_char, nrm, w_stream, w_conv, cid):
    rows, width = token_state.shape
    wide = 2 * width
    here = pl.BlockSpec(memory_space=pltpu.VMEM)
    far = pl.BlockSpec(memory_space=pl.ANY)
    low, full = jax.ShapeDtypeStruct((rows, width), BF), jax.ShapeDtypeStruct((rows, width), F32)
    both = jax.ShapeDtypeStruct((rows, wide), BF)
    D = pltpu.SemaphoreType.DMA
    return pl.pallas_call(
        functools.partial(conv_kernel, seqs),
        out_shape=[low, low, low, low, both, both, both, both, both, full, low, jax.ShapeDtypeStruct((8, width), F32)],
        in_specs=[here] * 6 + [far] * 3,
        out_specs=[here] * 12,
        scratch_shapes=[
            pltpu.VMEM((3, wide, wide), BF), pltpu.VMEM((rows, wide), F32), pltpu.VMEM((2, 2, 8, wide), F32),
            pltpu.VMEM((2, 8, wide), F32), pltpu.VMEM((2, 8, wide), F32), pltpu.VMEM((2, rows, wide), BF), pltpu.VMEM((rows, width), F32),
            D((3,)), D((2, 2)), D((2,)), D((2,)),
        ],
        compiler_params=pltpu.CompilerParams(collective_id=cid, has_side_effects=True, vmem_limit_bytes=60 << 20),
    )(token_state, pooled, grad_token, grad_char, nrm, w_stream, *w_conv)


RZ, RY, RC = 4, 2, 2
PW = 384
PR = 48
LD, LX, LY, LH, LF = 2, 8, 12, 3, 25
HRING = LY + 1


Group = collections.namedtuple("Group", ("left", "parts", "right", "col", "cols", "out", "lead", "at"))
GRU, TABLE, TINY = 5, 4, 8


def piece_groups(taps):
    rows = [(6 + k, 2, 5, 0, 4, 7, i) for i, k in enumerate(taps)]
    rows += [(4, 1, 4, 0, 2, 6, 0), (5, 1, 4, 768, 2, 6, 1), (3, 4, 3, 0, 2, 3, None), (2, 1, 2, 0, 8, 2, None), (1, 1, 1, 0, 2, 1, None), (0, 1, 0, 0, 6, 0, None)]
    out, at = [], 0
    for r in rows:
        out.append(Group(*r, at))
        at += r[1] * r[4]
    return tuple(out), at


MISC = (((GRU, 0), (GRU, 1), (GRU, 2)), ((GRU, 3), (TABLE, 0), (TABLE, 1)), ((TABLE, 2), (TINY, 0), (None, 0)))


def reduce_kernel(npieces, groups, *refs):
    lhs, rhs = refs[:9], refs[9:15]
    emb_ref, dpre_ref, demb_ref, ids_ref, tiny_ref = refs[15:20]
    outs = refs[20:29]
    (lt, done, part, r0, held, r1, r2, up, dn, fin, fx,
     d_send, d_recv, x_send, x_recv, y_send, y_recv, u_send, u_recv, n_send, n_recv, f_send, f_recv) = refs[29:]
    dp = lax.axis_index("dp")
    me = lax.axis_index("seq")
    c = lax.rem(me, RC)
    y = lax.rem(lax.div(me, RC), RY)
    z = lax.div(me, RC * RY)

    def to(zz, yy, cc):
        return (dp, (zz * RY + yy) * RC + cc)

    sib, ynb, zup, zdn, xnb = to(z, y, 1 - c), to(z, 1 - y, c), to(z + 1, y, c), to(z - 1, y, c), (1 - dp, me)
    bar = pltpu.get_barrier_semaphore()
    for where in (sib, ynb, xnb):
        pl.semaphore_signal(bar, inc=1, device_id=where, device_id_type=MESH)
    pl.when(z > 0)(lambda: pl.semaphore_signal(bar, inc=1, device_id=zdn, device_id_type=MESH))
    pl.when(z < RZ - 1)(lambda: pl.semaphore_signal(bar, inc=1, device_id=zup, device_id_type=MESH))
    pl.semaphore_wait(bar, 3 + (z > 0).astype(jnp.int32) + (z < RZ - 1).astype(jnp.int32))

    def copy(src, dst, send, recv, where):
        return pltpu.make_async_remote_copy(src_ref=src, dst_ref=dst, send_sem=send, recv_sem=recv, device_id=where, device_id_type=MESH)

    def d2d(t):
        b, k = lax.rem(t, LD + 1), lax.rem(t, 2 * LD)
        return copy(part.at[b, :, :, 1 - c], r0.at[k], d_send.at[b], d_recv.at[k], sib)

    def far(t):
        return lax.div(t, 11) * 3 + lax.div(lax.rem(t, 11), 3)

    def across(t):
        return copy(held.at[lax.rem(t, HRING)], r1.at[far(t)], x_send.at[t], x_recv.at[t], xnb)

    def along_y(t):
        return copy(held.at[lax.rem(t, HRING), :, 1 - y], r2.at[t], y_send.at[t], y_recv.at[t], ynb)

    def final(t):
        return copy(fin.at[t], fx.at[t], f_send.at[t], f_recv.at[t], xnb)

    def go_up(t, k):
        src = r2.at[t, pl.ds(k + 1, RZ - 1 - k)] if k == 0 else up.at[t, pl.ds(k, RZ - 1 - k)]
        return copy(src, up.at[t, pl.ds(k, RZ - 1 - k)], u_send.at[t], u_recv.at[t], zup)

    def from_below(t, k):
        ref = up.at[t, pl.ds(k - 1, RZ - k)]
        return copy(ref, ref, u_send.at[t], u_recv.at[t], zdn)

    def go_down(t, k):
        src = r2.at[t, pl.ds(0, k)] if k == RZ - 1 else dn.at[t, pl.ds(0, k)]
        return copy(src, dn.at[t, pl.ds(0, k)], n_send.at[t], n_recv.at[t], zdn)

    def from_above(t, k):
        ref = dn.at[t, pl.ds(0, k + 1)]
        return copy(ref, ref, n_send.at[t], n_recv.at[t], zup)

    def add(a, b):
        return (a.astype(F32) + b.astype(F32)).astype(BF)

    def live(t):
        return jnp.logical_and(t >= 0, t < npieces)

    def route(t):
        m = lax.rem(t, 11)
        return jnp.where(m < 9, lax.rem(m, 3), 0)

    def mine(t):
        r = route(t)
        return jnp.logical_or(r == 0, r - 1 == dp)

    def finish(t):
        r = route(t)

        @pl.when(r == 0)
        def _():
            final(t).wait_recv()
            done[...] = fin[t].astype(F32) + fx[t].astype(F32)

        @pl.when(jnp.logical_and(r > 0, r - 1 == dp))
        def _():
            done[...] = fin[t].astype(F32)

        @pl.when(jnp.logical_and(r > 0, r - 1 != dp))
        def _():
            final(t).wait_recv()
            done[...] = fx[t].astype(F32)

        pl.when(mine(t))(lambda: final(t).wait_send())
        for g in groups:
            @pl.when(jnp.logical_and(t >= g.at, t < g.at + g.parts * g.cols))
            def _(g=g):
                i = t - g.at
                rows = pl.ds(pl.multiple_of(lax.div(i, g.cols) * PR, PR), PR)
                cols = pl.ds(pl.multiple_of(lax.rem(i, g.cols) * PW, PW), PW)
                if g.lead is None:
                    outs[g.out][rows, cols] = done[...]
                else:
                    outs[g.out][g.lead, rows, cols] = done[...]
        for m, trio in enumerate(MISC):
            @pl.when(t == npieces - len(MISC) + m)
            def _(trio=trio):
                for i, (kind, cb) in enumerate(trio):
                    if kind is not None:
                        outs[kind][:, cb * PW : (cb + 1) * PW] = done[16 * i : 16 * i + 16, :]

    def sum_up(t):
        for k in range(RZ):
            @pl.when(z == k)
            def _(k=k):
                if k > 0:
                    from_below(t, k).wait_recv()
                    for q in range(k + 1, RZ):
                        up[t, q - 1] = add(up[t, q - 1], r2[t, q])
                if k < RZ - 1:
                    go_up(t, k).start()

    def sum_down(t):
        for k in range(RZ):
            @pl.when(z == k)
            def _(k=k):
                if k < RZ - 1:
                    from_above(t, k).wait_recv()
                    for q in range(k):
                        dn[t, q] = add(dn[t, q], r2[t, q])
                if k > 0:
                    go_down(t, k).start()

    def close(t):
        for k in range(RZ):
            @pl.when(z == k)
            def _(k=k):
                total = r2[t, k].astype(F32)
                if k > 0:
                    total = total + up[t, k - 1].astype(F32)
                    go_down(t, k).wait_send()
                if k < RZ - 1:
                    total = total + dn[t, k].astype(F32)
                    go_up(t, k).wait_send()
                fin[t] = total.astype(BF)
        final(t).start()

    def join_y(t):
        along_y(t).wait_recv()
        along_y(t).wait_send()
        h = lax.rem(t, HRING)
        for q in range(RZ):
            r2[t, q] = add(r2[t, q], held[h, q, y])

    def join_x(t):
        h = lax.rem(t, HRING)

        @pl.when(route(t) > 0)
        def _():
            across(t).wait_recv()
            for q in range(RZ):
                held[h, q] = add(held[h, q], r1[far(t), q])

        along_y(t).start()

    def join_core(t):
        b, k = lax.rem(t, LD + 1), lax.rem(t, 2 * LD)
        h = lax.rem(t, HRING)
        d2d(t).wait_recv()
        d2d(t).wait_send()
        for q in range(RZ):
            held[h, q] = add(part[b, q, :, c], r0[k, q])
        pl.when(jnp.logical_not(mine(t)))(lambda: across(t).start())

    def turn(ref):
        n = ref.shape[0]
        for k in range(0, ref.shape[1], 384):
            lt[k // PR : k // PR + 8, :, :n] = ref[:, k : k + 384].T.reshape(8, PR, n)

    def make(t):
        b = lax.rem(t, LD + 1)
        for g in groups:
            @pl.when(jnp.logical_and(t >= g.at, t < g.at + g.parts * g.cols))
            def _(g=g):
                i = t - g.at
                j, cb = lax.div(i, g.cols), lax.rem(i, g.cols)
                pl.when(i == 0)(lambda: turn(lhs[g.left]))
                right = rhs[g.right][:, pl.ds(pl.multiple_of(g.col + cb * PW, PW), PW)]
                for q in range(RZ // 2):
                    left = jnp.concatenate([lt[(8 * q + s) * g.parts + j] for s in range(8)], 0)
                    part[b, 2 * q : 2 * q + 2] = dot(left, right).astype(BF).reshape(2, RY, RC, PR, PW)
        for m, trio in enumerate(MISC):
            @pl.when(t == npieces - len(MISC) + m)
            def _(trio=trio):
                for i, (kind, cb) in enumerate(trio):
                    if kind == GRU:
                        val = wgrad(emb_ref[...], dpre_ref[:, cb * PW : (cb + 1) * PW]).astype(BF).reshape(RZ, RY, RC, 16, PW)
                    elif kind == TABLE:
                        unit = lax.broadcasted_iota(jnp.int32, (ids_ref.shape[0], PW), 1) + cb * PW
                        hot = jnp.where(unit == ids_ref[...], 1.0, 0.0).astype(BF)
                        val = wgrad(demb_ref[...], hot).astype(BF).reshape(RZ, RY, RC, 16, PW)
                    elif kind == TINY:
                        val = tiny_ref[...].reshape(RZ, RY, RC, 16, PW)
                    else:
                        val = jnp.zeros((RZ, RY, RC, 16, PW), BF)
                    part[b, :, :, :, 16 * i : 16 * i + 16, :] = val
        d2d(t).start()

    def tick(T, _):
        def do(t, f, cond=None):
            ok = live(t)
            pl.when(ok if cond is None else jnp.logical_and(ok, cond(t)))(lambda: f(t))

        do(T - LF, finish)
        do(T - LY - z * LH, sum_up, mine)
        do(T - LY - (RZ - 1 - z) * LH, sum_down, mine)
        do(T - LY - (RZ - 1) * LH, close, mine)
        do(T - LY + 1, join_y, mine)
        do(T - LX, join_x, mine)
        do(T - LX, lambda t: across(t).wait_send(), lambda t: jnp.logical_not(mine(t)))
        do(T - LD, join_core)
        do(T, make)
        return 0

    lax.fori_loop(0, npieces + LF + 1, tick, 0)


def reduce_all(lhs, rhs, emb, dpre, demb, ids, g_bias, g_norms, n_table, nseq, cid, taps=(0, 1, 2)):
    width = lhs[0].shape[1]
    per = g_bias.shape[0] // nseq
    tiny = jnp.concatenate([g_bias.reshape(nseq, per), g_norms.reshape(8, nseq, -1).transpose(1, 0, 2).reshape(nseq, -1)], 1).astype(BF)
    tiny = jnp.pad(tiny, ((0, 0), (0, 16 * PW - tiny.shape[1]))).reshape(nseq, 16, PW)
    groups, npieces = piece_groups(taps)
    npieces += len(MISC)
    D = pltpu.SemaphoreType.DMA
    v = lambda *s: pltpu.VMEM(s, BF)
    spec = pl.BlockSpec(memory_space=pltpu.VMEM)
    f = lambda *s: jax.ShapeDtypeStruct(s, F32)
    wide = 2 * width
    got = pl.pallas_call(
        functools.partial(reduce_kernel, npieces, groups),
        out_shape=[
            f(width // nseq, 3 * width), f(width // nseq, width), f(width // nseq, 4 * width), f(4 * width // nseq, width),
            f(16, 3 * PW), f(16, 4 * PW), f(2, width // nseq, width), f(max(len(taps), 1), wide // nseq, wide), f(16, PW),
        ],
        in_specs=[spec] * 20,
        out_specs=[spec] * 9,
        scratch_shapes=[
            v(64, PR, lhs[0].shape[0]), pltpu.VMEM((PR, PW), F32),
            v(LD + 1, RZ, RY, RC, PR, PW), v(2 * LD, RZ, RY, PR, PW), v(HRING, RZ, RY, PR, PW), v(3 * (npieces // 11 + 1), RZ, RY, PR, PW),
            v(npieces, RZ, PR, PW), v(npieces, RZ - 1, PR, PW), v(npieces, RZ - 1, PR, PW), v(npieces, PR, PW), v(npieces, PR, PW),
            D((LD + 1,)), D((2 * LD,)), D((npieces,)), D((npieces,)), D((npieces,)), D((npieces,)),
            D((npieces,)), D((npieces,)), D((npieces,)), D((npieces,)), D((npieces,)), D((npieces,)),
        ],
        compiler_params=pltpu.CompilerParams(collective_id=cid, has_side_effects=True, vmem_limit_bytes=62 << 20),
    )(*lhs, *rhs, emb, dpre, demb, ids, tiny)
    small = got[8].reshape(-1)
    return tuple(got[:4]) + (
        got[4][:, :n_table], got[5], small[:per], got[6], got[7], small[per : per + 8 * width // nseq].reshape(4, 2, -1),
    )


def join_taps(late, early):
    parts = [None] * 3
    rest = [k for k in range(3) if k not in TAPS]
    for i, k in enumerate(TAPS):
        parts[k] = late[i]
    for i, k in enumerate(rest):
        parts[k] = early[i]
    return jnp.stack(parts)


def scatter(total, axis):
    part = lax.psum_scatter(total, "seq", scatter_dimension=axis, tiled=True)
    return lax.psum(part, "dp").astype(F32)


def body(tokens, char_ids, span_lengths, script_group, w_qkv, w_out, w_up, w_down, char_table, w_gru, gru_bias, w_stream, w_conv, norms, grad_token, grad_char):
    nseq, planes = lax.axis_size("seq"), lax.axis_size("dp")
    seqs, toks, width = tokens.shape
    chars = char_ids.shape[1]
    rows = seqs * toks
    bias_n, norm_n = gru_bias.shape[0], norms.shape[2]
    small = jnp.concatenate([gru_bias, norms.reshape(-1)])
    small = jnp.pad(small, (0, 2048 - small.shape[0])).reshape(16, 128)
    routed = ((w_up, 0, 1, 0), (w_conv[0], 0, 1, 0), (w_down, 0, 2, 0), (w_conv[2], 0, 2, 0))
    if CONV1:
        routed += ((w_conv[1], 0, 0, 0),)
    got = gather(
        routed + ((w_out, 0, 0, 0), (w_stream, 1, 0, 0), (w_qkv, 0, 0, 0), (w_gru, 0, 0, 0), (char_table, 0, 0, 0), (small, 0, 0, 0)), 1, planes, nseq
    )
    w_out, w_stream, w_qkv, w_gru, char_table, small = got[-6:]
    w_up, conv0, w_down, conv2 = got[:4]
    if CONV1:
        conv1 = got[4]
    else:
        conv1, small = lax.optimization_barrier((w_conv[1], small))
        conv1 = lax.all_gather(conv1, "seq", axis=0, tiled=True)
    w_conv = (conv0, conv1, conv2)
    small = small.reshape(nseq, 2048)
    bias = small[:, :bias_n].reshape(-1).astype(F32)
    nrm = small[:, bias_n : bias_n + 8 * norm_n].reshape(nseq, 4, 2, norm_n).transpose(1, 2, 0, 3).reshape(4, 2, width).astype(F32)

    x_low = tokens.reshape(rows, width)
    x = x_low.astype(F32)
    qkv = dot(x_low, w_qkv).astype(BF)
    qkv3 = qkv.reshape(seqs, toks, 3 * width)

    char_rows = (char_ids + script_group[:, None] * GROUP_CHARS).reshape(seqs * chars, 1)
    onehot = (char_rows == jnp.arange(VOCAB_CHAR, dtype=jnp.int32)).astype(BF)
    embedded = dot_t(onehot, char_table).astype(BF)
    pre = dot(embedded, w_gru) + bias
    tot, chunk = char_totals(pre, seqs, chars)

    span = span_lengths[:, 0]
    span_ends = jnp.cumsum(span, -1)
    starts = span_ends - span
    ends_col = jnp.stack([starts, span_ends], -1).reshape(rows, 2)
    ends_row = jnp.pad(jnp.stack([starts, span_ends], 1), ((0, 0), (0, 6), (0, 0))).reshape(seqs * 8, toks)
    block = pltpu.VMEM((2 * HB, chars, 128), F32)
    keys, values, tot_all, pooled, prev = gather_with(
        lambda me, q, *refs: states_work(me, q, seqs, *refs), tot.reshape(4 * seqs, HG),
        [(qkv3[..., width : 2 * width], 1, 0, 0), (qkv3[..., 2 * width :], 1, 0, 0)], 2, planes, nseq, (pre, chunk, ends_col),
        [jax.ShapeDtypeStruct((rows, width), F32), jax.ShapeDtypeStruct((seqs * chars, width), F32)], [block] * 4,
    )
    own_q, keys = lax.optimization_barrier((qkv3[..., :width], keys))
    queries = lax.all_gather(own_q, "seq", axis=1, tiled=True)

    ctx3, ctx_low3, lse = attention_fwd(qkv3, keys, values)
    context, context_low = ctx3.reshape(rows, width), ctx_low3.reshape(rows, width)
    normed, back_one = jax.vjp(layer_norm, x + dot(context_low, w_out), nrm[0, 0], nrm[0, 1])
    normed_low = normed.astype(BF)
    raised = dot(normed_low, w_up)
    hidden_full, gelu_up = jax.vjp(jax.nn.gelu, raised)
    hidden = hidden_full.astype(BF)
    token_state, back_two = jax.vjp(layer_norm, normed + dot(hidden, w_down), nrm[1, 0], nrm[1, 1])
    (out_token, out_char, state_low, pooled_low, mprev, merged, mnext, dmixed_low, dfused, dstate, dpooled, dnorm) = conv_both(
        seqs, token_state, pooled, grad_token.reshape(rows, width), grad_char.reshape(rows, width), nrm.reshape(8, width), w_stream, w_conv, 5
    )
    early = None
    if len(TAPS) < 3 and seq_dims(nseq) == (RZ, RY, RC) and planes == 2:
        sides = [(mprev, merged, mnext)[k] for k in range(3) if k not in TAPS]
        g_sides = wgrad(jnp.concatenate(sides, 1), dmixed_low).astype(BF).reshape(len(sides), 2 * width, 2 * width)
        early = scatter(g_sides, 1)
    ds, gtot, gch = char_flows(pre, dpooled, ends_row, chunk, seqs, chars, toks)

    dstate_sum, gain_two, shift_two = back_two(dstate)
    dlowered = dstate_sum.astype(BF)
    (draised,) = gelu_up(dot_t(dlowered, w_down))
    draised_low = draised.astype(BF)
    dinput_sum, gain_one, shift_one = back_one(dstate_sum + dot_t(draised_low, w_up))
    dattended = dinput_sum.astype(BF)
    dctx = dot_t(dattended, w_out).astype(BF)
    delta = jnp.sum((dctx.astype(F32) * context).reshape(seqs, toks, HEADS // 2, 2, HDIM), -1).transpose(0, 2, 1, 3)
    col = jnp.concatenate([lse, delta], -1)
    stat_rows = seqs * (HEADS // 2) * 4
    stat = jnp.swapaxes(col, 2, 3).reshape(stat_rows, toks)
    dctx3 = dctx.reshape(seqs, toks, width)
    dctx_all, stat_all, _, dpre, dbias = gather_with(
        lambda me, q, *refs: dpre_work(me, q, seqs, *refs), gtot.reshape(4 * seqs, HG),
        [(dctx3, 1, 0, 0), (stat, 0, 0, 0)], 3, planes, nseq, (tot_all, pre, ds, prev, chunk, gch),
        [jax.ShapeDtypeStruct((seqs * chars, 4 * HG), BF), jax.ShapeDtypeStruct((seqs * 8, 4 * HG), F32)], [block] * 2,
    )
    stat_all = stat_all.reshape(nseq, seqs, HEADS // 2, 4, toks).transpose(1, 2, 3, 0, 4).reshape(seqs, HEADS // 2, 4, nseq * toks)
    g_bias = dbias.reshape(seqs, 8, 4 * HG)[:, 0].sum(0)
    dembed = dot_t(dpre, w_gru).astype(BF)

    dq, dk, dv = attention_bwd(qkv3, dctx3, col, keys, values, queries, dctx_all, stat_all)
    dqkv = jnp.concatenate([dq, dk, dv], -1).reshape(rows, 3 * width)
    dinputs = dinput_sum + dot_t(dqkv, w_qkv)
    g_norms = jnp.concatenate([jnp.stack([gain_one, shift_one, gain_two, shift_two]), dnorm[:4]]).reshape(4, 2, width)
    shape = (seqs, toks, width)
    if seq_dims(nseq) == (RZ, RY, RC) and planes == 2:
        lhs = (x_low, context_low, normed_low, hidden, state_low, pooled_low, mprev, merged, mnext)
        rhs = (dqkv, dattended, draised_low, dlowered, dfused, dmixed_low)
        owned = reduce_all(lhs, rhs, embedded, dpre, dembed, char_rows, g_bias, g_norms, VOCAB_CHAR, nseq, 4, TAPS)
        owned = owned[:8] + (join_taps(owned[8], early),) + owned[9:]
    else:
        g_stream = [wgrad(state_low, dfused[:, :width]), wgrad(pooled_low, dfused[:, width:])]
        owned = (
            scatter(wgrad(x_low, dqkv).astype(BF), 0),
            scatter(wgrad(context_low, dattended).astype(BF), 0),
            scatter(wgrad(normed_low, draised_low).astype(BF), 0),
            scatter(wgrad(hidden, dlowered).astype(BF), 0),
            scatter(wgrad(dembed, onehot).astype(BF), 0),
            scatter(wgrad(embedded, dpre).astype(BF), 0),
            scatter(g_bias.astype(BF), 0),
            scatter(jnp.stack(g_stream).astype(BF), 1),
            scatter(jnp.stack([wgrad(m, dmixed_low) for m in (mprev, merged, mnext)]).astype(BF), 1),
            scatter(g_norms.astype(BF), 2),
        )
    return (
        out_token.reshape(shape),
        out_char.reshape(shape),
        dinputs.reshape(shape),
    ) + owned


def solution(mesh):
    placed = (
        P("dp", "seq", None),
        P("dp", "seq"),
        P("dp", "seq", None),
        P("dp"),
        P("seq", None),
        P("seq", None),
        P("seq", None),
        P("seq", None),
        P("seq", None),
        P("seq", None),
        P("seq"),
        P(None, "seq", None),
        P(None, "seq", None),
        P(None, None, "seq"),
        P("dp", "seq", None),
        P("dp", "seq", None),
    )
    return jax.shard_map(
        body,
        mesh=mesh,
        in_specs=placed,
        out_specs=(
            P("dp", "seq", None),
            P("dp", "seq", None),
            P("dp", "seq", None),
            P("seq", None),
            P("seq", None),
            P("seq", None),
            P("seq", None),
            P("seq", None),
            P("seq", None),
            P("seq"),
            P(None, "seq", None),
            P(None, "seq", None),
            P(None, None, "seq"),
        ),
        check_vma=False,
    )
```

```python
import collections
import functools
import jax
import jax.numpy as jnp
from jax import lax
from jax.experimental import pallas as pl
from jax.experimental.pallas import tpu as pltpu
from jax.sharding import PartitionSpec as P

HEADS = 12
HDIM = 64
VOCAB_CHAR = 1000
GROUP_CHARS = 250
HG = 384
EPSILON = 1e-05
MESH = pl.DeviceIdType.MESH
BF = jnp.bfloat16
F32 = jnp.float32
NCH = 8
UNROLL = 8
SHARE = (1, 2, 3, 6)
CONV1, TAPS = False, (0, 1, 2)
HB = HG // 128

def seq_dims(n):
    return {16: (4, 2, 2), 32: (8, 4, 1)}.get(n, (n, 1, 1))


Move = collections.namedtuple("Move", ("array", "axis", "rows", "lead", "route"))


def gather_kernel(dims, planes, moves, n_arrays, task, *refs):
    Z, Y, C = dims
    n = len(moves)
    n_in, n_out = (task.n_in, task.n_out) if task else (0, 0)
    src, task_in = refs[:n_arrays], refs[n_arrays : n_arrays + n_in]
    refs = refs[n_arrays + n_in :]
    dst, task_out = refs[:n_arrays], refs[n_arrays : n_arrays + n_out]
    own_sem, recv, zs, ds, ys, ss, xs, *task_scratch = refs[n_arrays + n_out :]
    dp = lax.axis_index("dp")
    me = lax.axis_index("seq")
    c = lax.rem(me, C)
    y = lax.rem(lax.div(me, C), Y)
    z = lax.div(me, C * Y)
    up_z, down_z = z < Z - 1, z > 0

    def at(zz, yy, cc):
        return (zz * Y + yy) * C + cc

    def to(zz, yy, cc):
        return (dp, at(zz, yy, cc))

    def view(i, slot):
        m = moves[i]
        s = pl.ds(pl.multiple_of(slot * m.rows, m.rows), m.rows)
        ref = dst[m.array]
        return ref.at[s] if m.axis == 0 else ref.at[:, s]

    def mine(i):
        m = moves[i]
        return src[m.array] if m.lead is None else src[m.array].at[m.lead]

    def copy(i, slot, send, where, own=False):
        return pltpu.make_async_remote_copy(
            src_ref=mine(i) if own else view(i, slot), dst_ref=view(i, slot),
            send_sem=send, recv_sem=recv.at[i, slot], device_id=where, device_id_type=MESH)

    sib = to(z, y, 1 - c) if C == 2 else None
    xp = (1 - dp, me)
    use_x = planes == 2 and any(m.route for m in moves)
    some = sib if C == 2 else to(z, y, c)

    def owner(i):
        return None if not (use_x and moves[i].route) else dp == moves[i].route - 1

    def when(cond, f):
        if cond is None:
            f()
        else:
            pl.when(cond)(f)

    def both(a, b):
        return b if a is None else jnp.logical_and(a, b)

    nseq = Z * Y * C
    if task:
        push_all, *task_out = task_out
        push, p_send, p_recv, i_sem, *task_scratch = task_scratch
        n_held = n_in - task.n_stay
        held, task_scratch = task_scratch[:n_held], task_scratch[n_held:]
        loads = [pltpu.make_async_copy(a, b, i_sem.at[k]) for k, (a, b) in enumerate(zip(task_in[:n_held], held))]
        for load in loads:
            load.start()
    bar = pltpu.get_barrier_semaphore()
    if task:
        peers = [(None, (dp, lax.rem(me + k, nseq))) for k in range(1, nseq)]
    else:
        peers = [(z > 0, to(z - 1, y, c)), (z < Z - 1, to(z + 1, y, c))]
        if Y > 1:
            peers += [(y > 0, to(z, y - 1, c)), (y < Y - 1, to(z, y + 1, c))]
        if C == 2:
            peers.append((None, sib))
    if use_x:
        peers.append((None, xp))
    count = 0
    for cond, where in peers:
        when(cond, functools.partial(pl.semaphore_signal, bar, inc=1, device_id=where, device_id_type=MESH))
        count = count + (1 if cond is None else cond.astype(jnp.int32))
    pl.semaphore_wait(bar, count)
    if task:

        def pushed(k, slot, where):
            return pltpu.make_async_remote_copy(
                src_ref=push, dst_ref=push_all.at[slot], send_sem=p_send.at[k], recv_sem=p_recv.at[slot], device_id=where, device_id_type=MESH)

        def push_one(k, _):
            pushed(k, me, (dp, lax.rem(me + k, nseq))).start()
            return 0

        def push_wait(k, _):
            other = lax.rem(me + k, nseq)
            pushed(k, other, (dp, other)).wait_recv()
            pushed(k, me, (dp, other)).wait_send()
            return 0

    def work(point):
        if task:
            task.run(point, me, push, push_all, tuple(held) + tuple(task_in[n_held:]), task_out, task_scratch)

    def go_z(i, slot, up, sem, own=False):
        where = to(z + 1, y, c) if up else to(z - 1, y, c)
        pl.when(up_z if up else down_z)(lambda: copy(i, slot, sem, where, own).start())

    def go_y(i, slot, up, sem, own=False):
        where = to(z, y + 1, c) if up else to(z, y - 1, c)
        pl.when(y < Y - 1 if up else y > 0)(lambda: copy(i, slot, sem, where, own).start())

    def go_core(i, slot, own=False):
        if C == 2:
            copy(i, slot, ss.at[i, slot], sib, own).start()

    def wait_in(i, slot):
        copy(i, slot, ss.at[i, slot], some).wait_recv()

    for i in range(n):
        pltpu.make_async_copy(mine(i), view(i, me), own_sem.at[i]).start()

        def own_sends(i=i):
            go_z(i, me, True, zs.at[i, me], True)
            go_z(i, me, False, ds.at[i, 0], True)
            if Y > 1:
                go_y(i, me, True, ys.at[i, me], True)
                go_y(i, me, False, ds.at[i, 1], True)

        when(owner(i), own_sends)
        go_core(i, me, True)

    def arrive_z(zz, up):
        slot = at(zz, y, c)

        def one(i):
            wait_in(i, slot)
            go_z(i, slot, up, zs.at[i, slot])
            if Y > 1:
                go_y(i, slot, True, ys.at[i, slot])
                go_y(i, slot, False, ys.at[i, slot] if Y == 2 else xs.at[i, slot])
            if use_x and moves[i].route:
                copy(i, slot, xs.at[i, slot], xp).start()
            go_core(i, slot)

        for i in range(n):
            when(owner(i), functools.partial(one, i))

    def arrive_y(zz, yy, up):
        slot = at(zz, yy, c)

        def one(i):
            wait_in(i, slot)
            if Y > 2:
                go_y(i, slot, up, ys.at[i, slot])
            if use_x and moves[i].route:
                copy(i, slot, xs.at[i, slot], xp).start()
            go_core(i, slot)

        for i in range(n):
            when(owner(i), functools.partial(one, i))

    def all_y(zz):
        for t in range(1, Y):
            pl.when(y - t >= 0)(lambda: arrive_y(zz, y - t, True))
            pl.when(y + t < Y)(lambda: arrive_y(zz, y + t, False))

    if task:
        for load in loads:
            load.wait()
        work(0)
        push_all[me] = push[...]
        lax.fori_loop(1, nseq, push_one, 0)
    def step(s, _):
        pl.when(z - s >= 0)(lambda: arrive_z(z - s, True))
        pl.when(z + s < Z)(lambda: arrive_z(z + s, False))
        q = s - 1
        pl.when(z - q >= 0)(lambda: all_y(z - q))
        pl.when(jnp.logical_and(q > 0, z + q < Z))(lambda: all_y(z + q))
        return 0

    if task:
        for s in (1, 2):
            if s < Z:
                step(s, 0)
            if s == 1:
                lax.fori_loop(1, nseq, push_wait, 0)
            work(s)
        lax.fori_loop(3, Z, step, 0)
        work(3)
    else:
        lax.fori_loop(1, Z, step, 0)
    q = Z - 1
    pl.when(z - q >= 0)(lambda: all_y(z - q))
    pl.when(z + q < Z)(lambda: all_y(z + q))

    if use_x:

        def far(k, _):
            slot = at(lax.rem(z + lax.div(k, Y), Z), lax.rem(y + lax.rem(k, Y), Y), c)

            def one(i):
                wait_in(i, slot)
                go_core(i, slot)

            for i in range(n):
                if moves[i].route:
                    pl.when(dp != moves[i].route - 1)(functools.partial(one, i))
            return 0

        lax.fori_loop(1, Z * Y, far, 0)

    def drain(k, _):
        zz, yy = lax.div(k, Y), lax.rem(k, Y)
        slot = at(zz, yy, c)
        is_own = slot == me
        own_y = yy == y
        fz = jnp.logical_or(jnp.logical_and(zz <= z, up_z), jnp.logical_and(zz > z, down_z))
        for i in range(n):
            o = owner(i)
            if C == 2:
                wait_in(i, at(zz, yy, 1 - c))
                copy(i, slot, ss.at[i, slot], some).wait_send()
            sent = lambda sem: copy(i, slot, sem, some).wait_send()
            pl.when(both(o, jnp.logical_and(own_y, fz)))(lambda: sent(zs.at[i, slot]))
            if Y == 2:
                pl.when(both(o, jnp.logical_and(own_y, jnp.logical_or(jnp.logical_not(is_own), y < Y - 1))))(lambda: sent(ys.at[i, slot]))
            elif Y > 2:
                fy = jnp.logical_or(jnp.logical_and(yy <= y, y < Y - 1), jnp.logical_and(yy > y, y > 0))
                pl.when(both(o, fy))(lambda: sent(ys.at[i, slot]))
                fy2 = jnp.logical_and(jnp.logical_and(own_y, y > 0), jnp.logical_not(is_own))
                pl.when(both(o, fy2))(lambda: sent(xs.at[i, slot]))
            if use_x and moves[i].route:
                pl.when(both(o, jnp.logical_not(is_own)))(lambda: sent(xs.at[i, slot]))
        return 0

    lax.fori_loop(0, Z * Y, drain, 0)
    for i in range(n):
        pltpu.make_async_copy(mine(i), view(i, me), own_sem.at[i]).wait()
        o = owner(i)
        pl.when(both(o, down_z))(lambda: copy(i, me, ds.at[i, 0], some, True).wait_send())
        if Y > 1:
            pl.when(both(o, y > 0))(lambda: copy(i, me, ds.at[i, 1], some, True).wait_send())


Task = collections.namedtuple("Task", ("n_in", "n_stay", "n_out", "run"))


def gather(arrays, cid, planes, nseq, task=None, inputs=(), outputs=(), scratch=()):
    dims = seq_dims(nseq)
    moves, shapes = [], []
    for k, (x, axis, route, lead) in enumerate(arrays):
        shape = list(x.shape if lead is None else x.shape[1:])
        moves.append(Move(k, axis, shape[axis], lead, route if planes == 2 and dims[1:] == (2, 2) else 0))
        shape[axis] *= nseq
        shapes.append(jax.ShapeDtypeStruct(tuple(shape), x.dtype))
    moves.sort(key=lambda m: not m.route)
    n = len(moves)
    D = pltpu.SemaphoreType.DMA
    scratch = [D((n,)), D((n, nseq)), D((n, nseq)), D((n, 2)), D((n, nseq)), D((n, nseq)), D((n, nseq))] + list(scratch)
    far, here = pl.BlockSpec(memory_space=pl.ANY), pl.BlockSpec(memory_space=pltpu.VMEM)
    return pl.pallas_call(
        functools.partial(gather_kernel, dims, planes, tuple(moves), len(arrays), task),
        out_shape=shapes + list(outputs),
        in_specs=[far] * (len(arrays) + len(inputs)),
        out_specs=[far] * len(arrays) + [here] * len(outputs),
        scratch_shapes=scratch,
        compiler_params=pltpu.CompilerParams(collective_id=cid, has_side_effects=True, vmem_limit_bytes=60 << 20),
    )(*[x for x, _, _, _ in arrays], *inputs)


def gather_with(run, arrays, cid, planes, nseq, inputs, stay, outputs, scratch):
    D = pltpu.SemaphoreType.DMA
    push = (8, HG)
    outputs = [jax.ShapeDtypeStruct((nseq,) + push, F32)] + outputs
    scratch = [pltpu.VMEM(push, F32), D((nseq,)), D((nseq,)), D((len(inputs),))] + [pltpu.VMEM(a.shape, a.dtype) for a in inputs] + scratch
    inputs = tuple(inputs) + tuple(stay)
    return gather(arrays, cid, planes, nseq, Task(len(inputs), len(stay), len(outputs), run), inputs, outputs, scratch)


def dot(a, b):
    return jnp.dot(a, b, preferred_element_type=F32)


def dot_t(a, b):
    return lax.dot_general(a, b, (((1,), (1,)), ((), ())), preferred_element_type=F32)


def wgrad(a, b):
    return lax.dot_general(a, b, (((0,), (0,)), ((), ())), preferred_element_type=F32)


def vmem(mib):
    return pltpu.CompilerParams(vmem_limit_bytes=mib << 20)


def layer_norm(values, gain_row, shift_row):
    center = values - jnp.mean(values, -1, keepdims=True)
    spread = jnp.mean(center * center, -1, keepdims=True)
    return center * lax.rsqrt(spread + EPSILON) * gain_row + shift_row


def fill(pre_ref, decay, drive=None):
    for k in range(2):
        for j in range(HB):
            at = 2 * k * HG + j * 128
            rate = jax.nn.sigmoid(pre_ref[:, at : at + 128])
            decay[k * HB + j] = 1.0 - rate
            if drive is not None:
                drive[k * HB + j] = rate * pre_ref[:, at + HG : at + HG + 128]


def row(x, i):
    return lax.slice_in_dim(x, i, i + 1, axis=0)


def cat(parts):
    return jnp.concatenate(parts, 1)


def blocks(x):
    return [x[:, j * 128 : (j + 1) * 128] for j in range(HB)]


def totals_kernel(pre_ref, tot_ref, chunk_ref, decay, drive):
    length = pre_ref.shape[0] // NCH
    fill(pre_ref, decay, drive)

    def step(t, carry):
        place = (pl.ds(t, NCH, stride=length), pl.ds(length - 1 - t, NCH, stride=length))
        out = []
        for i in range(2 * HB):
            c, h = carry[i]
            a = decay[i, place[i // HB], :]
            out.append((c * a, a * h + drive[i, place[i // HB], :]))
        return tuple(out)

    one, zero = jnp.ones((NCH, 128), F32), jnp.zeros((NCH, 128), F32)
    ends = lax.fori_loop(0, length, step, ((one, zero),) * (2 * HB), unroll=UNROLL)
    cf, hf = cat([e[0] for e in ends[:HB]]), cat([e[1] for e in ends[:HB]])
    cb, hb = cat([e[0] for e in ends[HB:]]), cat([e[1] for e in ends[HB:]])
    chunk_ref[0:NCH, :] = cf
    chunk_ref[NCH : 2 * NCH, :] = hf
    chunk_ref[2 * NCH : 3 * NCH, :] = cb
    chunk_ref[3 * NCH :, :] = hb
    one, zero = jnp.ones((1, HG), F32), jnp.zeros((1, HG), F32)
    tf, sf, tb, sb = one, zero, one, zero
    for k in range(NCH):
        sf, tf = row(cf, k) * sf + row(hf, k), tf * row(cf, k)
        j = NCH - 1 - k
        sb, tb = row(cb, j) * sb + row(hb, j), tb * row(cb, j)
    tot_ref[...] = jnp.concatenate([tf, sf, tb, sb], 0)


def states_work(me, q, seqs, all_ref, pre_all, chunk_all, ends_all, pooled_all, prev_all, decay, drive, state, prev):
    pre_ref, chunk_ref, ends_ref, pooled_ref, prev_ref = (
        r.at[pl.ds(q * (r.shape[0] // seqs), r.shape[0] // seqs)] for r in (pre_all, chunk_all, ends_all, pooled_all, prev_all)
    )
    chars = pre_all.shape[0] // seqs
    length = chars // NCH
    nseq = all_ref.shape[0]
    fill(pre_ref, decay, drive)
    ef = jnp.zeros((1, HG), F32)
    eb = ef
    for d in range(nseq):
        got = all_ref[d]
        ef = jnp.where(d < me, row(got, 4 * q) * ef + row(got, 4 * q + 1), ef)
        got = all_ref[nseq - 1 - d]
        eb = jnp.where(nseq - 1 - d > me, row(got, 4 * q + 2) * eb + row(got, 4 * q + 3), eb)
    cf, hf = chunk_ref[0:NCH, :], chunk_ref[NCH : 2 * NCH, :]
    cb, hb = chunk_ref[2 * NCH : 3 * NCH, :], chunk_ref[3 * NCH :, :]
    rows_f, rows_b = [], []
    for k in range(NCH):
        rows_f.append(ef)
        ef = row(cf, k) * ef + row(hf, k)
        j = NCH - 1 - k
        rows_b.append(eb)
        eb = row(cb, j) * eb + row(hb, j)

    def step(t, carry):
        place = (pl.ds(t, NCH, stride=length), pl.ds(length - 1 - t, NCH, stride=length))
        out = []
        for i in range(2 * HB):
            at = place[i // HB]
            prev[i, at, :] = carry[i]
            h = decay[i, at, :] * carry[i] + drive[i, at, :]
            state[i, at, :] = h
            out.append(h)
        return tuple(out)

    lax.fori_loop(0, length, step, tuple(blocks(jnp.concatenate(rows_f, 0)) + blocks(jnp.concatenate(rows_b[::-1], 0))), unroll=UNROLL)
    first = ends_ref[:, 0:1]
    last = ends_ref[:, 1:2]
    place = lax.broadcasted_iota(jnp.int32, (ends_all.shape[0] // seqs, chars), 1)
    member = jnp.where((place >= first) & (place < last), 1.0, 0.0).astype(BF)
    prev_ref[...] = cat([prev[i] for i in range(2 * HB)])
    pooled_ref[...] = dot(member, cat([state[i].astype(BF) for i in range(2 * HB)])) / (last - first).astype(F32)


def flows_kernel(pre_ref, dpool_ref, ends_ref, chunk_ref, ds_ref, tot_ref, gch_ref, decay, ds):
    chars = pre_ref.shape[0]
    length = chars // NCH
    fill(pre_ref, decay)
    first = ends_ref[0:1, :]
    last = ends_ref[1:2, :]
    place = lax.broadcasted_iota(jnp.int32, (chars, ends_ref.shape[1]), 0)
    inside = (place >= first) & (place < last)
    span = jnp.sum(jnp.where(inside, (last - first).astype(F32), 0.0), 1, keepdims=True)
    member = jnp.where(inside, 1.0, 0.0).astype(BF)
    spread = dot(member, dpool_ref[...]) / span
    ds_ref[...] = spread
    for i in range(2 * HB):
        ds[i] = spread[:, i * 128 : (i + 1) * 128]

    def step(t, carry):
        place = (pl.ds(length - 1 - t, NCH, stride=length), pl.ds(t, NCH, stride=length))
        return tuple(
            decay[i, place[i // HB], :] * (ds[i, place[i // HB], :] + carry[i]) for i in range(2 * HB)
        )

    ends = lax.fori_loop(0, length, step, (jnp.zeros((NCH, 128), F32),) * (2 * HB), unroll=UNROLL)
    gf, gb = cat(ends[:HB]), cat(ends[HB:])
    gch_ref[0:NCH, :] = gf
    gch_ref[NCH:, :] = gb
    cf, cb = chunk_ref[0:NCH, :], chunk_ref[2 * NCH : 3 * NCH, :]
    zero = jnp.zeros((1, HG), F32)
    tf, tb = zero, zero
    for k in range(NCH):
        j = NCH - 1 - k
        tf = row(cf, j) * tf + row(gf, j)
        tb = row(cb, k) * tb + row(gb, k)
    tot_ref[...] = jnp.concatenate([tf, tb, zero, zero], 0)


def dpre_work(me, q, seqs, gall_ref, all_ref, pre_all, ds_all, prev_all, chunk_all, gch_all, dpre_all, bias_all, decay, ds):
    pre_ref, ds_ref, prev_ref, chunk_ref, gch_ref, dpre_ref, bias_ref = (
        r.at[pl.ds(q * (r.shape[0] // seqs), r.shape[0] // seqs)] for r in (pre_all, ds_all, prev_all, chunk_all, gch_all, dpre_all, bias_all)
    )
    chars = pre_all.shape[0] // seqs
    length = chars // NCH
    nseq = all_ref.shape[0]
    fill(pre_ref, decay)
    for i in range(2 * HB):
        ds[i] = ds_ref[:, i * 128 : (i + 1) * 128]
    ef = jnp.zeros((1, HG), F32)
    eb = ef
    for d in range(nseq):
        j = nseq - 1 - d
        ef = jnp.where(j > me, row(all_ref[j], 4 * q) * ef + row(gall_ref[j], 4 * q), ef)
        eb = jnp.where(d < me, row(all_ref[d], 4 * q + 2) * eb + row(gall_ref[d], 4 * q + 1), eb)
    cf, cb = chunk_ref[0:NCH, :], chunk_ref[2 * NCH : 3 * NCH, :]
    gf, gb = gch_ref[0:NCH, :], gch_ref[NCH:, :]
    rows_f, rows_b = [], []
    for k in range(NCH):
        j = NCH - 1 - k
        rows_f.append(ef)
        ef = row(cf, j) * ef + row(gf, j)
        rows_b.append(eb)
        eb = row(cb, k) * eb + row(gb, k)

    def step(t, carry):
        place = (pl.ds(length - 1 - t, NCH, stride=length), pl.ds(t, NCH, stride=length))
        out = []
        for i in range(2 * HB):
            at = place[i // HB]
            g = ds[i, at, :] + carry[i]
            ds[i, at, :] = g
            out.append(decay[i, at, :] * g)
        return tuple(out)

    lax.fori_loop(0, length, step, tuple(blocks(jnp.concatenate(rows_f[::-1], 0)) + blocks(jnp.concatenate(rows_b, 0))), unroll=UNROLL)
    for i in range(2 * HB):
        k, j = i // HB, i % HB
        at = 2 * k * HG + j * 128
        g = ds[i]
        rate = jax.nn.sigmoid(pre_ref[:, at : at + 128])
        cand = pre_ref[:, at + HG : at + HG + 128]
        prev = prev_ref[:, i * 128 : (i + 1) * 128]
        dgate = (g * (cand - prev) * rate * decay[i]).astype(BF)
        dcand = (g * rate).astype(BF)
        for to, v in ((at, dgate), (at + HG, dcand)):
            dpre_ref[:, to : to + 128] = v
            bias_ref[:, to : to + 128] = jnp.broadcast_to(jnp.sum(v.astype(F32), 0, keepdims=True), (8, 128))


def part_of(ref, q, seqs):
    n = ref.shape[0] // seqs
    return ref.at[pl.ds(q * n, n)]


def forward_run(seqs, point, me, push, push_all, inputs, outputs, scratch):
    pre, ends = inputs
    pooled, prev, chunk = outputs
    if point == 0:
        for q in range(seqs):
            totals_kernel(part_of(pre, q, seqs), push.at[pl.ds(4 * q, 4)], part_of(chunk, q, seqs), *scratch[:2])
    elif point <= seqs:
        states_work(me, point - 1, seqs, push_all, pre, chunk, ends, pooled, prev, *scratch)


def backward_run(seqs, point, me, push, push_all, inputs, outputs, scratch):
    pre, prev, chunk, tot_all, dpool, ends, q_ref, dc_ref, col_ref, keys, values = inputs
    dpre, dbias, dq = outputs
    ds_all, gch, decay, ds, kbuf, vbuf, k_sem, v_sem = scratch
    pairs = HEADS // 2
    steps = seqs * pairs

    def fetch(i):
        s, p = lax.div(i, pairs), lax.rem(i, pairs)
        cols = pl.ds(pl.multiple_of(p * 2 * HDIM, 2 * HDIM), 2 * HDIM)
        b = lax.rem(i, 2)
        return (pltpu.make_async_copy(keys.at[s, :, cols], kbuf.at[b], k_sem.at[b]), pltpu.make_async_copy(values.at[s, :, cols], vbuf.at[b], v_sem.at[b]))

    def one(i, _):
        s, p = lax.div(i, pairs), lax.rem(i, pairs)
        cols = pl.ds(pl.multiple_of(p * 2 * HDIM, 2 * HDIM), 2 * HDIM)
        b = lax.rem(i, 2)

        @pl.when(i + 1 < steps)
        def _():
            for c in fetch(i + 1):
                c.start()

        for c in fetch(i):
            c.wait()
        dq[s, :, cols] = query_grad(q_ref[s, :, cols], kbuf[b], vbuf[b], dc_ref[s, :, cols], col_ref[s, p])
        return 0

    if point == 0:
        for c in fetch(0):
            c.start()
        for q in range(seqs):
            flows_kernel(*(part_of(r, q, seqs) for r in (pre, dpool, ends, chunk, ds_all)), push.at[pl.ds(4 * q, 4)], part_of(gch, q, seqs), decay, ds)
    elif point <= seqs:
        dpre_work(me, point - 1, seqs, push_all, tot_all, pre, ds_all, prev, chunk, gch, dpre, dbias, decay, ds)
    bounds = (0,) + tuple(steps * k // 6 for k in SHARE)
    lax.fori_loop(bounds[point], bounds[point + 1], one, 0)


def pair_rows(x):
    lane = lax.broadcasted_iota(jnp.int32, x.shape, 1)
    zero = jnp.zeros_like(x)
    return jnp.concatenate([jnp.where(lane < HDIM, x, zero), jnp.where(lane >= HDIM, x, zero)], 0)


def pair_lanes(x):
    half = x.shape[0] // 2
    lane = lax.broadcasted_iota(jnp.int32, (half, x.shape[1]), 1)
    return jnp.where(lane < HDIM, x[:half], x[half:])


def attn_fwd_kernel(q_ref, k_ref, v_ref, ctx_ref, low_ref, lse_ref):
    toks = q_ref.shape[0]
    s = dot_t(pair_rows(q_ref[...] * (HDIM ** -0.5)), k_ref[...])
    top = jnp.max(s, 1, keepdims=True)
    p = jnp.exp(s - top)
    total = jnp.sum(p, 1, keepdims=True)
    o = pair_lanes(dot(p.astype(BF), v_ref[...]) / total)
    ctx_ref[...] = o
    low_ref[...] = o.astype(BF)
    lse = top + jnp.log(total)
    lse_ref[...] = jnp.concatenate([lse[:toks], lse[toks:]], 1)


def head_spec(rows, base=0):
    return pl.BlockSpec((None, rows, 2 * HDIM), lambda s, h: (s, 0, h + base))


def attention_fwd(qkv, keys, values):
    seqs, toks, _ = qkv.shape
    length = keys.shape[1]
    pairs = HEADS // 2
    return pl.pallas_call(
        attn_fwd_kernel,
        grid=(seqs, pairs),
        out_shape=[
            jax.ShapeDtypeStruct((seqs, toks, HEADS * HDIM), F32),
            jax.ShapeDtypeStruct((seqs, toks, HEADS * HDIM), BF),
            jax.ShapeDtypeStruct((seqs, pairs, toks, 2), F32),
        ],
        in_specs=[head_spec(toks), head_spec(length), head_spec(length)],
        out_specs=[head_spec(toks), head_spec(toks), pl.BlockSpec((None, None, toks, 2), lambda s, h: (s, h, 0, 0))],
        compiler_params=vmem(48),
    )(qkv, keys, values)


def query_grad(q, keys, values, dc, col):
    scale = HDIM ** -0.5
    lse = jnp.concatenate([col[:, 0:1], col[:, 1:2]], 0)
    delta = jnp.concatenate([col[:, 2:3], col[:, 3:4]], 0)
    p = jnp.exp(dot_t(pair_rows(q * scale), keys) - lse)
    ds = (p * (dot_t(pair_rows(dc), values) - delta)).astype(BF)
    return (pair_lanes(dot(ds, keys)) * scale).astype(BF)


def attn_bwd_kernel(ko_ref, vo_ref, qa_ref, dca_ref, row_ref, dk_ref, dv_ref):
    toks = ko_ref.shape[0]
    scale = HDIM ** -0.5

    def spread(i):
        n = row_ref.shape[1]
        return jnp.concatenate(
            [jnp.broadcast_to(row_ref[i : i + 1, :], (toks, n)), jnp.broadcast_to(row_ref[i + 1 : i + 2, :], (toks, n))], 0
        )

    p = jnp.exp(dot_t(pair_rows(ko_ref[...] * scale), qa_ref[...]) - spread(0))
    dv_ref[...] = pair_lanes(dot(p.astype(BF), dca_ref[...])).astype(BF)
    dp = dot_t(pair_rows(vo_ref[...]), dca_ref[...])
    ds = (p * (dp - spread(2))).astype(BF)
    dk_ref[...] = (pair_lanes(dot(ds, qa_ref[...])) * scale).astype(BF)


def attention_bwd(qkv, queries, dctx_all, rows):
    seqs, toks, _ = qkv.shape
    length = queries.shape[1]
    pairs = HEADS // 2
    stat = lambda a, b: pl.BlockSpec((None, None, a, b), lambda s, h: (s, h, 0, 0))
    return pl.pallas_call(
        attn_bwd_kernel,
        grid=(seqs, pairs),
        out_shape=[jax.ShapeDtypeStruct((seqs, toks, HEADS * HDIM), BF)] * 2,
        in_specs=[head_spec(toks, pairs), head_spec(toks, 2 * pairs), head_spec(length), head_spec(length), stat(4, length)],
        out_specs=[head_spec(toks)] * 2,
        compiler_params=vmem(56),
    )(qkv, qkv, queries, dctx_all, rows)


GELU_A = 0.7978845608028654
GELU_B = 0.044715


def norm_both(v, gain, shift, dy):
    center = v - jnp.mean(v, -1, keepdims=True)
    inv = lax.rsqrt(jnp.mean(center * center, -1, keepdims=True) + EPSILON)
    hat = center * inv
    dhat = dy * gain
    dv = inv * (dhat - jnp.mean(dhat, -1, keepdims=True) - hat * jnp.mean(dhat * hat, -1, keepdims=True))
    return hat * gain + shift, dv, jnp.sum(dy * hat, 0, keepdims=True), jnp.sum(dy, 0, keepdims=True)


def conv_kernel(seqs, state_ref, pooled_ref, gtok_ref, gchr_ref, nrm_ref, ws_ref, c0_ref, c1_ref, c2_ref,
                otok_ref, ochr_ref, slow_ref, plow_ref, mprev_ref, merged_ref, mnext_ref, dmix_ref, dfus_ref, dstate_ref, dpool_ref, dnorm_ref,
                taps, acc, edge, before, after, dside, dchar, w_sem, e_send, b_recv, a_recv):
    me = lax.axis_index("seq")
    dp = lax.axis_index("dp")
    n = lax.axis_size("seq")
    rows, width = state_ref.shape
    toks = rows // seqs
    wide = 2 * width
    loads = [pltpu.make_async_copy(c, taps.at[k], w_sem.at[k]) for k, c in ((1, c1_ref), (0, c0_ref), (2, c2_ref))]
    for load in loads:
        load.start()
    edge[...] = jnp.zeros_like(edge)
    dnorm_ref[4:8, :] = jnp.zeros((4, width), F32)
    right, left = (dp, me + 1), (dp, me - 1)
    has_l, has_r = me > 0, me < n - 1
    bar = pltpu.get_barrier_semaphore()
    pl.when(has_l)(lambda: pl.semaphore_signal(bar, inc=1, device_id=left, device_id_type=MESH))
    pl.when(has_r)(lambda: pl.semaphore_signal(bar, inc=1, device_id=right, device_id_type=MESH))
    pl.semaphore_wait(bar, has_l.astype(jnp.int32) + has_r.astype(jnp.int32))

    def send(k):
        def to_right():
            return pltpu.make_async_remote_copy(
                src_ref=edge.at[k, 0], dst_ref=before.at[k], send_sem=e_send.at[k, 0], recv_sem=b_recv.at[k], device_id=right, device_id_type=MESH)

        def to_left():
            return pltpu.make_async_remote_copy(
                src_ref=edge.at[k, 1], dst_ref=after.at[k], send_sem=e_send.at[k, 1], recv_sem=a_recv.at[k], device_id=left, device_id_type=MESH)

        return to_right, to_left

    def start(k, ref):
        for s in range(seqs):
            edge[k, 0, s : s + 1, :] = ref[(s + 1) * toks - 16 : (s + 1) * toks, :].astype(F32)[15:16]
            edge[k, 1, s : s + 1, :] = ref[s * toks : s * toks + 16, :].astype(F32)[0:1]
        to_right, to_left = send(k)
        pl.when(has_r)(lambda: to_right().start())
        pl.when(has_l)(lambda: to_left().start())

    def finish(k):
        to_right, to_left = send(k)
        pl.when(has_r)(lambda: to_left().wait_recv())
        pl.when(has_l)(lambda: to_right().wait_recv())
        pl.when(has_r)(lambda: to_right().wait_send())
        pl.when(has_l)(lambda: to_left().wait_send())

    def shifts(k, ref, prev_ref, next_ref):
        for j in range(0, wide, 512):
            x = ref[:, j : j + 512].astype(F32)
            at = lax.broadcasted_iota(jnp.int32, x.shape, 0)
            prev, follow = pltpu.roll(x, 1, 0), pltpu.roll(x, rows - 1, 0)
            for s in range(seqs):
                b = jnp.where(has_l, before[k, s : s + 1, j : j + 512], 0.0)
                a = jnp.where(has_r, after[k, s : s + 1, j : j + 512], 0.0)
                prev = jnp.where(at == s * toks, b, prev)
                follow = jnp.where(at == (s + 1) * toks - 1, a, follow)
            prev_ref[:, j : j + 512] = prev.astype(BF)
            next_ref[:, j : j + 512] = follow.astype(BF)

    slow = state_ref[...].astype(BF)
    plow = pooled_ref[...].astype(BF)
    slow_ref[...] = slow
    plow_ref[...] = plow
    merged_ref[:, :width] = dot(slow, ws_ref[0]).astype(BF)
    merged_ref[:, width:] = dot(plow, ws_ref[1]).astype(BF)
    start(0, merged_ref)
    loads[0].wait()

    def centre(j, _):
        cols = pl.ds(pl.multiple_of(j * 512, 512), 512)
        acc[:, cols] = dot(merged_ref[...], taps[1, :, cols])
        return 0

    lax.fori_loop(0, wide // 512, centre, 0)
    finish(0)
    shifts(0, merged_ref, mprev_ref, mnext_ref)
    loads[1].wait()
    loads[2].wait()

    def sides(j, _):
        cols = pl.ds(pl.multiple_of(j * 512, 512), 512)
        acc[:, cols] += dot(mprev_ref[...], taps[0, :, cols]) + dot(mnext_ref[...], taps[2, :, cols])
        return 0

    lax.fori_loop(0, wide // 512, sides, 0)
    for part, (base_ref, grad_ref, out_ref) in enumerate(((state_ref, gtok_ref, otok_ref), (pooled_ref, gchr_ref, ochr_ref))):
        mixed = acc[:, part * width : (part + 1) * width]
        square = mixed * mixed
        curve = jnp.tanh(GELU_A * (mixed + GELU_B * mixed * square))
        gated = 0.5 * mixed * (1.0 + curve)
        slope = 0.5 * (1.0 + curve) + 0.5 * mixed * (1.0 - curve * curve) * (GELU_A * (1.0 + 3.0 * GELU_B * square))
        r = 4 + 2 * part
        out, dsum, dgain, dshift = norm_both(base_ref[...] + gated, nrm_ref[r : r + 1, :], nrm_ref[r + 1 : r + 2, :], grad_ref[...].astype(F32))
        out_ref[...] = out.astype(BF)
        dnorm_ref[2 * part : 2 * part + 1, :] = dgain
        dnorm_ref[2 * part + 1 : 2 * part + 2, :] = dshift
        dmix_ref[:, part * width : (part + 1) * width] = (dsum * slope).astype(BF)
        if part == 0:
            dstate_ref[...] = dsum
        else:
            dchar[...] = dsum
    start(1, dmix_ref)

    def centre_back(j, _):
        cols = pl.ds(pl.multiple_of(j * 512, 512), 512)
        acc[:, cols] = dot_t(dmix_ref[...], taps[1, cols, :])
        return 0

    lax.fori_loop(0, wide // 512, centre_back, 0)
    finish(1)
    shifts(1, dmix_ref, dside.at[0], dside.at[1])

    def sides_back(j, _):
        cols = pl.ds(pl.multiple_of(j * 512, 512), 512)
        dfus_ref[:, cols] = (acc[:, cols] + dot_t(dside[1], taps[0, cols, :]) + dot_t(dside[0], taps[2, cols, :])).astype(BF)
        return 0

    lax.fori_loop(0, wide // 512, sides_back, 0)
    dstate_ref[...] += dot_t(dfus_ref[:, :width], ws_ref[0])
    dpool_ref[...] = (dchar[...] + dot_t(dfus_ref[:, width:], ws_ref[1])).astype(BF)


def conv_both(seqs, token_state, pooled, grad_token, grad_char, nrm, w_stream, w_conv, cid):
    rows, width = token_state.shape
    wide = 2 * width
    here = pl.BlockSpec(memory_space=pltpu.VMEM)
    far = pl.BlockSpec(memory_space=pl.ANY)
    low, full = jax.ShapeDtypeStruct((rows, width), BF), jax.ShapeDtypeStruct((rows, width), F32)
    both = jax.ShapeDtypeStruct((rows, wide), BF)
    D = pltpu.SemaphoreType.DMA
    return pl.pallas_call(
        functools.partial(conv_kernel, seqs),
        out_shape=[low, low, low, low, both, both, both, both, both, full, low, jax.ShapeDtypeStruct((8, width), F32)],
        in_specs=[here] * 6 + [far] * 3,
        out_specs=[here] * 12,
        scratch_shapes=[
            pltpu.VMEM((3, wide, wide), BF), pltpu.VMEM((rows, wide), F32), pltpu.VMEM((2, 2, 8, wide), F32),
            pltpu.VMEM((2, 8, wide), F32), pltpu.VMEM((2, 8, wide), F32), pltpu.VMEM((2, rows, wide), BF), pltpu.VMEM((rows, width), F32),
            D((3,)), D((2, 2)), D((2,)), D((2,)),
        ],
        compiler_params=pltpu.CompilerParams(collective_id=cid, has_side_effects=True, vmem_limit_bytes=60 << 20),
    )(token_state, pooled, grad_token, grad_char, nrm, w_stream, *w_conv)


RZ, RY, RC = 4, 2, 2
PW = 384
PR = 48
LD, LX, LY, LH, LF = 2, 8, 12, 3, 25
HRING = LY + 1
PER, PK = 11, 3


Group = collections.namedtuple("Group", ("left", "parts", "right", "col", "cols", "out", "lead", "at"))
GRU, TABLE, TINY = 5, 4, 8


def piece_groups(taps):
    rows = [(6 + k, 2, 5, 0, 4, 7, i) for i, k in enumerate(taps)]
    rows += [(4, 1, 4, 0, 2, 6, 0), (5, 1, 4, 768, 2, 6, 1), (3, 4, 3, 0, 2, 3, None), (2, 1, 2, 0, 8, 2, None), (1, 1, 1, 0, 2, 1, None), (0, 1, 0, 0, 6, 0, None)]
    out, at = [], 0
    for r in rows:
        out.append(Group(*r, at))
        at += r[1] * r[4]
    return tuple(out), at


MISC = (((GRU, 0), (GRU, 1), (GRU, 2)), ((GRU, 3), (TABLE, 0), (TABLE, 1)), ((TABLE, 2), (TINY, 0), (None, 0)))


def reduce_kernel(npieces, groups, *refs):
    lhs, rhs = refs[:9], refs[9:15]
    emb_ref, dpre_ref, demb_ref, ids_ref, tiny_ref = refs[15:20]
    outs = refs[20:29]
    (lt, done, part, r0, held, r1, r2, up, dn, fin, fx,
     d_send, d_recv, x_send, x_recv, y_send, y_recv, u_send, u_recv, n_send, n_recv, f_send, f_recv) = refs[29:]
    dp = lax.axis_index("dp")
    me = lax.axis_index("seq")
    c = lax.rem(me, RC)
    y = lax.rem(lax.div(me, RC), RY)
    z = lax.div(me, RC * RY)

    def to(zz, yy, cc):
        return (dp, (zz * RY + yy) * RC + cc)

    sib, ynb, zup, zdn, xnb = to(z, y, 1 - c), to(z, 1 - y, c), to(z + 1, y, c), to(z - 1, y, c), (1 - dp, me)
    bar = pltpu.get_barrier_semaphore()
    for where in (sib, ynb, xnb):
        pl.semaphore_signal(bar, inc=1, device_id=where, device_id_type=MESH)
    pl.when(z > 0)(lambda: pl.semaphore_signal(bar, inc=1, device_id=zdn, device_id_type=MESH))
    pl.when(z < RZ - 1)(lambda: pl.semaphore_signal(bar, inc=1, device_id=zup, device_id_type=MESH))
    pl.semaphore_wait(bar, 3 + (z > 0).astype(jnp.int32) + (z < RZ - 1).astype(jnp.int32))

    def copy(src, dst, send, recv, where):
        return pltpu.make_async_remote_copy(src_ref=src, dst_ref=dst, send_sem=send, recv_sem=recv, device_id=where, device_id_type=MESH)

    def d2d(t):
        b, k = lax.rem(t, LD + 1), lax.rem(t, 2 * LD)
        return copy(part.at[b, :, :, 1 - c], r0.at[k], d_send.at[b], d_recv.at[k], sib)

    def far(t):
        return lax.div(t, PER) * PK + lax.div(lax.rem(t, PER), 3)

    def across(t):
        return copy(held.at[lax.rem(t, HRING)], r1.at[far(t)], x_send.at[t], x_recv.at[t], xnb)

    def along_y(t):
        return copy(held.at[lax.rem(t, HRING), :, 1 - y], r2.at[t], y_send.at[t], y_recv.at[t], ynb)

    def final(t):
        return copy(fin.at[t], fx.at[t], f_send.at[t], f_recv.at[t], xnb)

    def go_up(t, k):
        src = r2.at[t, pl.ds(k + 1, RZ - 1 - k)] if k == 0 else up.at[t, pl.ds(k, RZ - 1 - k)]
        return copy(src, up.at[t, pl.ds(k, RZ - 1 - k)], u_send.at[t], u_recv.at[t], zup)

    def from_below(t, k):
        ref = up.at[t, pl.ds(k - 1, RZ - k)]
        return copy(ref, ref, u_send.at[t], u_recv.at[t], zdn)

    def go_down(t, k):
        src = r2.at[t, pl.ds(0, k)] if k == RZ - 1 else dn.at[t, pl.ds(0, k)]
        return copy(src, dn.at[t, pl.ds(0, k)], n_send.at[t], n_recv.at[t], zdn)

    def from_above(t, k):
        ref = dn.at[t, pl.ds(0, k + 1)]
        return copy(ref, ref, n_send.at[t], n_recv.at[t], zup)

    def add(a, b):
        return (a.astype(F32) + b.astype(F32)).astype(BF)

    def live(t):
        return jnp.logical_and(t >= 0, t < npieces)

    def route(t):
        m = lax.rem(t, PER)
        return jnp.where(m < 3 * PK, lax.rem(m, 3), 0)

    def mine(t):
        r = route(t)
        return jnp.logical_or(r == 0, r - 1 == dp)

    def finish(t):
        r = route(t)

        @pl.when(r == 0)
        def _():
            final(t).wait_recv()
            done[...] = add(fin[t], fx[t])

        @pl.when(jnp.logical_and(r > 0, r - 1 == dp))
        def _():
            done[...] = fin[t]

        @pl.when(jnp.logical_and(r > 0, r - 1 != dp))
        def _():
            final(t).wait_recv()
            done[...] = fx[t]

        pl.when(mine(t))(lambda: final(t).wait_send())
        for g in groups:
            @pl.when(jnp.logical_and(t >= g.at, t < g.at + g.parts * g.cols))
            def _(g=g):
                i = t - g.at
                rows = pl.ds(pl.multiple_of(lax.div(i, g.cols) * PR, PR), PR)
                cols = pl.ds(pl.multiple_of(lax.rem(i, g.cols) * PW, PW), PW)
                if g.lead is None:
                    outs[g.out][rows, cols] = done[...]
                else:
                    outs[g.out][g.lead, rows, cols] = done[...]
        for m, trio in enumerate(MISC):
            @pl.when(t == npieces - len(MISC) + m)
            def _(trio=trio):
                for i, (kind, cb) in enumerate(trio):
                    if kind is not None:
                        outs[kind][:, cb * PW : (cb + 1) * PW] = done[16 * i : 16 * i + 16, :]

    def sum_up(t):
        for k in range(RZ):
            @pl.when(z == k)
            def _(k=k):
                if k > 0:
                    from_below(t, k).wait_recv()
                    for q in range(k + 1, RZ):
                        up[t, q - 1] = add(up[t, q - 1], r2[t, q])
                if k < RZ - 1:
                    go_up(t, k).start()

    def sum_down(t):
        for k in range(RZ):
            @pl.when(z == k)
            def _(k=k):
                if k < RZ - 1:
                    from_above(t, k).wait_recv()
                    for q in range(k):
                        dn[t, q] = add(dn[t, q], r2[t, q])
                if k > 0:
                    go_down(t, k).start()

    def close(t):
        for k in range(RZ):
            @pl.when(z == k)
            def _(k=k):
                total = r2[t, k].astype(F32)
                if k > 0:
                    total = total + up[t, k - 1].astype(F32)
                    go_down(t, k).wait_send()
                if k < RZ - 1:
                    total = total + dn[t, k].astype(F32)
                    go_up(t, k).wait_send()
                fin[t] = total.astype(BF)
        final(t).start()

    def join_y(t):
        along_y(t).wait_recv()
        along_y(t).wait_send()
        h = lax.rem(t, HRING)
        for q in range(RZ):
            r2[t, q] = add(r2[t, q], held[h, q, y])

    def join_x(t):
        h = lax.rem(t, HRING)
        across(t).wait_recv()
        for q in range(RZ):
            held[h, q] = add(held[h, q], r1[far(t), q])
        along_y(t).start()

    def join_core(t):
        b, k = lax.rem(t, LD + 1), lax.rem(t, 2 * LD)
        h = lax.rem(t, HRING)
        d2d(t).wait_recv()
        d2d(t).wait_send()
        for q in range(RZ):
            held[h, q] = add(part[b, q, :, c], r0[k, q])
        pl.when(route(t) == 0)(lambda: along_y(t).start())
        pl.when(jnp.logical_not(mine(t)))(lambda: across(t).start())

    def turn(ref):
        n = ref.shape[0]
        for k in range(0, ref.shape[1], 384):
            lt[k // PR : k // PR + 8, :, :n] = ref[:, k : k + 384].T.reshape(8, PR, n)

    def make(t):
        b = lax.rem(t, LD + 1)
        for g in groups:
            @pl.when(jnp.logical_and(t >= g.at, t < g.at + g.parts * g.cols))
            def _(g=g):
                i = t - g.at
                j, cb = lax.div(i, g.cols), lax.rem(i, g.cols)
                pl.when(i == 0)(lambda: turn(lhs[g.left]))
                right = rhs[g.right][:, pl.ds(pl.multiple_of(g.col + cb * PW, PW), PW)]
                for q in range(RZ // 2):
                    left = jnp.concatenate([lt[(8 * q + s) * g.parts + j] for s in range(8)], 0)
                    part[b, 2 * q : 2 * q + 2] = dot(left, right).astype(BF).reshape(2, RY, RC, PR, PW)
        for m, trio in enumerate(MISC):
            @pl.when(t == npieces - len(MISC) + m)
            def _(trio=trio):
                for i, (kind, cb) in enumerate(trio):
                    if kind == GRU:
                        val = wgrad(emb_ref[...], dpre_ref[:, cb * PW : (cb + 1) * PW]).astype(BF).reshape(RZ, RY, RC, 16, PW)
                    elif kind == TABLE:
                        unit = lax.broadcasted_iota(jnp.int32, (ids_ref.shape[0], PW), 1) + cb * PW
                        hot = jnp.where(unit == ids_ref[...], 1.0, 0.0).astype(BF)
                        val = wgrad(demb_ref[...], hot).astype(BF).reshape(RZ, RY, RC, 16, PW)
                    elif kind == TINY:
                        val = tiny_ref[...].reshape(RZ, RY, RC, 16, PW)
                    else:
                        val = jnp.zeros((RZ, RY, RC, 16, PW), BF)
                    part[b, :, :, :, 16 * i : 16 * i + 16, :] = val
        d2d(t).start()

    def tick(T, _):
        def do(t, f, cond=None):
            ok = live(t)
            pl.when(ok if cond is None else jnp.logical_and(ok, cond(t)))(lambda: f(t))

        do(T - LF, finish)
        do(T - LY - z * LH, sum_up, mine)
        do(T - LY - (RZ - 1 - z) * LH, sum_down, mine)
        do(T - LY - (RZ - 1) * LH, close, mine)
        do(T - LY + 1, join_y, mine)
        do(T - LX, join_x, lambda t: jnp.logical_and(route(t) > 0, mine(t)))
        do(T - LX, lambda t: across(t).wait_send(), lambda t: jnp.logical_not(mine(t)))
        do(T - LD, join_core)
        do(T, make)
        return 0

    lax.fori_loop(0, npieces + LF + 1, tick, 0)


def widen_kernel(*refs):
    half = len(refs) // 2
    for a, b in zip(refs[:half], refs[half:]):
        if a.shape == b.shape:
            b[...] = a[...].astype(F32)
        else:
            b[...] = a[:, : b.shape[1]].astype(F32)


def reduce_all(lhs, rhs, emb, dpre, demb, ids, g_bias, g_norms, n_table, nseq, cid, taps=(0, 1, 2)):
    width = lhs[0].shape[1]
    per = g_bias.shape[0] // nseq
    tiny = jnp.concatenate([g_bias.reshape(nseq, per), g_norms.reshape(8, nseq, -1).transpose(1, 0, 2).reshape(nseq, -1)], 1).astype(BF)
    tiny = jnp.pad(tiny, ((0, 0), (0, 16 * PW - tiny.shape[1]))).reshape(nseq, 16, PW)
    groups, npieces = piece_groups(taps)
    npieces += len(MISC)
    D = pltpu.SemaphoreType.DMA
    v = lambda *s: pltpu.VMEM(s, BF)
    spec = pl.BlockSpec(memory_space=pltpu.VMEM)
    f = lambda *s: jax.ShapeDtypeStruct(s, BF)
    wide = 2 * width
    got = pl.pallas_call(
        functools.partial(reduce_kernel, npieces, groups),
        out_shape=[
            f(width // nseq, 3 * width), f(width // nseq, width), f(width // nseq, 4 * width), f(4 * width // nseq, width),
            f(16, 3 * PW), f(16, 4 * PW), f(2, width // nseq, width), f(max(len(taps), 1), wide // nseq, wide), f(16, PW),
        ],
        in_specs=[spec] * 20,
        out_specs=[spec] * 9,
        scratch_shapes=[
            v(64, PR, lhs[0].shape[0]), v(PR, PW),
            v(LD + 1, RZ, RY, RC, PR, PW), v(2 * LD, RZ, RY, PR, PW), v(HRING, RZ, RY, PR, PW), v(PK * (npieces // PER + 1), RZ, RY, PR, PW),
            v(npieces, RZ, PR, PW), v(npieces, RZ - 1, PR, PW), v(npieces, RZ - 1, PR, PW), v(npieces, PR, PW), v(npieces, PR, PW),
            D((LD + 1,)), D((2 * LD,)), D((npieces,)), D((npieces,)), D((npieces,)), D((npieces,)),
            D((npieces,)), D((npieces,)), D((npieces,)), D((npieces,)), D((npieces,)), D((npieces,)),
        ],
        compiler_params=pltpu.CompilerParams(collective_id=cid, has_side_effects=True, vmem_limit_bytes=62 << 20),
    )(*lhs, *rhs, emb, dpre, demb, ids, tiny)
    got = pl.pallas_call(
        widen_kernel,
        out_shape=[jax.ShapeDtypeStruct((16, n_table) if k == TABLE else a.shape, F32) for k, a in enumerate(got)],
        in_specs=[spec] * 9,
        out_specs=[spec] * 9,
        compiler_params=vmem(32),
    )(*got)
    small = got[8].reshape(-1)
    return tuple(got[:4]) + (
        got[4], got[5], small[:per], got[6], got[7], small[per : per + 8 * width // nseq].reshape(4, 2, -1),
    )


def join_taps(late, early):
    parts = [None] * 3
    rest = [k for k in range(3) if k not in TAPS]
    for i, k in enumerate(TAPS):
        parts[k] = late[i]
    for i, k in enumerate(rest):
        parts[k] = early[i]
    return jnp.stack(parts)


def scatter(total, axis):
    part = lax.psum_scatter(total, "seq", scatter_dimension=axis, tiled=True)
    return lax.psum(part, "dp").astype(F32)


def body(tokens, char_ids, span_lengths, script_group, w_qkv, w_out, w_up, w_down, char_table, w_gru, gru_bias, w_stream, w_conv, norms, grad_token, grad_char):
    nseq, planes = lax.axis_size("seq"), lax.axis_size("dp")
    seqs, toks, width = tokens.shape
    chars = char_ids.shape[1]
    rows = seqs * toks
    bias_n, norm_n = gru_bias.shape[0], norms.shape[2]
    small = jnp.concatenate([gru_bias, norms.reshape(-1)])
    small = jnp.pad(small, (0, 2048 - small.shape[0])).reshape(16, 128)
    routed = ((w_up, 0, 1, None), (w_conv, 0, 1, 0), (w_down, 0, 2, None), (w_conv, 0, 2, 2))
    if CONV1:
        routed += ((w_conv, 0, 0, 1),)
    got = gather(
        routed + ((w_out, 0, 0, None), (w_stream, 1, 0, None), (w_qkv, 0, 0, None), (w_gru, 0, 0, None), (char_table, 0, 0, None), (small, 0, 0, None)), 1, planes, nseq
    )
    w_out, w_stream, w_qkv, w_gru, char_table, small = got[-6:]
    w_up, conv0, w_down, conv2 = got[:4]
    if CONV1:
        conv1 = got[4]
    else:
        conv1, small = lax.optimization_barrier((w_conv[1], small))
        conv1 = lax.all_gather(conv1, "seq", axis=0, tiled=True)
    w_conv = (conv0, conv1, conv2)
    small = small.reshape(nseq, 2048)
    bias = small[:, :bias_n].reshape(-1).astype(F32)
    nrm = small[:, bias_n : bias_n + 8 * norm_n].reshape(nseq, 4, 2, norm_n).transpose(1, 2, 0, 3).reshape(4, 2, width).astype(F32)

    x_low = tokens.reshape(rows, width)
    x = x_low.astype(F32)
    qkv = dot(x_low, w_qkv).astype(BF)
    qkv3 = qkv.reshape(seqs, toks, 3 * width)

    char_rows = (char_ids + script_group[:, None] * GROUP_CHARS).reshape(seqs * chars, 1)
    onehot = (char_rows == jnp.arange(VOCAB_CHAR, dtype=jnp.int32)).astype(BF)
    embedded = dot_t(onehot, char_table).astype(BF)
    pre = dot(embedded, w_gru) + bias

    span = span_lengths[:, 0]
    span_ends = jnp.cumsum(span, -1)
    starts = span_ends - span
    ends_col = jnp.stack([starts, span_ends], -1).reshape(rows, 2)
    ends_row = jnp.pad(jnp.stack([starts, span_ends], 1), ((0, 0), (0, 6), (0, 0))).reshape(seqs * 8, toks)
    block = pltpu.VMEM((2 * HB, chars, 128), F32)
    full = lambda *d: jax.ShapeDtypeStruct(d, F32)
    keys, values, tot_all, pooled, prev, chunk = gather_with(
        functools.partial(forward_run, seqs), [(qkv3[..., width : 2 * width], 1, 0, None), (qkv3[..., 2 * width :], 1, 0, None)],
        2, planes, nseq, (pre, ends_col), (), [full(rows, width), full(seqs * chars, width), full(seqs * 4 * NCH, HG)], [block] * 4,
    )
    own_q, keys = lax.optimization_barrier((qkv3[..., :width], keys))
    queries = lax.all_gather(own_q, "seq", axis=1, tiled=True)

    ctx3, ctx_low3, lse = attention_fwd(qkv3, keys, values)
    context, context_low = ctx3.reshape(rows, width), ctx_low3.reshape(rows, width)
    normed, back_one = jax.vjp(layer_norm, x + dot(context_low, w_out), nrm[0, 0], nrm[0, 1])
    normed_low = normed.astype(BF)
    raised = dot(normed_low, w_up)
    hidden_full, gelu_up = jax.vjp(jax.nn.gelu, raised)
    hidden = hidden_full.astype(BF)
    token_state, back_two = jax.vjp(layer_norm, normed + dot(hidden, w_down), nrm[1, 0], nrm[1, 1])
    (out_token, out_char, state_low, pooled_low, mprev, merged, mnext, dmixed_low, dfused, dstate, dpooled, dnorm) = conv_both(
        seqs, token_state, pooled, grad_token.reshape(rows, width), grad_char.reshape(rows, width), nrm.reshape(8, width), w_stream, w_conv, 5
    )
    early = None
    if len(TAPS) < 3 and seq_dims(nseq) == (RZ, RY, RC) and planes == 2:
        sides = [(mprev, merged, mnext)[k] for k in range(3) if k not in TAPS]
        g_sides = wgrad(jnp.concatenate(sides, 1), dmixed_low).astype(BF).reshape(len(sides), 2 * width, 2 * width)
        early = scatter(g_sides, 1)

    dstate_sum, gain_two, shift_two = back_two(dstate)
    dlowered = dstate_sum.astype(BF)
    (draised,) = gelu_up(dot_t(dlowered, w_down))
    draised_low = draised.astype(BF)
    dinput_sum, gain_one, shift_one = back_one(dstate_sum + dot_t(draised_low, w_up))
    dattended = dinput_sum.astype(BF)
    dctx = dot_t(dattended, w_out).astype(BF)
    delta = jnp.sum((dctx.astype(F32) * context).reshape(seqs, toks, HEADS // 2, 2, HDIM), -1).transpose(0, 2, 1, 3)
    col = jnp.concatenate([lse, delta], -1)
    stat_rows = seqs * (HEADS // 2) * 4
    stat = jnp.swapaxes(col, 2, 3).reshape(stat_rows, toks)
    dctx3 = dctx.reshape(seqs, toks, width)
    length = nseq * toks
    dctx_all, stat_all, _, dpre, dbias, dq = gather_with(
        functools.partial(backward_run, seqs), [(dctx3, 1, 0, None), (stat, 0, 0, None)], 3, planes, nseq,
        (pre, prev, chunk, tot_all, dpooled, ends_row, own_q, dctx3, col), (keys, values),
        [jax.ShapeDtypeStruct((seqs * chars, 4 * HG), BF), full(seqs * 8, 4 * HG), jax.ShapeDtypeStruct((seqs, toks, width), BF)],
        [pltpu.VMEM((seqs * chars, width), F32), pltpu.VMEM((seqs * 2 * NCH, HG), F32)] + [block] * 2
        + [pltpu.VMEM((2, length, 2 * HDIM), BF)] * 2 + [pltpu.SemaphoreType.DMA((2,))] * 2,
    )
    stat_all = stat_all.reshape(nseq, seqs, HEADS // 2, 4, toks).transpose(1, 2, 3, 0, 4).reshape(seqs, HEADS // 2, 4, nseq * toks)
    g_bias = dbias.reshape(seqs, 8, 4 * HG)[:, 0].sum(0)
    dembed = dot_t(dpre, w_gru).astype(BF)

    dk, dv = attention_bwd(qkv3, queries, dctx_all, stat_all)
    dqkv = jnp.concatenate([dq, dk, dv], -1).reshape(rows, 3 * width)
    dinputs = dinput_sum + dot_t(dqkv, w_qkv)
    g_norms = jnp.concatenate([jnp.stack([gain_one, shift_one, gain_two, shift_two]), dnorm[:4]]).reshape(4, 2, width)
    shape = (seqs, toks, width)
    if seq_dims(nseq) == (RZ, RY, RC) and planes == 2:
        lhs = (x_low, context_low, normed_low, hidden, state_low, pooled_low, mprev, merged, mnext)
        rhs = (dqkv, dattended, draised_low, dlowered, dfused, dmixed_low)
        owned = reduce_all(lhs, rhs, embedded, dpre, dembed, char_rows, g_bias, g_norms, VOCAB_CHAR, nseq, 4, TAPS)
        owned = owned[:8] + (join_taps(owned[8], early),) + owned[9:]
    else:
        g_stream = [wgrad(state_low, dfused[:, :width]), wgrad(pooled_low, dfused[:, width:])]
        owned = (
            scatter(wgrad(x_low, dqkv).astype(BF), 0),
            scatter(wgrad(context_low, dattended).astype(BF), 0),
            scatter(wgrad(normed_low, draised_low).astype(BF), 0),
            scatter(wgrad(hidden, dlowered).astype(BF), 0),
            scatter(wgrad(dembed, onehot).astype(BF), 0),
            scatter(wgrad(embedded, dpre).astype(BF), 0),
            scatter(g_bias.astype(BF), 0),
            scatter(jnp.stack(g_stream).astype(BF), 1),
            scatter(jnp.stack([wgrad(m, dmixed_low) for m in (mprev, merged, mnext)]).astype(BF), 1),
            scatter(g_norms.astype(BF), 2),
        )
    return (
        out_token.reshape(shape),
        out_char.reshape(shape),
        dinputs.reshape(shape),
    ) + owned


def solution(mesh):
    placed = (
        P("dp", "seq", None),
        P("dp", "seq"),
        P("dp", "seq", None),
        P("dp"),
        P("seq", None),
        P("seq", None),
        P("seq", None),
        P("seq", None),
        P("seq", None),
        P("seq", None),
        P("seq"),
        P(None, "seq", None),
        P(None, "seq", None),
        P(None, None, "seq"),
        P("dp", "seq", None),
        P("dp", "seq", None),
    )
    return jax.shard_map(
        body,
        mesh=mesh,
        in_specs=placed,
        out_specs=(
            P("dp", "seq", None),
            P("dp", "seq", None),
            P("dp", "seq", None),
            P("seq", None),
            P("seq", None),
            P("seq", None),
            P("seq", None),
            P("seq", None),
            P("seq", None),
            P("seq"),
            P(None, "seq", None),
            P(None, "seq", None),
            P(None, None, "seq"),
        ),
        check_vma=False,
    )
```

```python
import collections
import functools
import jax
import jax.numpy as jnp
from jax import lax
from jax.experimental import pallas as pl
from jax.experimental.pallas import tpu as pltpu
from jax.sharding import PartitionSpec as P

HEADS = 12
HDIM = 64
VOCAB_CHAR = 1000
GROUP_CHARS = 250
HG = 384
EPSILON = 1e-05
MESH = pl.DeviceIdType.MESH
BF = jnp.bfloat16
F32 = jnp.float32
NCH = 8
UNROLL = 8
SHARE = (1, 2, 3, 6)
HB = HG // 128

def seq_dims(n):
    return {16: (4, 2, 2), 32: (8, 4, 1)}.get(n, (n, 1, 1))


Move = collections.namedtuple("Move", ("array", "axis", "rows", "lead", "route"))


def gather_kernel(dims, planes, moves, n_arrays, task, *refs):
    Z, Y, C = dims
    n = len(moves)
    n_in, n_out = (task.n_in, task.n_out) if task else (0, 0)
    src, task_in = refs[:n_arrays], refs[n_arrays : n_arrays + n_in]
    refs = refs[n_arrays + n_in :]
    dst, task_out = refs[:n_arrays], refs[n_arrays : n_arrays + n_out]
    own_sem, recv, zs, ds, ys, ss, xs, *task_scratch = refs[n_arrays + n_out :]
    dp = lax.axis_index("dp")
    me = lax.axis_index("seq")
    c = lax.rem(me, C)
    y = lax.rem(lax.div(me, C), Y)
    z = lax.div(me, C * Y)
    up_z, down_z = z < Z - 1, z > 0

    def at(zz, yy, cc):
        return (zz * Y + yy) * C + cc

    def to(zz, yy, cc):
        return (dp, at(zz, yy, cc))

    def view(i, slot):
        m = moves[i]
        s = pl.ds(pl.multiple_of(slot * m.rows, m.rows), m.rows)
        ref = dst[m.array]
        return ref.at[s] if m.axis == 0 else ref.at[:, s]

    def mine(i):
        m = moves[i]
        return src[m.array] if m.lead is None else src[m.array].at[m.lead]

    def copy(i, slot, send, where, own=False):
        return pltpu.make_async_remote_copy(
            src_ref=mine(i) if own else view(i, slot), dst_ref=view(i, slot),
            send_sem=send, recv_sem=recv.at[i, slot], device_id=where, device_id_type=MESH)

    sib = to(z, y, 1 - c) if C == 2 else None
    xp = (1 - dp, me)
    use_x = planes == 2 and any(m.route for m in moves)
    some = sib if C == 2 else to(z, y, c)

    def owner(i):
        return None if not (use_x and moves[i].route) else dp == moves[i].route - 1

    def when(cond, f):
        if cond is None:
            f()
        else:
            pl.when(cond)(f)

    def both(a, b):
        return b if a is None else jnp.logical_and(a, b)

    nseq = Z * Y * C
    if task:
        push_all, *task_out = task_out
        push, p_send, p_recv, i_sem, *task_scratch = task_scratch
        n_held = n_in - task.n_stay
        held, task_scratch = task_scratch[:n_held], task_scratch[n_held:]
        loads = [pltpu.make_async_copy(a, b, i_sem.at[k]) for k, (a, b) in enumerate(zip(task_in[:n_held], held))]
        for load in loads:
            load.start()
    bar = pltpu.get_barrier_semaphore()
    if task:
        peers = [(None, (dp, lax.rem(me + k, nseq))) for k in range(1, nseq)]
    else:
        peers = [(z > 0, to(z - 1, y, c)), (z < Z - 1, to(z + 1, y, c))]
        if Y > 1:
            peers += [(y > 0, to(z, y - 1, c)), (y < Y - 1, to(z, y + 1, c))]
        if C == 2:
            peers.append((None, sib))
    if use_x:
        peers.append((None, xp))
    count = 0
    for cond, where in peers:
        when(cond, functools.partial(pl.semaphore_signal, bar, inc=1, device_id=where, device_id_type=MESH))
        count = count + (1 if cond is None else cond.astype(jnp.int32))
    pl.semaphore_wait(bar, count)
    if task:

        def pushed(k, slot, where):
            return pltpu.make_async_remote_copy(
                src_ref=push, dst_ref=push_all.at[slot], send_sem=p_send.at[k], recv_sem=p_recv.at[slot], device_id=where, device_id_type=MESH)

        def push_one(k, _):
            pushed(k, me, (dp, lax.rem(me + k, nseq))).start()
            return 0

        def push_wait(k, _):
            other = lax.rem(me + k, nseq)
            pushed(k, other, (dp, other)).wait_recv()
            pushed(k, me, (dp, other)).wait_send()
            return 0

    def work(point):
        if task:
            task.run(point, me, push, push_all, tuple(held) + tuple(task_in[n_held:]), task_out, task_scratch)

    def go_z(i, slot, up, sem, own=False):
        where = to(z + 1, y, c) if up else to(z - 1, y, c)
        pl.when(up_z if up else down_z)(lambda: copy(i, slot, sem, where, own).start())

    def go_y(i, slot, up, sem, own=False):
        where = to(z, y + 1, c) if up else to(z, y - 1, c)
        pl.when(y < Y - 1 if up else y > 0)(lambda: copy(i, slot, sem, where, own).start())

    def go_core(i, slot, own=False):
        if C == 2:
            copy(i, slot, ss.at[i, slot], sib, own).start()

    def wait_in(i, slot):
        copy(i, slot, ss.at[i, slot], some).wait_recv()

    for i in range(n):
        pltpu.make_async_copy(mine(i), view(i, me), own_sem.at[i]).start()

        def own_sends(i=i):
            go_z(i, me, True, zs.at[i, me], True)
            go_z(i, me, False, ds.at[i, 0], True)
            if Y > 1:
                go_y(i, me, True, ys.at[i, me], True)
                go_y(i, me, False, ds.at[i, 1], True)

        when(owner(i), own_sends)
        go_core(i, me, True)

    def arrive_z(zz, up):
        slot = at(zz, y, c)

        def one(i):
            wait_in(i, slot)
            go_z(i, slot, up, zs.at[i, slot])
            if Y > 1:
                go_y(i, slot, True, ys.at[i, slot])
                go_y(i, slot, False, ys.at[i, slot] if Y == 2 else xs.at[i, slot])
            if use_x and moves[i].route:
                copy(i, slot, xs.at[i, slot], xp).start()
            go_core(i, slot)

        for i in range(n):
            when(owner(i), functools.partial(one, i))

    def arrive_y(zz, yy, up):
        slot = at(zz, yy, c)

        def one(i):
            wait_in(i, slot)
            if Y > 2:
                go_y(i, slot, up, ys.at[i, slot])
            if use_x and moves[i].route:
                copy(i, slot, xs.at[i, slot], xp).start()
            go_core(i, slot)

        for i in range(n):
            when(owner(i), functools.partial(one, i))

    def all_y(zz):
        for t in range(1, Y):
            pl.when(y - t >= 0)(lambda: arrive_y(zz, y - t, True))
            pl.when(y + t < Y)(lambda: arrive_y(zz, y + t, False))

    if task:
        for load in loads:
            load.wait()
        work(0)
        push_all[me] = push[...]
        lax.fori_loop(1, nseq, push_one, 0)
    def step(s, _):
        pl.when(z - s >= 0)(lambda: arrive_z(z - s, True))
        pl.when(z + s < Z)(lambda: arrive_z(z + s, False))
        q = s - 1
        pl.when(z - q >= 0)(lambda: all_y(z - q))
        pl.when(jnp.logical_and(q > 0, z + q < Z))(lambda: all_y(z + q))
        return 0

    if task:
        for s in (1, 2):
            if s < Z:
                step(s, 0)
            if s == 1:
                lax.fori_loop(1, nseq, push_wait, 0)
            work(s)
        lax.fori_loop(3, Z, step, 0)
        work(3)
    else:
        lax.fori_loop(1, Z, step, 0)
    q = Z - 1
    pl.when(z - q >= 0)(lambda: all_y(z - q))
    pl.when(z + q < Z)(lambda: all_y(z + q))

    if use_x:

        def far(k, _):
            slot = at(lax.rem(z + lax.div(k, Y), Z), lax.rem(y + lax.rem(k, Y), Y), c)

            def one(i):
                wait_in(i, slot)
                go_core(i, slot)

            for i in range(n):
                if moves[i].route:
                    pl.when(dp != moves[i].route - 1)(functools.partial(one, i))
            return 0

        lax.fori_loop(1, Z * Y, far, 0)

    def drain(k, _):
        zz, yy = lax.div(k, Y), lax.rem(k, Y)
        slot = at(zz, yy, c)
        is_own = slot == me
        own_y = yy == y
        fz = jnp.logical_or(jnp.logical_and(zz <= z, up_z), jnp.logical_and(zz > z, down_z))
        for i in range(n):
            o = owner(i)
            if C == 2:
                wait_in(i, at(zz, yy, 1 - c))
                copy(i, slot, ss.at[i, slot], some).wait_send()
            sent = lambda sem: copy(i, slot, sem, some).wait_send()
            pl.when(both(o, jnp.logical_and(own_y, fz)))(lambda: sent(zs.at[i, slot]))
            if Y == 2:
                pl.when(both(o, jnp.logical_and(own_y, jnp.logical_or(jnp.logical_not(is_own), y < Y - 1))))(lambda: sent(ys.at[i, slot]))
            elif Y > 2:
                fy = jnp.logical_or(jnp.logical_and(yy <= y, y < Y - 1), jnp.logical_and(yy > y, y > 0))
                pl.when(both(o, fy))(lambda: sent(ys.at[i, slot]))
                fy2 = jnp.logical_and(jnp.logical_and(own_y, y > 0), jnp.logical_not(is_own))
                pl.when(both(o, fy2))(lambda: sent(xs.at[i, slot]))
            if use_x and moves[i].route:
                pl.when(both(o, jnp.logical_not(is_own)))(lambda: sent(xs.at[i, slot]))
        return 0

    lax.fori_loop(0, Z * Y, drain, 0)
    for i in range(n):
        pltpu.make_async_copy(mine(i), view(i, me), own_sem.at[i]).wait()
        o = owner(i)
        pl.when(both(o, down_z))(lambda: copy(i, me, ds.at[i, 0], some, True).wait_send())
        if Y > 1:
            pl.when(both(o, y > 0))(lambda: copy(i, me, ds.at[i, 1], some, True).wait_send())


Task = collections.namedtuple("Task", ("n_in", "n_stay", "n_out", "run"))


def gather(arrays, cid, planes, nseq, task=None, inputs=(), outputs=(), scratch=()):
    dims = seq_dims(nseq)
    moves, shapes = [], []
    for k, (x, axis, route, lead) in enumerate(arrays):
        shape = list(x.shape if lead is None else x.shape[1:])
        moves.append(Move(k, axis, shape[axis], lead, route if planes == 2 and dims[1:] == (2, 2) else 0))
        shape[axis] *= nseq
        shapes.append(jax.ShapeDtypeStruct(tuple(shape), x.dtype))
    moves.sort(key=lambda m: not m.route)
    n = len(moves)
    D = pltpu.SemaphoreType.DMA
    scratch = [D((n,)), D((n, nseq)), D((n, nseq)), D((n, 2)), D((n, nseq)), D((n, nseq)), D((n, nseq))] + list(scratch)
    far, here = pl.BlockSpec(memory_space=pl.ANY), pl.BlockSpec(memory_space=pltpu.VMEM)
    return pl.pallas_call(
        functools.partial(gather_kernel, dims, planes, tuple(moves), len(arrays), task),
        out_shape=shapes + list(outputs),
        in_specs=[far] * (len(arrays) + len(inputs)),
        out_specs=[far] * len(arrays) + [here] * len(outputs),
        scratch_shapes=scratch,
        compiler_params=pltpu.CompilerParams(collective_id=cid, has_side_effects=True, vmem_limit_bytes=60 << 20),
    )(*[x for x, _, _, _ in arrays], *inputs)


def gather_with(run, arrays, cid, planes, nseq, inputs, stay, outputs, scratch):
    D = pltpu.SemaphoreType.DMA
    push = (8, HG)
    outputs = [jax.ShapeDtypeStruct((nseq,) + push, F32)] + outputs
    scratch = [pltpu.VMEM(push, F32), D((nseq,)), D((nseq,)), D((len(inputs),))] + [pltpu.VMEM(a.shape, a.dtype) for a in inputs] + scratch
    inputs = tuple(inputs) + tuple(stay)
    return gather(arrays, cid, planes, nseq, Task(len(inputs), len(stay), len(outputs), run), inputs, outputs, scratch)


def dot(a, b):
    return jnp.dot(a, b, preferred_element_type=F32)


def dot_t(a, b):
    return lax.dot_general(a, b, (((1,), (1,)), ((), ())), preferred_element_type=F32)


def wgrad(a, b):
    return lax.dot_general(a, b, (((0,), (0,)), ((), ())), preferred_element_type=F32)


def vmem(mib):
    return pltpu.CompilerParams(vmem_limit_bytes=mib << 20)


def layer_norm(values, gain_row, shift_row):
    center = values - jnp.mean(values, -1, keepdims=True)
    spread = jnp.mean(center * center, -1, keepdims=True)
    return center * lax.rsqrt(spread + EPSILON) * gain_row + shift_row


def fill(pre_ref, decay, drive=None):
    for k in range(2):
        for j in range(HB):
            at = 2 * k * HG + j * 128
            rate = jax.nn.sigmoid(pre_ref[:, at : at + 128])
            decay[k * HB + j] = 1.0 - rate
            if drive is not None:
                drive[k * HB + j] = rate * pre_ref[:, at + HG : at + HG + 128]


def row(x, i):
    return lax.slice_in_dim(x, i, i + 1, axis=0)


def cat(parts):
    return jnp.concatenate(parts, 1)


def blocks(x):
    return [x[:, j * 128 : (j + 1) * 128] for j in range(HB)]


def totals_kernel(pre_ref, tot_ref, chunk_ref, decay, drive):
    length = pre_ref.shape[0] // NCH
    fill(pre_ref, decay, drive)

    def step(t, carry):
        place = (pl.ds(t, NCH, stride=length), pl.ds(length - 1 - t, NCH, stride=length))
        out = []
        for i in range(2 * HB):
            c, h = carry[i]
            a = decay[i, place[i // HB], :]
            out.append((c * a, a * h + drive[i, place[i // HB], :]))
        return tuple(out)

    one, zero = jnp.ones((NCH, 128), F32), jnp.zeros((NCH, 128), F32)
    ends = lax.fori_loop(0, length, step, ((one, zero),) * (2 * HB), unroll=UNROLL)
    cf, hf = cat([e[0] for e in ends[:HB]]), cat([e[1] for e in ends[:HB]])
    cb, hb = cat([e[0] for e in ends[HB:]]), cat([e[1] for e in ends[HB:]])
    chunk_ref[0:NCH, :] = cf
    chunk_ref[NCH : 2 * NCH, :] = hf
    chunk_ref[2 * NCH : 3 * NCH, :] = cb
    chunk_ref[3 * NCH :, :] = hb
    one, zero = jnp.ones((1, HG), F32), jnp.zeros((1, HG), F32)
    tf, sf, tb, sb = one, zero, one, zero
    for k in range(NCH):
        sf, tf = row(cf, k) * sf + row(hf, k), tf * row(cf, k)
        j = NCH - 1 - k
        sb, tb = row(cb, j) * sb + row(hb, j), tb * row(cb, j)
    tot_ref[...] = jnp.concatenate([tf, sf, tb, sb], 0)


def states_work(me, q, seqs, all_ref, pre_all, chunk_all, ends_all, pooled_all, prev_all, decay, drive, state, prev):
    pre_ref, chunk_ref, ends_ref, pooled_ref, prev_ref = (
        r.at[pl.ds(q * (r.shape[0] // seqs), r.shape[0] // seqs)] for r in (pre_all, chunk_all, ends_all, pooled_all, prev_all)
    )
    chars = pre_all.shape[0] // seqs
    length = chars // NCH
    nseq = all_ref.shape[0]
    fill(pre_ref, decay, drive)
    ef = jnp.zeros((1, HG), F32)
    eb = ef
    for d in range(nseq):
        got = all_ref[d]
        ef = jnp.where(d < me, row(got, 4 * q) * ef + row(got, 4 * q + 1), ef)
        got = all_ref[nseq - 1 - d]
        eb = jnp.where(nseq - 1 - d > me, row(got, 4 * q + 2) * eb + row(got, 4 * q + 3), eb)
    cf, hf = chunk_ref[0:NCH, :], chunk_ref[NCH : 2 * NCH, :]
    cb, hb = chunk_ref[2 * NCH : 3 * NCH, :], chunk_ref[3 * NCH :, :]
    rows_f, rows_b = [], []
    for k in range(NCH):
        rows_f.append(ef)
        ef = row(cf, k) * ef + row(hf, k)
        j = NCH - 1 - k
        rows_b.append(eb)
        eb = row(cb, j) * eb + row(hb, j)

    def step(t, carry):
        place = (pl.ds(t, NCH, stride=length), pl.ds(length - 1 - t, NCH, stride=length))
        out = []
        for i in range(2 * HB):
            at = place[i // HB]
            prev[i, at, :] = carry[i]
            h = decay[i, at, :] * carry[i] + drive[i, at, :]
            state[i, at, :] = h
            out.append(h)
        return tuple(out)

    lax.fori_loop(0, length, step, tuple(blocks(jnp.concatenate(rows_f, 0)) + blocks(jnp.concatenate(rows_b[::-1], 0))), unroll=UNROLL)
    first = ends_ref[:, 0:1]
    last = ends_ref[:, 1:2]
    place = lax.broadcasted_iota(jnp.int32, (ends_all.shape[0] // seqs, chars), 1)
    member = jnp.where((place >= first) & (place < last), 1.0, 0.0).astype(BF)
    prev_ref[...] = cat([prev[i] for i in range(2 * HB)])
    pooled_ref[...] = dot(member, cat([state[i].astype(BF) for i in range(2 * HB)])) / (last - first).astype(F32)


def flows_kernel(pre_ref, dpool_ref, ends_ref, chunk_ref, ds_ref, tot_ref, gch_ref, decay, ds):
    chars = pre_ref.shape[0]
    length = chars // NCH
    fill(pre_ref, decay)
    first = ends_ref[0:1, :]
    last = ends_ref[1:2, :]
    place = lax.broadcasted_iota(jnp.int32, (chars, ends_ref.shape[1]), 0)
    inside = (place >= first) & (place < last)
    span = jnp.sum(jnp.where(inside, (last - first).astype(F32), 0.0), 1, keepdims=True)
    member = jnp.where(inside, 1.0, 0.0).astype(BF)
    spread = dot(member, dpool_ref[...]) / span
    ds_ref[...] = spread
    for i in range(2 * HB):
        ds[i] = spread[:, i * 128 : (i + 1) * 128]

    def step(t, carry):
        place = (pl.ds(length - 1 - t, NCH, stride=length), pl.ds(t, NCH, stride=length))
        return tuple(
            decay[i, place[i // HB], :] * (ds[i, place[i // HB], :] + carry[i]) for i in range(2 * HB)
        )

    ends = lax.fori_loop(0, length, step, (jnp.zeros((NCH, 128), F32),) * (2 * HB), unroll=UNROLL)
    gf, gb = cat(ends[:HB]), cat(ends[HB:])
    gch_ref[0:NCH, :] = gf
    gch_ref[NCH:, :] = gb
    cf, cb = chunk_ref[0:NCH, :], chunk_ref[2 * NCH : 3 * NCH, :]
    zero = jnp.zeros((1, HG), F32)
    tf, tb = zero, zero
    for k in range(NCH):
        j = NCH - 1 - k
        tf = row(cf, j) * tf + row(gf, j)
        tb = row(cb, k) * tb + row(gb, k)
    tot_ref[...] = jnp.concatenate([tf, tb, zero, zero], 0)


def dpre_work(me, q, seqs, gall_ref, all_ref, pre_all, ds_all, prev_all, chunk_all, gch_all, dpre_all, bias_all, decay, ds):
    pre_ref, ds_ref, prev_ref, chunk_ref, gch_ref, dpre_ref, bias_ref = (
        r.at[pl.ds(q * (r.shape[0] // seqs), r.shape[0] // seqs)] for r in (pre_all, ds_all, prev_all, chunk_all, gch_all, dpre_all, bias_all)
    )
    chars = pre_all.shape[0] // seqs
    length = chars // NCH
    nseq = all_ref.shape[0]
    fill(pre_ref, decay)
    for i in range(2 * HB):
        ds[i] = ds_ref[:, i * 128 : (i + 1) * 128]
    ef = jnp.zeros((1, HG), F32)
    eb = ef
    for d in range(nseq):
        j = nseq - 1 - d
        ef = jnp.where(j > me, row(all_ref[j], 4 * q) * ef + row(gall_ref[j], 4 * q), ef)
        eb = jnp.where(d < me, row(all_ref[d], 4 * q + 2) * eb + row(gall_ref[d], 4 * q + 1), eb)
    cf, cb = chunk_ref[0:NCH, :], chunk_ref[2 * NCH : 3 * NCH, :]
    gf, gb = gch_ref[0:NCH, :], gch_ref[NCH:, :]
    rows_f, rows_b = [], []
    for k in range(NCH):
        j = NCH - 1 - k
        rows_f.append(ef)
        ef = row(cf, j) * ef + row(gf, j)
        rows_b.append(eb)
        eb = row(cb, k) * eb + row(gb, k)

    def step(t, carry):
        place = (pl.ds(length - 1 - t, NCH, stride=length), pl.ds(t, NCH, stride=length))
        out = []
        for i in range(2 * HB):
            at = place[i // HB]
            g = ds[i, at, :] + carry[i]
            ds[i, at, :] = g
            out.append(decay[i, at, :] * g)
        return tuple(out)

    lax.fori_loop(0, length, step, tuple(blocks(jnp.concatenate(rows_f[::-1], 0)) + blocks(jnp.concatenate(rows_b, 0))), unroll=UNROLL)
    for i in range(2 * HB):
        k, j = i // HB, i % HB
        at = 2 * k * HG + j * 128
        g = ds[i]
        rate = jax.nn.sigmoid(pre_ref[:, at : at + 128])
        cand = pre_ref[:, at + HG : at + HG + 128]
        prev = prev_ref[:, i * 128 : (i + 1) * 128]
        dgate = (g * (cand - prev) * rate * decay[i]).astype(BF)
        dcand = (g * rate).astype(BF)
        for to, v in ((at, dgate), (at + HG, dcand)):
            dpre_ref[:, to : to + 128] = v
            bias_ref[:, to : to + 128] = jnp.broadcast_to(jnp.sum(v.astype(F32), 0, keepdims=True), (8, 128))


def part_of(ref, q, seqs):
    n = ref.shape[0] // seqs
    return ref.at[pl.ds(q * n, n)]


def forward_run(seqs, point, me, push, push_all, inputs, outputs, scratch):
    pre, ends = inputs
    pooled, prev, chunk = outputs
    if point == 0:
        for q in range(seqs):
            totals_kernel(part_of(pre, q, seqs), push.at[pl.ds(4 * q, 4)], part_of(chunk, q, seqs), *scratch[:2])
    elif point <= seqs:
        states_work(me, point - 1, seqs, push_all, pre, chunk, ends, pooled, prev, *scratch)


def backward_run(seqs, point, me, push, push_all, inputs, outputs, scratch):
    pre, prev, chunk, tot_all, dpool, ends, q_ref, dc_ref, col_ref, gru_ref, keys, values = inputs
    dpre, dbias, dq, demb = outputs
    ds_all, gch, decay, ds, kbuf, vbuf, k_sem, v_sem = scratch
    pairs = HEADS // 2
    steps = seqs * pairs

    def fetch(i):
        s, p = lax.div(i, pairs), lax.rem(i, pairs)
        cols = pl.ds(pl.multiple_of(p * 2 * HDIM, 2 * HDIM), 2 * HDIM)
        b = lax.rem(i, 2)
        return (pltpu.make_async_copy(keys.at[s, :, cols], kbuf.at[b], k_sem.at[b]), pltpu.make_async_copy(values.at[s, :, cols], vbuf.at[b], v_sem.at[b]))

    def one(i, _):
        s, p = lax.div(i, pairs), lax.rem(i, pairs)
        cols = pl.ds(pl.multiple_of(p * 2 * HDIM, 2 * HDIM), 2 * HDIM)
        b = lax.rem(i, 2)

        @pl.when(i + 1 < steps)
        def _():
            for c in fetch(i + 1):
                c.start()

        for c in fetch(i):
            c.wait()
        dq[s, :, cols] = query_grad(q_ref[s, :, cols], kbuf[b], vbuf[b], dc_ref[s, :, cols], col_ref[s, p])
        return 0

    if point == 0:
        for c in fetch(0):
            c.start()
        for q in range(seqs):
            flows_kernel(*(part_of(r, q, seqs) for r in (pre, dpool, ends, chunk, ds_all)), push.at[pl.ds(4 * q, 4)], part_of(gch, q, seqs), decay, ds)
    elif point <= seqs:
        dpre_work(me, point - 1, seqs, push_all, tot_all, pre, ds_all, prev, chunk, gch, dpre, dbias, decay, ds)
        part_of(demb, point - 1, seqs)[...] = dot_t(part_of(dpre, point - 1, seqs)[...], gru_ref[...]).astype(BF)
    bounds = (0,) + tuple(steps * k // 6 for k in SHARE)
    lax.fori_loop(bounds[point], bounds[point + 1], one, 0)


def pair_rows(x):
    lane = lax.broadcasted_iota(jnp.int32, x.shape, 1)
    zero = jnp.zeros_like(x)
    return jnp.concatenate([jnp.where(lane < HDIM, x, zero), jnp.where(lane >= HDIM, x, zero)], 0)


def pair_lanes(x):
    half = x.shape[0] // 2
    lane = lax.broadcasted_iota(jnp.int32, (half, x.shape[1]), 1)
    return jnp.where(lane < HDIM, x[:half], x[half:])


def attn_fwd_kernel(q_ref, k_ref, v_ref, ctx_ref, low_ref, lse_ref):
    toks = q_ref.shape[0]
    s = dot_t(pair_rows(q_ref[...] * (HDIM ** -0.5)), k_ref[...])
    top = jnp.max(s, 1, keepdims=True)
    p = jnp.exp(s - top)
    total = jnp.sum(p, 1, keepdims=True)
    o = pair_lanes(dot(p.astype(BF), v_ref[...]) / total)
    ctx_ref[...] = o
    low_ref[...] = o.astype(BF)
    lse = top + jnp.log(total)
    lse_ref[...] = jnp.concatenate([lse[:toks], lse[toks:]], 1)


def head_spec(rows, base=0):
    return pl.BlockSpec((None, rows, 2 * HDIM), lambda s, h: (s, 0, h + base))


def attention_fwd(qkv, keys, values):
    seqs, toks, _ = qkv.shape
    length = keys.shape[1]
    pairs = HEADS // 2
    return pl.pallas_call(
        attn_fwd_kernel,
        grid=(seqs, pairs),
        out_shape=[
            jax.ShapeDtypeStruct((seqs, toks, HEADS * HDIM), F32),
            jax.ShapeDtypeStruct((seqs, toks, HEADS * HDIM), BF),
            jax.ShapeDtypeStruct((seqs, pairs, toks, 2), F32),
        ],
        in_specs=[head_spec(toks), head_spec(length), head_spec(length)],
        out_specs=[head_spec(toks), head_spec(toks), pl.BlockSpec((None, None, toks, 2), lambda s, h: (s, h, 0, 0))],
        compiler_params=vmem(48),
    )(qkv, keys, values)


def query_grad(q, keys, values, dc, col):
    scale = HDIM ** -0.5
    lse = jnp.concatenate([col[:, 0:1], col[:, 1:2]], 0)
    delta = jnp.concatenate([col[:, 2:3], col[:, 3:4]], 0)
    p = jnp.exp(dot_t(pair_rows(q * scale), keys) - lse)
    ds = (p * (dot_t(pair_rows(dc), values) - delta)).astype(BF)
    return (pair_lanes(dot(ds, keys)) * scale).astype(BF)


def context_kernel(datt_ref, w_ref, ctx_ref, lse_ref, dctx_ref, col_ref, stat_ref):
    seqs, toks, _ = dctx_ref.shape
    pairs = HEADS // 2
    low = dot_t(datt_ref[...], w_ref[...]).astype(BF)
    prod = low.astype(F32) * ctx_ref[...]
    lane = lax.broadcasted_iota(jnp.int32, (toks, 2 * HDIM), 1)
    for s in range(seqs):
        dctx_ref[s] = low[s * toks : (s + 1) * toks]
        cols = []
        for p in range(pairs):
            x = prod[s * toks : (s + 1) * toks, p * 2 * HDIM : (p + 1) * 2 * HDIM]
            a = jnp.sum(jnp.where(lane < HDIM, x, 0.0), 1, keepdims=True)
            b = jnp.sum(jnp.where(lane >= HDIM, x, 0.0), 1, keepdims=True)
            col = jnp.concatenate([lse_ref[s, p], a, b], 1)
            col_ref[s, p] = col
            cols.append(col)
        flat = jnp.concatenate(cols + [jnp.zeros((toks, 128 - 4 * pairs), F32)], 1)
        stat_ref[s * 4 * pairs : (s + 1) * 4 * pairs, :] = flat.T[: 4 * pairs]


def context_grad(dattended, w_out, context, lse):
    seqs, pairs, toks, _ = lse.shape
    here = pl.BlockSpec(memory_space=pltpu.VMEM)
    return pl.pallas_call(
        context_kernel,
        out_shape=[
            jax.ShapeDtypeStruct((seqs, toks, context.shape[1]), BF), jax.ShapeDtypeStruct((seqs, pairs, toks, 4), F32),
            jax.ShapeDtypeStruct((seqs * pairs * 4, toks), F32),
        ],
        in_specs=[here] * 4,
        out_specs=[here] * 3,
        compiler_params=vmem(24),
    )(dattended, w_out, context, lse)


def attn_bwd_kernel(ko_ref, vo_ref, qa_ref, dca_ref, row_ref, dk_ref, dv_ref):
    toks = ko_ref.shape[0]
    scale = HDIM ** -0.5

    def spread(i):
        n = row_ref.shape[1]
        return jnp.concatenate(
            [jnp.broadcast_to(row_ref[i : i + 1, :], (toks, n)), jnp.broadcast_to(row_ref[i + 1 : i + 2, :], (toks, n))], 0
        )

    p = jnp.exp(dot_t(pair_rows(ko_ref[...] * scale), qa_ref[...]) - spread(0))
    dv_ref[...] = pair_lanes(dot(p.astype(BF), dca_ref[...])).astype(BF)
    dp = dot_t(pair_rows(vo_ref[...]), dca_ref[...])
    ds = (p * (dp - spread(2))).astype(BF)
    dk_ref[...] = (pair_lanes(dot(ds, qa_ref[...])) * scale).astype(BF)


def attention_bwd(qkv, queries, dctx_all, rows):
    seqs, toks, _ = qkv.shape
    length = queries.shape[1]
    pairs = HEADS // 2
    stat = lambda a, b: pl.BlockSpec((None, None, a, b), lambda s, h: (s, h, 0, 0))
    return pl.pallas_call(
        attn_bwd_kernel,
        grid=(seqs, pairs),
        out_shape=[jax.ShapeDtypeStruct((seqs, toks, HEADS * HDIM), BF)] * 2,
        in_specs=[head_spec(toks, pairs), head_spec(toks, 2 * pairs), head_spec(length), head_spec(length), stat(4, length)],
        out_specs=[head_spec(toks)] * 2,
        compiler_params=vmem(56),
    )(qkv, qkv, queries, dctx_all, rows)


GELU_A = 0.7978845608028654
GELU_B = 0.044715


def norm_both(v, gain, shift, dy):
    center = v - jnp.mean(v, -1, keepdims=True)
    inv = lax.rsqrt(jnp.mean(center * center, -1, keepdims=True) + EPSILON)
    hat = center * inv
    dhat = dy * gain
    dv = inv * (dhat - jnp.mean(dhat, -1, keepdims=True) - hat * jnp.mean(dhat * hat, -1, keepdims=True))
    return hat * gain + shift, dv, jnp.sum(dy * hat, 0, keepdims=True), jnp.sum(dy, 0, keepdims=True)


def conv_kernel(seqs, state_ref, pooled_ref, gtok_ref, gchr_ref, nrm_ref, ws_ref, c0_ref, c1_ref, c2_ref,
                otok_ref, ochr_ref, slow_ref, plow_ref, mprev_ref, merged_ref, mnext_ref, dmix_ref, dfus_ref, dstate_ref, dpool_ref, dnorm_ref,
                taps, acc, edge, before, after, dside, dchar, w_sem, e_send, b_recv, a_recv):
    me = lax.axis_index("seq")
    dp = lax.axis_index("dp")
    n = lax.axis_size("seq")
    rows, width = state_ref.shape
    toks = rows // seqs
    wide = 2 * width
    loads = [pltpu.make_async_copy(c, taps.at[k], w_sem.at[k]) for k, c in ((1, c1_ref), (0, c0_ref), (2, c2_ref))]
    for load in loads:
        load.start()
    edge[...] = jnp.zeros_like(edge)
    dnorm_ref[4:8, :] = jnp.zeros((4, width), F32)
    right, left = (dp, me + 1), (dp, me - 1)
    has_l, has_r = me > 0, me < n - 1
    bar = pltpu.get_barrier_semaphore()
    pl.when(has_l)(lambda: pl.semaphore_signal(bar, inc=1, device_id=left, device_id_type=MESH))
    pl.when(has_r)(lambda: pl.semaphore_signal(bar, inc=1, device_id=right, device_id_type=MESH))
    pl.semaphore_wait(bar, has_l.astype(jnp.int32) + has_r.astype(jnp.int32))

    def send(k):
        def to_right():
            return pltpu.make_async_remote_copy(
                src_ref=edge.at[k, 0], dst_ref=before.at[k], send_sem=e_send.at[k, 0], recv_sem=b_recv.at[k], device_id=right, device_id_type=MESH)

        def to_left():
            return pltpu.make_async_remote_copy(
                src_ref=edge.at[k, 1], dst_ref=after.at[k], send_sem=e_send.at[k, 1], recv_sem=a_recv.at[k], device_id=left, device_id_type=MESH)

        return to_right, to_left

    def start(k, ref):
        for s in range(seqs):
            edge[k, 0, s : s + 1, :] = ref[(s + 1) * toks - 16 : (s + 1) * toks, :].astype(F32)[15:16]
            edge[k, 1, s : s + 1, :] = ref[s * toks : s * toks + 16, :].astype(F32)[0:1]
        to_right, to_left = send(k)
        pl.when(has_r)(lambda: to_right().start())
        pl.when(has_l)(lambda: to_left().start())

    def finish(k):
        to_right, to_left = send(k)
        pl.when(has_r)(lambda: to_left().wait_recv())
        pl.when(has_l)(lambda: to_right().wait_recv())
        pl.when(has_r)(lambda: to_right().wait_send())
        pl.when(has_l)(lambda: to_left().wait_send())

    def shifts(k, ref, prev_ref, next_ref):
        for j in range(0, wide, 512):
            x = ref[:, j : j + 512].astype(F32)
            at = lax.broadcasted_iota(jnp.int32, x.shape, 0)
            prev, follow = pltpu.roll(x, 1, 0), pltpu.roll(x, rows - 1, 0)
            for s in range(seqs):
                b = jnp.where(has_l, before[k, s : s + 1, j : j + 512], 0.0)
                a = jnp.where(has_r, after[k, s : s + 1, j : j + 512], 0.0)
                prev = jnp.where(at == s * toks, b, prev)
                follow = jnp.where(at == (s + 1) * toks - 1, a, follow)
            prev_ref[:, j : j + 512] = prev.astype(BF)
            next_ref[:, j : j + 512] = follow.astype(BF)

    slow = state_ref[...].astype(BF)
    plow = pooled_ref[...].astype(BF)
    slow_ref[...] = slow
    plow_ref[...] = plow
    merged_ref[:, :width] = dot(slow, ws_ref[0]).astype(BF)
    merged_ref[:, width:] = dot(plow, ws_ref[1]).astype(BF)
    start(0, merged_ref)
    loads[0].wait()

    def centre(j, _):
        cols = pl.ds(pl.multiple_of(j * 512, 512), 512)
        acc[:, cols] = dot(merged_ref[...], taps[1, :, cols])
        return 0

    lax.fori_loop(0, wide // 512, centre, 0)
    finish(0)
    shifts(0, merged_ref, mprev_ref, mnext_ref)
    loads[1].wait()
    loads[2].wait()

    def sides(j, _):
        cols = pl.ds(pl.multiple_of(j * 512, 512), 512)
        acc[:, cols] += dot(mprev_ref[...], taps[0, :, cols]) + dot(mnext_ref[...], taps[2, :, cols])
        return 0

    lax.fori_loop(0, wide // 512, sides, 0)
    for part, (base_ref, grad_ref, out_ref) in enumerate(((state_ref, gtok_ref, otok_ref), (pooled_ref, gchr_ref, ochr_ref))):
        mixed = acc[:, part * width : (part + 1) * width]
        square = mixed * mixed
        curve = jnp.tanh(GELU_A * (mixed + GELU_B * mixed * square))
        gated = 0.5 * mixed * (1.0 + curve)
        slope = 0.5 * (1.0 + curve) + 0.5 * mixed * (1.0 - curve * curve) * (GELU_A * (1.0 + 3.0 * GELU_B * square))
        r = 4 + 2 * part
        out, dsum, dgain, dshift = norm_both(base_ref[...] + gated, nrm_ref[r : r + 1, :], nrm_ref[r + 1 : r + 2, :], grad_ref[...].astype(F32))
        out_ref[...] = out.astype(BF)
        dnorm_ref[2 * part : 2 * part + 1, :] = dgain
        dnorm_ref[2 * part + 1 : 2 * part + 2, :] = dshift
        dmix_ref[:, part * width : (part + 1) * width] = (dsum * slope).astype(BF)
        if part == 0:
            dstate_ref[...] = dsum
        else:
            dchar[...] = dsum
    start(1, dmix_ref)

    def centre_back(j, _):
        cols = pl.ds(pl.multiple_of(j * 512, 512), 512)
        acc[:, cols] = dot_t(dmix_ref[...], taps[1, cols, :])
        return 0

    lax.fori_loop(0, wide // 512, centre_back, 0)
    finish(1)
    shifts(1, dmix_ref, dside.at[0], dside.at[1])

    def sides_back(j, _):
        cols = pl.ds(pl.multiple_of(j * 512, 512), 512)
        dfus_ref[:, cols] = (acc[:, cols] + dot_t(dside[1], taps[0, cols, :]) + dot_t(dside[0], taps[2, cols, :])).astype(BF)
        return 0

    lax.fori_loop(0, wide // 512, sides_back, 0)
    dstate_ref[...] += dot_t(dfus_ref[:, :width], ws_ref[0])
    dpool_ref[...] = (dchar[...] + dot_t(dfus_ref[:, width:], ws_ref[1])).astype(BF)


def conv_both(seqs, token_state, pooled, grad_token, grad_char, nrm, w_stream, w_conv, cid):
    rows, width = token_state.shape
    wide = 2 * width
    here = pl.BlockSpec(memory_space=pltpu.VMEM)
    far = pl.BlockSpec(memory_space=pl.ANY)
    low, full = jax.ShapeDtypeStruct((rows, width), BF), jax.ShapeDtypeStruct((rows, width), F32)
    both = jax.ShapeDtypeStruct((rows, wide), BF)
    D = pltpu.SemaphoreType.DMA
    return pl.pallas_call(
        functools.partial(conv_kernel, seqs),
        out_shape=[low, low, low, low, both, both, both, both, both, full, low, jax.ShapeDtypeStruct((8, width), F32)],
        in_specs=[here] * 6 + [far] * 3,
        out_specs=[here] * 12,
        scratch_shapes=[
            pltpu.VMEM((3, wide, wide), BF), pltpu.VMEM((rows, wide), F32), pltpu.VMEM((2, 2, 8, wide), F32),
            pltpu.VMEM((2, 8, wide), F32), pltpu.VMEM((2, 8, wide), F32), pltpu.VMEM((2, rows, wide), BF), pltpu.VMEM((rows, width), F32),
            D((3,)), D((2, 2)), D((2,)), D((2,)),
        ],
        compiler_params=pltpu.CompilerParams(collective_id=cid, has_side_effects=True, vmem_limit_bytes=60 << 20),
    )(token_state, pooled, grad_token, grad_char, nrm, w_stream, *w_conv)


RZ, RY, RC = 4, 2, 2
PW = 384
PR = 48
LD, LX, LY, LH, LF = 2, 8, 12, 3, 25
HRING = LY + 1
PER, PK = 11, 3
JOB = 6


Group = collections.namedtuple("Group", ("left", "parts", "right", "col", "cols", "out", "lead", "base", "at"))
GRU, TABLE, TINY = 5, 4, 8


def piece_groups(taps):
    rows = [(6 + k, 2, 5, 0, 4, 7, i, 0) for i, k in enumerate(taps)]
    rows += [(4, 1, 4, 0, 2, 6, 0, 0), (5, 1, 4, 768, 2, 6, 1, 0), (3, 4, 3, 0, 2, 3, None, 0), (2, 1, 2, 0, 8, 2, None, 0), (1, 1, 1, 0, 2, 1, None, 0),
             (0, 1, 0, 0, 2, 0, None, 0), (0, 1, 6, 0, 4, 0, None, 2)]
    out, at = [], 0
    for r in rows:
        out.append(Group(*r, at))
        at += r[1] * r[4]
    return tuple(out), at


MISC = (((GRU, 0), (GRU, 1), (GRU, 2)), ((GRU, 3), (TABLE, 0), (TABLE, 1)), ((TABLE, 2), (TINY, 0), (None, 0)))


def reduce_kernel(npieces, groups, *refs):
    out_ref, dkv_ref = refs[24:26]
    width = refs[0].shape[1]
    dk_ref, dv_ref = dkv_ref.at[:, pl.ds(0, width)], dkv_ref.at[:, pl.ds(width, width)]
    lhs, rhs = refs[:9], refs[9:15] + (dkv_ref,)
    emb_ref, dpre_ref, demb_ref, ids_ref, tiny_ref, kv_ref, stat_ref, qa_ref, dca_ref = refs[15:24]
    (lt, part, r0, held, r1, r2, up, dn, fin, fx,
     d_send, d_recv, x_send, x_recv, y_send, y_recv, u_send, u_recv, n_send, n_recv, f_send, f_recv, qbuf, cbuf, dk_acc, dv_acc, q_sem, c_sem) = refs[26:]
    dp = lax.axis_index("dp")
    me = lax.axis_index("seq")
    c = lax.rem(me, RC)
    y = lax.rem(lax.div(me, RC), RY)
    z = lax.div(me, RC * RY)

    def to(zz, yy, cc):
        return (dp, (zz * RY + yy) * RC + cc)

    sib, ynb, zup, zdn, xnb = to(z, y, 1 - c), to(z, 1 - y, c), to(z + 1, y, c), to(z - 1, y, c), (1 - dp, me)
    bar = pltpu.get_barrier_semaphore()
    for where in (sib, ynb, xnb):
        pl.semaphore_signal(bar, inc=1, device_id=where, device_id_type=MESH)
    pl.when(z > 0)(lambda: pl.semaphore_signal(bar, inc=1, device_id=zdn, device_id_type=MESH))
    pl.when(z < RZ - 1)(lambda: pl.semaphore_signal(bar, inc=1, device_id=zup, device_id_type=MESH))
    pl.semaphore_wait(bar, 3 + (z > 0).astype(jnp.int32) + (z < RZ - 1).astype(jnp.int32))

    def copy(src, dst, send, recv, where):
        return pltpu.make_async_remote_copy(src_ref=src, dst_ref=dst, send_sem=send, recv_sem=recv, device_id=where, device_id_type=MESH)

    def d2d(t):
        b, k = lax.rem(t, LD + 1), lax.rem(t, 2 * LD)
        return copy(part.at[b, :, :, 1 - c], r0.at[k], d_send.at[b], d_recv.at[k], sib)

    def far(t):
        return lax.div(t, PER) * PK + lax.div(lax.rem(t, PER), 3)

    def mi(t):
        m = lax.rem(t, PER)
        return lax.div(t, PER) * (PER - PK) + m - jnp.minimum(lax.div(m + dp, 3), PK)

    def across(t):
        return copy(held.at[lax.rem(t, HRING)], r1.at[far(t)], x_send.at[t], x_recv.at[t], xnb)

    def along_y(t):
        return copy(held.at[lax.rem(t, HRING), :, 1 - y], r2.at[mi(t)], y_send.at[t], y_recv.at[t], ynb)

    def final(t):
        return copy(fin.at[t], fx.at[t], f_send.at[t], f_recv.at[t], xnb)

    def go_up(t, k):
        src = r2.at[mi(t), pl.ds(k + 1, RZ - 1 - k)] if k == 0 else up.at[mi(t), pl.ds(k, RZ - 1 - k)]
        return copy(src, up.at[mi(t), pl.ds(k, RZ - 1 - k)], u_send.at[t], u_recv.at[t], zup)

    def from_below(t, k):
        ref = up.at[mi(t), pl.ds(k - 1, RZ - k)]
        return copy(ref, ref, u_send.at[t], u_recv.at[t], zdn)

    def go_down(t, k):
        src = r2.at[mi(t), pl.ds(0, k)] if k == RZ - 1 else dn.at[mi(t), pl.ds(0, k)]
        return copy(src, dn.at[mi(t), pl.ds(0, k)], n_send.at[t], n_recv.at[t], zdn)

    def from_above(t, k):
        ref = dn.at[mi(t), pl.ds(0, k + 1)]
        return copy(ref, ref, n_send.at[t], n_recv.at[t], zup)

    def add(a, b):
        return (a.astype(F32) + b.astype(F32)).astype(BF)

    def live(t):
        return jnp.logical_and(t >= 0, t < npieces)

    def route(t):
        m = lax.rem(t, PER)
        return jnp.where(m < 3 * PK, lax.rem(m, 3), 0)

    def mine(t):
        r = route(t)
        return jnp.logical_or(r == 0, r - 1 == dp)

    def finish(t):
        r = route(t)

        @pl.when(r == 0)
        def _():
            final(t).wait_recv()
            out_ref[t] = add(fin[t], fx[t])

        @pl.when(jnp.logical_and(r > 0, r - 1 == dp))
        def _():
            out_ref[t] = fin[t]

        @pl.when(jnp.logical_and(r > 0, r - 1 != dp))
        def _():
            final(t).wait_recv()
            out_ref[t] = fx[t]

        pl.when(mine(t))(lambda: final(t).wait_send())

    def sum_up(t):
        i = mi(t)
        for k in range(RZ):
            @pl.when(z == k)
            def _(k=k):
                if k > 0:
                    from_below(t, k).wait_recv()
                    for q in range(k + 1, RZ):
                        up[i, q - 1] = add(up[i, q - 1], r2[i, q])
                if k < RZ - 1:
                    go_up(t, k).start()

    def sum_down(t):
        i = mi(t)
        for k in range(RZ):
            @pl.when(z == k)
            def _(k=k):
                if k < RZ - 1:
                    from_above(t, k).wait_recv()
                    for q in range(k):
                        dn[i, q] = add(dn[i, q], r2[i, q])
                if k > 0:
                    go_down(t, k).start()

    def close(t):
        i = mi(t)
        for k in range(RZ):
            @pl.when(z == k)
            def _(k=k):
                total = r2[i, k].astype(F32)
                if k > 0:
                    total = total + up[i, k - 1].astype(F32)
                    go_down(t, k).wait_send()
                if k < RZ - 1:
                    total = total + dn[i, k].astype(F32)
                    go_up(t, k).wait_send()
                fin[t] = total.astype(BF)
        final(t).start()

    def join_y(t):
        i = mi(t)
        along_y(t).wait_recv()
        along_y(t).wait_send()
        h = lax.rem(t, HRING)
        for q in range(RZ):
            r2[i, q] = add(r2[i, q], held[h, q, y])

    def join_x(t):
        h = lax.rem(t, HRING)
        across(t).wait_recv()
        for q in range(RZ):
            held[h, q] = add(held[h, q], r1[far(t), q])
        along_y(t).start()

    def join_core(t):
        b, k = lax.rem(t, LD + 1), lax.rem(t, 2 * LD)
        h = lax.rem(t, HRING)
        d2d(t).wait_recv()
        d2d(t).wait_send()
        for q in range(RZ):
            held[h, q] = add(part[b, q, :, c], r0[k, q])
        pl.when(route(t) == 0)(lambda: along_y(t).start())
        pl.when(jnp.logical_not(mine(t)))(lambda: across(t).start())

    def turn(ref):
        n = ref.shape[0]
        for k in range(0, ref.shape[1], 384):
            lt[k // PR : k // PR + 8, :, :n] = ref[:, k : k + 384].T.reshape(8, PR, n)

    def make(t):
        b = lax.rem(t, LD + 1)
        for g in groups:
            @pl.when(jnp.logical_and(t >= g.at, t < g.at + g.parts * g.cols))
            def _(g=g):
                i = t - g.at
                j, cb = lax.div(i, g.cols), lax.rem(i, g.cols)
                pl.when(i == 0)(lambda: turn(lhs[g.left]))
                right = rhs[g.right][:, pl.ds(pl.multiple_of(g.col + cb * PW, PW), PW)]
                for q in range(RZ // 2):
                    left = jnp.concatenate([lt[(8 * q + s) * g.parts + j] for s in range(8)], 0)
                    part[b, 2 * q : 2 * q + 2] = dot(left, right).astype(BF).reshape(2, RY, RC, PR, PW)
        for m, trio in enumerate(MISC):
            @pl.when(t == npieces - len(MISC) + m)
            def _(trio=trio):
                for i, (kind, cb) in enumerate(trio):
                    if kind == GRU:
                        val = wgrad(emb_ref[...], dpre_ref[:, cb * PW : (cb + 1) * PW]).astype(BF).reshape(RZ, RY, RC, 16, PW)
                    elif kind == TABLE:
                        unit = lax.broadcasted_iota(jnp.int32, (ids_ref.shape[0], PW), 1) + cb * PW
                        hot = jnp.where(unit == ids_ref[...], 1.0, 0.0).astype(BF)
                        val = wgrad(demb_ref[...], hot).astype(BF).reshape(RZ, RY, RC, 16, PW)
                    elif kind == TINY:
                        val = tiny_ref[...].reshape(RZ, RY, RC, 16, PW)
                    else:
                        val = jnp.zeros((RZ, RY, RC, 16, PW), BF)
                    part[b, :, :, :, 16 * i : 16 * i + 16, :] = val
        d2d(t).start()

    pairs = HEADS // 2
    toks = kv_ref.shape[1]
    half = qa_ref.shape[1] // 2
    jobs = 2 * pairs * kv_ref.shape[0]

    def fetch(i):
        s, p, h = lax.div(i, 2 * pairs), lax.rem(lax.div(i, 2), pairs), lax.rem(i, 2)
        cols = pl.ds(pl.multiple_of(p * 2 * HDIM, 2 * HDIM), 2 * HDIM)
        part = pl.ds(pl.multiple_of(h * half, half), half)
        return (pltpu.make_async_copy(qa_ref.at[s, part, cols], qbuf.at[h], q_sem.at[h]), pltpu.make_async_copy(dca_ref.at[s, part, cols], cbuf.at[h], c_sem.at[h]))

    def key_work(i):
        s, p, h = lax.div(i, 2 * pairs), lax.rem(lax.div(i, 2), pairs), lax.rem(i, 2)
        at = pl.multiple_of(p * 2 * HDIM, 2 * HDIM)
        slots = half // toks

        @pl.when(i + 1 < jobs)
        def _():
            for load in fetch(i + 1):
                load.start()

        for load in fetch(i):
            load.wait()
        scale = HDIM ** -0.5
        queries, dctx = qbuf[h], cbuf[h]

        def spread(k):
            at = (s * pairs + p) * 4 + k
            one = lambda r: jnp.concatenate([stat_ref[h * slots + d, pl.ds(r, 1), :] for d in range(slots)], 1)
            return jnp.concatenate([jnp.broadcast_to(one(at), (toks, half)), jnp.broadcast_to(one(at + 1), (toks, half))], 0)

        prob = jnp.exp(dot_t(pair_rows(kv_ref[s, :, pl.ds(at, 2 * HDIM)] * scale), queries) - spread(0))
        dv = dot(prob.astype(BF), dctx)
        dprob = dot_t(pair_rows(kv_ref[s, :, pl.ds(at + pairs * 2 * HDIM, 2 * HDIM)]), dctx)
        dk = dot((prob * (dprob - spread(2))).astype(BF), queries)

        @pl.when(h == 0)
        def _():
            dk_acc[...] = dk
            dv_acc[...] = dv

        @pl.when(h == 1)
        def _():
            rows = pl.ds(pl.multiple_of(s * toks, toks), toks)
            cols = pl.ds(at, 2 * HDIM)
            dk_ref[rows, cols] = (pair_lanes(dk_acc[...] + dk) * scale).astype(BF)
            dv_ref[rows, cols] = pair_lanes(dv_acc[...] + dv).astype(BF)

    for load in fetch(0):
        load.start()

    def tick(T, _):
        def do(t, f, cond=None):
            ok = live(t)
            pl.when(ok if cond is None else jnp.logical_and(ok, cond(t)))(lambda: f(t))

        do(T - LF, finish)
        do(T - LY - z * LH, sum_up, mine)
        do(T - LY - (RZ - 1 - z) * LH, sum_down, mine)
        do(T - LY - (RZ - 1) * LH, close, mine)
        do(T - LY + 1, join_y, mine)
        do(T - LX, join_x, lambda t: jnp.logical_and(route(t) > 0, mine(t)))
        do(T - LX, lambda t: across(t).wait_send(), lambda t: jnp.logical_not(mine(t)))
        do(T - LD, join_core)
        do(T, make)
        job = T - JOB
        pl.when(jnp.logical_and(job >= 0, job < jobs))(lambda: key_work(job))
        return 0

    lax.fori_loop(0, npieces + LF + 1, tick, 0)


def finish_kernel(groups, pieces, dq, dkv, w, base, *outs):
    for g in groups:
        for j in range(g.parts):
            for cb in range(g.cols):
                rows, cols = slice(j * PR, (j + 1) * PR), slice((g.base + cb) * PW, (g.base + cb + 1) * PW)
                val = pieces[g.at + j * g.cols + cb].astype(F32)
                if g.lead is None:
                    outs[g.out][rows, cols] = val
                else:
                    outs[g.out][g.lead, rows, cols] = val
    first = groups[-1].at + groups[-1].parts * groups[-1].cols
    bias, norms, dinput = outs[8:]
    for m, trio in enumerate(MISC):
        for i, (kind, cb) in enumerate(trio):
            val = pieces[first + m, 16 * i : 16 * i + 16, :].astype(F32)
            if kind == TINY:
                bias[...] = val[0:1, : bias.shape[1]]
                for k in range(4):
                    norms[k] = val[1 + 2 * k : 3 + 2 * k, : norms.shape[2]]
            elif kind is not None:
                n = min(PW, outs[kind].shape[1] - cb * PW)
                outs[kind][:, cb * PW : cb * PW + n] = val[:, :n]
    n = dq.shape[1]
    dinput[...] = base[...] + dot_t(dq[...], w[:, :n]) + dot_t(dkv[:, :n], w[:, n : 2 * n]) + dot_t(dkv[:, n:], w[:, 2 * n :])


def reduce_all(lhs, rhs, emb, dpre, demb, ids, kv, stat, queries, dctx, w_qkv, dsum, g_bias, g_norms, n_table, nseq, cid, taps=(0, 1, 2)):
    width = lhs[0].shape[1]
    per = g_bias.shape[0] // nseq
    tiny = jnp.concatenate([
        jnp.pad(g_bias.reshape(nseq, 1, per), ((0, 0), (0, 0), (0, PW - per))),
        jnp.pad(g_norms.reshape(8, nseq, -1).transpose(1, 0, 2), ((0, 0), (0, 7), (0, PW - width // nseq))),
    ], 1).astype(BF)
    groups, npieces = piece_groups(taps)
    npieces += len(MISC)
    dense = -(-npieces // PER) * (PER - PK)
    D = pltpu.SemaphoreType.DMA
    v = lambda *s: pltpu.VMEM(s, BF)
    spec = pl.BlockSpec(memory_space=pltpu.VMEM)
    pieces, dkv = pl.pallas_call(
        functools.partial(reduce_kernel, npieces, groups),
        out_shape=[jax.ShapeDtypeStruct((npieces, PR, PW), BF), jax.ShapeDtypeStruct((lhs[0].shape[0], 2 * width), BF)],
        in_specs=[spec] * 22 + [pl.BlockSpec(memory_space=pl.ANY)] * 2,
        out_specs=[spec] * 2,
        scratch_shapes=[
            v(64, PR, lhs[0].shape[0]),
            v(LD + 1, RZ, RY, RC, PR, PW), v(2 * LD, RZ, RY, PR, PW), v(HRING, RZ, RY, PR, PW), v(PK * (npieces // PER + 1), RZ, RY, PR, PW),
            v(dense, RZ, PR, PW), v(dense, RZ - 1, PR, PW), v(dense, RZ - 1, PR, PW), v(npieces, PR, PW), v(npieces, PR, PW),
            D((LD + 1,)), D((2 * LD,)), D((npieces,)), D((npieces,)), D((npieces,)), D((npieces,)),
            D((npieces,)), D((npieces,)), D((npieces,)), D((npieces,)), D((npieces,)), D((npieces,)),
            v(2, queries.shape[1] // 2, 2 * HDIM), v(2, queries.shape[1] // 2, 2 * HDIM),
            pltpu.VMEM((2 * kv.shape[1], 2 * HDIM), F32), pltpu.VMEM((2 * kv.shape[1], 2 * HDIM), F32), D((2,)), D((2,)),
        ],
        compiler_params=pltpu.CompilerParams(collective_id=cid, has_side_effects=True, vmem_limit_bytes=62 << 20),
    )(*lhs, *rhs, emb, dpre, demb, ids, tiny, kv, stat, queries, dctx)
    f = lambda *s: jax.ShapeDtypeStruct(s, F32)
    wide = 2 * width
    share = width // nseq
    return pl.pallas_call(
        functools.partial(finish_kernel, groups),
        out_shape=[
            f(share, 3 * width), f(share, width), f(share, 4 * width), f(4 * share, width), f(16, n_table), f(16, 4 * PW),
            f(2, share, width), f(3, 2 * share, wide), f(1, per), f(4, 2, share), f(*dsum.shape),
        ],
        in_specs=[spec] * 5,
        out_specs=[spec] * 11,
        compiler_params=vmem(40),
    )(pieces, rhs[0], dkv, w_qkv, dsum)


def scatter(total, axis):
    part = lax.psum_scatter(total, "seq", scatter_dimension=axis, tiled=True)
    return lax.psum(part, "dp").astype(F32)


def body(tokens, char_ids, span_lengths, script_group, w_qkv, w_out, w_up, w_down, char_table, w_gru, gru_bias, w_stream, w_conv, norms, grad_token, grad_char):
    nseq, planes = lax.axis_size("seq"), lax.axis_size("dp")
    seqs, toks, width = tokens.shape
    chars = char_ids.shape[1]
    rows = seqs * toks
    bias_n, norm_n = gru_bias.shape[0], norms.shape[2]
    small = jnp.concatenate([gru_bias, norms.reshape(-1)])
    small = jnp.pad(small, (0, 2048 - small.shape[0])).reshape(16, 128)
    conv0, w_down, conv1, conv2, w_out, w_stream, w_qkv, w_gru, char_table, small = gather(
        [(w_conv, 0, 1, 0), (w_down, 0, 1, None), (w_conv, 0, 2, 1), (w_conv, 0, 2, 2), (w_out, 0, 0, None), (w_stream, 1, 0, None), (w_qkv, 0, 0, None),
         (w_gru, 0, 0, None), (char_table, 0, 0, None), (small, 0, 0, None)], 1, planes, nseq
    )
    w_up, small = lax.optimization_barrier((w_up, small))
    w_up = lax.all_gather(w_up, "seq", axis=0, tiled=True)
    w_conv = (conv0, conv1, conv2)
    small = small.reshape(nseq, 2048)
    bias = small[:, :bias_n].reshape(-1).astype(F32)
    nrm = small[:, bias_n : bias_n + 8 * norm_n].reshape(nseq, 4, 2, norm_n).transpose(1, 2, 0, 3).reshape(4, 2, width).astype(F32)

    x_low = tokens.reshape(rows, width)
    x = x_low.astype(F32)
    qkv = dot(x_low, w_qkv).astype(BF)
    qkv3 = qkv.reshape(seqs, toks, 3 * width)

    char_rows = (char_ids + script_group[:, None] * GROUP_CHARS).reshape(seqs * chars, 1)
    onehot = (char_rows == jnp.arange(VOCAB_CHAR, dtype=jnp.int32)).astype(BF)
    embedded = dot_t(onehot, char_table).astype(BF)
    pre = dot(embedded, w_gru) + bias

    span = span_lengths[:, 0]
    span_ends = jnp.cumsum(span, -1)
    starts = span_ends - span
    ends_col = jnp.stack([starts, span_ends], -1).reshape(rows, 2)
    ends_row = jnp.pad(jnp.stack([starts, span_ends], 1), ((0, 0), (0, 6), (0, 0))).reshape(seqs * 8, toks)
    block = pltpu.VMEM((2 * HB, chars, 128), F32)
    full = lambda *d: jax.ShapeDtypeStruct(d, F32)
    keys, values, tot_all, pooled, prev, chunk = gather_with(
        functools.partial(forward_run, seqs), [(qkv3[..., width : 2 * width], 1, 0, None), (qkv3[..., 2 * width :], 1, 0, None)],
        2, planes, nseq, (pre, ends_col), (), [full(rows, width), full(seqs * chars, width), full(seqs * 4 * NCH, HG)], [block] * 4,
    )
    own_q, keys = lax.optimization_barrier((qkv3[..., :width], keys))
    queries = lax.all_gather(own_q, "seq", axis=1, tiled=True)

    ctx3, ctx_low3, lse = attention_fwd(qkv3, keys, values)
    context, context_low = ctx3.reshape(rows, width), ctx_low3.reshape(rows, width)
    normed, back_one = jax.vjp(layer_norm, x + dot(context_low, w_out), nrm[0, 0], nrm[0, 1])
    normed_low = normed.astype(BF)
    raised = dot(normed_low, w_up)
    hidden_full, gelu_up = jax.vjp(jax.nn.gelu, raised)
    hidden = hidden_full.astype(BF)
    token_state, back_two = jax.vjp(layer_norm, normed + dot(hidden, w_down), nrm[1, 0], nrm[1, 1])
    (out_token, out_char, state_low, pooled_low, mprev, merged, mnext, dmixed_low, dfused, dstate, dpooled, dnorm) = conv_both(
        seqs, token_state, pooled, grad_token.reshape(rows, width), grad_char.reshape(rows, width), nrm.reshape(8, width), w_stream, w_conv, 5
    )
    dstate_sum, gain_two, shift_two = back_two(dstate)
    dlowered = dstate_sum.astype(BF)
    (draised,) = gelu_up(dot_t(dlowered, w_down))
    draised_low = draised.astype(BF)
    dinput_sum, gain_one, shift_one = back_one(dstate_sum + dot_t(draised_low, w_up))
    dattended = dinput_sum.astype(BF)
    dctx3, col, stat = context_grad(dattended, w_out, context, lse)
    length = nseq * toks
    dctx_all, stat_all, _, dpre, dbias, dq, dembed = gather_with(
        functools.partial(backward_run, seqs), [(dctx3, 1, 0, None), (stat, 0, 0, None)], 3, planes, nseq,
        (pre, prev, chunk, tot_all, dpooled, ends_row, own_q, dctx3, col, w_gru), (keys, values),
        [jax.ShapeDtypeStruct((seqs * chars, 4 * HG), BF), full(seqs * 8, 4 * HG), jax.ShapeDtypeStruct((seqs, toks, width), BF),
         jax.ShapeDtypeStruct(embedded.shape, BF)],
        [pltpu.VMEM((seqs * chars, width), F32), pltpu.VMEM((seqs * 2 * NCH, HG), F32)] + [block] * 2
        + [pltpu.VMEM((2, length, 2 * HDIM), BF)] * 2 + [pltpu.SemaphoreType.DMA((2,))] * 2,
    )
    g_bias = dbias.reshape(seqs, 8, 4 * HG)[:, 0].sum(0)

    g_norms = jnp.concatenate([jnp.stack([gain_one, shift_one, gain_two, shift_two]), dnorm[:4]]).reshape(4, 2, width)
    shape = (seqs, toks, width)
    if seq_dims(nseq) == (RZ, RY, RC) and planes == 2:
        lhs = (x_low, context_low, normed_low, hidden, state_low, pooled_low, mprev, merged, mnext)
        rhs = (dq.reshape(rows, width), dattended, draised_low, dlowered, dfused, dmixed_low)
        *owned, dinputs = reduce_all(
            lhs, rhs, embedded, dpre, dembed, char_rows, qkv3[..., width:], stat_all.reshape(nseq, -1, toks), queries, dctx_all, w_qkv, dinput_sum, g_bias, g_norms, VOCAB_CHAR, nseq, 4
        )
        owned[8] = owned[8].reshape(-1)
        owned = [owned[k] for k in (0, 1, 2, 3, 4, 5, 8, 6, 7, 9)]
        owned = tuple(owned)
    else:
        stat_all = stat_all.reshape(nseq, seqs, HEADS // 2, 4, toks).transpose(1, 2, 3, 0, 4).reshape(seqs, HEADS // 2, 4, nseq * toks)
        dk, dv = attention_bwd(qkv3, queries, dctx_all, stat_all)
        dqkv = jnp.concatenate([dq, dk, dv], -1).reshape(rows, 3 * width)
        dinputs = dinput_sum + dot_t(dqkv, w_qkv)
        g_stream = [wgrad(state_low, dfused[:, :width]), wgrad(pooled_low, dfused[:, width:])]
        owned = (
            scatter(wgrad(x_low, dqkv).astype(BF), 0),
            scatter(wgrad(context_low, dattended).astype(BF), 0),
            scatter(wgrad(normed_low, draised_low).astype(BF), 0),
            scatter(wgrad(hidden, dlowered).astype(BF), 0),
            scatter(wgrad(dembed, onehot).astype(BF), 0),
            scatter(wgrad(embedded, dpre).astype(BF), 0),
            scatter(g_bias.astype(BF), 0),
            scatter(jnp.stack(g_stream).astype(BF), 1),
            scatter(jnp.stack([wgrad(m, dmixed_low) for m in (mprev, merged, mnext)]).astype(BF), 1),
            scatter(g_norms.astype(BF), 2),
        )
    return (
        out_token.reshape(shape),
        out_char.reshape(shape),
        dinputs.reshape(shape),
    ) + owned


def solution(mesh):
    placed = (
        P("dp", "seq", None),
        P("dp", "seq"),
        P("dp", "seq", None),
        P("dp"),
        P("seq", None),
        P("seq", None),
        P("seq", None),
        P("seq", None),
        P("seq", None),
        P("seq", None),
        P("seq"),
        P(None, "seq", None),
        P(None, "seq", None),
        P(None, None, "seq"),
        P("dp", "seq", None),
        P("dp", "seq", None),
    )
    return jax.shard_map(
        body,
        mesh=mesh,
        in_specs=placed,
        out_specs=(
            P("dp", "seq", None),
            P("dp", "seq", None),
            P("dp", "seq", None),
            P("seq", None),
            P("seq", None),
            P("seq", None),
            P("seq", None),
            P("seq", None),
            P("seq", None),
            P("seq"),
            P(None, "seq", None),
            P(None, "seq", None),
            P(None, None, "seq"),
        ),
        check_vma=False,
    )
```

```python
import collections
import functools
import jax
import jax.numpy as jnp
from jax import lax
from jax.experimental import pallas as pl
from jax.experimental.pallas import tpu as pltpu
from jax.sharding import PartitionSpec as P

HEADS = 12
HDIM = 64
VOCAB_CHAR = 1000
GROUP_CHARS = 250
HG = 384
EPSILON = 1e-05
MESH = pl.DeviceIdType.MESH
BF = jnp.bfloat16
F32 = jnp.float32
NCH = 8
UNROLL = 8
SHARE = (1, 2, 3, 6)
HB = HG // 128

def seq_dims(n):
    return {16: (4, 2, 2), 32: (8, 4, 1)}.get(n, (n, 1, 1))


Move = collections.namedtuple("Move", ("array", "axis", "rows", "lead", "route"))


def gather_kernel(dims, planes, moves, n_arrays, task, *refs):
    Z, Y, C = dims
    n = len(moves)
    n_in, n_out = (task.n_in, task.n_out) if task else (0, 0)
    src, task_in = refs[:n_arrays], refs[n_arrays : n_arrays + n_in]
    refs = refs[n_arrays + n_in :]
    dst, task_out = refs[:n_arrays], refs[n_arrays : n_arrays + n_out]
    own_sem, recv, zs, ds, ys, ss, xs, *task_scratch = refs[n_arrays + n_out :]
    dp = lax.axis_index("dp")
    me = lax.axis_index("seq")
    c = lax.rem(me, C)
    y = lax.rem(lax.div(me, C), Y)
    z = lax.div(me, C * Y)
    up_z, down_z = z < Z - 1, z > 0

    def at(zz, yy, cc):
        return (zz * Y + yy) * C + cc

    def to(zz, yy, cc):
        return (dp, at(zz, yy, cc))

    def view(i, slot):
        m = moves[i]
        s = pl.ds(pl.multiple_of(slot * m.rows, m.rows), m.rows)
        ref = dst[m.array]
        return ref.at[s] if m.axis == 0 else ref.at[:, s]

    def mine(i):
        m = moves[i]
        return src[m.array] if m.lead is None else src[m.array].at[m.lead]

    def copy(i, slot, send, where, own=False):
        return pltpu.make_async_remote_copy(
            src_ref=mine(i) if own else view(i, slot), dst_ref=view(i, slot),
            send_sem=send, recv_sem=recv.at[i, slot], device_id=where, device_id_type=MESH)

    sib = to(z, y, 1 - c) if C == 2 else None
    xp = (1 - dp, me)
    use_x = planes == 2 and any(m.route for m in moves)
    some = sib if C == 2 else to(z, y, c)

    def owner(i):
        return None if not (use_x and moves[i].route) else dp == moves[i].route - 1

    def when(cond, f):
        if cond is None:
            f()
        else:
            pl.when(cond)(f)

    def both(a, b):
        return b if a is None else jnp.logical_and(a, b)

    nseq = Z * Y * C
    if task:
        push_all, *task_out = task_out
        push, p_send, p_recv, i_sem, *task_scratch = task_scratch
        n_held = n_in - task.n_stay
        held, task_scratch = task_scratch[:n_held], task_scratch[n_held:]
        loads = [pltpu.make_async_copy(a, b, i_sem.at[k]) for k, (a, b) in enumerate(zip(task_in[:n_held], held))]
        for load in loads:
            load.start()
    bar = pltpu.get_barrier_semaphore()
    if task:
        peers = [(None, (dp, lax.rem(me + k, nseq))) for k in range(1, nseq)]
    else:
        peers = [(z > 0, to(z - 1, y, c)), (z < Z - 1, to(z + 1, y, c))]
        if Y > 1:
            peers += [(y > 0, to(z, y - 1, c)), (y < Y - 1, to(z, y + 1, c))]
        if C == 2:
            peers.append((None, sib))
    if use_x:
        peers.append((None, xp))
    count = 0
    for cond, where in peers:
        when(cond, functools.partial(pl.semaphore_signal, bar, inc=1, device_id=where, device_id_type=MESH))
        count = count + (1 if cond is None else cond.astype(jnp.int32))
    pl.semaphore_wait(bar, count)
    if task:

        def pushed(k, slot, where):
            return pltpu.make_async_remote_copy(
                src_ref=push, dst_ref=push_all.at[slot], send_sem=p_send.at[k], recv_sem=p_recv.at[slot], device_id=where, device_id_type=MESH)

        def push_one(k, _):
            pushed(k, me, (dp, lax.rem(me + k, nseq))).start()
            return 0

        def push_wait(k, _):
            other = lax.rem(me + k, nseq)
            pushed(k, other, (dp, other)).wait_recv()
            pushed(k, me, (dp, other)).wait_send()
            return 0

    def work(point):
        if task:
            task.run(point, me, push, push_all, tuple(held) + tuple(task_in[n_held:]), task_out, task_scratch)

    def go_z(i, slot, up, sem, own=False):
        where = to(z + 1, y, c) if up else to(z - 1, y, c)
        pl.when(up_z if up else down_z)(lambda: copy(i, slot, sem, where, own).start())

    def go_y(i, slot, up, sem, own=False):
        where = to(z, y + 1, c) if up else to(z, y - 1, c)
        pl.when(y < Y - 1 if up else y > 0)(lambda: copy(i, slot, sem, where, own).start())

    def go_core(i, slot, own=False):
        if C == 2:
            copy(i, slot, ss.at[i, slot], sib, own).start()

    def wait_in(i, slot):
        copy(i, slot, ss.at[i, slot], some).wait_recv()

    for i in range(n):
        pltpu.make_async_copy(mine(i), view(i, me), own_sem.at[i]).start()

        def own_sends(i=i):
            go_z(i, me, True, zs.at[i, me], True)
            go_z(i, me, False, ds.at[i, 0], True)
            if Y > 1:
                go_y(i, me, True, ys.at[i, me], True)
                go_y(i, me, False, ds.at[i, 1], True)

        when(owner(i), own_sends)
        go_core(i, me, True)

    def arrive_z(zz, up):
        slot = at(zz, y, c)

        def one(i):
            wait_in(i, slot)
            go_z(i, slot, up, zs.at[i, slot])
            if Y > 1:
                go_y(i, slot, True, ys.at[i, slot])
                go_y(i, slot, False, ys.at[i, slot] if Y == 2 else xs.at[i, slot])
            if use_x and moves[i].route:
                copy(i, slot, xs.at[i, slot], xp).start()
            go_core(i, slot)

        for i in range(n):
            when(owner(i), functools.partial(one, i))

    def arrive_y(zz, yy, up):
        slot = at(zz, yy, c)

        def one(i):
            wait_in(i, slot)
            if Y > 2:
                go_y(i, slot, up, ys.at[i, slot])
            if use_x and moves[i].route:
                copy(i, slot, xs.at[i, slot], xp).start()
            go_core(i, slot)

        for i in range(n):
            when(owner(i), functools.partial(one, i))

    def all_y(zz):
        for t in range(1, Y):
            pl.when(y - t >= 0)(lambda: arrive_y(zz, y - t, True))
            pl.when(y + t < Y)(lambda: arrive_y(zz, y + t, False))

    if task:
        for load in loads:
            load.wait()
        work(0)
        push_all[me] = push[...]
        lax.fori_loop(1, nseq, push_one, 0)
    def step(s, _):
        pl.when(z - s >= 0)(lambda: arrive_z(z - s, True))
        pl.when(z + s < Z)(lambda: arrive_z(z + s, False))
        q = s - 1
        pl.when(z - q >= 0)(lambda: all_y(z - q))
        pl.when(jnp.logical_and(q > 0, z + q < Z))(lambda: all_y(z + q))
        return 0

    if task:
        for s in (1, 2):
            if s < Z:
                step(s, 0)
            if s == 1:
                lax.fori_loop(1, nseq, push_wait, 0)
            work(s)
        lax.fori_loop(3, Z, step, 0)
        work(3)
    else:
        lax.fori_loop(1, Z, step, 0)
    q = Z - 1
    pl.when(z - q >= 0)(lambda: all_y(z - q))
    pl.when(z + q < Z)(lambda: all_y(z + q))

    if use_x:

        def far(k, _):
            slot = at(lax.rem(z + lax.div(k, Y), Z), lax.rem(y + lax.rem(k, Y), Y), c)

            def one(i):
                wait_in(i, slot)
                go_core(i, slot)

            for i in range(n):
                if moves[i].route:
                    pl.when(dp != moves[i].route - 1)(functools.partial(one, i))
            return 0

        lax.fori_loop(1, Z * Y, far, 0)

    def drain(k, _):
        zz, yy = lax.div(k, Y), lax.rem(k, Y)
        slot = at(zz, yy, c)
        is_own = slot == me
        own_y = yy == y
        fz = jnp.logical_or(jnp.logical_and(zz <= z, up_z), jnp.logical_and(zz > z, down_z))
        for i in range(n):
            o = owner(i)
            if C == 2:
                wait_in(i, at(zz, yy, 1 - c))
                copy(i, slot, ss.at[i, slot], some).wait_send()
            sent = lambda sem: copy(i, slot, sem, some).wait_send()
            pl.when(both(o, jnp.logical_and(own_y, fz)))(lambda: sent(zs.at[i, slot]))
            if Y == 2:
                pl.when(both(o, jnp.logical_and(own_y, jnp.logical_or(jnp.logical_not(is_own), y < Y - 1))))(lambda: sent(ys.at[i, slot]))
            elif Y > 2:
                fy = jnp.logical_or(jnp.logical_and(yy <= y, y < Y - 1), jnp.logical_and(yy > y, y > 0))
                pl.when(both(o, fy))(lambda: sent(ys.at[i, slot]))
                fy2 = jnp.logical_and(jnp.logical_and(own_y, y > 0), jnp.logical_not(is_own))
                pl.when(both(o, fy2))(lambda: sent(xs.at[i, slot]))
            if use_x and moves[i].route:
                pl.when(both(o, jnp.logical_not(is_own)))(lambda: sent(xs.at[i, slot]))
        return 0

    lax.fori_loop(0, Z * Y, drain, 0)
    for i in range(n):
        pltpu.make_async_copy(mine(i), view(i, me), own_sem.at[i]).wait()
        o = owner(i)
        pl.when(both(o, down_z))(lambda: copy(i, me, ds.at[i, 0], some, True).wait_send())
        if Y > 1:
            pl.when(both(o, y > 0))(lambda: copy(i, me, ds.at[i, 1], some, True).wait_send())


Task = collections.namedtuple("Task", ("n_in", "n_stay", "n_out", "run"))


def gather(arrays, cid, planes, nseq, task=None, inputs=(), outputs=(), scratch=()):
    dims = seq_dims(nseq)
    moves, shapes = [], []
    for k, (x, axis, route, lead) in enumerate(arrays):
        shape = list(x.shape if lead is None else x.shape[1:])
        moves.append(Move(k, axis, shape[axis], lead, route if planes == 2 and dims[1:] == (2, 2) else 0))
        shape[axis] *= nseq
        shapes.append(jax.ShapeDtypeStruct(tuple(shape), x.dtype))
    moves.sort(key=lambda m: not m.route)
    n = len(moves)
    D = pltpu.SemaphoreType.DMA
    scratch = [D((n,)), D((n, nseq)), D((n, nseq)), D((n, 2)), D((n, nseq)), D((n, nseq)), D((n, nseq))] + list(scratch)
    far, here = pl.BlockSpec(memory_space=pl.ANY), pl.BlockSpec(memory_space=pltpu.VMEM)
    return pl.pallas_call(
        functools.partial(gather_kernel, dims, planes, tuple(moves), len(arrays), task),
        out_shape=shapes + list(outputs),
        in_specs=[far] * (len(arrays) + len(inputs)),
        out_specs=[far] * len(arrays) + [here] * len(outputs),
        scratch_shapes=scratch,
        compiler_params=pltpu.CompilerParams(collective_id=cid, has_side_effects=True, vmem_limit_bytes=60 << 20),
    )(*[x for x, _, _, _ in arrays], *inputs)


def gather_with(run, arrays, cid, planes, nseq, inputs, stay, outputs, scratch):
    D = pltpu.SemaphoreType.DMA
    push = (8, HG)
    outputs = [jax.ShapeDtypeStruct((nseq,) + push, F32)] + outputs
    scratch = [pltpu.VMEM(push, F32), D((nseq,)), D((nseq,)), D((len(inputs),))] + [pltpu.VMEM(a.shape, a.dtype) for a in inputs] + scratch
    inputs = tuple(inputs) + tuple(stay)
    return gather(arrays, cid, planes, nseq, Task(len(inputs), len(stay), len(outputs), run), inputs, outputs, scratch)


def dot(a, b):
    return jnp.dot(a, b, preferred_element_type=F32)


def dot_t(a, b):
    return lax.dot_general(a, b, (((1,), (1,)), ((), ())), preferred_element_type=F32)


def wgrad(a, b):
    return lax.dot_general(a, b, (((0,), (0,)), ((), ())), preferred_element_type=F32)


def vmem(mib):
    return pltpu.CompilerParams(vmem_limit_bytes=mib << 20)


def layer_norm(values, gain_row, shift_row):
    center = values - jnp.mean(values, -1, keepdims=True)
    spread = jnp.mean(center * center, -1, keepdims=True)
    return center * lax.rsqrt(spread + EPSILON) * gain_row + shift_row


def fill(pre_ref, decay, drive=None):
    for k in range(2):
        for j in range(HB):
            at = 2 * k * HG + j * 128
            rate = jax.nn.sigmoid(pre_ref[:, at : at + 128])
            decay[k * HB + j] = 1.0 - rate
            if drive is not None:
                drive[k * HB + j] = rate * pre_ref[:, at + HG : at + HG + 128]


def row(x, i):
    return lax.slice_in_dim(x, i, i + 1, axis=0)


def cat(parts):
    return jnp.concatenate(parts, 1)


def blocks(x):
    return [x[:, j * 128 : (j + 1) * 128] for j in range(HB)]


def totals_kernel(pre_ref, tot_ref, chunk_ref, decay, drive):
    length = pre_ref.shape[0] // NCH
    fill(pre_ref, decay, drive)

    def step(t, carry):
        place = (pl.ds(t, NCH, stride=length), pl.ds(length - 1 - t, NCH, stride=length))
        out = []
        for i in range(2 * HB):
            c, h = carry[i]
            a = decay[i, place[i // HB], :]
            out.append((c * a, a * h + drive[i, place[i // HB], :]))
        return tuple(out)

    one, zero = jnp.ones((NCH, 128), F32), jnp.zeros((NCH, 128), F32)
    ends = lax.fori_loop(0, length, step, ((one, zero),) * (2 * HB), unroll=UNROLL)
    cf, hf = cat([e[0] for e in ends[:HB]]), cat([e[1] for e in ends[:HB]])
    cb, hb = cat([e[0] for e in ends[HB:]]), cat([e[1] for e in ends[HB:]])
    chunk_ref[0:NCH, :] = cf
    chunk_ref[NCH : 2 * NCH, :] = hf
    chunk_ref[2 * NCH : 3 * NCH, :] = cb
    chunk_ref[3 * NCH :, :] = hb
    one, zero = jnp.ones((1, HG), F32), jnp.zeros((1, HG), F32)
    tf, sf, tb, sb = one, zero, one, zero
    for k in range(NCH):
        sf, tf = row(cf, k) * sf + row(hf, k), tf * row(cf, k)
        j = NCH - 1 - k
        sb, tb = row(cb, j) * sb + row(hb, j), tb * row(cb, j)
    tot_ref[...] = jnp.concatenate([tf, sf, tb, sb], 0)


def states_work(me, q, seqs, all_ref, pre_all, chunk_all, ends_all, pooled_all, prev_all, decay, drive, state, prev):
    pre_ref, chunk_ref, ends_ref, pooled_ref, prev_ref = (
        r.at[pl.ds(q * (r.shape[0] // seqs), r.shape[0] // seqs)] for r in (pre_all, chunk_all, ends_all, pooled_all, prev_all)
    )
    chars = pre_all.shape[0] // seqs
    length = chars // NCH
    nseq = all_ref.shape[0]
    fill(pre_ref, decay, drive)
    ef = jnp.zeros((1, HG), F32)
    eb = ef
    for d in range(nseq):
        got = all_ref[d]
        ef = jnp.where(d < me, row(got, 4 * q) * ef + row(got, 4 * q + 1), ef)
        got = all_ref[nseq - 1 - d]
        eb = jnp.where(nseq - 1 - d > me, row(got, 4 * q + 2) * eb + row(got, 4 * q + 3), eb)
    cf, hf = chunk_ref[0:NCH, :], chunk_ref[NCH : 2 * NCH, :]
    cb, hb = chunk_ref[2 * NCH : 3 * NCH, :], chunk_ref[3 * NCH :, :]
    rows_f, rows_b = [], []
    for k in range(NCH):
        rows_f.append(ef)
        ef = row(cf, k) * ef + row(hf, k)
        j = NCH - 1 - k
        rows_b.append(eb)
        eb = row(cb, j) * eb + row(hb, j)

    def step(t, carry):
        place = (pl.ds(t, NCH, stride=length), pl.ds(length - 1 - t, NCH, stride=length))
        out = []
        for i in range(2 * HB):
            at = place[i // HB]
            prev[i, at, :] = carry[i]
            h = decay[i, at, :] * carry[i] + drive[i, at, :]
            state[i, at, :] = h
            out.append(h)
        return tuple(out)

    lax.fori_loop(0, length, step, tuple(blocks(jnp.concatenate(rows_f, 0)) + blocks(jnp.concatenate(rows_b[::-1], 0))), unroll=UNROLL)
    first = ends_ref[:, 0:1]
    last = ends_ref[:, 1:2]
    place = lax.broadcasted_iota(jnp.int32, (ends_all.shape[0] // seqs, chars), 1)
    member = jnp.where((place >= first) & (place < last), 1.0, 0.0).astype(BF)
    prev_ref[...] = cat([prev[i] for i in range(2 * HB)])
    pooled_ref[...] = dot(member, cat([state[i].astype(BF) for i in range(2 * HB)])) / (last - first).astype(F32)


def flows_kernel(pre_ref, dpool_ref, ends_ref, chunk_ref, ds_ref, tot_ref, gch_ref, decay, ds):
    chars = pre_ref.shape[0]
    length = chars // NCH
    fill(pre_ref, decay)
    first = ends_ref[0:1, :]
    last = ends_ref[1:2, :]
    place = lax.broadcasted_iota(jnp.int32, (chars, ends_ref.shape[1]), 0)
    inside = (place >= first) & (place < last)
    span = jnp.sum(jnp.where(inside, (last - first).astype(F32), 0.0), 1, keepdims=True)
    member = jnp.where(inside, 1.0, 0.0).astype(BF)
    spread = dot(member, dpool_ref[...]) / span
    ds_ref[...] = spread
    for i in range(2 * HB):
        ds[i] = spread[:, i * 128 : (i + 1) * 128]

    def step(t, carry):
        place = (pl.ds(length - 1 - t, NCH, stride=length), pl.ds(t, NCH, stride=length))
        return tuple(
            decay[i, place[i // HB], :] * (ds[i, place[i // HB], :] + carry[i]) for i in range(2 * HB)
        )

    ends = lax.fori_loop(0, length, step, (jnp.zeros((NCH, 128), F32),) * (2 * HB), unroll=UNROLL)
    gf, gb = cat(ends[:HB]), cat(ends[HB:])
    gch_ref[0:NCH, :] = gf
    gch_ref[NCH:, :] = gb
    cf, cb = chunk_ref[0:NCH, :], chunk_ref[2 * NCH : 3 * NCH, :]
    zero = jnp.zeros((1, HG), F32)
    tf, tb = zero, zero
    for k in range(NCH):
        j = NCH - 1 - k
        tf = row(cf, j) * tf + row(gf, j)
        tb = row(cb, k) * tb + row(gb, k)
    tot_ref[...] = jnp.concatenate([tf, tb, zero, zero], 0)


def dpre_work(me, q, seqs, gall_ref, all_ref, pre_all, ds_all, prev_all, chunk_all, gch_all, dpre_all, bias_all, decay, ds):
    pre_ref, ds_ref, prev_ref, chunk_ref, gch_ref, dpre_ref, bias_ref = (
        r.at[pl.ds(q * (r.shape[0] // seqs), r.shape[0] // seqs)] for r in (pre_all, ds_all, prev_all, chunk_all, gch_all, dpre_all, bias_all)
    )
    chars = pre_all.shape[0] // seqs
    length = chars // NCH
    nseq = all_ref.shape[0]
    fill(pre_ref, decay)
    for i in range(2 * HB):
        ds[i] = ds_ref[:, i * 128 : (i + 1) * 128]
    ef = jnp.zeros((1, HG), F32)
    eb = ef
    for d in range(nseq):
        j = nseq - 1 - d
        ef = jnp.where(j > me, row(all_ref[j], 4 * q) * ef + row(gall_ref[j], 4 * q), ef)
        eb = jnp.where(d < me, row(all_ref[d], 4 * q + 2) * eb + row(gall_ref[d], 4 * q + 1), eb)
    cf, cb = chunk_ref[0:NCH, :], chunk_ref[2 * NCH : 3 * NCH, :]
    gf, gb = gch_ref[0:NCH, :], gch_ref[NCH:, :]
    rows_f, rows_b = [], []
    for k in range(NCH):
        j = NCH - 1 - k
        rows_f.append(ef)
        ef = row(cf, j) * ef + row(gf, j)
        rows_b.append(eb)
        eb = row(cb, k) * eb + row(gb, k)

    def step(t, carry):
        place = (pl.ds(length - 1 - t, NCH, stride=length), pl.ds(t, NCH, stride=length))
        out = []
        for i in range(2 * HB):
            at = place[i // HB]
            g = ds[i, at, :] + carry[i]
            ds[i, at, :] = g
            out.append(decay[i, at, :] * g)
        return tuple(out)

    lax.fori_loop(0, length, step, tuple(blocks(jnp.concatenate(rows_f[::-1], 0)) + blocks(jnp.concatenate(rows_b, 0))), unroll=UNROLL)
    for i in range(2 * HB):
        k, j = i // HB, i % HB
        at = 2 * k * HG + j * 128
        g = ds[i]
        rate = jax.nn.sigmoid(pre_ref[:, at : at + 128])
        cand = pre_ref[:, at + HG : at + HG + 128]
        prev = prev_ref[:, i * 128 : (i + 1) * 128]
        dgate = (g * (cand - prev) * rate * decay[i]).astype(BF)
        dcand = (g * rate).astype(BF)
        for to, v in ((at, dgate), (at + HG, dcand)):
            dpre_ref[:, to : to + 128] = v
            bias_ref[:, to : to + 128] = jnp.broadcast_to(jnp.sum(v.astype(F32), 0, keepdims=True), (8, 128))


def part_of(ref, q, seqs):
    n = ref.shape[0] // seqs
    return ref.at[pl.ds(q * n, n)]


def forward_run(seqs, point, me, push, push_all, inputs, outputs, scratch):
    pre, ends = inputs
    pooled, prev, chunk = outputs
    if point == 0:
        for q in range(seqs):
            totals_kernel(part_of(pre, q, seqs), push.at[pl.ds(4 * q, 4)], part_of(chunk, q, seqs), *scratch[:2])
    elif point <= seqs:
        states_work(me, point - 1, seqs, push_all, pre, chunk, ends, pooled, prev, *scratch)


def backward_run(seqs, point, me, push, push_all, inputs, outputs, scratch):
    pre, prev, chunk, tot_all, dpool, ends, q_ref, dc_ref, col_ref, gru_ref, keys, values = inputs
    dpre, dbias, dq, demb = outputs
    ds_all, gch, decay, ds, kbuf, vbuf, k_sem, v_sem = scratch
    pairs = HEADS // 2
    steps = seqs * pairs

    def fetch(i):
        s, p = lax.div(i, pairs), lax.rem(i, pairs)
        cols = pl.ds(pl.multiple_of(p * 2 * HDIM, 2 * HDIM), 2 * HDIM)
        b = lax.rem(i, 2)
        return (pltpu.make_async_copy(keys.at[s, :, cols], kbuf.at[b], k_sem.at[b]), pltpu.make_async_copy(values.at[s, :, cols], vbuf.at[b], v_sem.at[b]))

    def one(i, _):
        s, p = lax.div(i, pairs), lax.rem(i, pairs)
        cols = pl.ds(pl.multiple_of(p * 2 * HDIM, 2 * HDIM), 2 * HDIM)
        b = lax.rem(i, 2)

        @pl.when(i + 1 < steps)
        def _():
            for c in fetch(i + 1):
                c.start()

        for c in fetch(i):
            c.wait()
        dq[s, :, cols] = query_grad(q_ref[s, :, cols], kbuf[b], vbuf[b], dc_ref[s, :, cols], col_ref[s, p])
        return 0

    if point == 0:
        for c in fetch(0):
            c.start()
        for q in range(seqs):
            flows_kernel(*(part_of(r, q, seqs) for r in (pre, dpool, ends, chunk, ds_all)), push.at[pl.ds(4 * q, 4)], part_of(gch, q, seqs), decay, ds)
    elif point <= seqs:
        dpre_work(me, point - 1, seqs, push_all, tot_all, pre, ds_all, prev, chunk, gch, dpre, dbias, decay, ds)
        part_of(demb, point - 1, seqs)[...] = dot_t(part_of(dpre, point - 1, seqs)[...], gru_ref[...]).astype(BF)
    bounds = (0,) + tuple(steps * k // 6 for k in SHARE)
    lax.fori_loop(bounds[point], bounds[point + 1], one, 0)


def pair_rows(x):
    lane = lax.broadcasted_iota(jnp.int32, x.shape, 1)
    zero = jnp.zeros_like(x)
    return jnp.concatenate([jnp.where(lane < HDIM, x, zero), jnp.where(lane >= HDIM, x, zero)], 0)


def pair_lanes(x):
    half = x.shape[0] // 2
    lane = lax.broadcasted_iota(jnp.int32, (half, x.shape[1]), 1)
    return jnp.where(lane < HDIM, x[:half], x[half:])


def attn_fwd_kernel(q_ref, k_ref, v_ref, ctx_ref, low_ref, lse_ref):
    toks = q_ref.shape[0]
    s = dot_t(pair_rows(q_ref[...] * (HDIM ** -0.5)), k_ref[...])
    top = jnp.max(s, 1, keepdims=True)
    p = jnp.exp(s - top)
    total = jnp.sum(p, 1, keepdims=True)
    o = pair_lanes(dot(p.astype(BF), v_ref[...]) / total)
    ctx_ref[...] = o
    low_ref[...] = o.astype(BF)
    lse = top + jnp.log(total)
    lse_ref[...] = jnp.concatenate([lse[:toks], lse[toks:]], 1)


def head_spec(rows, base=0):
    return pl.BlockSpec((None, rows, 2 * HDIM), lambda s, h: (s, 0, h + base))


def attention_fwd(qkv, keys, values):
    seqs, toks, _ = qkv.shape
    length = keys.shape[1]
    pairs = HEADS // 2
    return pl.pallas_call(
        attn_fwd_kernel,
        grid=(seqs, pairs),
        out_shape=[
            jax.ShapeDtypeStruct((seqs, toks, HEADS * HDIM), F32),
            jax.ShapeDtypeStruct((seqs, toks, HEADS * HDIM), BF),
            jax.ShapeDtypeStruct((seqs, pairs, toks, 2), F32),
        ],
        in_specs=[head_spec(toks), head_spec(length), head_spec(length)],
        out_specs=[head_spec(toks), head_spec(toks), pl.BlockSpec((None, None, toks, 2), lambda s, h: (s, h, 0, 0))],
        compiler_params=vmem(48),
    )(qkv, keys, values)


def query_grad(q, keys, values, dc, col):
    scale = HDIM ** -0.5
    lse = jnp.concatenate([col[:, 0:1], col[:, 1:2]], 0)
    delta = jnp.concatenate([col[:, 2:3], col[:, 3:4]], 0)
    p = jnp.exp(dot_t(pair_rows(q * scale), keys) - lse)
    ds = (p * (dot_t(pair_rows(dc), values) - delta)).astype(BF)
    return (pair_lanes(dot(ds, keys)) * scale).astype(BF)


def context_kernel(datt_ref, w_ref, ctx_ref, lse_ref, dctx_ref, col_ref, stat_ref):
    seqs, toks, _ = dctx_ref.shape
    pairs = HEADS // 2
    low = dot_t(datt_ref[...], w_ref[...]).astype(BF)
    prod = low.astype(F32) * ctx_ref[...]
    lane = lax.broadcasted_iota(jnp.int32, (toks, 2 * HDIM), 1)
    for s in range(seqs):
        dctx_ref[s] = low[s * toks : (s + 1) * toks]
        cols = []
        for p in range(pairs):
            x = prod[s * toks : (s + 1) * toks, p * 2 * HDIM : (p + 1) * 2 * HDIM]
            a = jnp.sum(jnp.where(lane < HDIM, x, 0.0), 1, keepdims=True)
            b = jnp.sum(jnp.where(lane >= HDIM, x, 0.0), 1, keepdims=True)
            col = jnp.concatenate([lse_ref[s, p], a, b], 1)
            col_ref[s, p] = col
            cols.append(col)
        flat = jnp.concatenate(cols + [jnp.zeros((toks, 128 - 4 * pairs), F32)], 1)
        stat_ref[s * 4 * pairs : (s + 1) * 4 * pairs, :] = flat.T[: 4 * pairs]


def attn_bwd_kernel(ko_ref, vo_ref, qa_ref, dca_ref, row_ref, dk_ref, dv_ref):
    toks = ko_ref.shape[0]
    scale = HDIM ** -0.5

    def spread(i):
        n = row_ref.shape[1]
        return jnp.concatenate(
            [jnp.broadcast_to(row_ref[i : i + 1, :], (toks, n)), jnp.broadcast_to(row_ref[i + 1 : i + 2, :], (toks, n))], 0
        )

    p = jnp.exp(dot_t(pair_rows(ko_ref[...] * scale), qa_ref[...]) - spread(0))
    dv_ref[...] = pair_lanes(dot(p.astype(BF), dca_ref[...])).astype(BF)
    dp = dot_t(pair_rows(vo_ref[...]), dca_ref[...])
    ds = (p * (dp - spread(2))).astype(BF)
    dk_ref[...] = (pair_lanes(dot(ds, qa_ref[...])) * scale).astype(BF)


def attention_bwd(qkv, queries, dctx_all, rows):
    seqs, toks, _ = qkv.shape
    length = queries.shape[1]
    pairs = HEADS // 2
    stat = lambda a, b: pl.BlockSpec((None, None, a, b), lambda s, h: (s, h, 0, 0))
    return pl.pallas_call(
        attn_bwd_kernel,
        grid=(seqs, pairs),
        out_shape=[jax.ShapeDtypeStruct((seqs, toks, HEADS * HDIM), BF)] * 2,
        in_specs=[head_spec(toks, pairs), head_spec(toks, 2 * pairs), head_spec(length), head_spec(length), stat(4, length)],
        out_specs=[head_spec(toks)] * 2,
        compiler_params=vmem(56),
    )(qkv, qkv, queries, dctx_all, rows)


GELU_A = 0.7978845608028654
GELU_B = 0.044715


def norm_both(v, gain, shift, dy):
    center = v - jnp.mean(v, -1, keepdims=True)
    inv = lax.rsqrt(jnp.mean(center * center, -1, keepdims=True) + EPSILON)
    hat = center * inv
    dhat = dy * gain
    dv = inv * (dhat - jnp.mean(dhat, -1, keepdims=True) - hat * jnp.mean(dhat * hat, -1, keepdims=True))
    return hat * gain + shift, dv, jnp.sum(dy * hat, 0, keepdims=True), jnp.sum(dy, 0, keepdims=True)


def norm_back(hat, inv, gain, dy):
    dhat = dy * gain
    dv = inv * (dhat - jnp.mean(dhat, -1, keepdims=True) - hat * jnp.mean(dhat * hat, -1, keepdims=True))
    return dv, jnp.sum(dy * hat, 0, keepdims=True), jnp.sum(dy, 0, keepdims=True)


def norm_parts(v):
    center = v - jnp.mean(v, -1, keepdims=True)
    inv = lax.rsqrt(jnp.mean(center * center, -1, keepdims=True) + EPSILON)
    return center * inv, inv


def gelu_parts(v):
    square = v * v
    curve = jnp.tanh(GELU_A * (v + GELU_B * v * square))
    return 0.5 * v * (1.0 + curve), 0.5 * (1.0 + curve) + 0.5 * v * (1.0 - curve * curve) * (GELU_A * (1.0 + 3.0 * GELU_B * square))


def middle_kernel(seqs, x_ref, clow_ref, ctx_ref, lse_ref, pooled_ref, gtok_ref, gchr_ref, nrm_ref, wo_hbm, wu_hbm, wd_hbm, ws_hbm, c0_hbm, c1_hbm, c2_hbm,
                  otok_ref, ochr_ref, nlow_ref, hid_ref, slow_ref, plow_ref, mprev_ref, merged_ref, mnext_ref, dmix_ref, dfus_ref, dlow_ref, drai_ref, datt_ref,
                  din_ref, dpool_ref, dnorm_ref, dctx_ref, col_ref, stat_ref,
                  wo_ref, wu_ref, wd_ref, ws_ref, taps, acc, edge, before, after, dside, dchar, slope_ref, hat0, hat1, state_ref, dstate_ref,
                  w_sem, e_send, b_recv, a_recv):
    me = lax.axis_index("seq")
    dp = lax.axis_index("dp")
    n = lax.axis_size("seq")
    rows, width = x_ref.shape
    toks = rows // seqs
    wide = 2 * width
    loads = [
        pltpu.make_async_copy(src, dst, w_sem.at[k]) for k, (src, dst) in enumerate((
            (wo_hbm, wo_ref), (wu_hbm, wu_ref), (wd_hbm, wd_ref), (ws_hbm, ws_ref), (c1_hbm, taps.at[1]), (c0_hbm, taps.at[0]), (c2_hbm, taps.at[2]),
        ))
    ]
    for load in loads:
        load.start()
    edge[...] = jnp.zeros_like(edge)
    right, left = (dp, me + 1), (dp, me - 1)
    has_l, has_r = me > 0, me < n - 1
    bar = pltpu.get_barrier_semaphore()
    pl.when(has_l)(lambda: pl.semaphore_signal(bar, inc=1, device_id=left, device_id_type=MESH))
    pl.when(has_r)(lambda: pl.semaphore_signal(bar, inc=1, device_id=right, device_id_type=MESH))
    pl.semaphore_wait(bar, has_l.astype(jnp.int32) + has_r.astype(jnp.int32))

    def send(k):
        def to_right():
            return pltpu.make_async_remote_copy(
                src_ref=edge.at[k, 0], dst_ref=before.at[k], send_sem=e_send.at[k, 0], recv_sem=b_recv.at[k], device_id=right, device_id_type=MESH)

        def to_left():
            return pltpu.make_async_remote_copy(
                src_ref=edge.at[k, 1], dst_ref=after.at[k], send_sem=e_send.at[k, 1], recv_sem=a_recv.at[k], device_id=left, device_id_type=MESH)

        return to_right, to_left

    def start(k, ref):
        for s in range(seqs):
            edge[k, 0, s : s + 1, :] = ref[(s + 1) * toks - 16 : (s + 1) * toks, :].astype(F32)[15:16]
            edge[k, 1, s : s + 1, :] = ref[s * toks : s * toks + 16, :].astype(F32)[0:1]
        to_right, to_left = send(k)
        pl.when(has_r)(lambda: to_right().start())
        pl.when(has_l)(lambda: to_left().start())

    def finish(k):
        to_right, to_left = send(k)
        pl.when(has_r)(lambda: to_left().wait_recv())
        pl.when(has_l)(lambda: to_right().wait_recv())
        pl.when(has_r)(lambda: to_right().wait_send())
        pl.when(has_l)(lambda: to_left().wait_send())

    def shifts(k, ref, prev_ref, next_ref):
        for j in range(0, wide, 512):
            x = ref[:, j : j + 512].astype(F32)
            at = lax.broadcasted_iota(jnp.int32, x.shape, 0)
            prev, follow = pltpu.roll(x, 1, 0), pltpu.roll(x, rows - 1, 0)
            for s in range(seqs):
                b = jnp.where(has_l, before[k, s : s + 1, j : j + 512], 0.0)
                a = jnp.where(has_r, after[k, s : s + 1, j : j + 512], 0.0)
                prev = jnp.where(at == s * toks, b, prev)
                follow = jnp.where(at == (s + 1) * toks - 1, a, follow)
            prev_ref[:, j : j + 512] = prev.astype(BF)
            next_ref[:, j : j + 512] = follow.astype(BF)

    chunk = 768
    loads[0].wait()
    hat, inv0 = norm_parts(x_ref[...].astype(F32) + dot(clow_ref[...], wo_ref[...]))
    hat0[...] = hat
    normed = hat * nrm_ref[0:1, :] + nrm_ref[1:2, :]
    nlow_ref[...] = normed.astype(BF)
    loads[1].wait()

    def raise_part(j, _):
        cols = pl.ds(pl.multiple_of(j * chunk, chunk), chunk)
        hidden, slope = gelu_parts(dot(nlow_ref[...], wu_ref[:, cols]))
        hid_ref[:, cols] = hidden.astype(BF)
        slope_ref[:, cols] = slope
        return 0

    lax.fori_loop(0, 4 * width // chunk, raise_part, 0)
    loads[2].wait()
    hat, inv1 = norm_parts(normed + dot(hid_ref[...], wd_ref[...]))
    hat1[...] = hat
    state = hat * nrm_ref[2:3, :] + nrm_ref[3:4, :]
    state_ref[...] = state
    loads[3].wait()
    slow = state.astype(BF)
    plow = pooled_ref[...].astype(BF)
    slow_ref[...] = slow
    plow_ref[...] = plow
    merged_ref[:, :width] = dot(slow, ws_ref[0]).astype(BF)
    merged_ref[:, width:] = dot(plow, ws_ref[1]).astype(BF)
    start(0, merged_ref)
    loads[4].wait()

    def centre(j, _):
        cols = pl.ds(pl.multiple_of(j * 512, 512), 512)
        acc[:, cols] = dot(merged_ref[...], taps[1, :, cols])
        return 0

    lax.fori_loop(0, wide // 512, centre, 0)
    finish(0)
    shifts(0, merged_ref, mprev_ref, mnext_ref)
    loads[5].wait()
    loads[6].wait()

    def sides(j, _):
        cols = pl.ds(pl.multiple_of(j * 512, 512), 512)
        acc[:, cols] += dot(mprev_ref[...], taps[0, :, cols]) + dot(mnext_ref[...], taps[2, :, cols])
        return 0

    lax.fori_loop(0, wide // 512, sides, 0)
    for part, (base_ref, grad_ref, out_ref) in enumerate(((state_ref, gtok_ref, otok_ref), (pooled_ref, gchr_ref, ochr_ref))):
        mixed = acc[:, part * width : (part + 1) * width]
        gated, slope = gelu_parts(mixed)
        r = 4 + 2 * part
        out, dsum, dgain, dshift = norm_both(base_ref[...] + gated, nrm_ref[r : r + 1, :], nrm_ref[r + 1 : r + 2, :], grad_ref[...].astype(F32))
        out_ref[...] = out.astype(BF)
        dnorm_ref[r : r + 1, :] = dgain
        dnorm_ref[r + 1 : r + 2, :] = dshift
        dmix_ref[:, part * width : (part + 1) * width] = (dsum * slope).astype(BF)
        if part == 0:
            dstate_ref[...] = dsum
        else:
            dchar[...] = dsum
    start(1, dmix_ref)

    def centre_back(j, _):
        cols = pl.ds(pl.multiple_of(j * 512, 512), 512)
        acc[:, cols] = dot_t(dmix_ref[...], taps[1, cols, :])
        return 0

    lax.fori_loop(0, wide // 512, centre_back, 0)
    finish(1)
    shifts(1, dmix_ref, dside.at[0], dside.at[1])

    def sides_back(j, _):
        cols = pl.ds(pl.multiple_of(j * 512, 512), 512)
        dfus_ref[:, cols] = (acc[:, cols] + dot_t(dside[1], taps[0, cols, :]) + dot_t(dside[0], taps[2, cols, :])).astype(BF)
        return 0

    lax.fori_loop(0, wide // 512, sides_back, 0)
    dpool_ref[...] = (dchar[...] + dot_t(dfus_ref[:, width:], ws_ref[1])).astype(BF)
    dstate = dstate_ref[...] + dot_t(dfus_ref[:, :width], ws_ref[0])
    dsum, dnorm_ref[2:3, :], dnorm_ref[3:4, :] = norm_back(hat1[...], inv1, nrm_ref[2:3, :], dstate)
    dlow_ref[...] = dsum.astype(BF)
    dstate_ref[...] = dsum

    def lower_part(j, _):
        cols = pl.ds(pl.multiple_of(j * chunk, chunk), chunk)
        drai_ref[:, cols] = (dot_t(dlow_ref[...], wd_ref[cols, :]) * slope_ref[:, cols]).astype(BF)
        return 0

    lax.fori_loop(0, 4 * width // chunk, lower_part, 0)
    dsum, dnorm_ref[0:1, :], dnorm_ref[1:2, :] = norm_back(hat0[...], inv0, nrm_ref[0:1, :], dstate_ref[...] + dot_t(drai_ref[...], wu_ref[...]))
    din_ref[...] = dsum
    datt_ref[...] = dsum.astype(BF)
    context_kernel(datt_ref, wo_ref, ctx_ref, lse_ref, dctx_ref, col_ref, stat_ref)


def middle(seqs, x, clow, context, lse, pooled, grad_token, grad_char, nrm, w_out, w_up, w_down, w_stream, w_conv, cid):
    rows, width = x.shape
    wide, ff = 2 * width, 4 * width
    pairs, toks = lse.shape[1:3]
    here = pl.BlockSpec(memory_space=pltpu.VMEM)
    far = pl.BlockSpec(memory_space=pl.ANY)
    low, full = (lambda c: jax.ShapeDtypeStruct((rows, c), BF)), jax.ShapeDtypeStruct((rows, width), F32)
    D = pltpu.SemaphoreType.DMA
    f = lambda *s: pltpu.VMEM(s, F32)
    v = lambda *s: pltpu.VMEM(s, BF)
    return pl.pallas_call(
        functools.partial(middle_kernel, seqs),
        out_shape=[low(width)] * 3 + [low(ff), low(width), low(width)] + [low(wide)] * 5 + [low(width), low(ff), low(width), full, low(width)] + [
            jax.ShapeDtypeStruct((8, width), F32), jax.ShapeDtypeStruct((seqs, toks, width), BF), jax.ShapeDtypeStruct((seqs, pairs, toks, 4), F32),
            jax.ShapeDtypeStruct((seqs * pairs * 4, toks), F32),
        ],
        in_specs=[here] * 8 + [far] * 7,
        out_specs=[here] * 20,
        scratch_shapes=[
            v(*w_out.shape), v(*w_up.shape), v(*w_down.shape), v(*w_stream.shape), v(3, wide, wide), f(rows, wide), f(2, 2, 8, wide),
            f(2, 8, wide), f(2, 8, wide), v(2, rows, wide), f(rows, width), f(rows, ff), f(rows, width), f(rows, width), f(rows, width), f(rows, width),
            D((7,)), D((2, 2)), D((2,)), D((2,)),
        ],
        compiler_params=pltpu.CompilerParams(collective_id=cid, has_side_effects=True, vmem_limit_bytes=62 << 20),
    )(x, clow, context, lse, pooled, grad_token, grad_char, nrm, w_out, w_up, w_down, w_stream, *w_conv)


RZ, RY, RC = 4, 2, 2
PW = 384
PR = 48
LD, LX, LY, LH, LF = 2, 8, 12, 3, 25
HRING = LY + 1
PER, PK = 11, 3
JOB = 6


Group = collections.namedtuple("Group", ("left", "parts", "right", "col", "cols", "out", "lead", "base", "at"))
GRU, TABLE, TINY = 5, 4, 8


def piece_groups(taps):
    rows = [(6 + k, 2, 5, 0, 4, 7, i, 0) for i, k in enumerate(taps)]
    rows += [(4, 1, 4, 0, 2, 6, 0, 0), (5, 1, 4, 768, 2, 6, 1, 0), (3, 4, 3, 0, 2, 3, None, 0), (2, 1, 2, 0, 8, 2, None, 0), (1, 1, 1, 0, 2, 1, None, 0),
             (0, 1, 0, 0, 2, 0, None, 0), (0, 1, 6, 0, 4, 0, None, 2)]
    out, at = [], 0
    for r in rows:
        out.append(Group(*r, at))
        at += r[1] * r[4]
    return tuple(out), at


MISC = (((GRU, 0), (GRU, 1), (GRU, 2)), ((GRU, 3), (TABLE, 0), (TABLE, 1)), ((TABLE, 2), (TINY, 0), (None, 0)))


def reduce_kernel(npieces, groups, *refs):
    out_ref, dkv_ref = refs[24:26]
    width = refs[0].shape[1]
    dk_ref, dv_ref = dkv_ref.at[:, pl.ds(0, width)], dkv_ref.at[:, pl.ds(width, width)]
    lhs, rhs = refs[:9], refs[9:15] + (dkv_ref,)
    emb_ref, dpre_ref, demb_ref, ids_ref, tiny_ref, kv_ref, stat_ref, qa_ref, dca_ref = refs[15:24]
    (lt, part, r0, held, r1, r2, up, dn, fin, fx,
     d_send, d_recv, x_send, x_recv, y_send, y_recv, u_send, u_recv, n_send, n_recv, f_send, f_recv, qbuf, cbuf, dk_acc, dv_acc, q_sem, c_sem) = refs[26:]
    dp = lax.axis_index("dp")
    me = lax.axis_index("seq")
    c = lax.rem(me, RC)
    y = lax.rem(lax.div(me, RC), RY)
    z = lax.div(me, RC * RY)

    def to(zz, yy, cc):
        return (dp, (zz * RY + yy) * RC + cc)

    sib, ynb, zup, zdn, xnb = to(z, y, 1 - c), to(z, 1 - y, c), to(z + 1, y, c), to(z - 1, y, c), (1 - dp, me)
    bar = pltpu.get_barrier_semaphore()
    for where in (sib, ynb, xnb):
        pl.semaphore_signal(bar, inc=1, device_id=where, device_id_type=MESH)
    pl.when(z > 0)(lambda: pl.semaphore_signal(bar, inc=1, device_id=zdn, device_id_type=MESH))
    pl.when(z < RZ - 1)(lambda: pl.semaphore_signal(bar, inc=1, device_id=zup, device_id_type=MESH))
    pl.semaphore_wait(bar, 3 + (z > 0).astype(jnp.int32) + (z < RZ - 1).astype(jnp.int32))

    def copy(src, dst, send, recv, where):
        return pltpu.make_async_remote_copy(src_ref=src, dst_ref=dst, send_sem=send, recv_sem=recv, device_id=where, device_id_type=MESH)

    def d2d(t):
        b, k = lax.rem(t, LD + 1), lax.rem(t, 2 * LD)
        return copy(part.at[b, :, :, 1 - c], r0.at[k], d_send.at[b], d_recv.at[k], sib)

    def far(t):
        return lax.div(t, PER) * PK + lax.div(lax.rem(t, PER), 3)

    def mi(t):
        m = lax.rem(t, PER)
        return lax.div(t, PER) * (PER - PK) + m - jnp.minimum(lax.div(m + dp, 3), PK)

    def across(t):
        return copy(held.at[lax.rem(t, HRING)], r1.at[far(t)], x_send.at[t], x_recv.at[t], xnb)

    def along_y(t):
        return copy(held.at[lax.rem(t, HRING), :, 1 - y], r2.at[mi(t)], y_send.at[t], y_recv.at[t], ynb)

    def final(t):
        return copy(fin.at[t], fx.at[t], f_send.at[t], f_recv.at[t], xnb)

    def go_up(t, k):
        src = r2.at[mi(t), pl.ds(k + 1, RZ - 1 - k)] if k == 0 else up.at[mi(t), pl.ds(k, RZ - 1 - k)]
        return copy(src, up.at[mi(t), pl.ds(k, RZ - 1 - k)], u_send.at[t], u_recv.at[t], zup)

    def from_below(t, k):
        ref = up.at[mi(t), pl.ds(k - 1, RZ - k)]
        return copy(ref, ref, u_send.at[t], u_recv.at[t], zdn)

    def go_down(t, k):
        src = r2.at[mi(t), pl.ds(0, k)] if k == RZ - 1 else dn.at[mi(t), pl.ds(0, k)]
        return copy(src, dn.at[mi(t), pl.ds(0, k)], n_send.at[t], n_recv.at[t], zdn)

    def from_above(t, k):
        ref = dn.at[mi(t), pl.ds(0, k + 1)]
        return copy(ref, ref, n_send.at[t], n_recv.at[t], zup)

    def add(a, b):
        return (a.astype(F32) + b.astype(F32)).astype(BF)

    def live(t):
        return jnp.logical_and(t >= 0, t < npieces)

    def route(t):
        m = lax.rem(t, PER)
        return jnp.where(m < 3 * PK, lax.rem(m, 3), 0)

    def mine(t):
        r = route(t)
        return jnp.logical_or(r == 0, r - 1 == dp)

    def finish(t):
        r = route(t)

        @pl.when(r == 0)
        def _():
            final(t).wait_recv()
            out_ref[t] = add(fin[t], fx[t])

        @pl.when(jnp.logical_and(r > 0, r - 1 == dp))
        def _():
            out_ref[t] = fin[t]

        @pl.when(jnp.logical_and(r > 0, r - 1 != dp))
        def _():
            final(t).wait_recv()
            out_ref[t] = fx[t]

        pl.when(mine(t))(lambda: final(t).wait_send())

    def sum_up(t):
        i = mi(t)
        for k in range(RZ):
            @pl.when(z == k)
            def _(k=k):
                if k > 0:
                    from_below(t, k).wait_recv()
                    for q in range(k + 1, RZ):
                        up[i, q - 1] = add(up[i, q - 1], r2[i, q])
                if k < RZ - 1:
                    go_up(t, k).start()

    def sum_down(t):
        i = mi(t)
        for k in range(RZ):
            @pl.when(z == k)
            def _(k=k):
                if k < RZ - 1:
                    from_above(t, k).wait_recv()
                    for q in range(k):
                        dn[i, q] = add(dn[i, q], r2[i, q])
                if k > 0:
                    go_down(t, k).start()

    def close(t):
        i = mi(t)
        for k in range(RZ):
            @pl.when(z == k)
            def _(k=k):
                total = r2[i, k].astype(F32)
                if k > 0:
                    total = total + up[i, k - 1].astype(F32)
                    go_down(t, k).wait_send()
                if k < RZ - 1:
                    total = total + dn[i, k].astype(F32)
                    go_up(t, k).wait_send()
                fin[t] = total.astype(BF)
        final(t).start()

    def join_y(t):
        i = mi(t)
        along_y(t).wait_recv()
        along_y(t).wait_send()
        h = lax.rem(t, HRING)
        for q in range(RZ):
            r2[i, q] = add(r2[i, q], held[h, q, y])

    def join_x(t):
        h = lax.rem(t, HRING)
        across(t).wait_recv()
        for q in range(RZ):
            held[h, q] = add(held[h, q], r1[far(t), q])
        along_y(t).start()

    def join_core(t):
        b, k = lax.rem(t, LD + 1), lax.rem(t, 2 * LD)
        h = lax.rem(t, HRING)
        d2d(t).wait_recv()
        d2d(t).wait_send()
        for q in range(RZ):
            held[h, q] = add(part[b, q, :, c], r0[k, q])
        pl.when(route(t) == 0)(lambda: along_y(t).start())
        pl.when(jnp.logical_not(mine(t)))(lambda: across(t).start())

    def turn(ref):
        n = ref.shape[0]
        for k in range(0, ref.shape[1], 384):
            lt[k // PR : k // PR + 8, :, :n] = ref[:, k : k + 384].T.reshape(8, PR, n)

    def make(t):
        b = lax.rem(t, LD + 1)
        for g in groups:
            @pl.when(jnp.logical_and(t >= g.at, t < g.at + g.parts * g.cols))
            def _(g=g):
                i = t - g.at
                j, cb = lax.div(i, g.cols), lax.rem(i, g.cols)
                pl.when(i == 0)(lambda: turn(lhs[g.left]))
                right = rhs[g.right][:, pl.ds(pl.multiple_of(g.col + cb * PW, PW), PW)]
                for q in range(RZ // 2):
                    left = jnp.concatenate([lt[(8 * q + s) * g.parts + j] for s in range(8)], 0)
                    part[b, 2 * q : 2 * q + 2] = dot(left, right).astype(BF).reshape(2, RY, RC, PR, PW)
        for m, trio in enumerate(MISC):
            @pl.when(t == npieces - len(MISC) + m)
            def _(trio=trio):
                for i, (kind, cb) in enumerate(trio):
                    if kind == GRU:
                        val = wgrad(emb_ref[...], dpre_ref[:, cb * PW : (cb + 1) * PW]).astype(BF).reshape(RZ, RY, RC, 16, PW)
                    elif kind == TABLE:
                        unit = lax.broadcasted_iota(jnp.int32, (ids_ref.shape[0], PW), 1) + cb * PW
                        hot = jnp.where(unit == ids_ref[...], 1.0, 0.0).astype(BF)
                        val = wgrad(demb_ref[...], hot).astype(BF).reshape(RZ, RY, RC, 16, PW)
                    elif kind == TINY:
                        val = tiny_ref[...].reshape(RZ, RY, RC, 16, PW)
                    else:
                        val = jnp.zeros((RZ, RY, RC, 16, PW), BF)
                    part[b, :, :, :, 16 * i : 16 * i + 16, :] = val
        d2d(t).start()

    pairs = HEADS // 2
    toks = kv_ref.shape[1]
    half = qa_ref.shape[1] // 2
    jobs = 2 * pairs * kv_ref.shape[0]

    def fetch(i):
        s, p, h = lax.div(i, 2 * pairs), lax.rem(lax.div(i, 2), pairs), lax.rem(i, 2)
        cols = pl.ds(pl.multiple_of(p * 2 * HDIM, 2 * HDIM), 2 * HDIM)
        part = pl.ds(pl.multiple_of(h * half, half), half)
        return (pltpu.make_async_copy(qa_ref.at[s, part, cols], qbuf.at[h], q_sem.at[h]), pltpu.make_async_copy(dca_ref.at[s, part, cols], cbuf.at[h], c_sem.at[h]))

    def key_work(i):
        s, p, h = lax.div(i, 2 * pairs), lax.rem(lax.div(i, 2), pairs), lax.rem(i, 2)
        at = pl.multiple_of(p * 2 * HDIM, 2 * HDIM)
        slots = half // toks

        @pl.when(i + 1 < jobs)
        def _():
            for load in fetch(i + 1):
                load.start()

        for load in fetch(i):
            load.wait()
        scale = HDIM ** -0.5
        queries, dctx = qbuf[h], cbuf[h]

        def spread(k):
            at = (s * pairs + p) * 4 + k
            one = lambda r: jnp.concatenate([stat_ref[h * slots + d, pl.ds(r, 1), :] for d in range(slots)], 1)
            return jnp.concatenate([jnp.broadcast_to(one(at), (toks, half)), jnp.broadcast_to(one(at + 1), (toks, half))], 0)

        prob = jnp.exp(dot_t(pair_rows(kv_ref[s, :, pl.ds(at, 2 * HDIM)] * scale), queries) - spread(0))
        dv = dot(prob.astype(BF), dctx)
        dprob = dot_t(pair_rows(kv_ref[s, :, pl.ds(at + pairs * 2 * HDIM, 2 * HDIM)]), dctx)
        dk = dot((prob * (dprob - spread(2))).astype(BF), queries)

        @pl.when(h == 0)
        def _():
            dk_acc[...] = dk
            dv_acc[...] = dv

        @pl.when(h == 1)
        def _():
            rows = pl.ds(pl.multiple_of(s * toks, toks), toks)
            cols = pl.ds(at, 2 * HDIM)
            dk_ref[rows, cols] = (pair_lanes(dk_acc[...] + dk) * scale).astype(BF)
            dv_ref[rows, cols] = pair_lanes(dv_acc[...] + dv).astype(BF)

    for load in fetch(0):
        load.start()

    def tick(T, _):
        def do(t, f, cond=None):
            ok = live(t)
            pl.when(ok if cond is None else jnp.logical_and(ok, cond(t)))(lambda: f(t))

        do(T - LF, finish)
        do(T - LY - z * LH, sum_up, mine)
        do(T - LY - (RZ - 1 - z) * LH, sum_down, mine)
        do(T - LY - (RZ - 1) * LH, close, mine)
        do(T - LY + 1, join_y, mine)
        do(T - LX, join_x, lambda t: jnp.logical_and(route(t) > 0, mine(t)))
        do(T - LX, lambda t: across(t).wait_send(), lambda t: jnp.logical_not(mine(t)))
        do(T - LD, join_core)
        do(T, make)
        job = T - JOB
        pl.when(jnp.logical_and(job >= 0, job < jobs))(lambda: key_work(job))
        return 0

    lax.fori_loop(0, npieces + LF + 1, tick, 0)


def finish_kernel(groups, pieces, dq, dkv, w, base, *outs):
    for g in groups:
        for j in range(g.parts):
            for cb in range(g.cols):
                rows, cols = slice(j * PR, (j + 1) * PR), slice((g.base + cb) * PW, (g.base + cb + 1) * PW)
                val = pieces[g.at + j * g.cols + cb].astype(F32)
                if g.lead is None:
                    outs[g.out][rows, cols] = val
                else:
                    outs[g.out][g.lead, rows, cols] = val
    first = groups[-1].at + groups[-1].parts * groups[-1].cols
    bias, norms, dinput = outs[8:]
    for m, trio in enumerate(MISC):
        for i, (kind, cb) in enumerate(trio):
            val = pieces[first + m, 16 * i : 16 * i + 16, :].astype(F32)
            if kind == TINY:
                bias[...] = val[0:1, : bias.shape[1]]
                for k in range(4):
                    norms[k] = val[1 + 2 * k : 3 + 2 * k, : norms.shape[2]]
            elif kind is not None:
                n = min(PW, outs[kind].shape[1] - cb * PW)
                outs[kind][:, cb * PW : cb * PW + n] = val[:, :n]
    n = dq.shape[1]
    dinput[...] = base[...] + dot_t(dq[...], w[:, :n]) + dot_t(dkv[:, :n], w[:, n : 2 * n]) + dot_t(dkv[:, n:], w[:, 2 * n :])


def reduce_all(lhs, rhs, emb, dpre, demb, ids, kv, stat, queries, dctx, w_qkv, dsum, g_bias, g_norms, n_table, nseq, cid, taps=(0, 1, 2)):
    width = lhs[0].shape[1]
    per = g_bias.shape[0] // nseq
    tiny = jnp.concatenate([
        jnp.pad(g_bias.reshape(nseq, 1, per), ((0, 0), (0, 0), (0, PW - per))),
        jnp.pad(g_norms.reshape(8, nseq, -1).transpose(1, 0, 2), ((0, 0), (0, 7), (0, PW - width // nseq))),
    ], 1).astype(BF)
    groups, npieces = piece_groups(taps)
    npieces += len(MISC)
    dense = -(-npieces // PER) * (PER - PK)
    D = pltpu.SemaphoreType.DMA
    v = lambda *s: pltpu.VMEM(s, BF)
    spec = pl.BlockSpec(memory_space=pltpu.VMEM)
    pieces, dkv = pl.pallas_call(
        functools.partial(reduce_kernel, npieces, groups),
        out_shape=[jax.ShapeDtypeStruct((npieces, PR, PW), BF), jax.ShapeDtypeStruct((lhs[0].shape[0], 2 * width), BF)],
        in_specs=[spec] * 22 + [pl.BlockSpec(memory_space=pl.ANY)] * 2,
        out_specs=[spec] * 2,
        scratch_shapes=[
            v(64, PR, lhs[0].shape[0]),
            v(LD + 1, RZ, RY, RC, PR, PW), v(2 * LD, RZ, RY, PR, PW), v(HRING, RZ, RY, PR, PW), v(PK * (npieces // PER + 1), RZ, RY, PR, PW),
            v(dense, RZ, PR, PW), v(dense, RZ - 1, PR, PW), v(dense, RZ - 1, PR, PW), v(npieces, PR, PW), v(npieces, PR, PW),
            D((LD + 1,)), D((2 * LD,)), D((npieces,)), D((npieces,)), D((npieces,)), D((npieces,)),
            D((npieces,)), D((npieces,)), D((npieces,)), D((npieces,)), D((npieces,)), D((npieces,)),
            v(2, queries.shape[1] // 2, 2 * HDIM), v(2, queries.shape[1] // 2, 2 * HDIM),
            pltpu.VMEM((2 * kv.shape[1], 2 * HDIM), F32), pltpu.VMEM((2 * kv.shape[1], 2 * HDIM), F32), D((2,)), D((2,)),
        ],
        compiler_params=pltpu.CompilerParams(collective_id=cid, has_side_effects=True, vmem_limit_bytes=62 << 20),
    )(*lhs, *rhs, emb, dpre, demb, ids, tiny, kv, stat, queries, dctx)
    f = lambda *s: jax.ShapeDtypeStruct(s, F32)
    wide = 2 * width
    share = width // nseq
    return pl.pallas_call(
        functools.partial(finish_kernel, groups),
        out_shape=[
            f(share, 3 * width), f(share, width), f(share, 4 * width), f(4 * share, width), f(16, n_table), f(16, 4 * PW),
            f(2, share, width), f(3, 2 * share, wide), f(1, per), f(4, 2, share), f(*dsum.shape),
        ],
        in_specs=[spec] * 5,
        out_specs=[spec] * 11,
        compiler_params=vmem(40),
    )(pieces, rhs[0], dkv, w_qkv, dsum)


def scatter(total, axis):
    part = lax.psum_scatter(total, "seq", scatter_dimension=axis, tiled=True)
    return lax.psum(part, "dp").astype(F32)


def body(tokens, char_ids, span_lengths, script_group, w_qkv, w_out, w_up, w_down, char_table, w_gru, gru_bias, w_stream, w_conv, norms, grad_token, grad_char):
    nseq, planes = lax.axis_size("seq"), lax.axis_size("dp")
    seqs, toks, width = tokens.shape
    chars = char_ids.shape[1]
    rows = seqs * toks
    bias_n, norm_n = gru_bias.shape[0], norms.shape[2]
    small = jnp.concatenate([gru_bias, norms.reshape(-1)])
    small = jnp.pad(small, (0, 2048 - small.shape[0])).reshape(16, 128)
    conv0, w_down, conv1, conv2, w_out, w_stream, w_qkv, w_gru, char_table, small = gather(
        [(w_conv, 0, 1, 0), (w_down, 0, 1, None), (w_conv, 0, 2, 1), (w_conv, 0, 2, 2), (w_out, 0, 0, None), (w_stream, 1, 0, None), (w_qkv, 0, 0, None),
         (w_gru, 0, 0, None), (char_table, 0, 0, None), (small, 0, 0, None)], 1, planes, nseq
    )
    w_up, small = lax.optimization_barrier((w_up, small))
    w_up = lax.all_gather(w_up, "seq", axis=0, tiled=True)
    w_conv = (conv0, conv1, conv2)
    small = small.reshape(nseq, 2048)
    bias = small[:, :bias_n].reshape(-1).astype(F32)
    nrm = small[:, bias_n : bias_n + 8 * norm_n].reshape(nseq, 4, 2, norm_n).transpose(1, 2, 0, 3).reshape(4, 2, width).astype(F32)

    x_low = tokens.reshape(rows, width)
    qkv = dot(x_low, w_qkv).astype(BF)
    qkv3 = qkv.reshape(seqs, toks, 3 * width)

    char_rows = (char_ids + script_group[:, None] * GROUP_CHARS).reshape(seqs * chars, 1)
    onehot = (char_rows == jnp.arange(VOCAB_CHAR, dtype=jnp.int32)).astype(BF)
    embedded = dot_t(onehot, char_table).astype(BF)
    pre = dot(embedded, w_gru) + bias

    span = span_lengths[:, 0]
    span_ends = jnp.cumsum(span, -1)
    starts = span_ends - span
    ends_col = jnp.stack([starts, span_ends], -1).reshape(rows, 2)
    ends_row = jnp.pad(jnp.stack([starts, span_ends], 1), ((0, 0), (0, 6), (0, 0))).reshape(seqs * 8, toks)
    block = pltpu.VMEM((2 * HB, chars, 128), F32)
    full = lambda *d: jax.ShapeDtypeStruct(d, F32)
    keys, values, tot_all, pooled, prev, chunk = gather_with(
        functools.partial(forward_run, seqs), [(qkv3[..., width : 2 * width], 1, 0, None), (qkv3[..., 2 * width :], 1, 0, None)],
        2, planes, nseq, (pre, ends_col), (), [full(rows, width), full(seqs * chars, width), full(seqs * 4 * NCH, HG)], [block] * 4,
    )
    own_q, keys = lax.optimization_barrier((qkv3[..., :width], keys))
    queries = lax.all_gather(own_q, "seq", axis=1, tiled=True)

    ctx3, ctx_low3, lse = attention_fwd(qkv3, keys, values)
    context, context_low = ctx3.reshape(rows, width), ctx_low3.reshape(rows, width)
    (out_token, out_char, normed_low, hidden, state_low, pooled_low, mprev, merged, mnext, dmixed_low, dfused, dlowered, draised_low, dattended,
     dinput_sum, dpooled, dnorm, dctx3, col, stat) = middle(
        seqs, x_low, context_low, context, lse, pooled, grad_token.reshape(rows, width), grad_char.reshape(rows, width), nrm.reshape(8, width),
        w_out, w_up, w_down, w_stream, w_conv, 5
    )
    length = nseq * toks
    dctx_all, stat_all, _, dpre, dbias, dq, dembed = gather_with(
        functools.partial(backward_run, seqs), [(dctx3, 1, 0, None), (stat, 0, 0, None)], 3, planes, nseq,
        (pre, prev, chunk, tot_all, dpooled, ends_row, own_q, dctx3, col, w_gru), (keys, values),
        [jax.ShapeDtypeStruct((seqs * chars, 4 * HG), BF), full(seqs * 8, 4 * HG), jax.ShapeDtypeStruct((seqs, toks, width), BF),
         jax.ShapeDtypeStruct(embedded.shape, BF)],
        [pltpu.VMEM((seqs * chars, width), F32), pltpu.VMEM((seqs * 2 * NCH, HG), F32)] + [block] * 2
        + [pltpu.VMEM((2, length, 2 * HDIM), BF)] * 2 + [pltpu.SemaphoreType.DMA((2,))] * 2,
    )
    g_bias = dbias.reshape(seqs, 8, 4 * HG)[:, 0].sum(0)

    g_norms = dnorm.reshape(4, 2, width)
    shape = (seqs, toks, width)
    if seq_dims(nseq) == (RZ, RY, RC) and planes == 2:
        lhs = (x_low, context_low, normed_low, hidden, state_low, pooled_low, mprev, merged, mnext)
        rhs = (dq.reshape(rows, width), dattended, draised_low, dlowered, dfused, dmixed_low)
        *owned, dinputs = reduce_all(
            lhs, rhs, embedded, dpre, dembed, char_rows, qkv3[..., width:], stat_all.reshape(nseq, -1, toks), queries, dctx_all, w_qkv, dinput_sum, g_bias, g_norms, VOCAB_CHAR, nseq, 4
        )
        owned[8] = owned[8].reshape(-1)
        owned = [owned[k] for k in (0, 1, 2, 3, 4, 5, 8, 6, 7, 9)]
        owned = tuple(owned)
    else:
        stat_all = stat_all.reshape(nseq, seqs, HEADS // 2, 4, toks).transpose(1, 2, 3, 0, 4).reshape(seqs, HEADS // 2, 4, nseq * toks)
        dk, dv = attention_bwd(qkv3, queries, dctx_all, stat_all)
        dqkv = jnp.concatenate([dq, dk, dv], -1).reshape(rows, 3 * width)
        dinputs = dinput_sum + dot_t(dqkv, w_qkv)
        g_stream = [wgrad(state_low, dfused[:, :width]), wgrad(pooled_low, dfused[:, width:])]
        owned = (
            scatter(wgrad(x_low, dqkv).astype(BF), 0),
            scatter(wgrad(context_low, dattended).astype(BF), 0),
            scatter(wgrad(normed_low, draised_low).astype(BF), 0),
            scatter(wgrad(hidden, dlowered).astype(BF), 0),
            scatter(wgrad(dembed, onehot).astype(BF), 0),
            scatter(wgrad(embedded, dpre).astype(BF), 0),
            scatter(g_bias.astype(BF), 0),
            scatter(jnp.stack(g_stream).astype(BF), 1),
            scatter(jnp.stack([wgrad(m, dmixed_low) for m in (mprev, merged, mnext)]).astype(BF), 1),
            scatter(g_norms.astype(BF), 2),
        )
    return (
        out_token.reshape(shape),
        out_char.reshape(shape),
        dinputs.reshape(shape),
    ) + owned


def solution(mesh):
    placed = (
        P("dp", "seq", None),
        P("dp", "seq"),
        P("dp", "seq", None),
        P("dp"),
        P("seq", None),
        P("seq", None),
        P("seq", None),
        P("seq", None),
        P("seq", None),
        P("seq", None),
        P("seq"),
        P(None, "seq", None),
        P(None, "seq", None),
        P(None, None, "seq"),
        P("dp", "seq", None),
        P("dp", "seq", None),
    )
    return jax.shard_map(
        body,
        mesh=mesh,
        in_specs=placed,
        out_specs=(
            P("dp", "seq", None),
            P("dp", "seq", None),
            P("dp", "seq", None),
            P("seq", None),
            P("seq", None),
            P("seq", None),
            P("seq", None),
            P("seq", None),
            P("seq", None),
            P("seq"),
            P(None, "seq", None),
            P(None, "seq", None),
            P(None, None, "seq"),
        ),
        check_vma=False,
    )
```

```python
import collections
import functools
import jax
import jax.numpy as jnp
from jax import lax
from jax.experimental import pallas as pl
from jax.experimental.pallas import tpu as pltpu
from jax.sharding import PartitionSpec as P

HEADS = 12
HDIM = 64
VOCAB_CHAR = 1000
GROUP_CHARS = 250
HG = 384
EPSILON = 1e-05
MESH = pl.DeviceIdType.MESH
BF = jnp.bfloat16
F32 = jnp.float32
NCH = 8
UNROLL = 8
SHARE = (1, 2, 3, 6)
HB = HG // 128

def seq_dims(n):
    return {16: (4, 2, 2), 32: (8, 4, 1)}.get(n, (n, 1, 1))


Move = collections.namedtuple("Move", ("array", "axis", "rows", "lead", "route"))


def gather_kernel(dims, planes, moves, n_arrays, task, *refs):
    Z, Y, C = dims
    n = len(moves)
    n_in, n_out = (task.n_in, task.n_out) if task else (0, 0)
    src, task_in = refs[:n_arrays], refs[n_arrays : n_arrays + n_in]
    refs = refs[n_arrays + n_in :]
    dst, task_out = refs[:n_arrays], refs[n_arrays : n_arrays + n_out]
    own_sem, recv, zs, ds, ys, ss, xs, *task_scratch = refs[n_arrays + n_out :]
    dp = lax.axis_index("dp")
    me = lax.axis_index("seq")
    c = lax.rem(me, C)
    y = lax.rem(lax.div(me, C), Y)
    z = lax.div(me, C * Y)
    up_z, down_z = z < Z - 1, z > 0

    def at(zz, yy, cc):
        return (zz * Y + yy) * C + cc

    def to(zz, yy, cc):
        return (dp, at(zz, yy, cc))

    def view(i, slot):
        m = moves[i]
        s = pl.ds(pl.multiple_of(slot * m.rows, m.rows), m.rows)
        ref = dst[m.array]
        return ref.at[s] if m.axis == 0 else ref.at[:, s]

    def mine(i):
        m = moves[i]
        if m.lead is None:
            return src[m.array]
        return src[m.array].at[:, :, pl.ds(*m.lead)] if isinstance(m.lead, tuple) else src[m.array].at[m.lead]

    def copy(i, slot, send, where, own=False):
        return pltpu.make_async_remote_copy(
            src_ref=mine(i) if own else view(i, slot), dst_ref=view(i, slot),
            send_sem=send, recv_sem=recv.at[i, slot], device_id=where, device_id_type=MESH)

    sib = to(z, y, 1 - c) if C == 2 else None
    xp = (1 - dp, me)
    use_x = planes == 2 and any(m.route for m in moves)
    some = sib if C == 2 else to(z, y, c)

    def owner(i):
        return None if not (use_x and moves[i].route) else dp == moves[i].route - 1

    def when(cond, f):
        if cond is None:
            f()
        else:
            pl.when(cond)(f)

    def both(a, b):
        return b if a is None else jnp.logical_and(a, b)

    nseq = Z * Y * C
    if task:
        push_all, *task_out = task_out
        push, p_send, p_recv, i_sem, *task_scratch = task_scratch
        n_held = n_in - task.n_stay
        held, task_scratch = task_scratch[:n_held], task_scratch[n_held:]
        loads = [pltpu.make_async_copy(a, b, i_sem.at[k]) for k, (a, b) in enumerate(zip(task_in[:n_held], held))]
        for load in loads:
            load.start()
    bar = pltpu.get_barrier_semaphore()
    if task:
        peers = [(None, (dp, lax.rem(me + k, nseq))) for k in range(1, nseq)]
    else:
        peers = [(z > 0, to(z - 1, y, c)), (z < Z - 1, to(z + 1, y, c))]
        if Y > 1:
            peers += [(y > 0, to(z, y - 1, c)), (y < Y - 1, to(z, y + 1, c))]
        if C == 2:
            peers.append((None, sib))
    if use_x:
        peers.append((None, xp))
    count = 0
    for cond, where in peers:
        when(cond, functools.partial(pl.semaphore_signal, bar, inc=1, device_id=where, device_id_type=MESH))
        count = count + (1 if cond is None else cond.astype(jnp.int32))
    pl.semaphore_wait(bar, count)
    if task:

        def pushed(k, slot, where):
            return pltpu.make_async_remote_copy(
                src_ref=push, dst_ref=push_all.at[slot], send_sem=p_send.at[k], recv_sem=p_recv.at[slot], device_id=where, device_id_type=MESH)

        def push_one(k, _):
            pushed(k, me, (dp, lax.rem(me + k, nseq))).start()
            return 0

        def push_wait(k, _):
            other = lax.rem(me + k, nseq)
            pushed(k, other, (dp, other)).wait_recv()
            pushed(k, me, (dp, other)).wait_send()
            return 0

    def work(point):
        if task:
            task.run(point, me, push, push_all, tuple(held) + tuple(task_in[n_held:]), task_out, task_scratch)

    def go_z(i, slot, up, sem, own=False):
        where = to(z + 1, y, c) if up else to(z - 1, y, c)
        pl.when(up_z if up else down_z)(lambda: copy(i, slot, sem, where, own).start())

    def go_y(i, slot, up, sem, own=False):
        where = to(z, y + 1, c) if up else to(z, y - 1, c)
        pl.when(y < Y - 1 if up else y > 0)(lambda: copy(i, slot, sem, where, own).start())

    def go_core(i, slot, own=False):
        if C == 2:
            copy(i, slot, ss.at[i, slot], sib, own).start()

    def wait_in(i, slot):
        copy(i, slot, ss.at[i, slot], some).wait_recv()

    for i in range(n):
        pltpu.make_async_copy(mine(i), view(i, me), own_sem.at[i]).start()

        def own_sends(i=i):
            go_z(i, me, True, zs.at[i, me], True)
            go_z(i, me, False, ds.at[i, 0], True)
            if Y > 1:
                go_y(i, me, True, ys.at[i, me], True)
                go_y(i, me, False, ds.at[i, 1], True)

        when(owner(i), own_sends)
        go_core(i, me, True)

    def arrive_z(zz, up):
        slot = at(zz, y, c)

        def one(i):
            wait_in(i, slot)
            go_z(i, slot, up, zs.at[i, slot])
            if Y > 1:
                go_y(i, slot, True, ys.at[i, slot])
                go_y(i, slot, False, ys.at[i, slot] if Y == 2 else xs.at[i, slot])
            if use_x and moves[i].route:
                copy(i, slot, xs.at[i, slot], xp).start()
            go_core(i, slot)

        for i in range(n):
            when(owner(i), functools.partial(one, i))

    def arrive_y(zz, yy, up):
        slot = at(zz, yy, c)

        def one(i):
            wait_in(i, slot)
            if Y > 2:
                go_y(i, slot, up, ys.at[i, slot])
            if use_x and moves[i].route:
                copy(i, slot, xs.at[i, slot], xp).start()
            go_core(i, slot)

        for i in range(n):
            when(owner(i), functools.partial(one, i))

    def all_y(zz):
        for t in range(1, Y):
            pl.when(y - t >= 0)(lambda: arrive_y(zz, y - t, True))
            pl.when(y + t < Y)(lambda: arrive_y(zz, y + t, False))

    if task:
        for load in loads:
            load.wait()
        work(0)
        push_all[me] = push[...]
        lax.fori_loop(1, nseq, push_one, 0)
    def step(s, _):
        pl.when(z - s >= 0)(lambda: arrive_z(z - s, True))
        pl.when(z + s < Z)(lambda: arrive_z(z + s, False))
        q = s - 1
        pl.when(z - q >= 0)(lambda: all_y(z - q))
        pl.when(jnp.logical_and(q > 0, z + q < Z))(lambda: all_y(z + q))
        return 0

    if task:
        for s in (1, 2):
            if s < Z:
                step(s, 0)
            if s == 1:
                lax.fori_loop(1, nseq, push_wait, 0)
            work(s)
        lax.fori_loop(3, Z, step, 0)
        work(3)
    else:
        lax.fori_loop(1, Z, step, 0)
    q = Z - 1
    pl.when(z - q >= 0)(lambda: all_y(z - q))
    pl.when(z + q < Z)(lambda: all_y(z + q))

    if use_x:

        def far(k, _):
            slot = at(lax.rem(z + lax.div(k, Y), Z), lax.rem(y + lax.rem(k, Y), Y), c)

            def one(i):
                wait_in(i, slot)
                go_core(i, slot)

            for i in range(n):
                if moves[i].route:
                    pl.when(dp != moves[i].route - 1)(functools.partial(one, i))
            return 0

        lax.fori_loop(1, Z * Y, far, 0)

    def drain(k, _):
        zz, yy = lax.div(k, Y), lax.rem(k, Y)
        slot = at(zz, yy, c)
        is_own = slot == me
        own_y = yy == y
        fz = jnp.logical_or(jnp.logical_and(zz <= z, up_z), jnp.logical_and(zz > z, down_z))
        for i in range(n):
            o = owner(i)
            if C == 2:
                wait_in(i, at(zz, yy, 1 - c))
                copy(i, slot, ss.at[i, slot], some).wait_send()
            sent = lambda sem: copy(i, slot, sem, some).wait_send()
            pl.when(both(o, jnp.logical_and(own_y, fz)))(lambda: sent(zs.at[i, slot]))
            if Y == 2:
                pl.when(both(o, jnp.logical_and(own_y, jnp.logical_or(jnp.logical_not(is_own), y < Y - 1))))(lambda: sent(ys.at[i, slot]))
            elif Y > 2:
                fy = jnp.logical_or(jnp.logical_and(yy <= y, y < Y - 1), jnp.logical_and(yy > y, y > 0))
                pl.when(both(o, fy))(lambda: sent(ys.at[i, slot]))
                fy2 = jnp.logical_and(jnp.logical_and(own_y, y > 0), jnp.logical_not(is_own))
                pl.when(both(o, fy2))(lambda: sent(xs.at[i, slot]))
            if use_x and moves[i].route:
                pl.when(both(o, jnp.logical_not(is_own)))(lambda: sent(xs.at[i, slot]))
        return 0

    lax.fori_loop(0, Z * Y, drain, 0)
    for i in range(n):
        pltpu.make_async_copy(mine(i), view(i, me), own_sem.at[i]).wait()
        o = owner(i)
        pl.when(both(o, down_z))(lambda: copy(i, me, ds.at[i, 0], some, True).wait_send())
        if Y > 1:
            pl.when(both(o, y > 0))(lambda: copy(i, me, ds.at[i, 1], some, True).wait_send())
    work(4)


Task = collections.namedtuple("Task", ("n_in", "n_stay", "n_out", "n_far", "run"))


def gather(arrays, cid, planes, nseq, task=None, inputs=(), outputs=(), scratch=()):
    dims = seq_dims(nseq)
    moves, shapes = [], []
    for k, (x, axis, route, lead) in enumerate(arrays):
        shape = list(x.shape[:-1] + lead[1:] if isinstance(lead, tuple) else x.shape if lead is None else x.shape[1:])
        moves.append(Move(k, axis, shape[axis], lead, route if planes == 2 and dims[1:] == (2, 2) else 0))
        shape[axis] *= nseq
        shapes.append(jax.ShapeDtypeStruct(tuple(shape), x.dtype))
    moves.sort(key=lambda m: not m.route)
    n = len(moves)
    D = pltpu.SemaphoreType.DMA
    scratch = [D((n,)), D((n, nseq)), D((n, nseq)), D((n, 2)), D((n, nseq)), D((n, nseq)), D((n, nseq))] + list(scratch)
    far, here = pl.BlockSpec(memory_space=pl.ANY), pl.BlockSpec(memory_space=pltpu.VMEM)
    n_far = task.n_far if task else 0
    return pl.pallas_call(
        functools.partial(gather_kernel, dims, planes, tuple(moves), len(arrays), task),
        out_shape=shapes + list(outputs),
        in_specs=[far] * (len(arrays) + len(inputs)),
        out_specs=[far] * len(arrays) + [here] * (len(outputs) - n_far) + [far] * n_far,
        scratch_shapes=scratch,
        compiler_params=pltpu.CompilerParams(collective_id=cid, has_side_effects=True, vmem_limit_bytes=60 << 20),
    )(*[x for x, _, _, _ in arrays], *inputs)


def gather_with(run, arrays, cid, planes, nseq, inputs, stay, outputs, late, scratch):
    D = pltpu.SemaphoreType.DMA
    push = (8, HG)
    outputs = [jax.ShapeDtypeStruct((nseq,) + push, F32)] + outputs + late
    scratch = [pltpu.VMEM(a.shape, a.dtype) for a in late] + [D((len(late),))] + scratch
    scratch = [pltpu.VMEM(push, F32), D((nseq,)), D((nseq,)), D((len(inputs),))] + [pltpu.VMEM(a.shape, a.dtype) for a in inputs] + scratch
    inputs = tuple(inputs) + tuple(stay)
    return gather(arrays, cid, planes, nseq, Task(len(inputs), len(stay), len(outputs), len(late), run), inputs, outputs, scratch)


def dot(a, b):
    return jnp.dot(a, b, preferred_element_type=F32)


def dot_t(a, b):
    return lax.dot_general(a, b, (((1,), (1,)), ((), ())), preferred_element_type=F32)


def wgrad(a, b):
    return lax.dot_general(a, b, (((0,), (0,)), ((), ())), preferred_element_type=F32)


def vmem(mib):
    return pltpu.CompilerParams(vmem_limit_bytes=mib << 20)


def layer_norm(values, gain_row, shift_row):
    center = values - jnp.mean(values, -1, keepdims=True)
    spread = jnp.mean(center * center, -1, keepdims=True)
    return center * lax.rsqrt(spread + EPSILON) * gain_row + shift_row


def fill(pre_ref, decay, drive=None):
    for k in range(2):
        for j in range(HB):
            at = 2 * k * HG + j * 128
            rate = jax.nn.sigmoid(pre_ref[:, at : at + 128])
            decay[k * HB + j] = 1.0 - rate
            if drive is not None:
                drive[k * HB + j] = rate * pre_ref[:, at + HG : at + HG + 128]


def row(x, i):
    return lax.slice_in_dim(x, i, i + 1, axis=0)


def cat(parts):
    return jnp.concatenate(parts, 1)


def blocks(x):
    return [x[:, j * 128 : (j + 1) * 128] for j in range(HB)]


def totals_kernel(pre_ref, tot_ref, chunk_ref, decay, drive):
    length = pre_ref.shape[0] // NCH
    fill(pre_ref, decay, drive)

    def step(t, carry):
        place = (pl.ds(t, NCH, stride=length), pl.ds(length - 1 - t, NCH, stride=length))
        out = []
        for i in range(2 * HB):
            c, h = carry[i]
            a = decay[i, place[i // HB], :]
            out.append((c * a, a * h + drive[i, place[i // HB], :]))
        return tuple(out)

    one, zero = jnp.ones((NCH, 128), F32), jnp.zeros((NCH, 128), F32)
    ends = lax.fori_loop(0, length, step, ((one, zero),) * (2 * HB), unroll=UNROLL)
    cf, hf = cat([e[0] for e in ends[:HB]]), cat([e[1] for e in ends[:HB]])
    cb, hb = cat([e[0] for e in ends[HB:]]), cat([e[1] for e in ends[HB:]])
    chunk_ref[0:NCH, :] = cf
    chunk_ref[NCH : 2 * NCH, :] = hf
    chunk_ref[2 * NCH : 3 * NCH, :] = cb
    chunk_ref[3 * NCH :, :] = hb
    one, zero = jnp.ones((1, HG), F32), jnp.zeros((1, HG), F32)
    tf, sf, tb, sb = one, zero, one, zero
    for k in range(NCH):
        sf, tf = row(cf, k) * sf + row(hf, k), tf * row(cf, k)
        j = NCH - 1 - k
        sb, tb = row(cb, j) * sb + row(hb, j), tb * row(cb, j)
    tot_ref[...] = jnp.concatenate([tf, sf, tb, sb], 0)


def states_work(me, q, seqs, all_ref, pre_all, chunk_all, ends_all, pooled_all, prev_all, decay, drive, state, prev):
    pre_ref, chunk_ref, ends_ref, pooled_ref, prev_ref = (
        r.at[pl.ds(q * (r.shape[0] // seqs), r.shape[0] // seqs)] for r in (pre_all, chunk_all, ends_all, pooled_all, prev_all)
    )
    chars = pre_all.shape[0] // seqs
    length = chars // NCH
    nseq = all_ref.shape[0]
    fill(pre_ref, decay, drive)
    ef = jnp.zeros((1, HG), F32)
    eb = ef
    for d in range(nseq):
        got = all_ref[d]
        ef = jnp.where(d < me, row(got, 4 * q) * ef + row(got, 4 * q + 1), ef)
        got = all_ref[nseq - 1 - d]
        eb = jnp.where(nseq - 1 - d > me, row(got, 4 * q + 2) * eb + row(got, 4 * q + 3), eb)
    cf, hf = chunk_ref[0:NCH, :], chunk_ref[NCH : 2 * NCH, :]
    cb, hb = chunk_ref[2 * NCH : 3 * NCH, :], chunk_ref[3 * NCH :, :]
    rows_f, rows_b = [], []
    for k in range(NCH):
        rows_f.append(ef)
        ef = row(cf, k) * ef + row(hf, k)
        j = NCH - 1 - k
        rows_b.append(eb)
        eb = row(cb, j) * eb + row(hb, j)

    def step(t, carry):
        place = (pl.ds(t, NCH, stride=length), pl.ds(length - 1 - t, NCH, stride=length))
        out = []
        for i in range(2 * HB):
            at = place[i // HB]
            prev[i, at, :] = carry[i]
            h = decay[i, at, :] * carry[i] + drive[i, at, :]
            state[i, at, :] = h
            out.append(h)
        return tuple(out)

    lax.fori_loop(0, length, step, tuple(blocks(jnp.concatenate(rows_f, 0)) + blocks(jnp.concatenate(rows_b[::-1], 0))), unroll=UNROLL)
    first = ends_ref[:, 0:1]
    last = ends_ref[:, 1:2]
    place = lax.broadcasted_iota(jnp.int32, (ends_all.shape[0] // seqs, chars), 1)
    member = jnp.where((place >= first) & (place < last), 1.0, 0.0).astype(BF)
    prev_ref[...] = cat([prev[i] for i in range(2 * HB)])
    pooled_ref[...] = dot(member, cat([state[i].astype(BF) for i in range(2 * HB)])) / (last - first).astype(F32)


def flows_kernel(pre_ref, dpool_ref, ends_ref, chunk_ref, ds_ref, tot_ref, gch_ref, decay, ds):
    chars = pre_ref.shape[0]
    length = chars // NCH
    fill(pre_ref, decay)
    first = ends_ref[0:1, :]
    last = ends_ref[1:2, :]
    place = lax.broadcasted_iota(jnp.int32, (chars, ends_ref.shape[1]), 0)
    inside = (place >= first) & (place < last)
    span = jnp.sum(jnp.where(inside, (last - first).astype(F32), 0.0), 1, keepdims=True)
    member = jnp.where(inside, 1.0, 0.0).astype(BF)
    spread = dot(member, dpool_ref[...]) / span
    ds_ref[...] = spread
    for i in range(2 * HB):
        ds[i] = spread[:, i * 128 : (i + 1) * 128]

    def step(t, carry):
        place = (pl.ds(length - 1 - t, NCH, stride=length), pl.ds(t, NCH, stride=length))
        return tuple(
            decay[i, place[i // HB], :] * (ds[i, place[i // HB], :] + carry[i]) for i in range(2 * HB)
        )

    ends = lax.fori_loop(0, length, step, (jnp.zeros((NCH, 128), F32),) * (2 * HB), unroll=UNROLL)
    gf, gb = cat(ends[:HB]), cat(ends[HB:])
    gch_ref[0:NCH, :] = gf
    gch_ref[NCH:, :] = gb
    cf, cb = chunk_ref[0:NCH, :], chunk_ref[2 * NCH : 3 * NCH, :]
    zero = jnp.zeros((1, HG), F32)
    tf, tb = zero, zero
    for k in range(NCH):
        j = NCH - 1 - k
        tf = row(cf, j) * tf + row(gf, j)
        tb = row(cb, k) * tb + row(gb, k)
    tot_ref[...] = jnp.concatenate([tf, tb, zero, zero], 0)


def dpre_work(me, q, seqs, gall_ref, all_ref, pre_all, ds_all, prev_all, chunk_all, gch_all, dpre_all, bias_all, decay, ds):
    pre_ref, ds_ref, prev_ref, chunk_ref, gch_ref, dpre_ref, bias_ref = (
        r.at[pl.ds(q * (r.shape[0] // seqs), r.shape[0] // seqs)] for r in (pre_all, ds_all, prev_all, chunk_all, gch_all, dpre_all, bias_all)
    )
    chars = pre_all.shape[0] // seqs
    length = chars // NCH
    nseq = all_ref.shape[0]
    fill(pre_ref, decay)
    for i in range(2 * HB):
        ds[i] = ds_ref[:, i * 128 : (i + 1) * 128]
    ef = jnp.zeros((1, HG), F32)
    eb = ef
    for d in range(nseq):
        j = nseq - 1 - d
        ef = jnp.where(j > me, row(all_ref[j], 4 * q) * ef + row(gall_ref[j], 4 * q), ef)
        eb = jnp.where(d < me, row(all_ref[d], 4 * q + 2) * eb + row(gall_ref[d], 4 * q + 1), eb)
    cf, cb = chunk_ref[0:NCH, :], chunk_ref[2 * NCH : 3 * NCH, :]
    gf, gb = gch_ref[0:NCH, :], gch_ref[NCH:, :]
    rows_f, rows_b = [], []
    for k in range(NCH):
        j = NCH - 1 - k
        rows_f.append(ef)
        ef = row(cf, j) * ef + row(gf, j)
        rows_b.append(eb)
        eb = row(cb, k) * eb + row(gb, k)

    def step(t, carry):
        place = (pl.ds(length - 1 - t, NCH, stride=length), pl.ds(t, NCH, stride=length))
        out = []
        for i in range(2 * HB):
            at = place[i // HB]
            g = ds[i, at, :] + carry[i]
            ds[i, at, :] = g
            out.append(decay[i, at, :] * g)
        return tuple(out)

    lax.fori_loop(0, length, step, tuple(blocks(jnp.concatenate(rows_f[::-1], 0)) + blocks(jnp.concatenate(rows_b, 0))), unroll=UNROLL)
    for i in range(2 * HB):
        k, j = i // HB, i % HB
        at = 2 * k * HG + j * 128
        g = ds[i]
        rate = jax.nn.sigmoid(pre_ref[:, at : at + 128])
        cand = pre_ref[:, at + HG : at + HG + 128]
        prev = prev_ref[:, i * 128 : (i + 1) * 128]
        dgate = (g * (cand - prev) * rate * decay[i]).astype(BF)
        dcand = (g * rate).astype(BF)
        for to, v in ((at, dgate), (at + HG, dcand)):
            dpre_ref[:, to : to + 128] = v
            bias_ref[:, to : to + 128] = jnp.broadcast_to(jnp.sum(v.astype(F32), 0, keepdims=True), (8, 128))


def part_of(ref, q, seqs):
    n = ref.shape[0] // seqs
    return ref.at[pl.ds(q * n, n)]


def forward_run(seqs, point, me, push, push_all, inputs, outputs, scratch):
    ids, table, gru, bias, ends = inputs
    pooled, chunk, *out = outputs
    pre, prev, emb = scratch[:3]
    o_sem = scratch[3]
    write = lambda k: pltpu.make_async_copy((pre, prev, emb)[k], out[k], o_sem.at[k])
    scratch = scratch[4:]
    if point == 0:
        n = 256

        def look(k, _):
            at = pl.ds(pl.multiple_of(k * n, n), n)
            unit = lax.broadcasted_iota(jnp.int32, (n, table.shape[1]), 1)
            hot = jnp.where(unit == ids[at, :], 1.0, 0.0).astype(BF)
            rows = dot_t(hot, table[...]).astype(BF)
            emb[at, :] = rows
            pre[at, :] = dot(rows, gru[...]) + bias[...]
            return 0

        lax.fori_loop(0, ids.shape[0] // n, look, 0)
        for q in range(seqs):
            totals_kernel(part_of(pre, q, seqs), push.at[pl.ds(4 * q, 4)], part_of(chunk, q, seqs), *scratch[:2])
        write(0).start()
        write(2).start()
    elif point <= seqs:
        states_work(me, point - 1, seqs, push_all, pre, chunk, ends, pooled, prev, *scratch)
        if point == seqs:
            write(1).start()
    elif point == 4:
        for k in range(3):
            write(k).wait()


def backward_run(seqs, point, me, push, push_all, inputs, outputs, scratch):
    pre, prev, chunk, tot_all, dpool, ends, q_ref, dc_ref, col_ref, gru_ref, keys, values = inputs
    dbias, dq, demb, dpre_out = outputs
    dpre, o_sem, ds_all, gch, decay, ds, kbuf, vbuf, k_sem, v_sem = scratch
    write = lambda: pltpu.make_async_copy(dpre, dpre_out, o_sem.at[0])
    if point == 4:
        write().wait()
        return
    pairs = HEADS // 2
    steps = seqs * pairs

    def fetch(i):
        s, p = lax.div(i, pairs), lax.rem(i, pairs)
        cols = pl.ds(pl.multiple_of(p * 2 * HDIM, 2 * HDIM), 2 * HDIM)
        b = lax.rem(i, 2)
        return (pltpu.make_async_copy(keys.at[s, :, cols], kbuf.at[b], k_sem.at[b]), pltpu.make_async_copy(values.at[s, :, cols], vbuf.at[b], v_sem.at[b]))

    def one(i, _):
        s, p = lax.div(i, pairs), lax.rem(i, pairs)
        cols = pl.ds(pl.multiple_of(p * 2 * HDIM, 2 * HDIM), 2 * HDIM)
        b = lax.rem(i, 2)

        @pl.when(i + 1 < steps)
        def _():
            for c in fetch(i + 1):
                c.start()

        for c in fetch(i):
            c.wait()
        dq[s, :, cols] = query_grad(q_ref[s, :, cols], kbuf[b], vbuf[b], dc_ref[s, :, cols], col_ref[s, p])
        return 0

    if point == 0:
        for c in fetch(0):
            c.start()
        for q in range(seqs):
            flows_kernel(*(part_of(r, q, seqs) for r in (pre, dpool, ends, chunk, ds_all)), push.at[pl.ds(4 * q, 4)], part_of(gch, q, seqs), decay, ds)
    elif point <= seqs:
        dpre_work(me, point - 1, seqs, push_all, tot_all, pre, ds_all, prev, chunk, gch, dpre, dbias, decay, ds)
        part_of(demb, point - 1, seqs)[...] = dot_t(part_of(dpre, point - 1, seqs)[...], gru_ref[...]).astype(BF)
        if point == seqs:
            write().start()
    bounds = (0,) + tuple(steps * k // 6 for k in SHARE)
    lax.fori_loop(bounds[point], bounds[point + 1], one, 0)


def pair_rows(x):
    lane = lax.broadcasted_iota(jnp.int32, x.shape, 1)
    zero = jnp.zeros_like(x)
    return jnp.concatenate([jnp.where(lane < HDIM, x, zero), jnp.where(lane >= HDIM, x, zero)], 0)


def pair_lanes(x):
    half = x.shape[0] // 2
    lane = lax.broadcasted_iota(jnp.int32, (half, x.shape[1]), 1)
    return jnp.where(lane < HDIM, x[:half], x[half:])


def attn_fwd_kernel(q_ref, k_ref, v_ref, ctx_ref, low_ref, lse_ref):
    toks = q_ref.shape[0]
    s = dot_t(pair_rows(q_ref[...] * (HDIM ** -0.5)), k_ref[...])
    top = jnp.max(s, 1, keepdims=True)
    p = jnp.exp(s - top)
    total = jnp.sum(p, 1, keepdims=True)
    o = pair_lanes(dot(p.astype(BF), v_ref[...]) / total)
    ctx_ref[...] = o
    low_ref[...] = o.astype(BF)
    lse = top + jnp.log(total)
    lse_ref[...] = jnp.concatenate([lse[:toks], lse[toks:]], 1)


def head_spec(rows, base=0):
    return pl.BlockSpec((None, rows, 2 * HDIM), lambda s, h: (s, 0, h + base))


def attention_fwd(qkv, keys, values):
    seqs, toks, _ = qkv.shape
    length = keys.shape[1]
    pairs = HEADS // 2
    return pl.pallas_call(
        attn_fwd_kernel,
        grid=(seqs, pairs),
        out_shape=[
            jax.ShapeDtypeStruct((seqs, toks, HEADS * HDIM), F32),
            jax.ShapeDtypeStruct((seqs, toks, HEADS * HDIM), BF),
            jax.ShapeDtypeStruct((seqs, pairs, toks, 2), F32),
        ],
        in_specs=[head_spec(toks), head_spec(length), head_spec(length)],
        out_specs=[head_spec(toks), head_spec(toks), pl.BlockSpec((None, None, toks, 2), lambda s, h: (s, h, 0, 0))],
        compiler_params=vmem(62),
    )(qkv, keys, values)


def query_grad(q, keys, values, dc, col):
    scale = HDIM ** -0.5
    lse = jnp.concatenate([col[:, 0:1], col[:, 1:2]], 0)
    delta = jnp.concatenate([col[:, 2:3], col[:, 3:4]], 0)
    p = jnp.exp(dot_t(pair_rows(q * scale), keys) - lse)
    ds = (p * (dot_t(pair_rows(dc), values) - delta)).astype(BF)
    return (pair_lanes(dot(ds, keys)) * scale).astype(BF)


def context_kernel(datt_ref, w_ref, ctx_ref, lse_ref, dctx_ref, col_ref, stat_ref):
    seqs, toks, _ = dctx_ref.shape
    pairs = HEADS // 2
    low = dot_t(datt_ref[...], w_ref[...]).astype(BF)
    prod = low.astype(F32) * ctx_ref[...]
    lane = lax.broadcasted_iota(jnp.int32, (toks, 2 * HDIM), 1)
    for s in range(seqs):
        dctx_ref[s] = low[s * toks : (s + 1) * toks]
        cols = []
        for p in range(pairs):
            x = prod[s * toks : (s + 1) * toks, p * 2 * HDIM : (p + 1) * 2 * HDIM]
            a = jnp.sum(jnp.where(lane < HDIM, x, 0.0), 1, keepdims=True)
            b = jnp.sum(jnp.where(lane >= HDIM, x, 0.0), 1, keepdims=True)
            col = jnp.concatenate([lse_ref[s, p], a, b], 1)
            col_ref[s, p] = col
            cols.append(col)
        flat = jnp.concatenate(cols + [jnp.zeros((toks, 128 - 4 * pairs), F32)], 1)
        stat_ref[s * 4 * pairs : (s + 1) * 4 * pairs, :] = flat.T[: 4 * pairs]


def attn_bwd_kernel(ko_ref, vo_ref, qa_ref, dca_ref, row_ref, dk_ref, dv_ref):
    toks = ko_ref.shape[0]
    scale = HDIM ** -0.5

    def spread(i):
        n = row_ref.shape[1]
        return jnp.concatenate(
            [jnp.broadcast_to(row_ref[i : i + 1, :], (toks, n)), jnp.broadcast_to(row_ref[i + 1 : i + 2, :], (toks, n))], 0
        )

    p = jnp.exp(dot_t(pair_rows(ko_ref[...] * scale), qa_ref[...]) - spread(0))
    dv_ref[...] = pair_lanes(dot(p.astype(BF), dca_ref[...])).astype(BF)
    dp = dot_t(pair_rows(vo_ref[...]), dca_ref[...])
    ds = (p * (dp - spread(2))).astype(BF)
    dk_ref[...] = (pair_lanes(dot(ds, qa_ref[...])) * scale).astype(BF)


def attention_bwd(qkv, queries, dctx_all, rows):
    seqs, toks, _ = qkv.shape
    length = queries.shape[1]
    pairs = HEADS // 2
    stat = lambda a, b: pl.BlockSpec((None, None, a, b), lambda s, h: (s, h, 0, 0))
    return pl.pallas_call(
        attn_bwd_kernel,
        grid=(seqs, pairs),
        out_shape=[jax.ShapeDtypeStruct((seqs, toks, HEADS * HDIM), BF)] * 2,
        in_specs=[head_spec(toks, pairs), head_spec(toks, 2 * pairs), head_spec(length), head_spec(length), stat(4, length)],
        out_specs=[head_spec(toks)] * 2,
        compiler_params=vmem(56),
    )(qkv, qkv, queries, dctx_all, rows)


GELU_A = 0.7978845608028654
GELU_B = 0.044715


def norm_both(v, gain, shift, dy):
    center = v - jnp.mean(v, -1, keepdims=True)
    inv = lax.rsqrt(jnp.mean(center * center, -1, keepdims=True) + EPSILON)
    hat = center * inv
    dhat = dy * gain
    dv = inv * (dhat - jnp.mean(dhat, -1, keepdims=True) - hat * jnp.mean(dhat * hat, -1, keepdims=True))
    return hat * gain + shift, dv, jnp.sum(dy * hat, 0, keepdims=True), jnp.sum(dy, 0, keepdims=True)


def norm_back(hat, inv, gain, dy):
    dhat = dy * gain
    dv = inv * (dhat - jnp.mean(dhat, -1, keepdims=True) - hat * jnp.mean(dhat * hat, -1, keepdims=True))
    return dv, jnp.sum(dy * hat, 0, keepdims=True), jnp.sum(dy, 0, keepdims=True)


def norm_parts(v):
    center = v - jnp.mean(v, -1, keepdims=True)
    inv = lax.rsqrt(jnp.mean(center * center, -1, keepdims=True) + EPSILON)
    return center * inv, inv


def gelu_parts(v):
    square = v * v
    curve = jnp.tanh(GELU_A * (v + GELU_B * v * square))
    return 0.5 * v * (1.0 + curve), 0.5 * (1.0 + curve) + 0.5 * v * (1.0 - curve * curve) * (GELU_A * (1.0 + 3.0 * GELU_B * square))


def middle_kernel(seqs, *refs):
    given, (wo_hbm, wu_hbm, wd_hbm, ws_hbm, c0_hbm, c1_hbm, c2_hbm), refs = refs[:8], refs[8:15], refs[15:]
    far = refs[:16]
    dnorm_ref, dctx_ref, col_ref, stat_ref = refs[16:20]
    own = refs[20:36]
    (otok_ref, ochr_ref, nlow_ref, hid_ref, slow_ref, plow_ref, mprev_ref, merged_ref, mnext_ref, dmix_ref, dfus_ref, dlow_ref, drai_ref, datt_ref,
     din_ref, dpool_ref) = own
    (
     wo_ref, wu_ref, wd_ref, ws_ref, taps, acc, edge, before, after, dside, dchar, slope_ref, hat0, hat1, state_ref, dstate_ref,
     w_sem, e_send, b_recv, a_recv, o_sem, *held, i_sem) = refs[36:]
    x_ref, clow_ref, nrm_ref, pooled_ref, gtok_ref, gchr_ref, ctx_ref, lse_ref = held

    def take(*ks):
        for k in ks:
            pltpu.make_async_copy(given[k], held[k], i_sem.at[k]).wait()

    for k in range(3):
        pltpu.make_async_copy(given[k], held[k], i_sem.at[k]).start()

    def put(*ks):
        for k in ks:
            pltpu.make_async_copy(own[k], far[k], o_sem.at[k]).start()

    me = lax.axis_index("seq")
    dp = lax.axis_index("dp")
    n = lax.axis_size("seq")
    rows, width = x_ref.shape
    toks = rows // seqs
    wide = 2 * width
    loads = [
        pltpu.make_async_copy(src, dst, w_sem.at[k]) for k, (src, dst) in enumerate((
            (wo_hbm, wo_ref), (wu_hbm, wu_ref), (wd_hbm, wd_ref), (ws_hbm, ws_ref), (c1_hbm, taps.at[1]), (c0_hbm, taps.at[0]), (c2_hbm, taps.at[2]),
        ))
    ]
    loads[0].start()
    for k in range(3, 8):
        pltpu.make_async_copy(given[k], held[k], i_sem.at[k]).start()
    for load in loads[1:]:
        load.start()
    edge[...] = jnp.zeros_like(edge)
    right, left = (dp, me + 1), (dp, me - 1)
    has_l, has_r = me > 0, me < n - 1
    bar = pltpu.get_barrier_semaphore()
    pl.when(has_l)(lambda: pl.semaphore_signal(bar, inc=1, device_id=left, device_id_type=MESH))
    pl.when(has_r)(lambda: pl.semaphore_signal(bar, inc=1, device_id=right, device_id_type=MESH))
    pl.semaphore_wait(bar, has_l.astype(jnp.int32) + has_r.astype(jnp.int32))

    def send(k):
        def to_right():
            return pltpu.make_async_remote_copy(
                src_ref=edge.at[k, 0], dst_ref=before.at[k], send_sem=e_send.at[k, 0], recv_sem=b_recv.at[k], device_id=right, device_id_type=MESH)

        def to_left():
            return pltpu.make_async_remote_copy(
                src_ref=edge.at[k, 1], dst_ref=after.at[k], send_sem=e_send.at[k, 1], recv_sem=a_recv.at[k], device_id=left, device_id_type=MESH)

        return to_right, to_left

    def start(k, ref):
        for s in range(seqs):
            edge[k, 0, s : s + 1, :] = ref[(s + 1) * toks - 16 : (s + 1) * toks, :].astype(F32)[15:16]
            edge[k, 1, s : s + 1, :] = ref[s * toks : s * toks + 16, :].astype(F32)[0:1]
        to_right, to_left = send(k)
        pl.when(has_r)(lambda: to_right().start())
        pl.when(has_l)(lambda: to_left().start())

    def finish(k):
        to_right, to_left = send(k)
        pl.when(has_r)(lambda: to_left().wait_recv())
        pl.when(has_l)(lambda: to_right().wait_recv())
        pl.when(has_r)(lambda: to_right().wait_send())
        pl.when(has_l)(lambda: to_left().wait_send())

    def shifts(k, ref, prev_ref, next_ref):
        for j in range(0, wide, 512):
            x = ref[:, j : j + 512].astype(F32)
            at = lax.broadcasted_iota(jnp.int32, x.shape, 0)
            prev, follow = pltpu.roll(x, 1, 0), pltpu.roll(x, rows - 1, 0)
            for s in range(seqs):
                b = jnp.where(has_l, before[k, s : s + 1, j : j + 512], 0.0)
                a = jnp.where(has_r, after[k, s : s + 1, j : j + 512], 0.0)
                prev = jnp.where(at == s * toks, b, prev)
                follow = jnp.where(at == (s + 1) * toks - 1, a, follow)
            prev_ref[:, j : j + 512] = prev.astype(BF)
            next_ref[:, j : j + 512] = follow.astype(BF)

    chunk = 768
    take(0, 1, 2)
    loads[0].wait()
    hat, inv0 = norm_parts(x_ref[...].astype(F32) + dot(clow_ref[...], wo_ref[...]))
    hat0[...] = hat
    normed = hat * nrm_ref[0:1, :] + nrm_ref[1:2, :]
    nlow_ref[...] = normed.astype(BF)
    loads[1].wait()

    def raise_part(j, _):
        cols = pl.ds(pl.multiple_of(j * chunk, chunk), chunk)
        hidden, slope = gelu_parts(dot(nlow_ref[...], wu_ref[:, cols]))
        hid_ref[:, cols] = hidden.astype(BF)
        slope_ref[:, cols] = slope
        return 0

    lax.fori_loop(0, 4 * width // chunk, raise_part, 0)
    loads[2].wait()
    hat, inv1 = norm_parts(normed + dot(hid_ref[...], wd_ref[...]))
    hat1[...] = hat
    state = hat * nrm_ref[2:3, :] + nrm_ref[3:4, :]
    state_ref[...] = state
    loads[3].wait()
    take(3, 4, 5, 6, 7)
    slow = state.astype(BF)
    plow = pooled_ref[...].astype(BF)
    slow_ref[...] = slow
    plow_ref[...] = plow
    merged_ref[:, :width] = dot(slow, ws_ref[0]).astype(BF)
    merged_ref[:, width:] = dot(plow, ws_ref[1]).astype(BF)
    start(0, merged_ref)
    loads[4].wait()

    def centre(j, _):
        cols = pl.ds(pl.multiple_of(j * 512, 512), 512)
        acc[:, cols] = dot(merged_ref[...], taps[1, :, cols])
        return 0

    lax.fori_loop(0, wide // 512, centre, 0)
    finish(0)
    shifts(0, merged_ref, mprev_ref, mnext_ref)
    loads[5].wait()
    loads[6].wait()

    def sides(j, _):
        cols = pl.ds(pl.multiple_of(j * 512, 512), 512)
        acc[:, cols] += dot(mprev_ref[...], taps[0, :, cols]) + dot(mnext_ref[...], taps[2, :, cols])
        return 0

    lax.fori_loop(0, wide // 512, sides, 0)
    for part, (base_ref, grad_ref, out_ref) in enumerate(((state_ref, gtok_ref, otok_ref), (pooled_ref, gchr_ref, ochr_ref))):
        mixed = acc[:, part * width : (part + 1) * width]
        gated, slope = gelu_parts(mixed)
        r = 4 + 2 * part
        out, dsum, dgain, dshift = norm_both(base_ref[...] + gated, nrm_ref[r : r + 1, :], nrm_ref[r + 1 : r + 2, :], grad_ref[...].astype(F32))
        out_ref[...] = out.astype(BF)
        dnorm_ref[r : r + 1, :] = dgain
        dnorm_ref[r + 1 : r + 2, :] = dshift
        dmix_ref[:, part * width : (part + 1) * width] = (dsum * slope).astype(BF)
        if part == 0:
            dstate_ref[...] = dsum
        else:
            dchar[...] = dsum
    start(1, dmix_ref)
    put(*range(10))

    def centre_back(j, _):
        cols = pl.ds(pl.multiple_of(j * 512, 512), 512)
        acc[:, cols] = dot_t(dmix_ref[...], taps[1, cols, :])
        return 0

    lax.fori_loop(0, wide // 512, centre_back, 0)
    finish(1)
    shifts(1, dmix_ref, dside.at[0], dside.at[1])

    def sides_back(j, _):
        cols = pl.ds(pl.multiple_of(j * 512, 512), 512)
        dfus_ref[:, cols] = (acc[:, cols] + dot_t(dside[1], taps[0, cols, :]) + dot_t(dside[0], taps[2, cols, :])).astype(BF)
        return 0

    lax.fori_loop(0, wide // 512, sides_back, 0)
    dpool_ref[...] = (dchar[...] + dot_t(dfus_ref[:, width:], ws_ref[1])).astype(BF)
    put(10, 15)
    dstate = dstate_ref[...] + dot_t(dfus_ref[:, :width], ws_ref[0])
    dsum, dnorm_ref[2:3, :], dnorm_ref[3:4, :] = norm_back(hat1[...], inv1, nrm_ref[2:3, :], dstate)
    dlow_ref[...] = dsum.astype(BF)
    dstate_ref[...] = dsum
    put(11)

    def lower_part(j, _):
        cols = pl.ds(pl.multiple_of(j * chunk, chunk), chunk)
        drai_ref[:, cols] = (dot_t(dlow_ref[...], wd_ref[cols, :]) * slope_ref[:, cols]).astype(BF)
        return 0

    lax.fori_loop(0, 4 * width // chunk, lower_part, 0)
    put(12)
    dsum, dnorm_ref[0:1, :], dnorm_ref[1:2, :] = norm_back(hat0[...], inv0, nrm_ref[0:1, :], dstate_ref[...] + dot_t(drai_ref[...], wu_ref[...]))
    din_ref[...] = dsum
    datt_ref[...] = dsum.astype(BF)
    put(13, 14)
    context_kernel(datt_ref, wo_ref, ctx_ref, lse_ref, dctx_ref, col_ref, stat_ref)
    for k in range(16):
        pltpu.make_async_copy(own[k], far[k], o_sem.at[k]).wait()


def middle(seqs, x, clow, context, lse, pooled, grad_token, grad_char, nrm, w_out, w_up, w_down, w_stream, w_conv, cid):
    rows, width = x.shape
    wide, ff = 2 * width, 4 * width
    pairs, toks = lse.shape[1:3]
    here = pl.BlockSpec(memory_space=pltpu.VMEM)
    far = pl.BlockSpec(memory_space=pl.ANY)
    low, full = (lambda c: jax.ShapeDtypeStruct((rows, c), BF)), jax.ShapeDtypeStruct((rows, width), F32)
    D = pltpu.SemaphoreType.DMA
    f = lambda *s: pltpu.VMEM(s, F32)
    v = lambda *s: pltpu.VMEM(s, BF)
    given = (x, clow, nrm, pooled, grad_token, grad_char, context, lse)
    large = [low(width)] * 3 + [low(ff), low(width), low(width)] + [low(wide)] * 5 + [low(width), low(ff), low(width), full, low(width)]
    return pl.pallas_call(
        functools.partial(middle_kernel, seqs),
        out_shape=large + [
            jax.ShapeDtypeStruct((8, width), F32), jax.ShapeDtypeStruct((seqs, toks, width), BF), jax.ShapeDtypeStruct((seqs, pairs, toks, 4), F32),
            jax.ShapeDtypeStruct((seqs * pairs * 4, toks), F32),
        ],
        in_specs=[far] * 15,
        out_specs=[far] * 16 + [here] * 4,
        scratch_shapes=[pltpu.VMEM(a.shape, a.dtype) for a in large] + [
            v(*w_out.shape), v(*w_up.shape), v(*w_down.shape), v(*w_stream.shape), v(3, wide, wide), f(rows, wide), f(2, 2, 8, wide),
            f(2, 8, wide), f(2, 8, wide), v(2, rows, wide), f(rows, width), f(rows, ff), f(rows, width), f(rows, width), f(rows, width), f(rows, width),
            D((7,)), D((2, 2)), D((2,)), D((2,)), D((16,)),
        ] + [pltpu.VMEM(a.shape, a.dtype) for a in given] + [D((8,))],
        compiler_params=pltpu.CompilerParams(collective_id=cid, has_side_effects=True, vmem_limit_bytes=62 << 20),
    )(*given, w_out, w_up, w_down, w_stream, *w_conv)


RZ, RY, RC = 4, 2, 2
PW = 384
PR = 48
LD, LX, LY, LH, LF = 2, 8, 12, 3, 25
HRING = LY + 1
PER, PK = 11, 3
JOB = 6


Group = collections.namedtuple("Group", ("left", "parts", "right", "col", "cols", "out", "lead", "base", "at"))
GRU, TABLE, TINY = 5, 4, 8


def piece_groups(taps):
    rows = [(6 + k, 2, 5, 0, 4, 7, i, 0) for i, k in enumerate(taps)]
    rows += [(4, 1, 4, 0, 2, 6, 0, 0), (5, 1, 4, 768, 2, 6, 1, 0), (3, 4, 3, 0, 2, 3, None, 0), (2, 1, 2, 0, 8, 2, None, 0), (1, 1, 1, 0, 2, 1, None, 0),
             (0, 1, 0, 0, 2, 0, None, 0), (0, 1, 6, 0, 4, 0, None, 2)]
    out, at = [], 0
    for r in rows:
        out.append(Group(*r, at))
        at += r[1] * r[4]
    return tuple(out), at


MISC = (((GRU, 0), (GRU, 1), (GRU, 2)), ((GRU, 3), (TABLE, 0), (TABLE, 1)), ((TABLE, 2), (TINY, 0), (None, 0)))


def reduce_kernel(npieces, groups, *refs):
    out_ref, dkv_ref = refs[24:26]
    width = refs[0].shape[1]
    dk_ref, dv_ref = dkv_ref.at[:, pl.ds(0, width)], dkv_ref.at[:, pl.ds(width, width)]
    qa_ref, dca_ref = refs[22:24]
    held, l_sem = refs[-23:-1], refs[-1]
    loads = [pltpu.make_async_copy(a, b, l_sem.at[k]) for k, (a, b) in enumerate(zip(refs[:22], held))]
    first = {}
    for g in groups:
        for k in (g.left, 9 + g.right):
            first.setdefault(k, g.at)

    for k in (8, 7, 6, 14, 20, 21, 4, 5, 13, 3, 12, 2, 11, 1, 10, 0, 9, 15, 16, 17, 18, 19):
        loads[k].start()
    lhs, rhs = held[:9], tuple(held[9:15]) + (dkv_ref,)
    emb_ref, dpre_ref, demb_ref, ids_ref, tiny_ref, kv_ref, stat_ref = held[15:]
    (lt, part, r0, held, r1, r2, up, dn, fin, fx,
     d_send, d_recv, x_send, x_recv, y_send, y_recv, u_send, u_recv, n_send, n_recv, f_send, f_recv, qbuf, cbuf, dk_acc, dv_acc, q_sem, c_sem) = refs[26:-23]
    dp = lax.axis_index("dp")
    me = lax.axis_index("seq")
    c = lax.rem(me, RC)
    y = lax.rem(lax.div(me, RC), RY)
    z = lax.div(me, RC * RY)

    def to(zz, yy, cc):
        return (dp, (zz * RY + yy) * RC + cc)

    sib, ynb, zup, zdn, xnb = to(z, y, 1 - c), to(z, 1 - y, c), to(z + 1, y, c), to(z - 1, y, c), (1 - dp, me)
    bar = pltpu.get_barrier_semaphore()
    for where in (sib, ynb, xnb):
        pl.semaphore_signal(bar, inc=1, device_id=where, device_id_type=MESH)
    pl.when(z > 0)(lambda: pl.semaphore_signal(bar, inc=1, device_id=zdn, device_id_type=MESH))
    pl.when(z < RZ - 1)(lambda: pl.semaphore_signal(bar, inc=1, device_id=zup, device_id_type=MESH))
    pl.semaphore_wait(bar, 3 + (z > 0).astype(jnp.int32) + (z < RZ - 1).astype(jnp.int32))

    def copy(src, dst, send, recv, where):
        return pltpu.make_async_remote_copy(src_ref=src, dst_ref=dst, send_sem=send, recv_sem=recv, device_id=where, device_id_type=MESH)

    def d2d(t):
        b, k = lax.rem(t, LD + 1), lax.rem(t, 2 * LD)
        return copy(part.at[b, :, :, 1 - c], r0.at[k], d_send.at[b], d_recv.at[k], sib)

    def far(t):
        return lax.div(t, PER) * PK + lax.div(lax.rem(t, PER), 3)

    def mi(t):
        m = lax.rem(t, PER)
        return lax.div(t, PER) * (PER - PK) + m - jnp.minimum(lax.div(m + dp, 3), PK)

    def across(t):
        return copy(held.at[lax.rem(t, HRING)], r1.at[far(t)], x_send.at[t], x_recv.at[t], xnb)

    def along_y(t):
        return copy(held.at[lax.rem(t, HRING), :, 1 - y], r2.at[mi(t)], y_send.at[t], y_recv.at[t], ynb)

    def final(t):
        return copy(fin.at[t], fx.at[t], f_send.at[t], f_recv.at[t], xnb)

    def go_up(t, k):
        src = r2.at[mi(t), pl.ds(k + 1, RZ - 1 - k)] if k == 0 else up.at[mi(t), pl.ds(k, RZ - 1 - k)]
        return copy(src, up.at[mi(t), pl.ds(k, RZ - 1 - k)], u_send.at[t], u_recv.at[t], zup)

    def from_below(t, k):
        ref = up.at[mi(t), pl.ds(k - 1, RZ - k)]
        return copy(ref, ref, u_send.at[t], u_recv.at[t], zdn)

    def go_down(t, k):
        src = r2.at[mi(t), pl.ds(0, k)] if k == RZ - 1 else dn.at[mi(t), pl.ds(0, k)]
        return copy(src, dn.at[mi(t), pl.ds(0, k)], n_send.at[t], n_recv.at[t], zdn)

    def from_above(t, k):
        ref = dn.at[mi(t), pl.ds(0, k + 1)]
        return copy(ref, ref, n_send.at[t], n_recv.at[t], zup)

    def add(a, b):
        return (a.astype(F32) + b.astype(F32)).astype(BF)

    def live(t):
        return jnp.logical_and(t >= 0, t < npieces)

    def route(t):
        m = lax.rem(t, PER)
        return jnp.where(m < 3 * PK, lax.rem(m, 3), 0)

    def mine(t):
        r = route(t)
        return jnp.logical_or(r == 0, r - 1 == dp)

    def finish(t):
        r = route(t)

        @pl.when(r == 0)
        def _():
            final(t).wait_recv()
            out_ref[t] = add(fin[t], fx[t])

        @pl.when(jnp.logical_and(r > 0, r - 1 == dp))
        def _():
            out_ref[t] = fin[t]

        @pl.when(jnp.logical_and(r > 0, r - 1 != dp))
        def _():
            final(t).wait_recv()
            out_ref[t] = fx[t]

        pl.when(mine(t))(lambda: final(t).wait_send())

    def sum_up(t):
        i = mi(t)
        for k in range(RZ):
            @pl.when(z == k)
            def _(k=k):
                if k > 0:
                    from_below(t, k).wait_recv()
                    for q in range(k + 1, RZ):
                        up[i, q - 1] = add(up[i, q - 1], r2[i, q])
                if k < RZ - 1:
                    go_up(t, k).start()

    def sum_down(t):
        i = mi(t)
        for k in range(RZ):
            @pl.when(z == k)
            def _(k=k):
                if k < RZ - 1:
                    from_above(t, k).wait_recv()
                    for q in range(k):
                        dn[i, q] = add(dn[i, q], r2[i, q])
                if k > 0:
                    go_down(t, k).start()

    def close(t):
        i = mi(t)
        for k in range(RZ):
            @pl.when(z == k)
            def _(k=k):
                total = r2[i, k].astype(F32)
                if k > 0:
                    total = total + up[i, k - 1].astype(F32)
                    go_down(t, k).wait_send()
                if k < RZ - 1:
                    total = total + dn[i, k].astype(F32)
                    go_up(t, k).wait_send()
                fin[t] = total.astype(BF)
        final(t).start()

    def join_y(t):
        i = mi(t)
        along_y(t).wait_recv()
        along_y(t).wait_send()
        h = lax.rem(t, HRING)
        for q in range(RZ):
            r2[i, q] = add(r2[i, q], held[h, q, y])

    def join_x(t):
        h = lax.rem(t, HRING)
        across(t).wait_recv()
        for q in range(RZ):
            held[h, q] = add(held[h, q], r1[far(t), q])
        along_y(t).start()

    def join_core(t):
        b, k = lax.rem(t, LD + 1), lax.rem(t, 2 * LD)
        h = lax.rem(t, HRING)
        d2d(t).wait_recv()
        d2d(t).wait_send()
        for q in range(RZ):
            held[h, q] = add(part[b, q, :, c], r0[k, q])
        pl.when(route(t) == 0)(lambda: along_y(t).start())
        pl.when(jnp.logical_not(mine(t)))(lambda: across(t).start())

    def turn(ref):
        n = ref.shape[0]
        for k in range(0, ref.shape[1], 384):
            lt[k // PR : k // PR + 8, :, :n] = ref[:, k : k + 384].T.reshape(8, PR, n)

    def make(t):
        b = lax.rem(t, LD + 1)
        for g in groups:
            @pl.when(jnp.logical_and(t >= g.at, t < g.at + g.parts * g.cols))
            def _(g=g):
                i = t - g.at
                j, cb = lax.div(i, g.cols), lax.rem(i, g.cols)

                @pl.when(i == 0)
                def _():
                    for k in (g.left, 9 + g.right):
                        if k < 15 and first[k] == g.at:
                            loads[k].wait()
                    turn(lhs[g.left])

                right = rhs[g.right][:, pl.ds(pl.multiple_of(g.col + cb * PW, PW), PW)]
                for q in range(RZ // 2):
                    left = jnp.concatenate([lt[(8 * q + s) * g.parts + j] for s in range(8)], 0)
                    part[b, 2 * q : 2 * q + 2] = dot(left, right).astype(BF).reshape(2, RY, RC, PR, PW)
        for m, trio in enumerate(MISC):
            @pl.when(t == npieces - len(MISC) + m)
            def _(m=m, trio=trio):
                if m == 0:
                    for k in range(15, 20):
                        loads[k].wait()
                for i, (kind, cb) in enumerate(trio):
                    if kind == GRU:
                        val = wgrad(emb_ref[...], dpre_ref[:, cb * PW : (cb + 1) * PW]).astype(BF).reshape(RZ, RY, RC, 16, PW)
                    elif kind == TABLE:
                        unit = lax.broadcasted_iota(jnp.int32, (ids_ref.shape[0], PW), 1) + cb * PW
                        hot = jnp.where(unit == ids_ref[...], 1.0, 0.0).astype(BF)
                        val = wgrad(demb_ref[...], hot).astype(BF).reshape(RZ, RY, RC, 16, PW)
                    elif kind == TINY:
                        val = tiny_ref[...].reshape(RZ, RY, RC, 16, PW)
                    else:
                        val = jnp.zeros((RZ, RY, RC, 16, PW), BF)
                    part[b, :, :, :, 16 * i : 16 * i + 16, :] = val
        d2d(t).start()

    pairs = HEADS // 2
    toks = kv_ref.shape[1]
    half = qa_ref.shape[1] // 2
    jobs = 2 * pairs * kv_ref.shape[0]

    def fetch(i):
        s, p, h = lax.div(i, 2 * pairs), lax.rem(lax.div(i, 2), pairs), lax.rem(i, 2)
        cols = pl.ds(pl.multiple_of(p * 2 * HDIM, 2 * HDIM), 2 * HDIM)
        part = pl.ds(pl.multiple_of(h * half, half), half)
        return (pltpu.make_async_copy(qa_ref.at[s, part, cols], qbuf.at[h], q_sem.at[h]), pltpu.make_async_copy(dca_ref.at[s, part, cols], cbuf.at[h], c_sem.at[h]))

    def key_work(i):
        s, p, h = lax.div(i, 2 * pairs), lax.rem(lax.div(i, 2), pairs), lax.rem(i, 2)
        at = pl.multiple_of(p * 2 * HDIM, 2 * HDIM)
        slots = half // toks

        @pl.when(i == 0)
        def _():
            loads[20].wait()
            loads[21].wait()


        @pl.when(i + 1 < jobs)
        def _():
            for load in fetch(i + 1):
                load.start()

        for load in fetch(i):
            load.wait()
        scale = HDIM ** -0.5
        queries, dctx = qbuf[h], cbuf[h]

        def spread(k):
            at = (s * pairs + p) * 4 + k
            one = lambda r: jnp.concatenate([stat_ref[h * slots + d, pl.ds(r, 1), :] for d in range(slots)], 1)
            return jnp.concatenate([jnp.broadcast_to(one(at), (toks, half)), jnp.broadcast_to(one(at + 1), (toks, half))], 0)

        prob = jnp.exp(dot_t(pair_rows(kv_ref[s, :, pl.ds(at + width, 2 * HDIM)] * scale), queries) - spread(0))
        dv = dot(prob.astype(BF), dctx)
        dprob = dot_t(pair_rows(kv_ref[s, :, pl.ds(at + 2 * width, 2 * HDIM)]), dctx)
        dk = dot((prob * (dprob - spread(2))).astype(BF), queries)

        @pl.when(h == 0)
        def _():
            dk_acc[...] = dk
            dv_acc[...] = dv

        @pl.when(h == 1)
        def _():
            rows = pl.ds(pl.multiple_of(s * toks, toks), toks)
            cols = pl.ds(at, 2 * HDIM)
            dk_ref[rows, cols] = (pair_lanes(dk_acc[...] + dk) * scale).astype(BF)
            dv_ref[rows, cols] = pair_lanes(dv_acc[...] + dv).astype(BF)

    for load in fetch(0):
        load.start()

    def tick(T, _):
        def do(t, f, cond=None):
            ok = live(t)
            pl.when(ok if cond is None else jnp.logical_and(ok, cond(t)))(lambda: f(t))

        do(T - LF, finish)
        do(T - LY - z * LH, sum_up, mine)
        do(T - LY - (RZ - 1 - z) * LH, sum_down, mine)
        do(T - LY - (RZ - 1) * LH, close, mine)
        do(T - LY + 1, join_y, mine)
        do(T - LX, join_x, lambda t: jnp.logical_and(route(t) > 0, mine(t)))
        do(T - LX, lambda t: across(t).wait_send(), lambda t: jnp.logical_not(mine(t)))
        do(T - LD, join_core)
        do(T, make)
        job = T - JOB
        pl.when(jnp.logical_and(job >= 0, job < jobs))(lambda: key_work(job))
        return 0

    lax.fori_loop(0, npieces + LF + 1, tick, 0)


def finish_kernel(groups, *refs):
    held, l_sem = refs[16:21], refs[21]
    loads = [pltpu.make_async_copy(a, b, l_sem.at[k]) for k, (a, b) in enumerate(zip(refs[:5], held))]
    for load in loads:
        load.start()
    pieces, dq, dkv, w, base = held
    outs = refs[5:16]
    loads[0].wait()
    for g in groups:
        for j in range(g.parts):
            for cb in range(g.cols):
                rows, cols = slice(j * PR, (j + 1) * PR), slice((g.base + cb) * PW, (g.base + cb + 1) * PW)
                val = pieces[g.at + j * g.cols + cb].astype(F32)
                if g.lead is None:
                    outs[g.out][rows, cols] = val
                else:
                    outs[g.out][g.lead, rows, cols] = val
    first = groups[-1].at + groups[-1].parts * groups[-1].cols
    bias, norms, dinput = outs[8:]
    for m, trio in enumerate(MISC):
        for i, (kind, cb) in enumerate(trio):
            val = pieces[first + m, 16 * i : 16 * i + 16, :].astype(F32)
            if kind == TINY:
                bias[...] = val[0:1, : bias.shape[1]]
                for k in range(4):
                    norms[k] = val[1 + 2 * k : 3 + 2 * k, : norms.shape[2]]
            elif kind is not None:
                n = min(PW, outs[kind].shape[1] - cb * PW)
                outs[kind][:, cb * PW : cb * PW + n] = val[:, :n]
    n = dq.shape[1]
    for load in loads[1:]:
        load.wait()
    dinput[...] = base[...] + dot_t(dq[...], w[:, :n]) + dot_t(dkv[:, :n], w[:, n : 2 * n]) + dot_t(dkv[:, n:], w[:, 2 * n :])


def reduce_all(lhs, rhs, emb, dpre, demb, ids, kv, stat, queries, dctx, w_qkv, dsum, g_bias, g_norms, n_table, nseq, cid, taps=(0, 1, 2)):
    width = lhs[0].shape[1]
    per = g_bias.shape[0] // nseq
    tiny = jnp.concatenate([
        jnp.pad(g_bias.reshape(nseq, 1, per), ((0, 0), (0, 0), (0, PW - per))),
        jnp.pad(g_norms.reshape(8, nseq, -1).transpose(1, 0, 2), ((0, 0), (0, 7), (0, PW - width // nseq))),
    ], 1).astype(BF)
    groups, npieces = piece_groups(taps)
    npieces += len(MISC)
    dense = -(-npieces // PER) * (PER - PK)
    D = pltpu.SemaphoreType.DMA
    v = lambda *s: pltpu.VMEM(s, BF)
    spec = pl.BlockSpec(memory_space=pltpu.VMEM)
    operands = (*lhs, *rhs, emb, dpre, demb, ids, tiny, kv, stat)
    pieces, dkv = pl.pallas_call(
        functools.partial(reduce_kernel, npieces, groups),
        out_shape=[jax.ShapeDtypeStruct((npieces, PR, PW), BF), jax.ShapeDtypeStruct((lhs[0].shape[0], 2 * width), BF)],
        in_specs=[pl.BlockSpec(memory_space=pl.ANY)] * 24,
        out_specs=[spec] * 2,
        scratch_shapes=[
            v(64, PR, lhs[0].shape[0]),
            v(LD + 1, RZ, RY, RC, PR, PW), v(2 * LD, RZ, RY, PR, PW), v(HRING, RZ, RY, PR, PW), v(PK * (npieces // PER + 1), RZ, RY, PR, PW),
            v(dense, RZ, PR, PW), v(dense, RZ - 1, PR, PW), v(dense, RZ - 1, PR, PW), v(npieces, PR, PW), v(npieces, PR, PW),
            D((LD + 1,)), D((2 * LD,)), D((npieces,)), D((npieces,)), D((npieces,)), D((npieces,)),
            D((npieces,)), D((npieces,)), D((npieces,)), D((npieces,)), D((npieces,)), D((npieces,)),
            v(2, queries.shape[1] // 2, 2 * HDIM), v(2, queries.shape[1] // 2, 2 * HDIM),
            pltpu.VMEM((2 * kv.shape[1], 2 * HDIM), F32), pltpu.VMEM((2 * kv.shape[1], 2 * HDIM), F32), D((2,)), D((2,)),
        ] + [pltpu.VMEM(a.shape, a.dtype) for a in operands] + [D((len(operands),))],
        compiler_params=pltpu.CompilerParams(collective_id=cid, has_side_effects=True, vmem_limit_bytes=62 << 20),
    )(*operands, queries, dctx)
    f = lambda *s: jax.ShapeDtypeStruct(s, F32)
    wide = 2 * width
    share = width // nseq
    return pl.pallas_call(
        functools.partial(finish_kernel, groups),
        out_shape=[
            f(share, 3 * width), f(share, width), f(share, 4 * width), f(4 * share, width), f(16, n_table), f(16, 4 * PW),
            f(2, share, width), f(3, 2 * share, wide), f(1, per), f(4, 2, share), f(*dsum.shape),
        ],
        in_specs=[pl.BlockSpec(memory_space=pl.ANY)] * 5,
        out_specs=[spec] * 11,
        scratch_shapes=[pltpu.VMEM(a.shape, a.dtype) for a in (pieces, rhs[0], dkv, w_qkv, dsum)] + [D((5,))],
        compiler_params=vmem(62),
    )(pieces, rhs[0], dkv, w_qkv, dsum)


def scatter(total, axis):
    part = lax.psum_scatter(total, "seq", scatter_dimension=axis, tiled=True)
    return lax.psum(part, "dp").astype(F32)


def body(tokens, char_ids, span_lengths, script_group, w_qkv, w_out, w_up, w_down, char_table, w_gru, gru_bias, w_stream, w_conv, norms, grad_token, grad_char):
    nseq, planes = lax.axis_size("seq"), lax.axis_size("dp")
    seqs, toks, width = tokens.shape
    chars = char_ids.shape[1]
    rows = seqs * toks
    bias_n, norm_n = gru_bias.shape[0], norms.shape[2]
    small = jnp.concatenate([gru_bias, norms.reshape(-1)])
    small = jnp.pad(small, (0, 2048 - small.shape[0])).reshape(16, 128)
    conv0, w_down, conv1, conv2, w_out, w_stream, w_qkv, w_gru, char_table, small = gather(
        [(w_conv, 0, 1, 0), (w_down, 0, 1, None), (w_conv, 0, 2, 1), (w_conv, 0, 2, 2), (w_out, 0, 0, None), (w_stream, 1, 0, None), (w_qkv, 0, 0, None),
         (w_gru, 0, 0, None), (char_table, 0, 0, None), (small, 0, 0, None)], 1, planes, nseq
    )
    w_up, small = lax.optimization_barrier((w_up, small))
    w_up = lax.all_gather(w_up, "seq", axis=0, tiled=True)
    w_conv = (conv0, conv1, conv2)
    small = small.reshape(nseq, 2048)
    bias = small[:, :bias_n].reshape(-1).astype(F32)
    nrm = small[:, bias_n : bias_n + 8 * norm_n].reshape(nseq, 4, 2, norm_n).transpose(1, 2, 0, 3).reshape(4, 2, width).astype(F32)

    x_low = tokens.reshape(rows, width)
    qkv = dot(x_low, w_qkv).astype(BF)
    qkv3 = qkv.reshape(seqs, toks, 3 * width)

    char_rows = (char_ids + script_group[:, None] * GROUP_CHARS).reshape(seqs * chars, 1)
    span = span_lengths[:, 0]
    span_ends = jnp.cumsum(span, -1)
    starts = span_ends - span
    ends_col = jnp.stack([starts, span_ends], -1).reshape(rows, 2)
    ends_row = jnp.pad(jnp.stack([starts, span_ends], 1), ((0, 0), (0, 6), (0, 0))).reshape(seqs * 8, toks)
    block = pltpu.VMEM((2 * HB, chars, 128), F32)
    full = lambda *d: jax.ShapeDtypeStruct(d, F32)
    keys, values, tot_all, pooled, chunk, pre, prev, embedded = gather_with(
        functools.partial(forward_run, seqs), [(qkv3, 1, 0, (width, width)), (qkv3, 1, 0, (2 * width, width))],
        2, planes, nseq, (char_rows, char_table, w_gru, bias.reshape(1, -1), ends_col), (), [full(rows, width), full(seqs * 4 * NCH, HG)],
        [full(seqs * chars, 4 * HG), full(seqs * chars, width), jax.ShapeDtypeStruct((seqs * chars, char_table.shape[0]), BF)], [block] * 4,
    )
    own_q, keys = lax.optimization_barrier((qkv3[..., :width], keys))
    queries = lax.all_gather(own_q, "seq", axis=1, tiled=True)

    ctx3, ctx_low3, lse = attention_fwd(qkv3, keys, values)
    context, context_low = ctx3.reshape(rows, width), ctx_low3.reshape(rows, width)
    (out_token, out_char, normed_low, hidden, state_low, pooled_low, mprev, merged, mnext, dmixed_low, dfused, dlowered, draised_low, dattended,
     dinput_sum, dpooled, dnorm, dctx3, col, stat) = middle(
        seqs, x_low, context_low, context, lse, pooled, grad_token.reshape(rows, width), grad_char.reshape(rows, width), nrm.reshape(8, width),
        w_out, w_up, w_down, w_stream, w_conv, 5
    )
    length = nseq * toks
    dctx_all, stat_all, _, dbias, dq, dembed, dpre = gather_with(
        functools.partial(backward_run, seqs), [(dctx3, 1, 0, None), (stat, 0, 0, None)], 3, planes, nseq,
        (pre, prev, chunk, tot_all, dpooled, ends_row, own_q, dctx3, col, w_gru), (keys, values),
        [full(seqs * 8, 4 * HG), jax.ShapeDtypeStruct((seqs, toks, width), BF), jax.ShapeDtypeStruct(embedded.shape, BF)],
        [jax.ShapeDtypeStruct((seqs * chars, 4 * HG), BF)],
        [pltpu.VMEM((seqs * chars, width), F32), pltpu.VMEM((seqs * 2 * NCH, HG), F32)] + [block] * 2
        + [pltpu.VMEM((2, length, 2 * HDIM), BF)] * 2 + [pltpu.SemaphoreType.DMA((2,))] * 2,
    )
    g_bias = dbias.reshape(seqs, 8, 4 * HG)[:, 0].sum(0)

    g_norms = dnorm.reshape(4, 2, width)
    shape = (seqs, toks, width)
    if seq_dims(nseq) == (RZ, RY, RC) and planes == 2:
        lhs = (x_low, context_low, normed_low, hidden, state_low, pooled_low, mprev, merged, mnext)
        rhs = (dq.reshape(rows, width), dattended, draised_low, dlowered, dfused, dmixed_low)
        *owned, dinputs = reduce_all(
            lhs, rhs, embedded, dpre, dembed, char_rows, qkv3, stat_all.reshape(nseq, -1, toks), queries, dctx_all, w_qkv, dinput_sum, g_bias, g_norms, VOCAB_CHAR, nseq, 4
        )
        owned[8] = owned[8].reshape(-1)
        owned = [owned[k] for k in (0, 1, 2, 3, 4, 5, 8, 6, 7, 9)]
        owned = tuple(owned)
    else:
        stat_all = stat_all.reshape(nseq, seqs, HEADS // 2, 4, toks).transpose(1, 2, 3, 0, 4).reshape(seqs, HEADS // 2, 4, nseq * toks)
        dk, dv = attention_bwd(qkv3, queries, dctx_all, stat_all)
        dqkv = jnp.concatenate([dq, dk, dv], -1).reshape(rows, 3 * width)
        dinputs = dinput_sum + dot_t(dqkv, w_qkv)
        g_stream = [wgrad(state_low, dfused[:, :width]), wgrad(pooled_low, dfused[:, width:])]
        owned = (
            scatter(wgrad(x_low, dqkv).astype(BF), 0),
            scatter(wgrad(context_low, dattended).astype(BF), 0),
            scatter(wgrad(normed_low, draised_low).astype(BF), 0),
            scatter(wgrad(hidden, dlowered).astype(BF), 0),
            scatter(wgrad(dembed, (char_rows == jnp.arange(VOCAB_CHAR, dtype=jnp.int32)).astype(BF)).astype(BF), 0),
            scatter(wgrad(embedded, dpre).astype(BF), 0),
            scatter(g_bias.astype(BF), 0),
            scatter(jnp.stack(g_stream).astype(BF), 1),
            scatter(jnp.stack([wgrad(m, dmixed_low) for m in (mprev, merged, mnext)]).astype(BF), 1),
            scatter(g_norms.astype(BF), 2),
        )
    return (
        out_token.reshape(shape),
        out_char.reshape(shape),
        dinputs.reshape(shape),
    ) + owned


def solution(mesh):
    placed = (
        P("dp", "seq", None),
        P("dp", "seq"),
        P("dp", "seq", None),
        P("dp"),
        P("seq", None),
        P("seq", None),
        P("seq", None),
        P("seq", None),
        P("seq", None),
        P("seq", None),
        P("seq"),
        P(None, "seq", None),
        P(None, "seq", None),
        P(None, None, "seq"),
        P("dp", "seq", None),
        P("dp", "seq", None),
    )
    return jax.shard_map(
        body,
        mesh=mesh,
        in_specs=placed,
        out_specs=(
            P("dp", "seq", None),
            P("dp", "seq", None),
            P("dp", "seq", None),
            P("seq", None),
            P("seq", None),
            P("seq", None),
            P("seq", None),
            P("seq", None),
            P("seq", None),
            P("seq"),
            P(None, "seq", None),
            P(None, "seq", None),
            P(None, None, "seq"),
        ),
        check_vma=False,
    )
```

```python
import collections
import functools
import jax
import jax.numpy as jnp
from jax import lax
from jax.experimental import pallas as pl
from jax.experimental.pallas import tpu as pltpu
from jax.sharding import PartitionSpec as P

HEADS = 12
HDIM = 64
VOCAB_CHAR = 1000
GROUP_CHARS = 250
HG = 384
EPSILON = 1e-05
MESH = pl.DeviceIdType.MESH
BF = jnp.bfloat16
F32 = jnp.float32
NCH = 8
TOGETHER = 2
UNROLL = 8
SHARE = (1, 2, 3, 6)
HB = HG // 128

def seq_dims(n):
    return {16: (4, 2, 2), 32: (8, 4, 1)}.get(n, (n, 1, 1))


Move = collections.namedtuple("Move", ("array", "axis", "rows", "lead", "route"))


def gather_kernel(dims, planes, moves, n_arrays, task, *refs):
    Z, Y, C = dims
    n = len(moves)
    n_in, n_out = (task.n_in, task.n_out) if task else (0, 0)
    src, task_in = refs[:n_arrays], refs[n_arrays : n_arrays + n_in]
    refs = refs[n_arrays + n_in :]
    dst, task_out = refs[:n_arrays], refs[n_arrays : n_arrays + n_out]
    own_sem, recv, zs, ds, ys, ss, xs, *task_scratch = refs[n_arrays + n_out :]
    dp = lax.axis_index("dp")
    me = lax.axis_index("seq")
    c = lax.rem(me, C)
    y = lax.rem(lax.div(me, C), Y)
    z = lax.div(me, C * Y)
    up_z, down_z = z < Z - 1, z > 0

    def at(zz, yy, cc):
        return (zz * Y + yy) * C + cc

    def to(zz, yy, cc):
        return (dp, at(zz, yy, cc))

    def view(i, slot):
        m = moves[i]
        s = pl.ds(pl.multiple_of(slot * m.rows, m.rows), m.rows)
        ref = dst[m.array]
        return ref.at[s] if m.axis == 0 else ref.at[:, s]

    def mine(i):
        m = moves[i]
        if m.lead is None:
            return src[m.array]
        return src[m.array].at[:, :, pl.ds(*m.lead)] if isinstance(m.lead, tuple) else src[m.array].at[m.lead]

    def copy(i, slot, send, where, own=False):
        return pltpu.make_async_remote_copy(
            src_ref=mine(i) if own else view(i, slot), dst_ref=view(i, slot),
            send_sem=send, recv_sem=recv.at[i, slot], device_id=where, device_id_type=MESH)

    sib = to(z, y, 1 - c) if C == 2 else None
    xp = (1 - dp, me)
    use_x = planes == 2 and any(m.route for m in moves)
    some = sib if C == 2 else to(z, y, c)

    def owner(i):
        return None if not (use_x and moves[i].route) else dp == moves[i].route - 1

    def when(cond, f):
        if cond is None:
            f()
        else:
            pl.when(cond)(f)

    def both(a, b):
        return b if a is None else jnp.logical_and(a, b)

    nseq = Z * Y * C
    if task:
        push_all, *task_out = task_out
        push, p_send, p_recv, i_sem, *task_scratch = task_scratch
        n_held = n_in - task.n_stay
        held, task_scratch = task_scratch[:n_held], task_scratch[n_held:]
        loads = [pltpu.make_async_copy(a, b, i_sem.at[k]) for k, (a, b) in enumerate(zip(task_in[:n_held], held))]
        for load in loads:
            load.start()
    bar = pltpu.get_barrier_semaphore()
    if task:
        peers = [(None, (dp, lax.rem(me + k, nseq))) for k in range(1, nseq)]
    else:
        peers = [(z > 0, to(z - 1, y, c)), (z < Z - 1, to(z + 1, y, c))]
        if Y > 1:
            peers += [(y > 0, to(z, y - 1, c)), (y < Y - 1, to(z, y + 1, c))]
        if C == 2:
            peers.append((None, sib))
    if use_x:
        peers.append((None, xp))
    count = 0
    for cond, where in peers:
        when(cond, functools.partial(pl.semaphore_signal, bar, inc=1, device_id=where, device_id_type=MESH))
        count = count + (1 if cond is None else cond.astype(jnp.int32))
    pl.semaphore_wait(bar, count)
    if task:

        def pushed(k, slot, where):
            return pltpu.make_async_remote_copy(
                src_ref=push, dst_ref=push_all.at[slot], send_sem=p_send.at[k], recv_sem=p_recv.at[slot], device_id=where, device_id_type=MESH)

        def push_one(k, _):
            pushed(k, me, (dp, lax.rem(me + k, nseq))).start()
            return 0

        def push_wait(k, _):
            other = lax.rem(me + k, nseq)
            pushed(k, other, (dp, other)).wait_recv()
            pushed(k, me, (dp, other)).wait_send()
            return 0

    def work(point):
        if task:
            task.run(point, me, push, push_all, tuple(held) + tuple(task_in[n_held:]), task_out, task_scratch)

    def go_z(i, slot, up, sem, own=False):
        where = to(z + 1, y, c) if up else to(z - 1, y, c)
        pl.when(up_z if up else down_z)(lambda: copy(i, slot, sem, where, own).start())

    def go_y(i, slot, up, sem, own=False):
        where = to(z, y + 1, c) if up else to(z, y - 1, c)
        pl.when(y < Y - 1 if up else y > 0)(lambda: copy(i, slot, sem, where, own).start())

    def go_core(i, slot, own=False):
        if C == 2:
            copy(i, slot, ss.at[i, slot], sib, own).start()

    def wait_in(i, slot):
        copy(i, slot, ss.at[i, slot], some).wait_recv()

    for i in range(n):
        pltpu.make_async_copy(mine(i), view(i, me), own_sem.at[i]).start()

        def own_sends(i=i):
            go_z(i, me, True, zs.at[i, me], True)
            go_z(i, me, False, ds.at[i, 0], True)
            if Y > 1:
                go_y(i, me, True, ys.at[i, me], True)
                go_y(i, me, False, ds.at[i, 1], True)

        when(owner(i), own_sends)
        go_core(i, me, True)

    def arrive_z(zz, up):
        slot = at(zz, y, c)

        def one(i):
            wait_in(i, slot)
            go_z(i, slot, up, zs.at[i, slot])
            if Y > 1:
                go_y(i, slot, True, ys.at[i, slot])
                go_y(i, slot, False, ys.at[i, slot] if Y == 2 else xs.at[i, slot])
            if use_x and moves[i].route:
                copy(i, slot, xs.at[i, slot], xp).start()
            go_core(i, slot)

        for i in range(n):
            when(owner(i), functools.partial(one, i))

    def arrive_y(zz, yy, up):
        slot = at(zz, yy, c)

        def one(i):
            wait_in(i, slot)
            if Y > 2:
                go_y(i, slot, up, ys.at[i, slot])
            if use_x and moves[i].route:
                copy(i, slot, xs.at[i, slot], xp).start()
            go_core(i, slot)

        for i in range(n):
            when(owner(i), functools.partial(one, i))

    def all_y(zz):
        for t in range(1, Y):
            pl.when(y - t >= 0)(lambda: arrive_y(zz, y - t, True))
            pl.when(y + t < Y)(lambda: arrive_y(zz, y + t, False))

    if task:
        for load in loads:
            load.wait()
        work(0)
        push_all[me] = push[...]
        lax.fori_loop(1, nseq, push_one, 0)
    def step(s, _):
        pl.when(z - s >= 0)(lambda: arrive_z(z - s, True))
        pl.when(z + s < Z)(lambda: arrive_z(z + s, False))
        q = s - 1
        pl.when(z - q >= 0)(lambda: all_y(z - q))
        pl.when(jnp.logical_and(q > 0, z + q < Z))(lambda: all_y(z + q))
        return 0

    if task:
        for s in (1, 2):
            if s < Z:
                step(s, 0)
            if s == 1:
                lax.fori_loop(1, nseq, push_wait, 0)
            work(s)
        lax.fori_loop(3, Z, step, 0)
        work(3)
    else:
        lax.fori_loop(1, Z, step, 0)
    q = Z - 1
    pl.when(z - q >= 0)(lambda: all_y(z - q))
    pl.when(z + q < Z)(lambda: all_y(z + q))

    if use_x:

        def far(k, _):
            slot = at(lax.rem(z + lax.div(k, Y), Z), lax.rem(y + lax.rem(k, Y), Y), c)

            def one(i):
                wait_in(i, slot)
                go_core(i, slot)

            for i in range(n):
                if moves[i].route:
                    pl.when(dp != moves[i].route - 1)(functools.partial(one, i))
            return 0

        lax.fori_loop(1, Z * Y, far, 0)

    def drain(k, _):
        zz, yy = lax.div(k, Y), lax.rem(k, Y)
        slot = at(zz, yy, c)
        is_own = slot == me
        own_y = yy == y
        fz = jnp.logical_or(jnp.logical_and(zz <= z, up_z), jnp.logical_and(zz > z, down_z))
        for i in range(n):
            o = owner(i)
            if C == 2:
                wait_in(i, at(zz, yy, 1 - c))
                copy(i, slot, ss.at[i, slot], some).wait_send()
            sent = lambda sem: copy(i, slot, sem, some).wait_send()
            pl.when(both(o, jnp.logical_and(own_y, fz)))(lambda: sent(zs.at[i, slot]))
            if Y == 2:
                pl.when(both(o, jnp.logical_and(own_y, jnp.logical_or(jnp.logical_not(is_own), y < Y - 1))))(lambda: sent(ys.at[i, slot]))
            elif Y > 2:
                fy = jnp.logical_or(jnp.logical_and(yy <= y, y < Y - 1), jnp.logical_and(yy > y, y > 0))
                pl.when(both(o, fy))(lambda: sent(ys.at[i, slot]))
                fy2 = jnp.logical_and(jnp.logical_and(own_y, y > 0), jnp.logical_not(is_own))
                pl.when(both(o, fy2))(lambda: sent(xs.at[i, slot]))
            if use_x and moves[i].route:
                pl.when(both(o, jnp.logical_not(is_own)))(lambda: sent(xs.at[i, slot]))
        return 0

    lax.fori_loop(0, Z * Y, drain, 0)
    for i in range(n):
        pltpu.make_async_copy(mine(i), view(i, me), own_sem.at[i]).wait()
        o = owner(i)
        pl.when(both(o, down_z))(lambda: copy(i, me, ds.at[i, 0], some, True).wait_send())
        if Y > 1:
            pl.when(both(o, y > 0))(lambda: copy(i, me, ds.at[i, 1], some, True).wait_send())
    work(4)


Task = collections.namedtuple("Task", ("n_in", "n_stay", "n_out", "n_far", "run"))


def gather(arrays, cid, planes, nseq, task=None, inputs=(), outputs=(), scratch=()):
    dims = seq_dims(nseq)
    moves, shapes = [], []
    for k, (x, axis, route, lead) in enumerate(arrays):
        shape = list(x.shape[:-1] + lead[1:] if isinstance(lead, tuple) else x.shape if lead is None else x.shape[1:])
        moves.append(Move(k, axis, shape[axis], lead, route if planes == 2 and dims[1:] == (2, 2) else 0))
        shape[axis] *= nseq
        shapes.append(jax.ShapeDtypeStruct(tuple(shape), x.dtype))
    moves.sort(key=lambda m: not m.route)
    n = len(moves)
    D = pltpu.SemaphoreType.DMA
    scratch = [D((n,)), D((n, nseq)), D((n, nseq)), D((n, 2)), D((n, nseq)), D((n, nseq)), D((n, nseq))] + list(scratch)
    far, here = pl.BlockSpec(memory_space=pl.ANY), pl.BlockSpec(memory_space=pltpu.VMEM)
    n_far = task.n_far if task else 0
    return pl.pallas_call(
        functools.partial(gather_kernel, dims, planes, tuple(moves), len(arrays), task),
        out_shape=shapes + list(outputs),
        in_specs=[far] * (len(arrays) + len(inputs)),
        out_specs=[far] * len(arrays) + [here] * (len(outputs) - n_far) + [far] * n_far,
        scratch_shapes=scratch,
        compiler_params=pltpu.CompilerParams(collective_id=cid, has_side_effects=True, vmem_limit_bytes=60 << 20),
    )(*[x for x, _, _, _ in arrays], *inputs)


def gather_with(run, arrays, cid, planes, nseq, inputs, stay, outputs, late, scratch):
    D = pltpu.SemaphoreType.DMA
    push = (8, HG)
    outputs = [jax.ShapeDtypeStruct((nseq,) + push, F32)] + outputs + late
    scratch = [pltpu.VMEM(a.shape, a.dtype) for a in late] + [D((len(late),))] + scratch
    scratch = [pltpu.VMEM(push, F32), D((nseq,)), D((nseq,)), D((len(inputs),))] + [pltpu.VMEM(a.shape, a.dtype) for a in inputs] + scratch
    inputs = tuple(inputs) + tuple(stay)
    return gather(arrays, cid, planes, nseq, Task(len(inputs), len(stay), len(outputs), len(late), run), inputs, outputs, scratch)


def dot(a, b):
    return jnp.dot(a, b, preferred_element_type=F32)


def dot_t(a, b):
    return lax.dot_general(a, b, (((1,), (1,)), ((), ())), preferred_element_type=F32)


def wgrad(a, b):
    return lax.dot_general(a, b, (((0,), (0,)), ((), ())), preferred_element_type=F32)


def vmem(mib):
    return pltpu.CompilerParams(vmem_limit_bytes=mib << 20)


def layer_norm(values, gain_row, shift_row):
    center = values - jnp.mean(values, -1, keepdims=True)
    spread = jnp.mean(center * center, -1, keepdims=True)
    return center * lax.rsqrt(spread + EPSILON) * gain_row + shift_row


def fill(pre_ref, decay, drive=None):
    for k in range(2):
        for j in range(HB):
            at = 2 * k * HG + j * 128
            rate = jax.nn.sigmoid(pre_ref[:, at : at + 128])
            decay[k * HB + j] = 1.0 - rate
            if drive is not None:
                drive[k * HB + j] = rate * pre_ref[:, at + HG : at + HG + 128]


def row(x, i):
    return lax.slice_in_dim(x, i, i + 1, axis=0)


def cat(parts):
    return jnp.concatenate(parts, 1)


def blocks(x):
    return [x[:, j * 128 : (j + 1) * 128] for j in range(HB)]


def totals_kernel(pre_ref, tot_ref, chunk_ref, decay, drive):
    length = pre_ref.shape[0] // NCH
    fill(pre_ref, decay, drive)

    def step(t, carry):
        place = (pl.ds(t, NCH, stride=length), pl.ds(length - 1 - t, NCH, stride=length))
        out = []
        for i in range(2 * HB):
            c, h = carry[i]
            a = decay[i, place[i // HB], :]
            out.append((c * a, a * h + drive[i, place[i // HB], :]))
        return tuple(out)

    one, zero = jnp.ones((NCH, 128), F32), jnp.zeros((NCH, 128), F32)
    ends = lax.fori_loop(0, length, step, ((one, zero),) * (2 * HB), unroll=UNROLL)
    cf, hf = cat([e[0] for e in ends[:HB]]), cat([e[1] for e in ends[:HB]])
    cb, hb = cat([e[0] for e in ends[HB:]]), cat([e[1] for e in ends[HB:]])
    chunk_ref[0:NCH, :] = cf
    chunk_ref[NCH : 2 * NCH, :] = hf
    chunk_ref[2 * NCH : 3 * NCH, :] = cb
    chunk_ref[3 * NCH :, :] = hb
    one, zero = jnp.ones((1, HG), F32), jnp.zeros((1, HG), F32)
    tf, sf, tb, sb = one, zero, one, zero
    for k in range(NCH):
        sf, tf = row(cf, k) * sf + row(hf, k), tf * row(cf, k)
        j = NCH - 1 - k
        sb, tb = row(cb, j) * sb + row(hb, j), tb * row(cb, j)
    tot_ref[...] = jnp.concatenate([tf, sf, tb, sb], 0)


def states_work(me, q, seqs, all_ref, pre_all, chunk_all, ends_all, pooled_all, prev_all, decay, drive, state, prev):
    pre_ref, chunk_ref, ends_ref, pooled_ref, prev_ref = (
        r.at[pl.ds(q * (r.shape[0] // seqs), r.shape[0] // seqs)] for r in (pre_all, chunk_all, ends_all, pooled_all, prev_all)
    )
    chars = pre_all.shape[0] // seqs
    length = chars // NCH
    nseq = all_ref.shape[0]
    fill(pre_ref, decay, drive)
    ef = jnp.zeros((1, HG), F32)
    eb = ef
    for d in range(nseq):
        got = all_ref[d]
        ef = jnp.where(d < me, row(got, 4 * q) * ef + row(got, 4 * q + 1), ef)
        got = all_ref[nseq - 1 - d]
        eb = jnp.where(nseq - 1 - d > me, row(got, 4 * q + 2) * eb + row(got, 4 * q + 3), eb)
    cf, hf = chunk_ref[0:NCH, :], chunk_ref[NCH : 2 * NCH, :]
    cb, hb = chunk_ref[2 * NCH : 3 * NCH, :], chunk_ref[3 * NCH :, :]
    rows_f, rows_b = [], []
    for k in range(NCH):
        rows_f.append(ef)
        ef = row(cf, k) * ef + row(hf, k)
        j = NCH - 1 - k
        rows_b.append(eb)
        eb = row(cb, j) * eb + row(hb, j)

    def step(t, carry):
        place = (pl.ds(t, NCH, stride=length), pl.ds(length - 1 - t, NCH, stride=length))
        out = []
        for i in range(2 * HB):
            at = place[i // HB]
            prev[i, at, :] = carry[i]
            h = decay[i, at, :] * carry[i] + drive[i, at, :]
            state[i, at, :] = h
            out.append(h)
        return tuple(out)

    lax.fori_loop(0, length, step, tuple(blocks(jnp.concatenate(rows_f, 0)) + blocks(jnp.concatenate(rows_b[::-1], 0))), unroll=UNROLL)
    first = ends_ref[:, 0:1]
    last = ends_ref[:, 1:2]
    place = lax.broadcasted_iota(jnp.int32, (ends_all.shape[0] // seqs, chars), 1)
    member = jnp.where((place >= first) & (place < last), 1.0, 0.0).astype(BF)
    prev_ref[...] = cat([prev[i] for i in range(2 * HB)])
    pooled_ref[...] = dot(member, cat([state[i].astype(BF) for i in range(2 * HB)])) / (last - first).astype(F32)


def flows_kernel(pre_ref, dpool_ref, ends_ref, chunk_ref, ds_ref, tot_ref, gch_ref, decay, ds):
    chars = pre_ref.shape[0]
    length = chars // NCH
    fill(pre_ref, decay)
    first = ends_ref[0:1, :]
    last = ends_ref[1:2, :]
    place = lax.broadcasted_iota(jnp.int32, (chars, ends_ref.shape[1]), 0)
    inside = (place >= first) & (place < last)
    span = jnp.sum(jnp.where(inside, (last - first).astype(F32), 0.0), 1, keepdims=True)
    member = jnp.where(inside, 1.0, 0.0).astype(BF)
    spread = dot(member, dpool_ref[...]) / span
    ds_ref[...] = spread
    for i in range(2 * HB):
        ds[i] = spread[:, i * 128 : (i + 1) * 128]

    def step(t, carry):
        place = (pl.ds(length - 1 - t, NCH, stride=length), pl.ds(t, NCH, stride=length))
        return tuple(
            decay[i, place[i // HB], :] * (ds[i, place[i // HB], :] + carry[i]) for i in range(2 * HB)
        )

    ends = lax.fori_loop(0, length, step, (jnp.zeros((NCH, 128), F32),) * (2 * HB), unroll=UNROLL)
    gf, gb = cat(ends[:HB]), cat(ends[HB:])
    gch_ref[0:NCH, :] = gf
    gch_ref[NCH:, :] = gb
    cf, cb = chunk_ref[0:NCH, :], chunk_ref[2 * NCH : 3 * NCH, :]
    zero = jnp.zeros((1, HG), F32)
    tf, tb = zero, zero
    for k in range(NCH):
        j = NCH - 1 - k
        tf = row(cf, j) * tf + row(gf, j)
        tb = row(cb, k) * tb + row(gb, k)
    tot_ref[...] = jnp.concatenate([tf, tb, zero, zero], 0)


def dpre_work(me, q, seqs, gall_ref, all_ref, pre_all, ds_all, prev_all, chunk_all, gch_all, dpre_all, bias_all, decay, ds):
    pre_ref, ds_ref, prev_ref, chunk_ref, gch_ref, dpre_ref, bias_ref = (
        r.at[pl.ds(q * (r.shape[0] // seqs), r.shape[0] // seqs)] for r in (pre_all, ds_all, prev_all, chunk_all, gch_all, dpre_all, bias_all)
    )
    chars = pre_all.shape[0] // seqs
    length = chars // NCH
    nseq = all_ref.shape[0]
    fill(pre_ref, decay)
    for i in range(2 * HB):
        ds[i] = ds_ref[:, i * 128 : (i + 1) * 128]
    ef = jnp.zeros((1, HG), F32)
    eb = ef
    for d in range(nseq):
        j = nseq - 1 - d
        ef = jnp.where(j > me, row(all_ref[j], 4 * q) * ef + row(gall_ref[j], 4 * q), ef)
        eb = jnp.where(d < me, row(all_ref[d], 4 * q + 2) * eb + row(gall_ref[d], 4 * q + 1), eb)
    cf, cb = chunk_ref[0:NCH, :], chunk_ref[2 * NCH : 3 * NCH, :]
    gf, gb = gch_ref[0:NCH, :], gch_ref[NCH:, :]
    rows_f, rows_b = [], []
    for k in range(NCH):
        j = NCH - 1 - k
        rows_f.append(ef)
        ef = row(cf, j) * ef + row(gf, j)
        rows_b.append(eb)
        eb = row(cb, k) * eb + row(gb, k)

    def step(t, carry):
        place = (pl.ds(length - 1 - t, NCH, stride=length), pl.ds(t, NCH, stride=length))
        out = []
        for i in range(2 * HB):
            at = place[i // HB]
            g = ds[i, at, :] + carry[i]
            ds[i, at, :] = g
            out.append(decay[i, at, :] * g)
        return tuple(out)

    lax.fori_loop(0, length, step, tuple(blocks(jnp.concatenate(rows_f[::-1], 0)) + blocks(jnp.concatenate(rows_b, 0))), unroll=UNROLL)
    for i in range(2 * HB):
        k, j = i // HB, i % HB
        at = 2 * k * HG + j * 128
        g = ds[i]
        rate = jax.nn.sigmoid(pre_ref[:, at : at + 128])
        cand = pre_ref[:, at + HG : at + HG + 128]
        prev = prev_ref[:, i * 128 : (i + 1) * 128]
        dgate = (g * (cand - prev) * rate * decay[i]).astype(BF)
        dcand = (g * rate).astype(BF)
        for to, v in ((at, dgate), (at + HG, dcand)):
            dpre_ref[:, to : to + 128] = v
            bias_ref[:, to : to + 128] = jnp.broadcast_to(jnp.sum(v.astype(F32), 0, keepdims=True), (8, 128))


def part_of(ref, q, seqs):
    n = ref.shape[0] // seqs
    return ref.at[pl.ds(q * n, n)]


def forward_run(seqs, point, me, push, push_all, inputs, outputs, scratch):
    ids, table, gru, bias, ends = inputs
    pooled, chunk, *out = outputs
    pre, prev, emb = scratch[:3]
    o_sem = scratch[3]
    write = lambda k: pltpu.make_async_copy((pre, prev, emb)[k], out[k], o_sem.at[k])
    scratch = scratch[4:]
    if point == 0:
        n = 256

        def look(k, _):
            at = pl.ds(pl.multiple_of(k * n, n), n)
            unit = lax.broadcasted_iota(jnp.int32, (n, table.shape[1]), 1)
            hot = jnp.where(unit == ids[at, :], 1.0, 0.0).astype(BF)
            rows = dot_t(hot, table[...]).astype(BF)
            emb[at, :] = rows
            pre[at, :] = dot(rows, gru[...]) + bias[...]
            return 0

        lax.fori_loop(0, ids.shape[0] // n, look, 0)
        for q in range(seqs):
            totals_kernel(part_of(pre, q, seqs), push.at[pl.ds(4 * q, 4)], part_of(chunk, q, seqs), *scratch[:2])
        write(0).start()
        write(2).start()
    elif point <= seqs:
        states_work(me, point - 1, seqs, push_all, pre, chunk, ends, pooled, prev, *scratch)
        if point == seqs:
            write(1).start()
    elif point == 4:
        for k in range(3):
            write(k).wait()


def backward_run(seqs, point, me, push, push_all, inputs, outputs, scratch):
    pre, prev, chunk, tot_all, dpool, ends, q_ref, dc_ref, col_ref, gru_ref, keys, values = inputs
    dbias, dq, demb, dpre_out = outputs
    dpre, o_sem, ds_all, gch, decay, ds, kbuf, vbuf, k_sem, v_sem = scratch
    write = lambda: pltpu.make_async_copy(dpre, dpre_out, o_sem.at[0])
    if point == 4:
        write().wait()
        return
    pairs = HEADS // 2
    steps = seqs * pairs

    def fetch(i):
        s, p = lax.div(i, pairs), lax.rem(i, pairs)
        cols = pl.ds(pl.multiple_of(p * 2 * HDIM, 2 * HDIM), 2 * HDIM)
        b = lax.rem(i, 2)
        return (pltpu.make_async_copy(keys.at[s, :, cols], kbuf.at[b], k_sem.at[b]), pltpu.make_async_copy(values.at[s, :, cols], vbuf.at[b], v_sem.at[b]))

    def one(i, _):
        s, p = lax.div(i, pairs), lax.rem(i, pairs)
        cols = pl.ds(pl.multiple_of(p * 2 * HDIM, 2 * HDIM), 2 * HDIM)
        b = lax.rem(i, 2)

        @pl.when(i + 1 < steps)
        def _():
            for c in fetch(i + 1):
                c.start()

        for c in fetch(i):
            c.wait()
        dq[s, :, cols] = query_grad(q_ref[s, :, cols], kbuf[b], vbuf[b], dc_ref[s, :, cols], col_ref[s, p])
        return 0

    if point == 0:
        for c in fetch(0):
            c.start()
        for q in range(seqs):
            flows_kernel(*(part_of(r, q, seqs) for r in (pre, dpool, ends, chunk, ds_all)), push.at[pl.ds(4 * q, 4)], part_of(gch, q, seqs), decay, ds)
    elif point <= seqs:
        dpre_work(me, point - 1, seqs, push_all, tot_all, pre, ds_all, prev, chunk, gch, dpre, dbias, decay, ds)
        part_of(demb, point - 1, seqs)[...] = dot_t(part_of(dpre, point - 1, seqs)[...], gru_ref[...]).astype(BF)
        if point == seqs:
            write().start()
    bounds = (0,) + tuple(steps * k // 6 for k in SHARE)
    lax.fori_loop(bounds[point], bounds[point + 1], one, 0)


def pair_rows(x):
    lane = lax.broadcasted_iota(jnp.int32, x.shape, 1)
    zero = jnp.zeros_like(x)
    return jnp.concatenate([jnp.where(lane < HDIM, x, zero), jnp.where(lane >= HDIM, x, zero)], 0)


def pair_lanes(x):
    half = x.shape[0] // 2
    lane = lax.broadcasted_iota(jnp.int32, (half, x.shape[1]), 1)
    return jnp.where(lane < HDIM, x[:half], x[half:])


def attn_fwd_kernel(q_ref, k_ref, v_ref, ctx_ref, low_ref, lse_ref):
    toks = q_ref.shape[0]
    for i in range(TOGETHER):
        at = slice(i * 2 * HDIM, (i + 1) * 2 * HDIM)
        s = dot_t(pair_rows(q_ref[:, at] * (HDIM ** -0.5)), k_ref[:, at])
        top = jnp.max(s, 1, keepdims=True)
        p = jnp.exp(s - top)
        total = jnp.sum(p, 1, keepdims=True)
        o = pair_lanes(dot(p.astype(BF), v_ref[:, at]) / total)
        ctx_ref[:, at] = o
        low_ref[:, at] = o.astype(BF)
        lse = top + jnp.log(total)
        lse_ref[i] = jnp.concatenate([lse[:toks], lse[toks:]], 1)


def head_spec(rows, base=0, many=1):
    return pl.BlockSpec((None, rows, many * 2 * HDIM), lambda s, h: (s, 0, h + base))


def attention_fwd(qkv, keys, values):
    seqs, toks, _ = qkv.shape
    length = keys.shape[1]
    pairs = HEADS // 2
    block = lambda rows: head_spec(rows, 0, TOGETHER)
    return pl.pallas_call(
        attn_fwd_kernel,
        grid=(seqs, pairs // TOGETHER),
        out_shape=[
            jax.ShapeDtypeStruct((seqs, toks, HEADS * HDIM), F32),
            jax.ShapeDtypeStruct((seqs, toks, HEADS * HDIM), BF),
            jax.ShapeDtypeStruct((seqs, pairs, toks, 2), F32),
        ],
        in_specs=[block(toks), block(length), block(length)],
        out_specs=[block(toks), block(toks), pl.BlockSpec((None, TOGETHER, toks, 2), lambda s, h: (s, h, 0, 0))],
        compiler_params=vmem(62),
    )(qkv, keys, values)


def query_grad(q, keys, values, dc, col):
    scale = HDIM ** -0.5
    lse = jnp.concatenate([col[:, 0:1], col[:, 1:2]], 0)
    delta = jnp.concatenate([col[:, 2:3], col[:, 3:4]], 0)
    p = jnp.exp(dot_t(pair_rows(q * scale), keys) - lse)
    ds = (p * (dot_t(pair_rows(dc), values) - delta)).astype(BF)
    return (pair_lanes(dot(ds, keys)) * scale).astype(BF)


def context_kernel(datt_ref, w_ref, ctx_ref, lse_ref, dctx_ref, col_ref, stat_ref):
    seqs, toks, _ = dctx_ref.shape
    pairs = HEADS // 2
    low = dot_t(datt_ref[...], w_ref[...]).astype(BF)
    prod = low.astype(F32) * ctx_ref[...]
    lane = lax.broadcasted_iota(jnp.int32, (toks, 2 * HDIM), 1)
    for s in range(seqs):
        dctx_ref[s] = low[s * toks : (s + 1) * toks]
        cols = []
        for p in range(pairs):
            x = prod[s * toks : (s + 1) * toks, p * 2 * HDIM : (p + 1) * 2 * HDIM]
            a = jnp.sum(jnp.where(lane < HDIM, x, 0.0), 1, keepdims=True)
            b = jnp.sum(jnp.where(lane >= HDIM, x, 0.0), 1, keepdims=True)
            col = jnp.concatenate([lse_ref[s, p], a, b], 1)
            col_ref[s, p] = col
            cols.append(col)
        flat = jnp.concatenate(cols + [jnp.zeros((toks, 128 - 4 * pairs), F32)], 1)
        stat_ref[s * 4 * pairs : (s + 1) * 4 * pairs, :] = flat.T[: 4 * pairs]


def attn_bwd_kernel(ko_ref, vo_ref, qa_ref, dca_ref, row_ref, dk_ref, dv_ref):
    toks = ko_ref.shape[0]
    scale = HDIM ** -0.5

    def spread(i):
        n = row_ref.shape[1]
        return jnp.concatenate(
            [jnp.broadcast_to(row_ref[i : i + 1, :], (toks, n)), jnp.broadcast_to(row_ref[i + 1 : i + 2, :], (toks, n))], 0
        )

    p = jnp.exp(dot_t(pair_rows(ko_ref[...] * scale), qa_ref[...]) - spread(0))
    dv_ref[...] = pair_lanes(dot(p.astype(BF), dca_ref[...])).astype(BF)
    dp = dot_t(pair_rows(vo_ref[...]), dca_ref[...])
    ds = (p * (dp - spread(2))).astype(BF)
    dk_ref[...] = (pair_lanes(dot(ds, qa_ref[...])) * scale).astype(BF)


def attention_bwd(qkv, queries, dctx_all, rows):
    seqs, toks, _ = qkv.shape
    length = queries.shape[1]
    pairs = HEADS // 2
    stat = lambda a, b: pl.BlockSpec((None, None, a, b), lambda s, h: (s, h, 0, 0))
    return pl.pallas_call(
        attn_bwd_kernel,
        grid=(seqs, pairs),
        out_shape=[jax.ShapeDtypeStruct((seqs, toks, HEADS * HDIM), BF)] * 2,
        in_specs=[head_spec(toks, pairs), head_spec(toks, 2 * pairs), head_spec(length), head_spec(length), stat(4, length)],
        out_specs=[head_spec(toks)] * 2,
        compiler_params=vmem(56),
    )(qkv, qkv, queries, dctx_all, rows)


GELU_A = 0.7978845608028654
GELU_B = 0.044715


def norm_both(v, gain, shift, dy):
    center = v - jnp.mean(v, -1, keepdims=True)
    inv = lax.rsqrt(jnp.mean(center * center, -1, keepdims=True) + EPSILON)
    hat = center * inv
    dhat = dy * gain
    dv = inv * (dhat - jnp.mean(dhat, -1, keepdims=True) - hat * jnp.mean(dhat * hat, -1, keepdims=True))
    return hat * gain + shift, dv, jnp.sum(dy * hat, 0, keepdims=True), jnp.sum(dy, 0, keepdims=True)


def norm_back(hat, inv, gain, dy):
    dhat = dy * gain
    dv = inv * (dhat - jnp.mean(dhat, -1, keepdims=True) - hat * jnp.mean(dhat * hat, -1, keepdims=True))
    return dv, jnp.sum(dy * hat, 0, keepdims=True), jnp.sum(dy, 0, keepdims=True)


def norm_parts(v):
    center = v - jnp.mean(v, -1, keepdims=True)
    inv = lax.rsqrt(jnp.mean(center * center, -1, keepdims=True) + EPSILON)
    return center * inv, inv


def gelu_parts(v):
    square = v * v
    curve = jnp.tanh(GELU_A * (v + GELU_B * v * square))
    return 0.5 * v * (1.0 + curve), 0.5 * (1.0 + curve) + 0.5 * v * (1.0 - curve * curve) * (GELU_A * (1.0 + 3.0 * GELU_B * square))


def middle_kernel(seqs, *refs):
    given, (wo_hbm, wu_hbm, wd_hbm, ws_hbm, c0_hbm, c1_hbm, c2_hbm), refs = refs[:8], refs[8:15], refs[15:]
    far = refs[:16]
    dnorm_ref, dctx_ref, col_ref, stat_ref = refs[16:20]
    own = refs[20:36]
    (otok_ref, ochr_ref, nlow_ref, hid_ref, slow_ref, plow_ref, mprev_ref, merged_ref, mnext_ref, dmix_ref, dfus_ref, dlow_ref, drai_ref, datt_ref,
     din_ref, dpool_ref) = own
    (
     wo_ref, wu_ref, wd_ref, ws_ref, taps, acc, edge, before, after, dside, dchar, slope_ref, hat0, hat1, state_ref, dstate_ref,
     w_sem, e_send, b_recv, a_recv, o_sem, *held, i_sem) = refs[36:]
    x_ref, clow_ref, nrm_ref, pooled_ref, gtok_ref, gchr_ref, ctx_ref, lse_ref = held

    def take(*ks):
        for k in ks:
            pltpu.make_async_copy(given[k], held[k], i_sem.at[k]).wait()

    for k in range(3):
        pltpu.make_async_copy(given[k], held[k], i_sem.at[k]).start()

    def put(*ks):
        for k in ks:
            pltpu.make_async_copy(own[k], far[k], o_sem.at[k]).start()

    me = lax.axis_index("seq")
    dp = lax.axis_index("dp")
    n = lax.axis_size("seq")
    rows, width = x_ref.shape
    toks = rows // seqs
    wide = 2 * width
    loads = [
        pltpu.make_async_copy(src, dst, w_sem.at[k]) for k, (src, dst) in enumerate((
            (wo_hbm, wo_ref), (wu_hbm, wu_ref), (wd_hbm, wd_ref), (ws_hbm, ws_ref), (c1_hbm, taps.at[1]), (c0_hbm, taps.at[0]), (c2_hbm, taps.at[2]),
        ))
    ]
    loads[0].start()
    for k in range(3, 8):
        pltpu.make_async_copy(given[k], held[k], i_sem.at[k]).start()
    for load in loads[1:]:
        load.start()
    edge[...] = jnp.zeros_like(edge)
    right, left = (dp, me + 1), (dp, me - 1)
    has_l, has_r = me > 0, me < n - 1
    bar = pltpu.get_barrier_semaphore()
    pl.when(has_l)(lambda: pl.semaphore_signal(bar, inc=1, device_id=left, device_id_type=MESH))
    pl.when(has_r)(lambda: pl.semaphore_signal(bar, inc=1, device_id=right, device_id_type=MESH))
    pl.semaphore_wait(bar, has_l.astype(jnp.int32) + has_r.astype(jnp.int32))

    def send(k):
        def to_right():
            return pltpu.make_async_remote_copy(
                src_ref=edge.at[k, 0], dst_ref=before.at[k], send_sem=e_send.at[k, 0], recv_sem=b_recv.at[k], device_id=right, device_id_type=MESH)

        def to_left():
            return pltpu.make_async_remote_copy(
                src_ref=edge.at[k, 1], dst_ref=after.at[k], send_sem=e_send.at[k, 1], recv_sem=a_recv.at[k], device_id=left, device_id_type=MESH)

        return to_right, to_left

    def start(k, ref):
        for s in range(seqs):
            edge[k, 0, s : s + 1, :] = ref[(s + 1) * toks - 16 : (s + 1) * toks, :].astype(F32)[15:16]
            edge[k, 1, s : s + 1, :] = ref[s * toks : s * toks + 16, :].astype(F32)[0:1]
        to_right, to_left = send(k)
        pl.when(has_r)(lambda: to_right().start())
        pl.when(has_l)(lambda: to_left().start())

    def finish(k):
        to_right, to_left = send(k)
        pl.when(has_r)(lambda: to_left().wait_recv())
        pl.when(has_l)(lambda: to_right().wait_recv())
        pl.when(has_r)(lambda: to_right().wait_send())
        pl.when(has_l)(lambda: to_left().wait_send())

    def shifts(k, ref, prev_ref, next_ref):
        for j in range(0, wide, 512):
            x = ref[:, j : j + 512].astype(F32)
            at = lax.broadcasted_iota(jnp.int32, x.shape, 0)
            prev, follow = pltpu.roll(x, 1, 0), pltpu.roll(x, rows - 1, 0)
            for s in range(seqs):
                b = jnp.where(has_l, before[k, s : s + 1, j : j + 512], 0.0)
                a = jnp.where(has_r, after[k, s : s + 1, j : j + 512], 0.0)
                prev = jnp.where(at == s * toks, b, prev)
                follow = jnp.where(at == (s + 1) * toks - 1, a, follow)
            prev_ref[:, j : j + 512] = prev.astype(BF)
            next_ref[:, j : j + 512] = follow.astype(BF)

    chunk = 768
    take(0, 1, 2)
    loads[0].wait()
    hat, inv0 = norm_parts(x_ref[...].astype(F32) + dot(clow_ref[...], wo_ref[...]))
    hat0[...] = hat
    normed = hat * nrm_ref[0:1, :] + nrm_ref[1:2, :]
    nlow_ref[...] = normed.astype(BF)
    loads[1].wait()

    def raise_part(j, _):
        cols = pl.ds(pl.multiple_of(j * chunk, chunk), chunk)
        hidden, slope = gelu_parts(dot(nlow_ref[...], wu_ref[:, cols]))
        hid_ref[:, cols] = hidden.astype(BF)
        slope_ref[:, cols] = slope
        return 0

    lax.fori_loop(0, 4 * width // chunk, raise_part, 0)
    loads[2].wait()
    hat, inv1 = norm_parts(normed + dot(hid_ref[...], wd_ref[...]))
    hat1[...] = hat
    state = hat * nrm_ref[2:3, :] + nrm_ref[3:4, :]
    state_ref[...] = state
    loads[3].wait()
    take(3, 4, 5, 6, 7)
    slow = state.astype(BF)
    plow = pooled_ref[...].astype(BF)
    slow_ref[...] = slow
    plow_ref[...] = plow
    merged_ref[:, :width] = dot(slow, ws_ref[0]).astype(BF)
    merged_ref[:, width:] = dot(plow, ws_ref[1]).astype(BF)
    start(0, merged_ref)
    loads[4].wait()

    def centre(j, _):
        cols = pl.ds(pl.multiple_of(j * 512, 512), 512)
        acc[:, cols] = dot(merged_ref[...], taps[1, :, cols])
        return 0

    lax.fori_loop(0, wide // 512, centre, 0)
    finish(0)
    shifts(0, merged_ref, mprev_ref, mnext_ref)
    loads[5].wait()
    loads[6].wait()

    def sides(j, _):
        cols = pl.ds(pl.multiple_of(j * 512, 512), 512)
        acc[:, cols] += dot(mprev_ref[...], taps[0, :, cols]) + dot(mnext_ref[...], taps[2, :, cols])
        return 0

    lax.fori_loop(0, wide // 512, sides, 0)
    for part, (base_ref, grad_ref, out_ref) in enumerate(((state_ref, gtok_ref, otok_ref), (pooled_ref, gchr_ref, ochr_ref))):
        mixed = acc[:, part * width : (part + 1) * width]
        gated, slope = gelu_parts(mixed)
        r = 4 + 2 * part
        out, dsum, dgain, dshift = norm_both(base_ref[...] + gated, nrm_ref[r : r + 1, :], nrm_ref[r + 1 : r + 2, :], grad_ref[...].astype(F32))
        out_ref[...] = out.astype(BF)
        dnorm_ref[r : r + 1, :] = dgain
        dnorm_ref[r + 1 : r + 2, :] = dshift
        dmix_ref[:, part * width : (part + 1) * width] = (dsum * slope).astype(BF)
        if part == 0:
            dstate_ref[...] = dsum
        else:
            dchar[...] = dsum
    start(1, dmix_ref)
    put(*range(10))

    def centre_back(j, _):
        cols = pl.ds(pl.multiple_of(j * 512, 512), 512)
        acc[:, cols] = dot_t(dmix_ref[...], taps[1, cols, :])
        return 0

    lax.fori_loop(0, wide // 512, centre_back, 0)
    finish(1)
    shifts(1, dmix_ref, dside.at[0], dside.at[1])

    def sides_back(j, _):
        cols = pl.ds(pl.multiple_of(j * 512, 512), 512)
        dfus_ref[:, cols] = (acc[:, cols] + dot_t(dside[1], taps[0, cols, :]) + dot_t(dside[0], taps[2, cols, :])).astype(BF)
        return 0

    lax.fori_loop(0, wide // 512, sides_back, 0)
    dpool_ref[...] = (dchar[...] + dot_t(dfus_ref[:, width:], ws_ref[1])).astype(BF)
    put(10, 15)
    dstate = dstate_ref[...] + dot_t(dfus_ref[:, :width], ws_ref[0])
    dsum, dnorm_ref[2:3, :], dnorm_ref[3:4, :] = norm_back(hat1[...], inv1, nrm_ref[2:3, :], dstate)
    dlow_ref[...] = dsum.astype(BF)
    dstate_ref[...] = dsum
    put(11)

    def lower_part(j, _):
        cols = pl.ds(pl.multiple_of(j * chunk, chunk), chunk)
        drai_ref[:, cols] = (dot_t(dlow_ref[...], wd_ref[cols, :]) * slope_ref[:, cols]).astype(BF)
        return 0

    lax.fori_loop(0, 4 * width // chunk, lower_part, 0)
    put(12)
    dsum, dnorm_ref[0:1, :], dnorm_ref[1:2, :] = norm_back(hat0[...], inv0, nrm_ref[0:1, :], dstate_ref[...] + dot_t(drai_ref[...], wu_ref[...]))
    din_ref[...] = dsum
    datt_ref[...] = dsum.astype(BF)
    put(13, 14)
    context_kernel(datt_ref, wo_ref, ctx_ref, lse_ref, dctx_ref, col_ref, stat_ref)
    for k in range(16):
        pltpu.make_async_copy(own[k], far[k], o_sem.at[k]).wait()


def middle(seqs, x, clow, context, lse, pooled, grad_token, grad_char, nrm, w_out, w_up, w_down, w_stream, w_conv, cid):
    rows, width = x.shape
    wide, ff = 2 * width, 4 * width
    pairs, toks = lse.shape[1:3]
    here = pl.BlockSpec(memory_space=pltpu.VMEM)
    far = pl.BlockSpec(memory_space=pl.ANY)
    low, full = (lambda c: jax.ShapeDtypeStruct((rows, c), BF)), jax.ShapeDtypeStruct((rows, width), F32)
    D = pltpu.SemaphoreType.DMA
    f = lambda *s: pltpu.VMEM(s, F32)
    v = lambda *s: pltpu.VMEM(s, BF)
    given = (x, clow, nrm, pooled, grad_token, grad_char, context, lse)
    large = [low(width)] * 3 + [low(ff), low(width), low(width)] + [low(wide)] * 5 + [low(width), low(ff), low(width), full, low(width)]
    return pl.pallas_call(
        functools.partial(middle_kernel, seqs),
        out_shape=large + [
            jax.ShapeDtypeStruct((8, width), F32), jax.ShapeDtypeStruct((seqs, toks, width), BF), jax.ShapeDtypeStruct((seqs, pairs, toks, 4), F32),
            jax.ShapeDtypeStruct((seqs * pairs * 4, toks), F32),
        ],
        in_specs=[far] * 15,
        out_specs=[far] * 16 + [here] * 4,
        scratch_shapes=[pltpu.VMEM(a.shape, a.dtype) for a in large] + [
            v(*w_out.shape), v(*w_up.shape), v(*w_down.shape), v(*w_stream.shape), v(3, wide, wide), f(rows, wide), f(2, 2, 8, wide),
            f(2, 8, wide), f(2, 8, wide), v(2, rows, wide), f(rows, width), f(rows, ff), f(rows, width), f(rows, width), f(rows, width), f(rows, width),
            D((7,)), D((2, 2)), D((2,)), D((2,)), D((16,)),
        ] + [pltpu.VMEM(a.shape, a.dtype) for a in given] + [D((8,))],
        compiler_params=pltpu.CompilerParams(collective_id=cid, has_side_effects=True, vmem_limit_bytes=62 << 20),
    )(*given, w_out, w_up, w_down, w_stream, *w_conv)


RZ, RY, RC = 4, 2, 2
PW = 384
PR = 48
LD, LX, LY, LH, LF = 2, 8, 12, 3, 25
HRING = LY + 1
PER, PK = 11, 3
JOB = 6


Group = collections.namedtuple("Group", ("left", "parts", "right", "col", "cols", "out", "lead", "base", "at"))
GRU, TABLE, TINY = 5, 4, 8


def piece_groups(taps):
    rows = [(6 + k, 2, 5, 0, 4, 7, i, 0) for i, k in enumerate(taps)]
    rows += [(4, 1, 4, 0, 2, 6, 0, 0), (5, 1, 4, 768, 2, 6, 1, 0), (3, 4, 3, 0, 2, 3, None, 0), (2, 1, 2, 0, 8, 2, None, 0), (1, 1, 1, 0, 2, 1, None, 0),
             (0, 1, 0, 0, 2, 0, None, 0), (0, 1, 6, 0, 4, 0, None, 2)]
    out, at = [], 0
    for r in rows:
        out.append(Group(*r, at))
        at += r[1] * r[4]
    return tuple(out), at


MISC = (((GRU, 0), (GRU, 1), (GRU, 2)), ((GRU, 3), (TABLE, 0), (TABLE, 1)), ((TABLE, 2), (TINY, 0), (None, 0)))


def reduce_kernel(npieces, groups, *refs):
    out_ref, dkv_ref = refs[24:26]
    width = refs[0].shape[1]
    dk_ref, dv_ref = dkv_ref.at[:, pl.ds(0, width)], dkv_ref.at[:, pl.ds(width, width)]
    qa_ref, dca_ref = refs[22:24]
    held, l_sem = refs[-23:-1], refs[-1]
    loads = [pltpu.make_async_copy(a, b, l_sem.at[k]) for k, (a, b) in enumerate(zip(refs[:22], held))]
    first = {}
    for g in groups:
        for k in (g.left, 9 + g.right):
            first.setdefault(k, g.at)

    for k in (8, 7, 6, 14, 20, 21, 4, 5, 13, 3, 12, 2, 11, 1, 10, 0, 9, 15, 16, 17, 18, 19):
        loads[k].start()
    lhs, rhs = held[:9], tuple(held[9:15]) + (dkv_ref,)
    emb_ref, dpre_ref, demb_ref, ids_ref, tiny_ref, kv_ref, stat_ref = held[15:]
    (lt, part, r0, held, r1, r2, up, dn, fin, fx,
     d_send, d_recv, x_send, x_recv, y_send, y_recv, u_send, u_recv, n_send, n_recv, f_send, f_recv, qbuf, cbuf, dk_acc, dv_acc, q_sem, c_sem) = refs[26:-23]
    dp = lax.axis_index("dp")
    me = lax.axis_index("seq")
    c = lax.rem(me, RC)
    y = lax.rem(lax.div(me, RC), RY)
    z = lax.div(me, RC * RY)

    def to(zz, yy, cc):
        return (dp, (zz * RY + yy) * RC + cc)

    sib, ynb, zup, zdn, xnb = to(z, y, 1 - c), to(z, 1 - y, c), to(z + 1, y, c), to(z - 1, y, c), (1 - dp, me)
    bar = pltpu.get_barrier_semaphore()
    for where in (sib, ynb, xnb):
        pl.semaphore_signal(bar, inc=1, device_id=where, device_id_type=MESH)
    pl.when(z > 0)(lambda: pl.semaphore_signal(bar, inc=1, device_id=zdn, device_id_type=MESH))
    pl.when(z < RZ - 1)(lambda: pl.semaphore_signal(bar, inc=1, device_id=zup, device_id_type=MESH))
    pl.semaphore_wait(bar, 3 + (z > 0).astype(jnp.int32) + (z < RZ - 1).astype(jnp.int32))

    def copy(src, dst, send, recv, where):
        return pltpu.make_async_remote_copy(src_ref=src, dst_ref=dst, send_sem=send, recv_sem=recv, device_id=where, device_id_type=MESH)

    def d2d(t):
        b, k = lax.rem(t, LD + 1), lax.rem(t, 2 * LD)
        return copy(part.at[b, :, :, 1 - c], r0.at[k], d_send.at[b], d_recv.at[k], sib)

    def far(t):
        return lax.div(t, PER) * PK + lax.div(lax.rem(t, PER), 3)

    def mi(t):
        m = lax.rem(t, PER)
        return lax.div(t, PER) * (PER - PK) + m - jnp.minimum(lax.div(m + dp, 3), PK)

    def across(t):
        return copy(held.at[lax.rem(t, HRING)], r1.at[far(t)], x_send.at[t], x_recv.at[t], xnb)

    def along_y(t):
        return copy(held.at[lax.rem(t, HRING), :, 1 - y], r2.at[mi(t)], y_send.at[t], y_recv.at[t], ynb)

    def final(t):
        return copy(fin.at[t], fx.at[t], f_send.at[t], f_recv.at[t], xnb)

    def go_up(t, k):
        src = r2.at[mi(t), pl.ds(k + 1, RZ - 1 - k)] if k == 0 else up.at[mi(t), pl.ds(k, RZ - 1 - k)]
        return copy(src, up.at[mi(t), pl.ds(k, RZ - 1 - k)], u_send.at[t], u_recv.at[t], zup)

    def from_below(t, k):
        ref = up.at[mi(t), pl.ds(k - 1, RZ - k)]
        return copy(ref, ref, u_send.at[t], u_recv.at[t], zdn)

    def go_down(t, k):
        src = r2.at[mi(t), pl.ds(0, k)] if k == RZ - 1 else dn.at[mi(t), pl.ds(0, k)]
        return copy(src, dn.at[mi(t), pl.ds(0, k)], n_send.at[t], n_recv.at[t], zdn)

    def from_above(t, k):
        ref = dn.at[mi(t), pl.ds(0, k + 1)]
        return copy(ref, ref, n_send.at[t], n_recv.at[t], zup)

    def add(a, b):
        return (a.astype(F32) + b.astype(F32)).astype(BF)

    def live(t):
        return jnp.logical_and(t >= 0, t < npieces)

    def route(t):
        m = lax.rem(t, PER)
        return jnp.where(m < 3 * PK, lax.rem(m, 3), 0)

    def mine(t):
        r = route(t)
        return jnp.logical_or(r == 0, r - 1 == dp)

    def finish(t):
        r = route(t)

        @pl.when(r == 0)
        def _():
            final(t).wait_recv()
            out_ref[t] = add(fin[t], fx[t])

        @pl.when(jnp.logical_and(r > 0, r - 1 == dp))
        def _():
            out_ref[t] = fin[t]

        @pl.when(jnp.logical_and(r > 0, r - 1 != dp))
        def _():
            final(t).wait_recv()
            out_ref[t] = fx[t]

        pl.when(mine(t))(lambda: final(t).wait_send())

    def sum_up(t):
        i = mi(t)
        for k in range(RZ):
            @pl.when(z == k)
            def _(k=k):
                if k > 0:
                    from_below(t, k).wait_recv()
                    for q in range(k + 1, RZ):
                        up[i, q - 1] = add(up[i, q - 1], r2[i, q])
                if k < RZ - 1:
                    go_up(t, k).start()

    def sum_down(t):
        i = mi(t)
        for k in range(RZ):
            @pl.when(z == k)
            def _(k=k):
                if k < RZ - 1:
                    from_above(t, k).wait_recv()
                    for q in range(k):
                        dn[i, q] = add(dn[i, q], r2[i, q])
                if k > 0:
                    go_down(t, k).start()

    def close(t):
        i = mi(t)
        for k in range(RZ):
            @pl.when(z == k)
            def _(k=k):
                total = r2[i, k].astype(F32)
                if k > 0:
                    total = total + up[i, k - 1].astype(F32)
                    go_down(t, k).wait_send()
                if k < RZ - 1:
                    total = total + dn[i, k].astype(F32)
                    go_up(t, k).wait_send()
                fin[t] = total.astype(BF)
        final(t).start()

    def join_y(t):
        i = mi(t)
        along_y(t).wait_recv()
        along_y(t).wait_send()
        h = lax.rem(t, HRING)
        for q in range(RZ):
            r2[i, q] = add(r2[i, q], held[h, q, y])

    def join_x(t):
        h = lax.rem(t, HRING)
        across(t).wait_recv()
        for q in range(RZ):
            held[h, q] = add(held[h, q], r1[far(t), q])
        along_y(t).start()

    def join_core(t):
        b, k = lax.rem(t, LD + 1), lax.rem(t, 2 * LD)
        h = lax.rem(t, HRING)
        d2d(t).wait_recv()
        d2d(t).wait_send()
        for q in range(RZ):
            held[h, q] = add(part[b, q, :, c], r0[k, q])
        pl.when(route(t) == 0)(lambda: along_y(t).start())
        pl.when(jnp.logical_not(mine(t)))(lambda: across(t).start())

    def turn(ref):
        n = ref.shape[0]
        for k in range(0, ref.shape[1], 384):
            lt[k // PR : k // PR + 8, :, :n] = ref[:, k : k + 384].T.reshape(8, PR, n)

    def make(t):
        b = lax.rem(t, LD + 1)
        for g in groups:
            @pl.when(jnp.logical_and(t >= g.at, t < g.at + g.parts * g.cols))
            def _(g=g):
                i = t - g.at
                j, cb = lax.div(i, g.cols), lax.rem(i, g.cols)

                @pl.when(i == 0)
                def _():
                    for k in (g.left, 9 + g.right):
                        if k < 15 and first[k] == g.at:
                            loads[k].wait()
                    turn(lhs[g.left])

                right = rhs[g.right][:, pl.ds(pl.multiple_of(g.col + cb * PW, PW), PW)]
                for q in range(RZ // 2):
                    left = jnp.concatenate([lt[(8 * q + s) * g.parts + j] for s in range(8)], 0)
                    part[b, 2 * q : 2 * q + 2] = dot(left, right).astype(BF).reshape(2, RY, RC, PR, PW)
        for m, trio in enumerate(MISC):
            @pl.when(t == npieces - len(MISC) + m)
            def _(m=m, trio=trio):
                if m == 0:
                    for k in range(15, 20):
                        loads[k].wait()
                for i, (kind, cb) in enumerate(trio):
                    if kind == GRU:
                        val = wgrad(emb_ref[...], dpre_ref[:, cb * PW : (cb + 1) * PW]).astype(BF).reshape(RZ, RY, RC, 16, PW)
                    elif kind == TABLE:
                        unit = lax.broadcasted_iota(jnp.int32, (ids_ref.shape[0], PW), 1) + cb * PW
                        hot = jnp.where(unit == ids_ref[...], 1.0, 0.0).astype(BF)
                        val = wgrad(demb_ref[...], hot).astype(BF).reshape(RZ, RY, RC, 16, PW)
                    elif kind == TINY:
                        val = tiny_ref[...].reshape(RZ, RY, RC, 16, PW)
                    else:
                        val = jnp.zeros((RZ, RY, RC, 16, PW), BF)
                    part[b, :, :, :, 16 * i : 16 * i + 16, :] = val
        d2d(t).start()

    pairs = HEADS // 2
    toks = kv_ref.shape[1]
    half = qa_ref.shape[1] // 2
    jobs = 2 * pairs * kv_ref.shape[0]

    def fetch(i):
        s, p, h = lax.div(i, 2 * pairs), lax.rem(lax.div(i, 2), pairs), lax.rem(i, 2)
        cols = pl.ds(pl.multiple_of(p * 2 * HDIM, 2 * HDIM), 2 * HDIM)
        part = pl.ds(pl.multiple_of(h * half, half), half)
        return (pltpu.make_async_copy(qa_ref.at[s, part, cols], qbuf.at[h], q_sem.at[h]), pltpu.make_async_copy(dca_ref.at[s, part, cols], cbuf.at[h], c_sem.at[h]))

    def key_work(i):
        s, p, h = lax.div(i, 2 * pairs), lax.rem(lax.div(i, 2), pairs), lax.rem(i, 2)
        at = pl.multiple_of(p * 2 * HDIM, 2 * HDIM)
        slots = half // toks

        @pl.when(i == 0)
        def _():
            loads[20].wait()
            loads[21].wait()


        @pl.when(i + 1 < jobs)
        def _():
            for load in fetch(i + 1):
                load.start()

        for load in fetch(i):
            load.wait()
        scale = HDIM ** -0.5
        queries, dctx = qbuf[h], cbuf[h]

        def spread(k):
            at = (s * pairs + p) * 4 + k
            one = lambda r: jnp.concatenate([stat_ref[h * slots + d, pl.ds(r, 1), :] for d in range(slots)], 1)
            return jnp.concatenate([jnp.broadcast_to(one(at), (toks, half)), jnp.broadcast_to(one(at + 1), (toks, half))], 0)

        prob = jnp.exp(dot_t(pair_rows(kv_ref[s, :, pl.ds(at + width, 2 * HDIM)] * scale), queries) - spread(0))
        dv = dot(prob.astype(BF), dctx)
        dprob = dot_t(pair_rows(kv_ref[s, :, pl.ds(at + 2 * width, 2 * HDIM)]), dctx)
        dk = dot((prob * (dprob - spread(2))).astype(BF), queries)

        @pl.when(h == 0)
        def _():
            dk_acc[...] = dk
            dv_acc[...] = dv

        @pl.when(h == 1)
        def _():
            rows = pl.ds(pl.multiple_of(s * toks, toks), toks)
            cols = pl.ds(at, 2 * HDIM)
            dk_ref[rows, cols] = (pair_lanes(dk_acc[...] + dk) * scale).astype(BF)
            dv_ref[rows, cols] = pair_lanes(dv_acc[...] + dv).astype(BF)

    for load in fetch(0):
        load.start()

    def tick(T, _):
        def do(t, f, cond=None):
            ok = live(t)
            pl.when(ok if cond is None else jnp.logical_and(ok, cond(t)))(lambda: f(t))

        do(T - LF, finish)
        do(T - LY - z * LH, sum_up, mine)
        do(T - LY - (RZ - 1 - z) * LH, sum_down, mine)
        do(T - LY - (RZ - 1) * LH, close, mine)
        do(T - LY + 1, join_y, mine)
        do(T - LX, join_x, lambda t: jnp.logical_and(route(t) > 0, mine(t)))
        do(T - LX, lambda t: across(t).wait_send(), lambda t: jnp.logical_not(mine(t)))
        do(T - LD, join_core)
        do(T, make)
        job = T - JOB
        pl.when(jnp.logical_and(job >= 0, job < jobs))(lambda: key_work(job))
        return 0

    lax.fori_loop(0, npieces + LF + 1, tick, 0)


def finish_kernel(groups, *refs):
    held, l_sem = refs[16:21], refs[21]
    loads = [pltpu.make_async_copy(a, b, l_sem.at[k]) for k, (a, b) in enumerate(zip(refs[:5], held))]
    for load in loads:
        load.start()
    pieces, dq, dkv, w, base = held
    outs = refs[5:16]
    loads[0].wait()
    for g in groups:
        for j in range(g.parts):
            for cb in range(g.cols):
                rows, cols = slice(j * PR, (j + 1) * PR), slice((g.base + cb) * PW, (g.base + cb + 1) * PW)
                val = pieces[g.at + j * g.cols + cb].astype(F32)
                if g.lead is None:
                    outs[g.out][rows, cols] = val
                else:
                    outs[g.out][g.lead, rows, cols] = val
    first = groups[-1].at + groups[-1].parts * groups[-1].cols
    bias, norms, dinput = outs[8:]
    for m, trio in enumerate(MISC):
        for i, (kind, cb) in enumerate(trio):
            val = pieces[first + m, 16 * i : 16 * i + 16, :].astype(F32)
            if kind == TINY:
                bias[...] = val[0:1, : bias.shape[1]]
                for k in range(4):
                    norms[k] = val[1 + 2 * k : 3 + 2 * k, : norms.shape[2]]
            elif kind is not None:
                n = min(PW, outs[kind].shape[1] - cb * PW)
                outs[kind][:, cb * PW : cb * PW + n] = val[:, :n]
    n = dq.shape[1]
    for load in loads[1:]:
        load.wait()
    dinput[...] = base[...] + dot_t(dq[...], w[:, :n]) + dot_t(dkv[:, :n], w[:, n : 2 * n]) + dot_t(dkv[:, n:], w[:, 2 * n :])


def reduce_all(lhs, rhs, emb, dpre, demb, ids, kv, stat, queries, dctx, w_qkv, dsum, g_bias, g_norms, n_table, nseq, cid, taps=(0, 1, 2)):
    width = lhs[0].shape[1]
    per = g_bias.shape[0] // nseq
    tiny = jnp.concatenate([
        jnp.pad(g_bias.reshape(nseq, 1, per), ((0, 0), (0, 0), (0, PW - per))),
        jnp.pad(g_norms.reshape(8, nseq, -1).transpose(1, 0, 2), ((0, 0), (0, 7), (0, PW - width // nseq))),
    ], 1).astype(BF)
    groups, npieces = piece_groups(taps)
    npieces += len(MISC)
    dense = -(-npieces // PER) * (PER - PK)
    D = pltpu.SemaphoreType.DMA
    v = lambda *s: pltpu.VMEM(s, BF)
    spec = pl.BlockSpec(memory_space=pltpu.VMEM)
    operands = (*lhs, *rhs, emb, dpre, demb, ids, tiny, kv, stat)
    pieces, dkv = pl.pallas_call(
        functools.partial(reduce_kernel, npieces, groups),
        out_shape=[jax.ShapeDtypeStruct((npieces, PR, PW), BF), jax.ShapeDtypeStruct((lhs[0].shape[0], 2 * width), BF)],
        in_specs=[pl.BlockSpec(memory_space=pl.ANY)] * 24,
        out_specs=[spec] * 2,
        scratch_shapes=[
            v(64, PR, lhs[0].shape[0]),
            v(LD + 1, RZ, RY, RC, PR, PW), v(2 * LD, RZ, RY, PR, PW), v(HRING, RZ, RY, PR, PW), v(PK * (npieces // PER + 1), RZ, RY, PR, PW),
            v(dense, RZ, PR, PW), v(dense, RZ - 1, PR, PW), v(dense, RZ - 1, PR, PW), v(npieces, PR, PW), v(npieces, PR, PW),
            D((LD + 1,)), D((2 * LD,)), D((npieces,)), D((npieces,)), D((npieces,)), D((npieces,)),
            D((npieces,)), D((npieces,)), D((npieces,)), D((npieces,)), D((npieces,)), D((npieces,)),
            v(2, queries.shape[1] // 2, 2 * HDIM), v(2, queries.shape[1] // 2, 2 * HDIM),
            pltpu.VMEM((2 * kv.shape[1], 2 * HDIM), F32), pltpu.VMEM((2 * kv.shape[1], 2 * HDIM), F32), D((2,)), D((2,)),
        ] + [pltpu.VMEM(a.shape, a.dtype) for a in operands] + [D((len(operands),))],
        compiler_params=pltpu.CompilerParams(collective_id=cid, has_side_effects=True, vmem_limit_bytes=62 << 20),
    )(*operands, queries, dctx)
    f = lambda *s: jax.ShapeDtypeStruct(s, F32)
    wide = 2 * width
    share = width // nseq
    return pl.pallas_call(
        functools.partial(finish_kernel, groups),
        out_shape=[
            f(share, 3 * width), f(share, width), f(share, 4 * width), f(4 * share, width), f(16, n_table), f(16, 4 * PW),
            f(2, share, width), f(3, 2 * share, wide), f(1, per), f(4, 2, share), f(*dsum.shape),
        ],
        in_specs=[pl.BlockSpec(memory_space=pl.ANY)] * 5,
        out_specs=[spec] * 11,
        scratch_shapes=[pltpu.VMEM(a.shape, a.dtype) for a in (pieces, rhs[0], dkv, w_qkv, dsum)] + [D((5,))],
        compiler_params=vmem(62),
    )(pieces, rhs[0], dkv, w_qkv, dsum)


def scatter(total, axis):
    part = lax.psum_scatter(total, "seq", scatter_dimension=axis, tiled=True)
    return lax.psum(part, "dp").astype(F32)


def body(tokens, char_ids, span_lengths, script_group, w_qkv, w_out, w_up, w_down, char_table, w_gru, gru_bias, w_stream, w_conv, norms, grad_token, grad_char):
    nseq, planes = lax.axis_size("seq"), lax.axis_size("dp")
    seqs, toks, width = tokens.shape
    chars = char_ids.shape[1]
    rows = seqs * toks
    bias_n, norm_n = gru_bias.shape[0], norms.shape[2]
    small = jnp.concatenate([gru_bias, norms.reshape(-1)])
    small = jnp.pad(small, (0, 2048 - small.shape[0])).reshape(16, 128)
    conv0, w_down, conv1, conv2, w_out, w_stream, w_qkv, w_gru, char_table, small = gather(
        [(w_conv, 0, 1, 0), (w_down, 0, 1, None), (w_conv, 0, 2, 1), (w_conv, 0, 2, 2), (w_out, 0, 0, None), (w_stream, 1, 0, None), (w_qkv, 0, 0, None),
         (w_gru, 0, 0, None), (char_table, 0, 0, None), (small, 0, 0, None)], 1, planes, nseq
    )
    w_up, small = lax.optimization_barrier((w_up, small))
    w_up = lax.all_gather(w_up, "seq", axis=0, tiled=True)
    w_conv = (conv0, conv1, conv2)
    small = small.reshape(nseq, 2048)
    bias = small[:, :bias_n].reshape(-1).astype(F32)
    nrm = small[:, bias_n : bias_n + 8 * norm_n].reshape(nseq, 4, 2, norm_n).transpose(1, 2, 0, 3).reshape(4, 2, width).astype(F32)

    x_low = tokens.reshape(rows, width)
    qkv = dot(x_low, w_qkv).astype(BF)
    qkv3 = qkv.reshape(seqs, toks, 3 * width)

    char_rows = (char_ids + script_group[:, None] * GROUP_CHARS).reshape(seqs * chars, 1)
    span = span_lengths[:, 0]
    span_ends = jnp.cumsum(span, -1)
    starts = span_ends - span
    ends_col = jnp.stack([starts, span_ends], -1).reshape(rows, 2)
    ends_row = jnp.pad(jnp.stack([starts, span_ends], 1), ((0, 0), (0, 6), (0, 0))).reshape(seqs * 8, toks)
    block = pltpu.VMEM((2 * HB, chars, 128), F32)
    full = lambda *d: jax.ShapeDtypeStruct(d, F32)
    keys, values, tot_all, pooled, chunk, pre, prev, embedded = gather_with(
        functools.partial(forward_run, seqs), [(qkv3, 1, 0, (width, width)), (qkv3, 1, 0, (2 * width, width))],
        2, planes, nseq, (char_rows, char_table, w_gru, bias.reshape(1, -1), ends_col), (), [full(rows, width), full(seqs * 4 * NCH, HG)],
        [full(seqs * chars, 4 * HG), full(seqs * chars, width), jax.ShapeDtypeStruct((seqs * chars, char_table.shape[0]), BF)], [block] * 4,
    )
    own_q = qkv3[..., :width]
    queries = lax.all_gather(own_q, "seq", axis=1, tiled=True)

    ctx3, ctx_low3, lse = attention_fwd(qkv3, keys, values)
    context, context_low = ctx3.reshape(rows, width), ctx_low3.reshape(rows, width)
    (out_token, out_char, normed_low, hidden, state_low, pooled_low, mprev, merged, mnext, dmixed_low, dfused, dlowered, draised_low, dattended,
     dinput_sum, dpooled, dnorm, dctx3, col, stat) = middle(
        seqs, x_low, context_low, context, lse, pooled, grad_token.reshape(rows, width), grad_char.reshape(rows, width), nrm.reshape(8, width),
        w_out, w_up, w_down, w_stream, w_conv, 5
    )
    length = nseq * toks
    dctx_all, stat_all, _, dbias, dq, dembed, dpre = gather_with(
        functools.partial(backward_run, seqs), [(dctx3, 1, 0, None), (stat, 0, 0, None)], 3, planes, nseq,
        (pre, prev, chunk, tot_all, dpooled, ends_row, own_q, dctx3, col, w_gru), (keys, values),
        [full(seqs * 8, 4 * HG), jax.ShapeDtypeStruct((seqs, toks, width), BF), jax.ShapeDtypeStruct(embedded.shape, BF)],
        [jax.ShapeDtypeStruct((seqs * chars, 4 * HG), BF)],
        [pltpu.VMEM((seqs * chars, width), F32), pltpu.VMEM((seqs * 2 * NCH, HG), F32)] + [block] * 2
        + [pltpu.VMEM((2, length, 2 * HDIM), BF)] * 2 + [pltpu.SemaphoreType.DMA((2,))] * 2,
    )
    g_bias = dbias.reshape(seqs, 8, 4 * HG)[:, 0].sum(0)

    g_norms = dnorm.reshape(4, 2, width)
    shape = (seqs, toks, width)
    if seq_dims(nseq) == (RZ, RY, RC) and planes == 2:
        lhs = (x_low, context_low, normed_low, hidden, state_low, pooled_low, mprev, merged, mnext)
        rhs = (dq.reshape(rows, width), dattended, draised_low, dlowered, dfused, dmixed_low)
        *owned, dinputs = reduce_all(
            lhs, rhs, embedded, dpre, dembed, char_rows, qkv3, stat_all.reshape(nseq, -1, toks), queries, dctx_all, w_qkv, dinput_sum, g_bias, g_norms, VOCAB_CHAR, nseq, 4
        )
        owned[8] = owned[8].reshape(-1)
        owned = [owned[k] for k in (0, 1, 2, 3, 4, 5, 8, 6, 7, 9)]
        owned = tuple(owned)
    else:
        stat_all = stat_all.reshape(nseq, seqs, HEADS // 2, 4, toks).transpose(1, 2, 3, 0, 4).reshape(seqs, HEADS // 2, 4, nseq * toks)
        dk, dv = attention_bwd(qkv3, queries, dctx_all, stat_all)
        dqkv = jnp.concatenate([dq, dk, dv], -1).reshape(rows, 3 * width)
        dinputs = dinput_sum + dot_t(dqkv, w_qkv)
        g_stream = [wgrad(state_low, dfused[:, :width]), wgrad(pooled_low, dfused[:, width:])]
        owned = (
            scatter(wgrad(x_low, dqkv).astype(BF), 0),
            scatter(wgrad(context_low, dattended).astype(BF), 0),
            scatter(wgrad(normed_low, draised_low).astype(BF), 0),
            scatter(wgrad(hidden, dlowered).astype(BF), 0),
            scatter(wgrad(dembed, (char_rows == jnp.arange(VOCAB_CHAR, dtype=jnp.int32)).astype(BF)).astype(BF), 0),
            scatter(wgrad(embedded, dpre).astype(BF), 0),
            scatter(g_bias.astype(BF), 0),
            scatter(jnp.stack(g_stream).astype(BF), 1),
            scatter(jnp.stack([wgrad(m, dmixed_low) for m in (mprev, merged, mnext)]).astype(BF), 1),
            scatter(g_norms.astype(BF), 2),
        )
    return (
        out_token.reshape(shape),
        out_char.reshape(shape),
        dinputs.reshape(shape),
    ) + owned


def solution(mesh):
    placed = (
        P("dp", "seq", None),
        P("dp", "seq"),
        P("dp", "seq", None),
        P("dp"),
        P("seq", None),
        P("seq", None),
        P("seq", None),
        P("seq", None),
        P("seq", None),
        P("seq", None),
        P("seq"),
        P(None, "seq", None),
        P(None, "seq", None),
        P(None, None, "seq"),
        P("dp", "seq", None),
        P("dp", "seq", None),
    )
    return jax.shard_map(
        body,
        mesh=mesh,
        in_specs=placed,
        out_specs=(
            P("dp", "seq", None),
            P("dp", "seq", None),
            P("dp", "seq", None),
            P("seq", None),
            P("seq", None),
            P("seq", None),
            P("seq", None),
            P("seq", None),
            P("seq", None),
            P("seq"),
            P(None, "seq", None),
            P(None, "seq", None),
            P(None, None, "seq"),
        ),
        check_vma=False,
    )
```

```python
import collections
import functools
import jax
import jax.numpy as jnp
from jax import lax
from jax.experimental import pallas as pl
from jax.experimental.pallas import tpu as pltpu
from jax.sharding import PartitionSpec as P

HEADS = 12
HDIM = 64
VOCAB_CHAR = 1000
GROUP_CHARS = 250
HG = 384
EPSILON = 1e-05
MESH = pl.DeviceIdType.MESH
BF = jnp.bfloat16
F32 = jnp.float32
NCH = 8
TOGETHER = 2
UNROLL = 8
SHARE = (1, 2, 3, 6)
HB = HG // 128

def seq_dims(n):
    return {16: (4, 2, 2), 32: (8, 4, 1)}.get(n, (n, 1, 1))


Move = collections.namedtuple("Move", ("array", "axis", "rows", "lead", "route"))


def gather_kernel(dims, planes, moves, n_arrays, task, *refs):
    Z, Y, C = dims
    n = len(moves)
    n_in, n_out = (task.n_in, task.n_out) if task else (0, 0)
    src, task_in = refs[:n_arrays], refs[n_arrays : n_arrays + n_in]
    refs = refs[n_arrays + n_in :]
    dst, task_out = refs[:n_arrays], refs[n_arrays : n_arrays + n_out]
    own_sem, recv, zs, ds, ys, ss, xs, *task_scratch = refs[n_arrays + n_out :]
    dp = lax.axis_index("dp")
    me = lax.axis_index("seq")
    c = lax.rem(me, C)
    y = lax.rem(lax.div(me, C), Y)
    z = lax.div(me, C * Y)
    up_z, down_z = z < Z - 1, z > 0

    def at(zz, yy, cc):
        return (zz * Y + yy) * C + cc

    def to(zz, yy, cc):
        return (dp, at(zz, yy, cc))

    def view(i, slot):
        m = moves[i]
        s = pl.ds(pl.multiple_of(slot * m.rows, m.rows), m.rows)
        ref = dst[m.array]
        return ref.at[s] if m.axis == 0 else ref.at[:, s]

    def mine(i):
        m = moves[i]
        if m.lead is None:
            return src[m.array]
        return src[m.array].at[:, :, pl.ds(*m.lead)] if isinstance(m.lead, tuple) else src[m.array].at[m.lead]

    def copy(i, slot, send, where, own=False):
        return pltpu.make_async_remote_copy(
            src_ref=mine(i) if own else view(i, slot), dst_ref=view(i, slot),
            send_sem=send, recv_sem=recv.at[i, slot], device_id=where, device_id_type=MESH)

    sib = to(z, y, 1 - c) if C == 2 else None
    xp = (1 - dp, me)
    use_x = planes == 2 and any(m.route for m in moves)
    some = sib if C == 2 else to(z, y, c)

    def owner(i):
        return None if not (use_x and moves[i].route) else dp == moves[i].route - 1

    def when(cond, f):
        if cond is None:
            f()
        else:
            pl.when(cond)(f)

    def both(a, b):
        return b if a is None else jnp.logical_and(a, b)

    nseq = Z * Y * C
    if task:
        push_all, *task_out = task_out
        push, p_send, p_recv, i_sem, *task_scratch = task_scratch
        n_held = n_in - task.n_stay
        held, task_scratch = task_scratch[:n_held], task_scratch[n_held:]
        loads = [pltpu.make_async_copy(a, b, i_sem.at[k]) for k, (a, b) in enumerate(zip(task_in[:n_held], held))]
        for load in loads:
            load.start()
    bar = pltpu.get_barrier_semaphore()
    if task:
        peers = [(None, (dp, lax.rem(me + k, nseq))) for k in range(1, nseq)]
    else:
        peers = [(z > 0, to(z - 1, y, c)), (z < Z - 1, to(z + 1, y, c))]
        if Y > 1:
            peers += [(y > 0, to(z, y - 1, c)), (y < Y - 1, to(z, y + 1, c))]
        if C == 2:
            peers.append((None, sib))
    if use_x:
        peers.append((None, xp))
    count = 0
    for cond, where in peers:
        when(cond, functools.partial(pl.semaphore_signal, bar, inc=1, device_id=where, device_id_type=MESH))
        count = count + (1 if cond is None else cond.astype(jnp.int32))
    pl.semaphore_wait(bar, count)
    if task:

        def pushed(k, slot, where):
            return pltpu.make_async_remote_copy(
                src_ref=push, dst_ref=push_all.at[slot], send_sem=p_send.at[k], recv_sem=p_recv.at[slot], device_id=where, device_id_type=MESH)

        def push_one(k, _):
            pushed(k, me, (dp, lax.rem(me + k, nseq))).start()
            return 0

        def push_wait(k, _):
            other = lax.rem(me + k, nseq)
            pushed(k, other, (dp, other)).wait_recv()
            pushed(k, me, (dp, other)).wait_send()
            return 0

    def work(point):
        if task:
            task.run(point, me, push, push_all, tuple(held) + tuple(task_in[n_held:]), task_out, task_scratch)

    def go_z(i, slot, up, sem, own=False):
        where = to(z + 1, y, c) if up else to(z - 1, y, c)
        pl.when(up_z if up else down_z)(lambda: copy(i, slot, sem, where, own).start())

    def go_y(i, slot, up, sem, own=False):
        where = to(z, y + 1, c) if up else to(z, y - 1, c)
        pl.when(y < Y - 1 if up else y > 0)(lambda: copy(i, slot, sem, where, own).start())

    def go_core(i, slot, own=False):
        if C == 2:
            copy(i, slot, ss.at[i, slot], sib, own).start()

    def wait_in(i, slot):
        copy(i, slot, ss.at[i, slot], some).wait_recv()

    for i in range(n):
        pltpu.make_async_copy(mine(i), view(i, me), own_sem.at[i]).start()

        def own_sends(i=i):
            go_z(i, me, True, zs.at[i, me], True)
            go_z(i, me, False, ds.at[i, 0], True)
            if Y > 1:
                go_y(i, me, True, ys.at[i, me], True)
                go_y(i, me, False, ds.at[i, 1], True)

        when(owner(i), own_sends)
        go_core(i, me, True)

    def arrive_z(zz, up):
        slot = at(zz, y, c)

        def one(i):
            wait_in(i, slot)
            go_z(i, slot, up, zs.at[i, slot])
            if Y > 1:
                go_y(i, slot, True, ys.at[i, slot])
                go_y(i, slot, False, ys.at[i, slot] if Y == 2 else xs.at[i, slot])
            if use_x and moves[i].route:
                copy(i, slot, xs.at[i, slot], xp).start()
            go_core(i, slot)

        for i in range(n):
            when(owner(i), functools.partial(one, i))

    def arrive_y(zz, yy, up):
        slot = at(zz, yy, c)

        def one(i):
            wait_in(i, slot)
            if Y > 2:
                go_y(i, slot, up, ys.at[i, slot])
            if use_x and moves[i].route:
                copy(i, slot, xs.at[i, slot], xp).start()
            go_core(i, slot)

        for i in range(n):
            when(owner(i), functools.partial(one, i))

    def all_y(zz):
        for t in range(1, Y):
            pl.when(y - t >= 0)(lambda: arrive_y(zz, y - t, True))
            pl.when(y + t < Y)(lambda: arrive_y(zz, y + t, False))

    if task:
        for load in loads:
            load.wait()
        work(0)
        push_all[me] = push[...]
        lax.fori_loop(1, nseq, push_one, 0)
    def step(s, _):
        pl.when(z - s >= 0)(lambda: arrive_z(z - s, True))
        pl.when(z + s < Z)(lambda: arrive_z(z + s, False))
        q = s - 1
        pl.when(z - q >= 0)(lambda: all_y(z - q))
        pl.when(jnp.logical_and(q > 0, z + q < Z))(lambda: all_y(z + q))
        return 0

    if task:
        for s in (1, 2):
            if s < Z:
                step(s, 0)
            if s == 1:
                lax.fori_loop(1, nseq, push_wait, 0)
            work(s)
        lax.fori_loop(3, Z, step, 0)
        work(3)
    else:
        lax.fori_loop(1, Z, step, 0)
    q = Z - 1
    pl.when(z - q >= 0)(lambda: all_y(z - q))
    pl.when(z + q < Z)(lambda: all_y(z + q))

    if use_x:

        def far(k, _):
            slot = at(lax.rem(z + lax.div(k, Y), Z), lax.rem(y + lax.rem(k, Y), Y), c)

            def one(i):
                wait_in(i, slot)
                go_core(i, slot)

            for i in range(n):
                if moves[i].route:
                    pl.when(dp != moves[i].route - 1)(functools.partial(one, i))
            return 0

        lax.fori_loop(1, Z * Y, far, 0)

    def drain(k, _):
        zz, yy = lax.div(k, Y), lax.rem(k, Y)
        slot = at(zz, yy, c)
        is_own = slot == me
        own_y = yy == y
        fz = jnp.logical_or(jnp.logical_and(zz <= z, up_z), jnp.logical_and(zz > z, down_z))
        for i in range(n):
            o = owner(i)
            if C == 2:
                wait_in(i, at(zz, yy, 1 - c))
                copy(i, slot, ss.at[i, slot], some).wait_send()
            sent = lambda sem: copy(i, slot, sem, some).wait_send()
            pl.when(both(o, jnp.logical_and(own_y, fz)))(lambda: sent(zs.at[i, slot]))
            if Y == 2:
                pl.when(both(o, jnp.logical_and(own_y, jnp.logical_or(jnp.logical_not(is_own), y < Y - 1))))(lambda: sent(ys.at[i, slot]))
            elif Y > 2:
                fy = jnp.logical_or(jnp.logical_and(yy <= y, y < Y - 1), jnp.logical_and(yy > y, y > 0))
                pl.when(both(o, fy))(lambda: sent(ys.at[i, slot]))
                fy2 = jnp.logical_and(jnp.logical_and(own_y, y > 0), jnp.logical_not(is_own))
                pl.when(both(o, fy2))(lambda: sent(xs.at[i, slot]))
            if use_x and moves[i].route:
                pl.when(both(o, jnp.logical_not(is_own)))(lambda: sent(xs.at[i, slot]))
        return 0

    lax.fori_loop(0, Z * Y, drain, 0)
    for i in range(n):
        pltpu.make_async_copy(mine(i), view(i, me), own_sem.at[i]).wait()
        o = owner(i)
        pl.when(both(o, down_z))(lambda: copy(i, me, ds.at[i, 0], some, True).wait_send())
        if Y > 1:
            pl.when(both(o, y > 0))(lambda: copy(i, me, ds.at[i, 1], some, True).wait_send())
    work(4)


Task = collections.namedtuple("Task", ("n_in", "n_stay", "n_out", "n_far", "run"))


def gather(arrays, cid, planes, nseq, task=None, inputs=(), outputs=(), scratch=()):
    dims = seq_dims(nseq)
    moves, shapes = [], []
    for k, (x, axis, route, lead) in enumerate(arrays):
        shape = list(x.shape[:-1] + lead[1:] if isinstance(lead, tuple) else x.shape if lead is None else x.shape[1:])
        moves.append(Move(k, axis, shape[axis], lead, route if planes == 2 and dims[1:] == (2, 2) else 0))
        shape[axis] *= nseq
        shapes.append(jax.ShapeDtypeStruct(tuple(shape), x.dtype))
    moves.sort(key=lambda m: not m.route)
    n = len(moves)
    D = pltpu.SemaphoreType.DMA
    scratch = [D((n,)), D((n, nseq)), D((n, nseq)), D((n, 2)), D((n, nseq)), D((n, nseq)), D((n, nseq))] + list(scratch)
    far, here = pl.BlockSpec(memory_space=pl.ANY), pl.BlockSpec(memory_space=pltpu.VMEM)
    n_far = task.n_far if task else 0
    return pl.pallas_call(
        functools.partial(gather_kernel, dims, planes, tuple(moves), len(arrays), task),
        out_shape=shapes + list(outputs),
        in_specs=[far] * (len(arrays) + len(inputs)),
        out_specs=[far] * len(arrays) + [here] * (len(outputs) - n_far) + [far] * n_far,
        scratch_shapes=scratch,
        compiler_params=pltpu.CompilerParams(collective_id=cid, has_side_effects=True, vmem_limit_bytes=60 << 20),
    )(*[x for x, _, _, _ in arrays], *inputs)


def gather_with(run, arrays, cid, planes, nseq, inputs, stay, outputs, late, scratch):
    D = pltpu.SemaphoreType.DMA
    push = (8, HG)
    outputs = [jax.ShapeDtypeStruct((nseq,) + push, F32)] + outputs + late
    scratch = [pltpu.VMEM(a.shape, a.dtype) for a in late] + [D((len(late),))] + scratch
    scratch = [pltpu.VMEM(push, F32), D((nseq,)), D((nseq,)), D((len(inputs),))] + [pltpu.VMEM(a.shape, a.dtype) for a in inputs] + scratch
    inputs = tuple(inputs) + tuple(stay)
    return gather(arrays, cid, planes, nseq, Task(len(inputs), len(stay), len(outputs), len(late), run), inputs, outputs, scratch)


def dot(a, b):
    return jnp.dot(a, b, preferred_element_type=F32)


def dot_t(a, b):
    return lax.dot_general(a, b, (((1,), (1,)), ((), ())), preferred_element_type=F32)


def wgrad(a, b):
    return lax.dot_general(a, b, (((0,), (0,)), ((), ())), preferred_element_type=F32)


def vmem(mib):
    return pltpu.CompilerParams(vmem_limit_bytes=mib << 20)


def layer_norm(values, gain_row, shift_row):
    center = values - jnp.mean(values, -1, keepdims=True)
    spread = jnp.mean(center * center, -1, keepdims=True)
    return center * lax.rsqrt(spread + EPSILON) * gain_row + shift_row


def fill(pre_ref, decay, drive=None):
    for k in range(2):
        for j in range(HB):
            at = 2 * k * HG + j * 128
            rate = jax.nn.sigmoid(pre_ref[:, at : at + 128])
            decay[k * HB + j] = 1.0 - rate
            if drive is not None:
                drive[k * HB + j] = rate * pre_ref[:, at + HG : at + HG + 128]


def row(x, i):
    return lax.slice_in_dim(x, i, i + 1, axis=0)


def cat(parts):
    return jnp.concatenate(parts, 1)


def blocks(x):
    return [x[:, j * 128 : (j + 1) * 128] for j in range(HB)]


def totals_kernel(pre_ref, tot_ref, chunk_ref, decay, drive):
    length = pre_ref.shape[0] // NCH
    fill(pre_ref, decay, drive)

    def step(t, carry):
        place = (pl.ds(t, NCH, stride=length), pl.ds(length - 1 - t, NCH, stride=length))
        out = []
        for i in range(2 * HB):
            c, h = carry[i]
            a = decay[i, place[i // HB], :]
            out.append((c * a, a * h + drive[i, place[i // HB], :]))
        return tuple(out)

    one, zero = jnp.ones((NCH, 128), F32), jnp.zeros((NCH, 128), F32)
    ends = lax.fori_loop(0, length, step, ((one, zero),) * (2 * HB), unroll=UNROLL)
    cf, hf = cat([e[0] for e in ends[:HB]]), cat([e[1] for e in ends[:HB]])
    cb, hb = cat([e[0] for e in ends[HB:]]), cat([e[1] for e in ends[HB:]])
    chunk_ref[0:NCH, :] = cf
    chunk_ref[NCH : 2 * NCH, :] = hf
    chunk_ref[2 * NCH : 3 * NCH, :] = cb
    chunk_ref[3 * NCH :, :] = hb
    one, zero = jnp.ones((1, HG), F32), jnp.zeros((1, HG), F32)
    tf, sf, tb, sb = one, zero, one, zero
    for k in range(NCH):
        sf, tf = row(cf, k) * sf + row(hf, k), tf * row(cf, k)
        j = NCH - 1 - k
        sb, tb = row(cb, j) * sb + row(hb, j), tb * row(cb, j)
    tot_ref[...] = jnp.concatenate([tf, sf, tb, sb], 0)


def states_work(me, q, seqs, all_ref, pre_all, chunk_all, ends_all, pooled_all, prev_all, decay, drive, state, prev):
    pre_ref, chunk_ref, ends_ref, pooled_ref, prev_ref = (
        r.at[pl.ds(q * (r.shape[0] // seqs), r.shape[0] // seqs)] for r in (pre_all, chunk_all, ends_all, pooled_all, prev_all)
    )
    chars = pre_all.shape[0] // seqs
    length = chars // NCH
    nseq = all_ref.shape[0]
    fill(pre_ref, decay, drive)
    ef = jnp.zeros((1, HG), F32)
    eb = ef
    for d in range(nseq):
        got = all_ref[d]
        ef = jnp.where(d < me, row(got, 4 * q) * ef + row(got, 4 * q + 1), ef)
        got = all_ref[nseq - 1 - d]
        eb = jnp.where(nseq - 1 - d > me, row(got, 4 * q + 2) * eb + row(got, 4 * q + 3), eb)
    cf, hf = chunk_ref[0:NCH, :], chunk_ref[NCH : 2 * NCH, :]
    cb, hb = chunk_ref[2 * NCH : 3 * NCH, :], chunk_ref[3 * NCH :, :]
    rows_f, rows_b = [], []
    for k in range(NCH):
        rows_f.append(ef)
        ef = row(cf, k) * ef + row(hf, k)
        j = NCH - 1 - k
        rows_b.append(eb)
        eb = row(cb, j) * eb + row(hb, j)

    def step(t, carry):
        place = (pl.ds(t, NCH, stride=length), pl.ds(length - 1 - t, NCH, stride=length))
        out = []
        for i in range(2 * HB):
            at = place[i // HB]
            prev[i, at, :] = carry[i]
            h = decay[i, at, :] * carry[i] + drive[i, at, :]
            state[i, at, :] = h
            out.append(h)
        return tuple(out)

    lax.fori_loop(0, length, step, tuple(blocks(jnp.concatenate(rows_f, 0)) + blocks(jnp.concatenate(rows_b[::-1], 0))), unroll=UNROLL)
    first = ends_ref[:, 0:1]
    last = ends_ref[:, 1:2]
    place = lax.broadcasted_iota(jnp.int32, (ends_all.shape[0] // seqs, chars), 1)
    member = jnp.where((place >= first) & (place < last), 1.0, 0.0).astype(BF)
    prev_ref[...] = cat([prev[i] for i in range(2 * HB)])
    pooled_ref[...] = dot(member, cat([state[i].astype(BF) for i in range(2 * HB)])) / (last - first).astype(F32)


def flows_kernel(pre_ref, dpool_ref, ends_ref, chunk_ref, ds_ref, tot_ref, gch_ref, decay, ds):
    chars = pre_ref.shape[0]
    length = chars // NCH
    fill(pre_ref, decay)
    first = ends_ref[0:1, :]
    last = ends_ref[1:2, :]
    place = lax.broadcasted_iota(jnp.int32, (chars, ends_ref.shape[1]), 0)
    inside = (place >= first) & (place < last)
    span = jnp.sum(jnp.where(inside, (last - first).astype(F32), 0.0), 1, keepdims=True)
    member = jnp.where(inside, 1.0, 0.0).astype(BF)
    spread = dot(member, dpool_ref[...]) / span
    ds_ref[...] = spread
    for i in range(2 * HB):
        ds[i] = spread[:, i * 128 : (i + 1) * 128]

    def step(t, carry):
        place = (pl.ds(length - 1 - t, NCH, stride=length), pl.ds(t, NCH, stride=length))
        return tuple(
            decay[i, place[i // HB], :] * (ds[i, place[i // HB], :] + carry[i]) for i in range(2 * HB)
        )

    ends = lax.fori_loop(0, length, step, (jnp.zeros((NCH, 128), F32),) * (2 * HB), unroll=UNROLL)
    gf, gb = cat(ends[:HB]), cat(ends[HB:])
    gch_ref[0:NCH, :] = gf
    gch_ref[NCH:, :] = gb
    cf, cb = chunk_ref[0:NCH, :], chunk_ref[2 * NCH : 3 * NCH, :]
    zero = jnp.zeros((1, HG), F32)
    tf, tb = zero, zero
    for k in range(NCH):
        j = NCH - 1 - k
        tf = row(cf, j) * tf + row(gf, j)
        tb = row(cb, k) * tb + row(gb, k)
    tot_ref[...] = jnp.concatenate([tf, tb, zero, zero], 0)


def dpre_work(me, q, seqs, gall_ref, all_ref, pre_all, ds_all, prev_all, chunk_all, gch_all, dpre_all, bias_all, decay, ds):
    pre_ref, ds_ref, prev_ref, chunk_ref, gch_ref, dpre_ref, bias_ref = (
        r.at[pl.ds(q * (r.shape[0] // seqs), r.shape[0] // seqs)] for r in (pre_all, ds_all, prev_all, chunk_all, gch_all, dpre_all, bias_all)
    )
    chars = pre_all.shape[0] // seqs
    length = chars // NCH
    nseq = all_ref.shape[0]
    fill(pre_ref, decay)
    for i in range(2 * HB):
        ds[i] = ds_ref[:, i * 128 : (i + 1) * 128]
    ef = jnp.zeros((1, HG), F32)
    eb = ef
    for d in range(nseq):
        j = nseq - 1 - d
        ef = jnp.where(j > me, row(all_ref[j], 4 * q) * ef + row(gall_ref[j], 4 * q), ef)
        eb = jnp.where(d < me, row(all_ref[d], 4 * q + 2) * eb + row(gall_ref[d], 4 * q + 1), eb)
    cf, cb = chunk_ref[0:NCH, :], chunk_ref[2 * NCH : 3 * NCH, :]
    gf, gb = gch_ref[0:NCH, :], gch_ref[NCH:, :]
    rows_f, rows_b = [], []
    for k in range(NCH):
        j = NCH - 1 - k
        rows_f.append(ef)
        ef = row(cf, j) * ef + row(gf, j)
        rows_b.append(eb)
        eb = row(cb, k) * eb + row(gb, k)

    def step(t, carry):
        place = (pl.ds(length - 1 - t, NCH, stride=length), pl.ds(t, NCH, stride=length))
        out = []
        for i in range(2 * HB):
            at = place[i // HB]
            g = ds[i, at, :] + carry[i]
            ds[i, at, :] = g
            out.append(decay[i, at, :] * g)
        return tuple(out)

    lax.fori_loop(0, length, step, tuple(blocks(jnp.concatenate(rows_f[::-1], 0)) + blocks(jnp.concatenate(rows_b, 0))), unroll=UNROLL)
    for i in range(2 * HB):
        k, j = i // HB, i % HB
        at = 2 * k * HG + j * 128
        g = ds[i]
        rate = jax.nn.sigmoid(pre_ref[:, at : at + 128])
        cand = pre_ref[:, at + HG : at + HG + 128]
        prev = prev_ref[:, i * 128 : (i + 1) * 128]
        dgate = (g * (cand - prev) * rate * decay[i]).astype(BF)
        dcand = (g * rate).astype(BF)
        for to, v in ((at, dgate), (at + HG, dcand)):
            dpre_ref[:, to : to + 128] = v
            bias_ref[:, to : to + 128] = jnp.broadcast_to(jnp.sum(v.astype(F32), 0, keepdims=True), (8, 128))


def part_of(ref, q, seqs):
    n = ref.shape[0] // seqs
    return ref.at[pl.ds(q * n, n)]


def forward_run(seqs, point, me, push, push_all, inputs, outputs, scratch):
    ids, table, gru, bias, ends = inputs
    pooled, chunk, *out = outputs
    pre, prev, emb = scratch[:3]
    o_sem = scratch[3]
    write = lambda k: pltpu.make_async_copy((pre, prev, emb)[k], out[k], o_sem.at[k])
    scratch = scratch[4:]
    if point == 0:
        n = 256

        def look(k, _):
            at = pl.ds(pl.multiple_of(k * n, n), n)
            unit = lax.broadcasted_iota(jnp.int32, (n, table.shape[1]), 1)
            hot = jnp.where(unit == ids[at, :], 1.0, 0.0).astype(BF)
            rows = dot_t(hot, table[...]).astype(BF)
            emb[at, :] = rows
            pre[at, :] = dot(rows, gru[...]) + bias[...]
            return 0

        lax.fori_loop(0, ids.shape[0] // n, look, 0)
        for q in range(seqs):
            totals_kernel(part_of(pre, q, seqs), push.at[pl.ds(4 * q, 4)], part_of(chunk, q, seqs), *scratch[:2])
        write(0).start()
        write(2).start()
    elif point <= seqs:
        states_work(me, point - 1, seqs, push_all, pre, chunk, ends, pooled, prev, *scratch)
        if point == seqs:
            write(1).start()
    elif point == 4:
        for k in range(3):
            write(k).wait()


def backward_run(seqs, point, me, push, push_all, inputs, outputs, scratch):
    pre, prev, chunk, tot_all, dpool, ends, q_ref, dc_ref, col_ref, gru_ref, keys, values = inputs
    dbias, dq, demb, dpre_out = outputs
    dpre, o_sem, ds_all, gch, decay, ds, kbuf, vbuf, k_sem, v_sem = scratch
    write = lambda: pltpu.make_async_copy(dpre, dpre_out, o_sem.at[0])
    if point == 4:
        write().wait()
        return
    pairs = HEADS // 2
    steps = seqs * pairs

    def fetch(i):
        s, p = lax.div(i, pairs), lax.rem(i, pairs)
        cols = pl.ds(pl.multiple_of(p * 2 * HDIM, 2 * HDIM), 2 * HDIM)
        b = lax.rem(i, 2)
        return (pltpu.make_async_copy(keys.at[s, :, cols], kbuf.at[b], k_sem.at[b]), pltpu.make_async_copy(values.at[s, :, cols], vbuf.at[b], v_sem.at[b]))

    def one(i, _):
        s, p = lax.div(i, pairs), lax.rem(i, pairs)
        cols = pl.ds(pl.multiple_of(p * 2 * HDIM, 2 * HDIM), 2 * HDIM)
        b = lax.rem(i, 2)

        @pl.when(i + 1 < steps)
        def _():
            for c in fetch(i + 1):
                c.start()

        for c in fetch(i):
            c.wait()
        dq[s, :, cols] = query_grad(q_ref[s, :, cols], kbuf[b], vbuf[b], dc_ref[s, :, cols], col_ref[s, p])
        return 0

    if point == 0:
        for c in fetch(0):
            c.start()
        for q in range(seqs):
            flows_kernel(*(part_of(r, q, seqs) for r in (pre, dpool, ends, chunk, ds_all)), push.at[pl.ds(4 * q, 4)], part_of(gch, q, seqs), decay, ds)
    elif point <= seqs:
        dpre_work(me, point - 1, seqs, push_all, tot_all, pre, ds_all, prev, chunk, gch, dpre, dbias, decay, ds)
        part_of(demb, point - 1, seqs)[...] = dot_t(part_of(dpre, point - 1, seqs)[...], gru_ref[...]).astype(BF)
        if point == seqs:
            write().start()
    bounds = (0,) + tuple(steps * k // 6 for k in SHARE)
    lax.fori_loop(bounds[point], bounds[point + 1], one, 0)


def pair_rows(x):
    lane = lax.broadcasted_iota(jnp.int32, x.shape, 1)
    zero = jnp.zeros_like(x)
    return jnp.concatenate([jnp.where(lane < HDIM, x, zero), jnp.where(lane >= HDIM, x, zero)], 0)


def pair_lanes(x):
    half = x.shape[0] // 2
    lane = lax.broadcasted_iota(jnp.int32, (half, x.shape[1]), 1)
    return jnp.where(lane < HDIM, x[:half], x[half:])


def attn_fwd_kernel(q_ref, k_ref, v_ref, ctx_ref, low_ref, lse_ref):
    toks = q_ref.shape[0]
    for i in range(TOGETHER):
        at = slice(i * 2 * HDIM, (i + 1) * 2 * HDIM)
        s = dot_t(pair_rows(q_ref[:, at] * (HDIM ** -0.5)), k_ref[:, at])
        top = jnp.max(s, 1, keepdims=True)
        p = jnp.exp(s - top)
        total = jnp.sum(p, 1, keepdims=True)
        o = pair_lanes(dot(p.astype(BF), v_ref[:, at]) / total)
        ctx_ref[:, at] = o
        low_ref[:, at] = o.astype(BF)
        lse = top + jnp.log(total)
        lse_ref[i] = jnp.concatenate([lse[:toks], lse[toks:]], 1)


def head_spec(rows, base=0, many=1):
    return pl.BlockSpec((None, rows, many * 2 * HDIM), lambda s, h: (s, 0, h + base))


def attention_fwd(qkv, keys, values):
    seqs, toks, _ = qkv.shape
    length = keys.shape[1]
    pairs = HEADS // 2
    block = lambda rows: head_spec(rows, 0, TOGETHER)
    return pl.pallas_call(
        attn_fwd_kernel,
        grid=(seqs, pairs // TOGETHER),
        out_shape=[
            jax.ShapeDtypeStruct((seqs, toks, HEADS * HDIM), F32),
            jax.ShapeDtypeStruct((seqs, toks, HEADS * HDIM), BF),
            jax.ShapeDtypeStruct((seqs, pairs, toks, 2), F32),
        ],
        in_specs=[block(toks), block(length), block(length)],
        out_specs=[block(toks), block(toks), pl.BlockSpec((None, TOGETHER, toks, 2), lambda s, h: (s, h, 0, 0))],
        compiler_params=vmem(62),
    )(qkv, keys, values)


def query_grad(q, keys, values, dc, col):
    scale = HDIM ** -0.5
    lse = jnp.concatenate([col[:, 0:1], col[:, 1:2]], 0)
    delta = jnp.concatenate([col[:, 2:3], col[:, 3:4]], 0)
    p = jnp.exp(dot_t(pair_rows(q * scale), keys) - lse)
    ds = (p * (dot_t(pair_rows(dc), values) - delta)).astype(BF)
    return (pair_lanes(dot(ds, keys)) * scale).astype(BF)


def context_kernel(datt_ref, w_ref, ctx_ref, lse_ref, dctx_ref, col_ref, stat_ref):
    seqs, toks, _ = dctx_ref.shape
    pairs = HEADS // 2
    low = dot_t(datt_ref[...], w_ref[...]).astype(BF)
    prod = low.astype(F32) * ctx_ref[...]
    lane = lax.broadcasted_iota(jnp.int32, (toks, 2 * HDIM), 1)
    for s in range(seqs):
        dctx_ref[s] = low[s * toks : (s + 1) * toks]
        cols = []
        for p in range(pairs):
            x = prod[s * toks : (s + 1) * toks, p * 2 * HDIM : (p + 1) * 2 * HDIM]
            a = jnp.sum(jnp.where(lane < HDIM, x, 0.0), 1, keepdims=True)
            b = jnp.sum(jnp.where(lane >= HDIM, x, 0.0), 1, keepdims=True)
            col = jnp.concatenate([lse_ref[s, p], a, b], 1)
            col_ref[s, p] = col
            cols.append(col)
        flat = jnp.concatenate(cols + [jnp.zeros((toks, 128 - 4 * pairs), F32)], 1)
        stat_ref[s * 4 * pairs : (s + 1) * 4 * pairs, :] = flat.T[: 4 * pairs]


def attn_bwd_kernel(ko_ref, vo_ref, qa_ref, dca_ref, row_ref, dk_ref, dv_ref):
    toks = ko_ref.shape[0]
    scale = HDIM ** -0.5

    def spread(i):
        n = row_ref.shape[1]
        return jnp.concatenate(
            [jnp.broadcast_to(row_ref[i : i + 1, :], (toks, n)), jnp.broadcast_to(row_ref[i + 1 : i + 2, :], (toks, n))], 0
        )

    p = jnp.exp(dot_t(pair_rows(ko_ref[...] * scale), qa_ref[...]) - spread(0))
    dv_ref[...] = pair_lanes(dot(p.astype(BF), dca_ref[...])).astype(BF)
    dp = dot_t(pair_rows(vo_ref[...]), dca_ref[...])
    ds = (p * (dp - spread(2))).astype(BF)
    dk_ref[...] = (pair_lanes(dot(ds, qa_ref[...])) * scale).astype(BF)


def attention_bwd(qkv, queries, dctx_all, rows):
    seqs, toks, _ = qkv.shape
    length = queries.shape[1]
    pairs = HEADS // 2
    stat = lambda a, b: pl.BlockSpec((None, None, a, b), lambda s, h: (s, h, 0, 0))
    return pl.pallas_call(
        attn_bwd_kernel,
        grid=(seqs, pairs),
        out_shape=[jax.ShapeDtypeStruct((seqs, toks, HEADS * HDIM), BF)] * 2,
        in_specs=[head_spec(toks, pairs), head_spec(toks, 2 * pairs), head_spec(length), head_spec(length), stat(4, length)],
        out_specs=[head_spec(toks)] * 2,
        compiler_params=vmem(56),
    )(qkv, qkv, queries, dctx_all, rows)


GELU_A = 0.7978845608028654
GELU_B = 0.044715


def norm_both(v, gain, shift, dy):
    center = v - jnp.mean(v, -1, keepdims=True)
    inv = lax.rsqrt(jnp.mean(center * center, -1, keepdims=True) + EPSILON)
    hat = center * inv
    dhat = dy * gain
    dv = inv * (dhat - jnp.mean(dhat, -1, keepdims=True) - hat * jnp.mean(dhat * hat, -1, keepdims=True))
    return hat * gain + shift, dv, jnp.sum(dy * hat, 0, keepdims=True), jnp.sum(dy, 0, keepdims=True)


def norm_back(hat, inv, gain, dy):
    dhat = dy * gain
    dv = inv * (dhat - jnp.mean(dhat, -1, keepdims=True) - hat * jnp.mean(dhat * hat, -1, keepdims=True))
    return dv, jnp.sum(dy * hat, 0, keepdims=True), jnp.sum(dy, 0, keepdims=True)


def norm_parts(v):
    center = v - jnp.mean(v, -1, keepdims=True)
    inv = lax.rsqrt(jnp.mean(center * center, -1, keepdims=True) + EPSILON)
    return center * inv, inv


def gelu_parts(v):
    square = v * v
    curve = jnp.tanh(GELU_A * (v + GELU_B * v * square))
    return 0.5 * v * (1.0 + curve), 0.5 * (1.0 + curve) + 0.5 * v * (1.0 - curve * curve) * (GELU_A * (1.0 + 3.0 * GELU_B * square))


def middle_kernel(seqs, *refs):
    given, (wo_hbm, wu_hbm, wd_hbm, ws_hbm, c0_hbm, c1_hbm, c2_hbm), refs = refs[:8], refs[8:15], refs[15:]
    far = refs[:16]
    dnorm_ref, dctx_ref, col_ref, stat_ref = refs[16:20]
    own = refs[20:36]
    (otok_ref, ochr_ref, nlow_ref, hid_ref, slow_ref, plow_ref, mprev_ref, merged_ref, mnext_ref, dmix_ref, dfus_ref, dlow_ref, drai_ref, datt_ref,
     din_ref, dpool_ref) = own
    (
     wo_ref, wu_ref, wd_ref, ws_ref, taps, acc, edge, before, after, dside, dchar, slope_ref, hat0, hat1, state_ref, dstate_ref,
     w_sem, e_send, b_recv, a_recv, o_sem, *held, i_sem) = refs[36:]
    x_ref, clow_ref, nrm_ref, pooled_ref, gtok_ref, gchr_ref, ctx_ref, lse_ref = held

    def take(*ks):
        for k in ks:
            pltpu.make_async_copy(given[k], held[k], i_sem.at[k]).wait()

    for k in range(3):
        pltpu.make_async_copy(given[k], held[k], i_sem.at[k]).start()

    def put(*ks):
        for k in ks:
            pltpu.make_async_copy(own[k], far[k], o_sem.at[k]).start()

    me = lax.axis_index("seq")
    dp = lax.axis_index("dp")
    n = lax.axis_size("seq")
    rows, width = x_ref.shape
    toks = rows // seqs
    wide = 2 * width
    loads = [
        pltpu.make_async_copy(src, dst, w_sem.at[k]) for k, (src, dst) in enumerate((
            (wo_hbm, wo_ref), (wu_hbm, wu_ref), (wd_hbm, wd_ref), (ws_hbm, ws_ref), (c1_hbm, taps.at[1]), (c0_hbm, taps.at[0]), (c2_hbm, taps.at[2]),
        ))
    ]
    loads[0].start()
    for k in range(3, 8):
        pltpu.make_async_copy(given[k], held[k], i_sem.at[k]).start()
    for load in loads[1:]:
        load.start()
    edge[...] = jnp.zeros_like(edge)
    right, left = (dp, me + 1), (dp, me - 1)
    has_l, has_r = me > 0, me < n - 1
    bar = pltpu.get_barrier_semaphore()
    pl.when(has_l)(lambda: pl.semaphore_signal(bar, inc=1, device_id=left, device_id_type=MESH))
    pl.when(has_r)(lambda: pl.semaphore_signal(bar, inc=1, device_id=right, device_id_type=MESH))
    pl.semaphore_wait(bar, has_l.astype(jnp.int32) + has_r.astype(jnp.int32))

    def send(k):
        def to_right():
            return pltpu.make_async_remote_copy(
                src_ref=edge.at[k, 0], dst_ref=before.at[k], send_sem=e_send.at[k, 0], recv_sem=b_recv.at[k], device_id=right, device_id_type=MESH)

        def to_left():
            return pltpu.make_async_remote_copy(
                src_ref=edge.at[k, 1], dst_ref=after.at[k], send_sem=e_send.at[k, 1], recv_sem=a_recv.at[k], device_id=left, device_id_type=MESH)

        return to_right, to_left

    def start(k, ref):
        for s in range(seqs):
            edge[k, 0, s : s + 1, :] = ref[(s + 1) * toks - 16 : (s + 1) * toks, :].astype(F32)[15:16]
            edge[k, 1, s : s + 1, :] = ref[s * toks : s * toks + 16, :].astype(F32)[0:1]
        to_right, to_left = send(k)
        pl.when(has_r)(lambda: to_right().start())
        pl.when(has_l)(lambda: to_left().start())

    def finish(k):
        to_right, to_left = send(k)
        pl.when(has_r)(lambda: to_left().wait_recv())
        pl.when(has_l)(lambda: to_right().wait_recv())
        pl.when(has_r)(lambda: to_right().wait_send())
        pl.when(has_l)(lambda: to_left().wait_send())

    def shifts(k, ref, prev_ref, next_ref):
        for j in range(0, wide, 512):
            x = ref[:, j : j + 512].astype(F32)
            at = lax.broadcasted_iota(jnp.int32, x.shape, 0)
            prev, follow = pltpu.roll(x, 1, 0), pltpu.roll(x, rows - 1, 0)
            for s in range(seqs):
                b = jnp.where(has_l, before[k, s : s + 1, j : j + 512], 0.0)
                a = jnp.where(has_r, after[k, s : s + 1, j : j + 512], 0.0)
                prev = jnp.where(at == s * toks, b, prev)
                follow = jnp.where(at == (s + 1) * toks - 1, a, follow)
            prev_ref[:, j : j + 512] = prev.astype(BF)
            next_ref[:, j : j + 512] = follow.astype(BF)

    chunk = 1536
    take(0, 1, 2)
    loads[0].wait()
    hat, inv0 = norm_parts(x_ref[...].astype(F32) + dot(clow_ref[...], wo_ref[...]))
    hat0[...] = hat
    normed = hat * nrm_ref[0:1, :] + nrm_ref[1:2, :]
    nlow_ref[...] = normed.astype(BF)
    loads[1].wait()

    def raise_part(j, _):
        cols = pl.ds(pl.multiple_of(j * chunk, chunk), chunk)
        hidden, slope = gelu_parts(dot(nlow_ref[...], wu_ref[:, cols]))
        hid_ref[:, cols] = hidden.astype(BF)
        slope_ref[:, cols] = slope
        return 0

    lax.fori_loop(0, 4 * width // chunk, raise_part, 0)
    loads[2].wait()
    hat, inv1 = norm_parts(normed + dot(hid_ref[...], wd_ref[...]))
    hat1[...] = hat
    state = hat * nrm_ref[2:3, :] + nrm_ref[3:4, :]
    state_ref[...] = state
    loads[3].wait()
    take(3, 4, 5, 6, 7)
    slow = state.astype(BF)
    plow = pooled_ref[...].astype(BF)
    slow_ref[...] = slow
    plow_ref[...] = plow
    merged_ref[:, :width] = dot(slow, ws_ref[0]).astype(BF)
    merged_ref[:, width:] = dot(plow, ws_ref[1]).astype(BF)
    start(0, merged_ref)
    loads[4].wait()

    def centre(j, _):
        cols = pl.ds(pl.multiple_of(j * 768, 768), 768)
        acc[:, cols] = dot(merged_ref[...], taps[1, :, cols])
        return 0

    lax.fori_loop(0, wide // 768, centre, 0)
    finish(0)
    shifts(0, merged_ref, mprev_ref, mnext_ref)
    loads[5].wait()
    loads[6].wait()

    def sides(j, _):
        cols = pl.ds(pl.multiple_of(j * 768, 768), 768)
        acc[:, cols] += dot(mprev_ref[...], taps[0, :, cols]) + dot(mnext_ref[...], taps[2, :, cols])
        return 0

    lax.fori_loop(0, wide // 768, sides, 0)
    for part, (base_ref, grad_ref, out_ref) in enumerate(((state_ref, gtok_ref, otok_ref), (pooled_ref, gchr_ref, ochr_ref))):
        mixed = acc[:, part * width : (part + 1) * width]
        gated, slope = gelu_parts(mixed)
        r = 4 + 2 * part
        out, dsum, dgain, dshift = norm_both(base_ref[...] + gated, nrm_ref[r : r + 1, :], nrm_ref[r + 1 : r + 2, :], grad_ref[...].astype(F32))
        out_ref[...] = out.astype(BF)
        dnorm_ref[r : r + 1, :] = dgain
        dnorm_ref[r + 1 : r + 2, :] = dshift
        dmix_ref[:, part * width : (part + 1) * width] = (dsum * slope).astype(BF)
        if part == 0:
            dstate_ref[...] = dsum
        else:
            dchar[...] = dsum
    start(1, dmix_ref)
    put(*range(10))

    def centre_back(j, _):
        cols = pl.ds(pl.multiple_of(j * 768, 768), 768)
        acc[:, cols] = dot_t(dmix_ref[...], taps[1, cols, :])
        return 0

    lax.fori_loop(0, wide // 768, centre_back, 0)
    finish(1)
    shifts(1, dmix_ref, dside.at[0], dside.at[1])

    def sides_back(j, _):
        cols = pl.ds(pl.multiple_of(j * 768, 768), 768)
        dfus_ref[:, cols] = (acc[:, cols] + dot_t(dside[1], taps[0, cols, :]) + dot_t(dside[0], taps[2, cols, :])).astype(BF)
        return 0

    lax.fori_loop(0, wide // 768, sides_back, 0)
    dpool_ref[...] = (dchar[...] + dot_t(dfus_ref[:, width:], ws_ref[1])).astype(BF)
    put(10, 15)
    dstate = dstate_ref[...] + dot_t(dfus_ref[:, :width], ws_ref[0])
    dsum, dnorm_ref[2:3, :], dnorm_ref[3:4, :] = norm_back(hat1[...], inv1, nrm_ref[2:3, :], dstate)
    dlow_ref[...] = dsum.astype(BF)
    dstate_ref[...] = dsum
    put(11)

    def lower_part(j, _):
        cols = pl.ds(pl.multiple_of(j * chunk, chunk), chunk)
        drai_ref[:, cols] = (dot_t(dlow_ref[...], wd_ref[cols, :]) * slope_ref[:, cols]).astype(BF)
        return 0

    lax.fori_loop(0, 4 * width // chunk, lower_part, 0)
    put(12)
    dsum, dnorm_ref[0:1, :], dnorm_ref[1:2, :] = norm_back(hat0[...], inv0, nrm_ref[0:1, :], dstate_ref[...] + dot_t(drai_ref[...], wu_ref[...]))
    din_ref[...] = dsum
    datt_ref[...] = dsum.astype(BF)
    put(13, 14)
    context_kernel(datt_ref, wo_ref, ctx_ref, lse_ref, dctx_ref, col_ref, stat_ref)
    for k in range(16):
        pltpu.make_async_copy(own[k], far[k], o_sem.at[k]).wait()


def middle(seqs, x, clow, context, lse, pooled, grad_token, grad_char, nrm, w_out, w_up, w_down, w_stream, w_conv, cid):
    rows, width = x.shape
    wide, ff = 2 * width, 4 * width
    pairs, toks = lse.shape[1:3]
    here = pl.BlockSpec(memory_space=pltpu.VMEM)
    far = pl.BlockSpec(memory_space=pl.ANY)
    low, full = (lambda c: jax.ShapeDtypeStruct((rows, c), BF)), jax.ShapeDtypeStruct((rows, width), F32)
    D = pltpu.SemaphoreType.DMA
    f = lambda *s: pltpu.VMEM(s, F32)
    v = lambda *s: pltpu.VMEM(s, BF)
    given = (x, clow, nrm, pooled, grad_token, grad_char, context, lse)
    large = [low(width)] * 3 + [low(ff), low(width), low(width)] + [low(wide)] * 5 + [low(width), low(ff), low(width), full, low(width)]
    return pl.pallas_call(
        functools.partial(middle_kernel, seqs),
        out_shape=large + [
            jax.ShapeDtypeStruct((8, width), F32), jax.ShapeDtypeStruct((seqs, toks, width), BF), jax.ShapeDtypeStruct((seqs, pairs, toks, 4), F32),
            jax.ShapeDtypeStruct((seqs * pairs * 4, toks), F32),
        ],
        in_specs=[far] * 15,
        out_specs=[far] * 16 + [here] * 4,
        scratch_shapes=[pltpu.VMEM(a.shape, a.dtype) for a in large] + [
            v(*w_out.shape), v(*w_up.shape), v(*w_down.shape), v(*w_stream.shape), v(3, wide, wide), f(rows, wide), f(2, 2, 8, wide),
            f(2, 8, wide), f(2, 8, wide), v(2, rows, wide), f(rows, width), f(rows, ff), f(rows, width), f(rows, width), f(rows, width), f(rows, width),
            D((7,)), D((2, 2)), D((2,)), D((2,)), D((16,)),
        ] + [pltpu.VMEM(a.shape, a.dtype) for a in given] + [D((8,))],
        compiler_params=pltpu.CompilerParams(collective_id=cid, has_side_effects=True, vmem_limit_bytes=62 << 20),
    )(*given, w_out, w_up, w_down, w_stream, *w_conv)


RZ, RY, RC = 4, 2, 2
PW = 384
PR = 48
LD, LX, LY, LH, LF = 2, 8, 12, 3, 25
HRING = LY + 1
PER, PK = 11, 3
JOB = 6


Group = collections.namedtuple("Group", ("left", "parts", "right", "col", "cols", "out", "lead", "base", "at"))
GRU, TABLE, TINY = 5, 4, 8


def piece_groups(taps):
    rows = [(6 + k, 2, 5, 0, 4, 7, i, 0) for i, k in enumerate(taps)]
    rows += [(4, 1, 4, 0, 2, 6, 0, 0), (5, 1, 4, 768, 2, 6, 1, 0), (3, 4, 3, 0, 2, 3, None, 0), (2, 1, 2, 0, 8, 2, None, 0), (1, 1, 1, 0, 2, 1, None, 0),
             (0, 1, 0, 0, 2, 0, None, 0), (0, 1, 6, 0, 4, 0, None, 2)]
    out, at = [], 0
    for r in rows:
        out.append(Group(*r, at))
        at += r[1] * r[4]
    return tuple(out), at


MISC = (((GRU, 0), (GRU, 1), (GRU, 2)), ((GRU, 3), (TABLE, 0), (TABLE, 1)), ((TABLE, 2), (TINY, 0), (None, 0)))


def reduce_kernel(npieces, groups, *refs):
    out_ref, dkv_ref = refs[24:26]
    width = refs[0].shape[1]
    dk_ref, dv_ref = dkv_ref.at[:, pl.ds(0, width)], dkv_ref.at[:, pl.ds(width, width)]
    qa_ref, dca_ref = refs[22:24]
    held, l_sem = refs[-23:-1], refs[-1]
    loads = [pltpu.make_async_copy(a, b, l_sem.at[k]) for k, (a, b) in enumerate(zip(refs[:22], held))]
    first = {}
    for g in groups:
        for k in (g.left, 9 + g.right):
            first.setdefault(k, g.at)

    for k in (8, 7, 6, 14, 20, 21, 4, 5, 13, 3, 12, 2, 11, 1, 10, 0, 9, 15, 16, 17, 18, 19):
        loads[k].start()
    lhs, rhs = held[:9], tuple(held[9:15]) + (dkv_ref,)
    emb_ref, dpre_ref, demb_ref, ids_ref, tiny_ref, kv_ref, stat_ref = held[15:]
    (lt, part, r0, held, r1, r2, up, dn, fin, fx,
     d_send, d_recv, x_send, x_recv, y_send, y_recv, u_send, u_recv, n_send, n_recv, f_send, f_recv, qbuf, cbuf, dk_acc, dv_acc, q_sem, c_sem) = refs[26:-23]
    dp = lax.axis_index("dp")
    me = lax.axis_index("seq")
    c = lax.rem(me, RC)
    y = lax.rem(lax.div(me, RC), RY)
    z = lax.div(me, RC * RY)

    def to(zz, yy, cc):
        return (dp, (zz * RY + yy) * RC + cc)

    sib, ynb, zup, zdn, xnb = to(z, y, 1 - c), to(z, 1 - y, c), to(z + 1, y, c), to(z - 1, y, c), (1 - dp, me)
    bar = pltpu.get_barrier_semaphore()
    for where in (sib, ynb, xnb):
        pl.semaphore_signal(bar, inc=1, device_id=where, device_id_type=MESH)
    pl.when(z > 0)(lambda: pl.semaphore_signal(bar, inc=1, device_id=zdn, device_id_type=MESH))
    pl.when(z < RZ - 1)(lambda: pl.semaphore_signal(bar, inc=1, device_id=zup, device_id_type=MESH))
    pl.semaphore_wait(bar, 3 + (z > 0).astype(jnp.int32) + (z < RZ - 1).astype(jnp.int32))

    def copy(src, dst, send, recv, where):
        return pltpu.make_async_remote_copy(src_ref=src, dst_ref=dst, send_sem=send, recv_sem=recv, device_id=where, device_id_type=MESH)

    def d2d(t):
        b, k = lax.rem(t, LD + 1), lax.rem(t, 2 * LD)
        return copy(part.at[b, :, :, 1 - c], r0.at[k], d_send.at[b], d_recv.at[k], sib)

    def far(t):
        return lax.div(t, PER) * PK + lax.div(lax.rem(t, PER), 3)

    def mi(t):
        m = lax.rem(t, PER)
        return lax.div(t, PER) * (PER - PK) + m - jnp.minimum(lax.div(m + dp, 3), PK)

    def across(t):
        return copy(held.at[lax.rem(t, HRING)], r1.at[far(t)], x_send.at[t], x_recv.at[t], xnb)

    def along_y(t):
        return copy(held.at[lax.rem(t, HRING), :, 1 - y], r2.at[mi(t)], y_send.at[t], y_recv.at[t], ynb)

    def final(t):
        return copy(fin.at[t], fx.at[t], f_send.at[t], f_recv.at[t], xnb)

    def go_up(t, k):
        src = r2.at[mi(t), pl.ds(k + 1, RZ - 1 - k)] if k == 0 else up.at[mi(t), pl.ds(k, RZ - 1 - k)]
        return copy(src, up.at[mi(t), pl.ds(k, RZ - 1 - k)], u_send.at[t], u_recv.at[t], zup)

    def from_below(t, k):
        ref = up.at[mi(t), pl.ds(k - 1, RZ - k)]
        return copy(ref, ref, u_send.at[t], u_recv.at[t], zdn)

    def go_down(t, k):
        src = r2.at[mi(t), pl.ds(0, k)] if k == RZ - 1 else dn.at[mi(t), pl.ds(0, k)]
        return copy(src, dn.at[mi(t), pl.ds(0, k)], n_send.at[t], n_recv.at[t], zdn)

    def from_above(t, k):
        ref = dn.at[mi(t), pl.ds(0, k + 1)]
        return copy(ref, ref, n_send.at[t], n_recv.at[t], zup)

    def add(a, b):
        return (a.astype(F32) + b.astype(F32)).astype(BF)

    def live(t):
        return jnp.logical_and(t >= 0, t < npieces)

    def route(t):
        m = lax.rem(t, PER)
        return jnp.where(m < 3 * PK, lax.rem(m, 3), 0)

    def mine(t):
        r = route(t)
        return jnp.logical_or(r == 0, r - 1 == dp)

    def finish(t):
        r = route(t)

        @pl.when(r == 0)
        def _():
            final(t).wait_recv()
            out_ref[t] = add(fin[t], fx[t])

        @pl.when(jnp.logical_and(r > 0, r - 1 == dp))
        def _():
            out_ref[t] = fin[t]

        @pl.when(jnp.logical_and(r > 0, r - 1 != dp))
        def _():
            final(t).wait_recv()
            out_ref[t] = fx[t]

        pl.when(mine(t))(lambda: final(t).wait_send())

    def sum_up(t):
        i = mi(t)
        for k in range(RZ):
            @pl.when(z == k)
            def _(k=k):
                if k > 0:
                    from_below(t, k).wait_recv()
                    for q in range(k + 1, RZ):
                        up[i, q - 1] = add(up[i, q - 1], r2[i, q])
                if k < RZ - 1:
                    go_up(t, k).start()

    def sum_down(t):
        i = mi(t)
        for k in range(RZ):
            @pl.when(z == k)
            def _(k=k):
                if k < RZ - 1:
                    from_above(t, k).wait_recv()
                    for q in range(k):
                        dn[i, q] = add(dn[i, q], r2[i, q])
                if k > 0:
                    go_down(t, k).start()

    def close(t):
        i = mi(t)
        for k in range(RZ):
            @pl.when(z == k)
            def _(k=k):
                total = r2[i, k].astype(F32)
                if k > 0:
                    total = total + up[i, k - 1].astype(F32)
                    go_down(t, k).wait_send()
                if k < RZ - 1:
                    total = total + dn[i, k].astype(F32)
                    go_up(t, k).wait_send()
                fin[t] = total.astype(BF)
        final(t).start()

    def join_y(t):
        i = mi(t)
        along_y(t).wait_recv()
        along_y(t).wait_send()
        h = lax.rem(t, HRING)
        for q in range(RZ):
            r2[i, q] = add(r2[i, q], held[h, q, y])

    def join_x(t):
        h = lax.rem(t, HRING)
        across(t).wait_recv()
        for q in range(RZ):
            held[h, q] = add(held[h, q], r1[far(t), q])
        along_y(t).start()

    def join_core(t):
        b, k = lax.rem(t, LD + 1), lax.rem(t, 2 * LD)
        h = lax.rem(t, HRING)
        d2d(t).wait_recv()
        d2d(t).wait_send()
        for q in range(RZ):
            held[h, q] = add(part[b, q, :, c], r0[k, q])
        pl.when(route(t) == 0)(lambda: along_y(t).start())
        pl.when(jnp.logical_not(mine(t)))(lambda: across(t).start())

    def turn(ref):
        n = ref.shape[0]
        for k in range(0, ref.shape[1], 384):
            lt[k // PR : k // PR + 8, :, :n] = ref[:, k : k + 384].T.reshape(8, PR, n)

    def make(t):
        b = lax.rem(t, LD + 1)
        for g in groups:
            @pl.when(jnp.logical_and(t >= g.at, t < g.at + g.parts * g.cols))
            def _(g=g):
                i = t - g.at
                j, cb = lax.div(i, g.cols), lax.rem(i, g.cols)

                @pl.when(i == 0)
                def _():
                    for k in (g.left, 9 + g.right):
                        if k < 15 and first[k] == g.at:
                            loads[k].wait()
                    turn(lhs[g.left])

                right = rhs[g.right][:, pl.ds(pl.multiple_of(g.col + cb * PW, PW), PW)]
                for q in range(RZ // 2):
                    left = jnp.concatenate([lt[(8 * q + s) * g.parts + j] for s in range(8)], 0)
                    part[b, 2 * q : 2 * q + 2] = dot(left, right).astype(BF).reshape(2, RY, RC, PR, PW)
        for m, trio in enumerate(MISC):
            @pl.when(t == npieces - len(MISC) + m)
            def _(m=m, trio=trio):
                if m == 0:
                    for k in range(15, 20):
                        loads[k].wait()
                for i, (kind, cb) in enumerate(trio):
                    if kind == GRU:
                        val = wgrad(emb_ref[...], dpre_ref[:, cb * PW : (cb + 1) * PW]).astype(BF).reshape(RZ, RY, RC, 16, PW)
                    elif kind == TABLE:
                        unit = lax.broadcasted_iota(jnp.int32, (ids_ref.shape[0], PW), 1) + cb * PW
                        hot = jnp.where(unit == ids_ref[...], 1.0, 0.0).astype(BF)
                        val = wgrad(demb_ref[...], hot).astype(BF).reshape(RZ, RY, RC, 16, PW)
                    elif kind == TINY:
                        val = tiny_ref[...].reshape(RZ, RY, RC, 16, PW)
                    else:
                        val = jnp.zeros((RZ, RY, RC, 16, PW), BF)
                    part[b, :, :, :, 16 * i : 16 * i + 16, :] = val
        d2d(t).start()

    pairs = HEADS // 2
    toks = kv_ref.shape[1]
    half = qa_ref.shape[1] // 2
    jobs = 2 * pairs * kv_ref.shape[0]

    def fetch(i):
        s, p, h = lax.div(i, 2 * pairs), lax.rem(lax.div(i, 2), pairs), lax.rem(i, 2)
        cols = pl.ds(pl.multiple_of(p * 2 * HDIM, 2 * HDIM), 2 * HDIM)
        part = pl.ds(pl.multiple_of(h * half, half), half)
        return (pltpu.make_async_copy(qa_ref.at[s, part, cols], qbuf.at[h], q_sem.at[h]), pltpu.make_async_copy(dca_ref.at[s, part, cols], cbuf.at[h], c_sem.at[h]))

    def key_work(i):
        s, p, h = lax.div(i, 2 * pairs), lax.rem(lax.div(i, 2), pairs), lax.rem(i, 2)
        at = pl.multiple_of(p * 2 * HDIM, 2 * HDIM)
        slots = half // toks

        @pl.when(i == 0)
        def _():
            loads[20].wait()
            loads[21].wait()


        @pl.when(i + 1 < jobs)
        def _():
            for load in fetch(i + 1):
                load.start()

        for load in fetch(i):
            load.wait()
        scale = HDIM ** -0.5
        queries, dctx = qbuf[h], cbuf[h]

        def spread(k):
            at = (s * pairs + p) * 4 + k
            one = lambda r: jnp.concatenate([stat_ref[h * slots + d, pl.ds(r, 1), :] for d in range(slots)], 1)
            return jnp.concatenate([jnp.broadcast_to(one(at), (toks, half)), jnp.broadcast_to(one(at + 1), (toks, half))], 0)

        prob = jnp.exp(dot_t(pair_rows(kv_ref[s, :, pl.ds(at + width, 2 * HDIM)] * scale), queries) - spread(0))
        dv = dot(prob.astype(BF), dctx)
        dprob = dot_t(pair_rows(kv_ref[s, :, pl.ds(at + 2 * width, 2 * HDIM)]), dctx)
        dk = dot((prob * (dprob - spread(2))).astype(BF), queries)

        @pl.when(h == 0)
        def _():
            dk_acc[...] = dk
            dv_acc[...] = dv

        @pl.when(h == 1)
        def _():
            rows = pl.ds(pl.multiple_of(s * toks, toks), toks)
            cols = pl.ds(at, 2 * HDIM)
            dk_ref[rows, cols] = (pair_lanes(dk_acc[...] + dk) * scale).astype(BF)
            dv_ref[rows, cols] = pair_lanes(dv_acc[...] + dv).astype(BF)

    for load in fetch(0):
        load.start()

    def tick(T, _):
        def do(t, f, cond=None):
            ok = live(t)
            pl.when(ok if cond is None else jnp.logical_and(ok, cond(t)))(lambda: f(t))

        do(T - LF, finish)
        do(T - LY - z * LH, sum_up, mine)
        do(T - LY - (RZ - 1 - z) * LH, sum_down, mine)
        do(T - LY - (RZ - 1) * LH, close, mine)
        do(T - LY + 1, join_y, mine)
        do(T - LX, join_x, lambda t: jnp.logical_and(route(t) > 0, mine(t)))
        do(T - LX, lambda t: across(t).wait_send(), lambda t: jnp.logical_not(mine(t)))
        do(T - LD, join_core)
        do(T, make)
        job = T - JOB
        pl.when(jnp.logical_and(job >= 0, job < jobs))(lambda: key_work(job))
        return 0

    lax.fori_loop(0, npieces + LF + 1, tick, 0)


def finish_kernel(groups, *refs):
    held, l_sem = refs[16:21], refs[21]
    loads = [pltpu.make_async_copy(a, b, l_sem.at[k]) for k, (a, b) in enumerate(zip(refs[:5], held))]
    for load in loads:
        load.start()
    pieces, dq, dkv, w, base = held
    outs = refs[5:16]
    loads[0].wait()
    for g in groups:
        for j in range(g.parts):
            for cb in range(g.cols):
                rows, cols = slice(j * PR, (j + 1) * PR), slice((g.base + cb) * PW, (g.base + cb + 1) * PW)
                val = pieces[g.at + j * g.cols + cb].astype(F32)
                if g.lead is None:
                    outs[g.out][rows, cols] = val
                else:
                    outs[g.out][g.lead, rows, cols] = val
    first = groups[-1].at + groups[-1].parts * groups[-1].cols
    bias, norms, dinput = outs[8:]
    for m, trio in enumerate(MISC):
        for i, (kind, cb) in enumerate(trio):
            val = pieces[first + m, 16 * i : 16 * i + 16, :].astype(F32)
            if kind == TINY:
                bias[...] = val[0:1, : bias.shape[1]]
                for k in range(4):
                    norms[k] = val[1 + 2 * k : 3 + 2 * k, : norms.shape[2]]
            elif kind is not None:
                n = min(PW, outs[kind].shape[1] - cb * PW)
                outs[kind][:, cb * PW : cb * PW + n] = val[:, :n]
    n = dq.shape[1]
    for load in loads[1:]:
        load.wait()
    dinput[...] = base[...] + dot_t(dq[...], w[:, :n]) + dot_t(dkv[:, :n], w[:, n : 2 * n]) + dot_t(dkv[:, n:], w[:, 2 * n :])


def reduce_all(lhs, rhs, emb, dpre, demb, ids, kv, stat, queries, dctx, w_qkv, dsum, g_bias, g_norms, n_table, nseq, cid, taps=(0, 1, 2)):
    width = lhs[0].shape[1]
    per = g_bias.shape[0] // nseq
    tiny = jnp.concatenate([
        jnp.pad(g_bias.reshape(nseq, 1, per), ((0, 0), (0, 0), (0, PW - per))),
        jnp.pad(g_norms.reshape(8, nseq, -1).transpose(1, 0, 2), ((0, 0), (0, 7), (0, PW - width // nseq))),
    ], 1).astype(BF)
    groups, npieces = piece_groups(taps)
    npieces += len(MISC)
    dense = -(-npieces // PER) * (PER - PK)
    D = pltpu.SemaphoreType.DMA
    v = lambda *s: pltpu.VMEM(s, BF)
    spec = pl.BlockSpec(memory_space=pltpu.VMEM)
    operands = (*lhs, *rhs, emb, dpre, demb, ids, tiny, kv, stat)
    pieces, dkv = pl.pallas_call(
        functools.partial(reduce_kernel, npieces, groups),
        out_shape=[jax.ShapeDtypeStruct((npieces, PR, PW), BF), jax.ShapeDtypeStruct((lhs[0].shape[0], 2 * width), BF)],
        in_specs=[pl.BlockSpec(memory_space=pl.ANY)] * 24,
        out_specs=[spec] * 2,
        scratch_shapes=[
            v(64, PR, lhs[0].shape[0]),
            v(LD + 1, RZ, RY, RC, PR, PW), v(2 * LD, RZ, RY, PR, PW), v(HRING, RZ, RY, PR, PW), v(PK * (npieces // PER + 1), RZ, RY, PR, PW),
            v(dense, RZ, PR, PW), v(dense, RZ - 1, PR, PW), v(dense, RZ - 1, PR, PW), v(npieces, PR, PW), v(npieces, PR, PW),
            D((LD + 1,)), D((2 * LD,)), D((npieces,)), D((npieces,)), D((npieces,)), D((npieces,)),
            D((npieces,)), D((npieces,)), D((npieces,)), D((npieces,)), D((npieces,)), D((npieces,)),
            v(2, queries.shape[1] // 2, 2 * HDIM), v(2, queries.shape[1] // 2, 2 * HDIM),
            pltpu.VMEM((2 * kv.shape[1], 2 * HDIM), F32), pltpu.VMEM((2 * kv.shape[1], 2 * HDIM), F32), D((2,)), D((2,)),
        ] + [pltpu.VMEM(a.shape, a.dtype) for a in operands] + [D((len(operands),))],
        compiler_params=pltpu.CompilerParams(collective_id=cid, has_side_effects=True, vmem_limit_bytes=62 << 20),
    )(*operands, queries, dctx)
    f = lambda *s: jax.ShapeDtypeStruct(s, F32)
    wide = 2 * width
    share = width // nseq
    return pl.pallas_call(
        functools.partial(finish_kernel, groups),
        out_shape=[
            f(share, 3 * width), f(share, width), f(share, 4 * width), f(4 * share, width), f(16, n_table), f(16, 4 * PW),
            f(2, share, width), f(3, 2 * share, wide), f(1, per), f(4, 2, share), f(*dsum.shape),
        ],
        in_specs=[pl.BlockSpec(memory_space=pl.ANY)] * 5,
        out_specs=[spec] * 11,
        scratch_shapes=[pltpu.VMEM(a.shape, a.dtype) for a in (pieces, rhs[0], dkv, w_qkv, dsum)] + [D((5,))],
        compiler_params=vmem(62),
    )(pieces, rhs[0], dkv, w_qkv, dsum)


def scatter(total, axis):
    part = lax.psum_scatter(total, "seq", scatter_dimension=axis, tiled=True)
    return lax.psum(part, "dp").astype(F32)


def body(tokens, char_ids, span_lengths, script_group, w_qkv, w_out, w_up, w_down, char_table, w_gru, gru_bias, w_stream, w_conv, norms, grad_token, grad_char):
    nseq, planes = lax.axis_size("seq"), lax.axis_size("dp")
    seqs, toks, width = tokens.shape
    chars = char_ids.shape[1]
    rows = seqs * toks
    bias_n, norm_n = gru_bias.shape[0], norms.shape[2]
    small = jnp.concatenate([gru_bias, norms.reshape(-1)])
    small = jnp.pad(small, (0, 2048 - small.shape[0])).reshape(16, 128)
    conv0, w_down, conv1, conv2, w_out, w_stream, w_qkv, w_gru, char_table, small = gather(
        [(w_conv, 0, 1, 0), (w_down, 0, 1, None), (w_conv, 0, 2, 1), (w_conv, 0, 2, 2), (w_out, 0, 0, None), (w_stream, 1, 0, None), (w_qkv, 0, 0, None),
         (w_gru, 0, 0, None), (char_table, 0, 0, None), (small, 0, 0, None)], 1, planes, nseq
    )
    w_up, small = lax.optimization_barrier((w_up, small))
    w_up = lax.all_gather(w_up, "seq", axis=0, tiled=True)
    w_conv = (conv0, conv1, conv2)
    small = small.reshape(nseq, 2048)
    bias = small[:, :bias_n].reshape(-1).astype(F32)
    nrm = small[:, bias_n : bias_n + 8 * norm_n].reshape(nseq, 4, 2, norm_n).transpose(1, 2, 0, 3).reshape(4, 2, width).astype(F32)

    x_low = tokens.reshape(rows, width)
    qkv = dot(x_low, w_qkv).astype(BF)
    qkv3 = qkv.reshape(seqs, toks, 3 * width)

    char_rows = (char_ids + script_group[:, None] * GROUP_CHARS).reshape(seqs * chars, 1)
    span = span_lengths[:, 0]
    span_ends = jnp.cumsum(span, -1)
    starts = span_ends - span
    ends_col = jnp.stack([starts, span_ends], -1).reshape(rows, 2)
    ends_row = jnp.pad(jnp.stack([starts, span_ends], 1), ((0, 0), (0, 6), (0, 0))).reshape(seqs * 8, toks)
    block = pltpu.VMEM((2 * HB, chars, 128), F32)
    full = lambda *d: jax.ShapeDtypeStruct(d, F32)
    keys, values, tot_all, pooled, chunk, pre, prev, embedded = gather_with(
        functools.partial(forward_run, seqs), [(qkv3, 1, 0, (width, width)), (qkv3, 1, 0, (2 * width, width))],
        2, planes, nseq, (char_rows, char_table, w_gru, bias.reshape(1, -1), ends_col), (), [full(rows, width), full(seqs * 4 * NCH, HG)],
        [full(seqs * chars, 4 * HG), full(seqs * chars, width), jax.ShapeDtypeStruct((seqs * chars, char_table.shape[0]), BF)], [block] * 4,
    )
    own_q = qkv3[..., :width]
    queries = lax.all_gather(own_q, "seq", axis=1, tiled=True)

    ctx3, ctx_low3, lse = attention_fwd(qkv3, keys, values)
    context, context_low = ctx3.reshape(rows, width), ctx_low3.reshape(rows, width)
    (out_token, out_char, normed_low, hidden, state_low, pooled_low, mprev, merged, mnext, dmixed_low, dfused, dlowered, draised_low, dattended,
     dinput_sum, dpooled, dnorm, dctx3, col, stat) = middle(
        seqs, x_low, context_low, context, lse, pooled, grad_token.reshape(rows, width), grad_char.reshape(rows, width), nrm.reshape(8, width),
        w_out, w_up, w_down, w_stream, w_conv, 5
    )
    length = nseq * toks
    dctx_all, stat_all, _, dbias, dq, dembed, dpre = gather_with(
        functools.partial(backward_run, seqs), [(dctx3, 1, 0, None), (stat, 0, 0, None)], 3, planes, nseq,
        (pre, prev, chunk, tot_all, dpooled, ends_row, own_q, dctx3, col, w_gru), (keys, values),
        [full(seqs * 8, 4 * HG), jax.ShapeDtypeStruct((seqs, toks, width), BF), jax.ShapeDtypeStruct(embedded.shape, BF)],
        [jax.ShapeDtypeStruct((seqs * chars, 4 * HG), BF)],
        [pltpu.VMEM((seqs * chars, width), F32), pltpu.VMEM((seqs * 2 * NCH, HG), F32)] + [block] * 2
        + [pltpu.VMEM((2, length, 2 * HDIM), BF)] * 2 + [pltpu.SemaphoreType.DMA((2,))] * 2,
    )
    g_bias = dbias.reshape(seqs, 8, 4 * HG)[:, 0].sum(0)

    g_norms = dnorm.reshape(4, 2, width)
    shape = (seqs, toks, width)
    if seq_dims(nseq) == (RZ, RY, RC) and planes == 2:
        lhs = (x_low, context_low, normed_low, hidden, state_low, pooled_low, mprev, merged, mnext)
        rhs = (dq.reshape(rows, width), dattended, draised_low, dlowered, dfused, dmixed_low)
        *owned, dinputs = reduce_all(
            lhs, rhs, embedded, dpre, dembed, char_rows, qkv3, stat_all.reshape(nseq, -1, toks), queries, dctx_all, w_qkv, dinput_sum, g_bias, g_norms, VOCAB_CHAR, nseq, 4
        )
        owned[8] = owned[8].reshape(-1)
        owned = [owned[k] for k in (0, 1, 2, 3, 4, 5, 8, 6, 7, 9)]
        owned = tuple(owned)
    else:
        stat_all = stat_all.reshape(nseq, seqs, HEADS // 2, 4, toks).transpose(1, 2, 3, 0, 4).reshape(seqs, HEADS // 2, 4, nseq * toks)
        dk, dv = attention_bwd(qkv3, queries, dctx_all, stat_all)
        dqkv = jnp.concatenate([dq, dk, dv], -1).reshape(rows, 3 * width)
        dinputs = dinput_sum + dot_t(dqkv, w_qkv)
        g_stream = [wgrad(state_low, dfused[:, :width]), wgrad(pooled_low, dfused[:, width:])]
        owned = (
            scatter(wgrad(x_low, dqkv).astype(BF), 0),
            scatter(wgrad(context_low, dattended).astype(BF), 0),
            scatter(wgrad(normed_low, draised_low).astype(BF), 0),
            scatter(wgrad(hidden, dlowered).astype(BF), 0),
            scatter(wgrad(dembed, (char_rows == jnp.arange(VOCAB_CHAR, dtype=jnp.int32)).astype(BF)).astype(BF), 0),
            scatter(wgrad(embedded, dpre).astype(BF), 0),
            scatter(g_bias.astype(BF), 0),
            scatter(jnp.stack(g_stream).astype(BF), 1),
            scatter(jnp.stack([wgrad(m, dmixed_low) for m in (mprev, merged, mnext)]).astype(BF), 1),
            scatter(g_norms.astype(BF), 2),
        )
    return (
        out_token.reshape(shape),
        out_char.reshape(shape),
        dinputs.reshape(shape),
    ) + owned


def solution(mesh):
    placed = (
        P("dp", "seq", None),
        P("dp", "seq"),
        P("dp", "seq", None),
        P("dp"),
        P("seq", None),
        P("seq", None),
        P("seq", None),
        P("seq", None),
        P("seq", None),
        P("seq", None),
        P("seq"),
        P(None, "seq", None),
        P(None, "seq", None),
        P(None, None, "seq"),
        P("dp", "seq", None),
        P("dp", "seq", None),
    )
    return jax.shard_map(
        body,
        mesh=mesh,
        in_specs=placed,
        out_specs=(
            P("dp", "seq", None),
            P("dp", "seq", None),
            P("dp", "seq", None),
            P("seq", None),
            P("seq", None),
            P("seq", None),
            P("seq", None),
            P("seq", None),
            P("seq", None),
            P("seq"),
            P(None, "seq", None),
            P(None, "seq", None),
            P(None, None, "seq"),
        ),
        check_vma=False,
    )
```
